32 devices in a mesh: seq: 4 (over y, x), fsdp: 8 (over z, core).
Axes of the slice: x: 2, y: 2, z: 4, core: 2. Of those that a mesh axis runs over, the one named last changes fastest.
Arguments:
- tokens: bfloat16 [8, 1024, 2048], P('fsdp', 'seq'), may hold values from -6 to 6
- positions: int32 [8, 1024], P('fsdp', 'seq'), may hold values from 0 to 1023, as said below
- w_qkv: bfloat16 [2048, 6144], P(('seq', 'fsdp')), may hold values from -0.125 to 0.125
- w_out: bfloat16 [2048, 2048], P(('seq', 'fsdp')), may hold values from -1 to 1
- gain_attn: bfloat16 [2048], P(('seq', 'fsdp')), may hold values from 0.25 to 1.75
- w_gate_up: bfloat16 [2048, 16384], P(('seq', 'fsdp')), may hold values from -0.125 to 0.125
- w_down: bfloat16 [2048, 8192], P(('seq', 'fsdp')), may hold values from -0.0625 to 0.0625
- gain_mlp: bfloat16 [2048], P(('seq', 'fsdp')), may hold values from 0.25 to 1.75
- cotangent: bfloat16 [8, 1024, 2048], P('fsdp', 'seq'), may hold values from -6 to 6
Outputs:
- layer_out: bfloat16 [8, 1024, 2048], P('fsdp', 'seq')
- input_grad: float32 [8, 1024, 2048], P('fsdp', 'seq')
- grad_qkv: float32 [2048, 6144], P(('seq', 'fsdp'))
- grad_out: float32 [2048, 2048], P(('seq', 'fsdp'))
- grad_gain_attn: float32 [2048], P(('seq', 'fsdp'))
- grad_gate_up: float32 [2048, 16384], P(('seq', 'fsdp'))
- grad_down: float32 [2048, 8192], P(('seq', 'fsdp'))
- grad_gain_mlp: float32 [2048], P(('seq', 'fsdp'))
The draws below stay inside these ranges and needn't reach their ends.
Inputs may be any that keep to these rules, and one draw needn't show every extreme that they name: `positions`: each sequence packs documents; a token's position counts from the start of its document. One sequence, drawn from the seed, is a single document.
All inputs are finite; a program needn't handle non-finite values.
Results may differ from the reference program's by a relative error of at most 0.014.
Values may be sent and summed in bfloat16 or wider, within the bound.
A program may use at most 1.0625 GiB of HBM per device.

```python
import math
from functools import partial
import jax
import jax.numpy as jnp
from jax import lax

D = 2048
HEADS = 32
HEAD_DIM = 64
FF = 8192
LENGTH = 1024
SEQS = 8


def draw_positions(key, part):
    key = jax.random.fold_in(key, 11)
    key_marks, key_whole = jax.random.split(key)
    marks = jax.random.randint(key_marks, (SEQS, LENGTH), 0, LENGTH) < 4
    whole = jax.random.randint(key_whole, (), 0, SEQS)
    index = jnp.arange(LENGTH, dtype=jnp.int32)
    seq_index = jnp.arange(SEQS, dtype=jnp.int32)
    marks = marks & (seq_index[:, None] != whole) & (index[None, :] > 0)
    starts = lax.cummax(jnp.where(marks, index[None, :], 0), axis=1)
    return (index[None, :] - starts).astype(jnp.int32)


def raised(entries, rng, source, target, shards_of, factor):
    def block_of(axis_at):
        return (jnp.arange(entries.shape[axis_at]) // (entries.shape[axis_at] // shards_of)).reshape((-1,) + (1,) * (entries.ndim - 1 - axis_at))

    first = jax.random.permutation(rng, shards_of)[block_of(target)]
    far = (block_of(target) + shards_of // 2) % shards_of
    return jnp.where((block_of(source) == first) | (block_of(source) == far), factor * entries, entries)


def shard_levels(stream_key, dims, cuts, low, high):
    def one(axis_at, blocks):
        heights = jax.random.uniform(jax.random.fold_in(jax.random.fold_in(stream_key, 6), axis_at), (blocks,), jnp.float32, low / len(cuts), high / len(cuts))
        return jnp.repeat(jnp.exp(heights), dims[axis_at] // blocks).reshape((-1,) + (1,) * (len(dims) - axis_at - 1))

    gain = one(*cuts[0])
    for cut in cuts[1:]:
        gain = gain * one(*cut)
    return gain


def scatter_about(stream_key, extent, scale, reach, shards=(), kind=jnp.bfloat16):
    factor_of = shard_levels(stream_key, extent, shards, -0.22, 0.18) if shards else 1.0
    values = jax.random.normal(stream_key, extent, jnp.float32) * scale * factor_of
    return jnp.minimum(jnp.maximum(values, -reach), reach).astype(kind)


def gaussian_with(rng, dims, spread, most, cuts, heavy, kind=jnp.bfloat16):
    array = spread * jax.random.normal(rng, dims, jnp.float32)
    if cuts:
        array = array * shard_levels(rng, dims, cuts, -0.22, 0.18)
    return jnp.clip(raised(array, jax.random.fold_in(rng, 3), *heavy), -most, most).astype(kind)


def setup_inputs(seed: int = 0) -> dict:
    arg_keys = jax.random.split(jax.random.key(seed), 10)
    tokens = scatter_about(arg_keys[0], (SEQS, LENGTH, D), 1.0, 6.0, ((0, 8), (1, 4)))
    positions = draw_positions(jax.random.fold_in(arg_keys[9], 71), 0)
    w_qkv = scatter_about(arg_keys[2], (D, 3 * D), D ** -0.5, 0.125, ((0, 32),))
    w_out = scatter_about(arg_keys[3], (D, D), (20 * D // LENGTH) ** -0.5, 1.0, ((0, 32),))
    gain_attn = jnp.clip(1.0 + 0.15 * jax.random.normal(arg_keys[4], (D,), jnp.float32), 0.25, 1.75).astype(jnp.bfloat16)
    w_gate_up = scatter_about(arg_keys[5], (D, 2 * FF), D ** -0.5, 0.125, ((0, 32),))
    w_down = scatter_about(arg_keys[6], (D, FF), FF ** -0.5, 0.0625, ((0, 32),))
    gain_mlp = jnp.clip(1.0 + 0.15 * jax.random.normal(arg_keys[7], (D,), jnp.float32), 0.25, 1.75).astype(jnp.bfloat16)
    cotangent = gaussian_with(arg_keys[8], (SEQS, LENGTH, D), 1.0, 6.0, ((0, 8), (1, 4)), (0, 2, 8, 2.0))
    return {"tokens": tokens, "positions": positions, "w_qkv": w_qkv, "w_out": w_out, "gain_attn": gain_attn, "w_gate_up": w_gate_up, "w_down": w_down, "gain_mlp": gain_mlp, "cotangent": cotangent}


EPS = 1e-05
ROPE_BASE = 130000.0
HIGHEST = lax.Precision.HIGHEST

@jax.custom_vjp
def low(v):
    return lax.optimization_barrier(v.astype(jnp.bfloat16)).astype(jnp.float32)

@jax.custom_vjp
def low_back(v):
    return v

def low_keep(v):
    return (low(v), None)

def low_pass(kept, grad):
    return (grad,)

def back_keep(v):
    return (v, None)

def back_low(kept, grad):
    return (low(grad),)
low.defvjp(low_keep, low_pass)
low_back.defvjp(back_keep, back_low)

def rope_tables(places, width):
    indices = jnp.arange(width // 2).astype(jnp.float32)
    inverse = ROPE_BASE ** (-2.0 * indices / width)
    angles = places.astype(jnp.float32)[:, None] * inverse[None, :]
    return (jnp.cos(angles), jnp.sin(angles))

def rotate(values, cosine, sine, direction):
    row_count = values.shape[0]
    halves = values.reshape(row_count, -1, 2, cosine.shape[1])
    leading = halves[:, :, 0]
    trailing = halves[:, :, 1]
    cos_rows = cosine[:, None, :]
    sin_rows = direction * sine[:, None, :]
    turned = jnp.stack([leading * cos_rows - trailing * sin_rows, trailing * cos_rows + leading * sin_rows], 2)
    return turned.reshape(row_count, -1)

@partial(jax.checkpoint, static_argnums=(3,))
def attend_block(queries, keys_seen, values_seen, offset):
    scale = 1.0 / math.sqrt(queries.shape[-1])
    scores = jnp.einsum('qhd,khd->hqk', queries, keys_seen, precision=HIGHEST) * scale
    scores = low_back(scores)
    row_index = offset + jnp.arange(queries.shape[0])
    col_index = jnp.arange(keys_seen.shape[0])
    scores = jnp.where(col_index[None, None, :] <= row_index[None, :, None], scores, -1e+30)
    highest = lax.optimization_barrier(jnp.max(scores, -1, keepdims=True))
    weights = jnp.exp(scores - highest)
    probs = weights / lax.optimization_barrier(jnp.sum(weights, -1, keepdims=True))
    return jnp.einsum('hqk,khd->qhd', low(probs), values_seen, precision=HIGHEST)

def layer(inputs, places, w_qkv, w_out, gain_attn, w_gate_up, w_down, gain_mlp):
    length = inputs.shape[0]
    normed = inputs * lax.rsqrt(lax.optimization_barrier(jnp.mean(inputs * inputs, -1, keepdims=True)) + EPS)
    acts = low(normed * gain_attn)
    mixed = jnp.dot(acts, w_qkv, precision=HIGHEST)
    cosine, sine = rope_tables(places, HEAD_DIM)
    queries = low_back(low(rotate(low_back(mixed[:, :D]), cosine, sine, 1.0)))
    keys_rot = low_back(low(rotate(low_back(mixed[:, D:2 * D]), cosine, sine, 1.0)))
    values_all = low_back(low(mixed[:, 2 * D:]))
    head_q = queries.reshape(length, HEADS, HEAD_DIM)
    head_k = keys_rot.reshape(length, HEADS, HEAD_DIM)
    head_v = values_all.reshape(length, HEADS, HEAD_DIM)
    block = min(512, length)
    pieces = []
    for index in range(length // block):
        finish = (index + 1) * block
        pieces.append(attend_block(head_q[index * block:finish], head_k[:finish], head_v[:finish], index * block))
    attended = low_back(low(jnp.concatenate(pieces, 0).reshape(length, D)))
    branch = low_back(jnp.dot(attended, w_out.T, precision=HIGHEST))
    middle = inputs + branch
    normed_mid = middle * lax.rsqrt(lax.optimization_barrier(jnp.mean(middle * middle, -1, keepdims=True)) + EPS)
    acts_mid = low(normed_mid * gain_mlp)
    gate = low_back(jnp.dot(acts_mid, w_gate_up[:, :FF], precision=HIGHEST))
    upper = low_back(jnp.dot(acts_mid, w_gate_up[:, FF:], precision=HIGHEST))
    hidden = low(gate * jax.nn.sigmoid(gate) * upper)
    mlp_out = low_back(jnp.dot(hidden, w_down.T, precision=HIGHEST))
    return middle + mlp_out

def reference(tokens, positions, w_qkv, w_out, gain_attn, w_gate_up, w_down, gain_mlp, cotangent):
    params = tuple((item.astype(jnp.float32) for item in (w_qkv, w_out, gain_attn, w_gate_up, w_down, gain_mlp)))

    def one_sequence(running, items):
        inputs, places, upstream = items

        def forward(inputs_f, p_qkv, p_out, p_ga, p_gu, p_down, p_gm):
            return layer(inputs_f, places, p_qkv, p_out, p_ga, p_gu, p_down, p_gm)
        result, pull = jax.vjp(forward, inputs.astype(jnp.float32), *params)
        grads = pull(upstream.astype(jnp.float32))
        running = tuple((held + fresh for held, fresh in zip(running, grads[1:])))
        return (running, (result.astype(jnp.bfloat16), grads[0]))
    zeros = tuple((jnp.zeros(item.shape, jnp.float32) for item in params))
    running, stacked = lax.scan(one_sequence, zeros, (tokens, positions, cotangent))
    return (stacked[0], stacked[1], running[0], running[1], running[2], running[3], running[4], running[5])
```

```python
import math

import jax
import jax.numpy as jnp
from jax import lax
from jax.sharding import PartitionSpec as P

HEAD_DIM = 64
EPS = 1e-05
ROPE_BASE = 130000.0
BF = jnp.bfloat16
F32 = jnp.float32


def after(value, *others):
    return lax.optimization_barrier((value,) + others)[0]


def rope_tables(places, width):
    indices = jnp.arange(width // 2).astype(F32)
    inverse = ROPE_BASE ** (-2.0 * indices / width)
    angles = places.astype(F32)[:, None] * inverse[None, :]
    return (jnp.cos(angles), jnp.sin(angles))


def rotate(values, cosine, sine, direction):
    row_count = values.shape[0]
    halves = values.reshape(row_count, -1, 2, cosine.shape[1])
    leading = halves[:, :, 0]
    trailing = halves[:, :, 1]
    cos_rows = cosine[:, None, :]
    sin_rows = direction * sine[:, None, :]
    turned = jnp.stack(
        [leading * cos_rows - trailing * sin_rows, trailing * cos_rows + leading * sin_rows], 2
    )
    return turned.reshape(row_count, -1)


def causal_mask(offset, block_rows, key_count):
    row_index = offset + jnp.arange(block_rows)
    return jnp.arange(key_count)[None, :] <= row_index[:, None]


def head_forward(items):
    queries, keys_all, values_all = items
    length = queries.shape[0]
    block = min(512, length)
    scale = 1.0 / math.sqrt(queries.shape[1])
    outputs = []
    log_parts = []
    for index in range(length // block):
        begin = index * block
        finish = begin + block
        scores = (
            jnp.einsum(
                "qd,kd->qk", queries[begin:finish], keys_all[:finish], preferred_element_type=F32
            )
            * scale
        )
        scores = jnp.where(causal_mask(begin, block, finish), scores, -1e30)
        highest = jnp.max(scores, -1, keepdims=True)
        weights = jnp.exp(scores - highest)
        summed = jnp.sum(weights, -1, keepdims=True)
        probs = (weights / summed).astype(BF)
        outputs.append(
            jnp.dot(probs, values_all[:finish], preferred_element_type=F32).astype(BF)
        )
        log_parts.append((highest + jnp.log(summed))[:, 0])
    return (jnp.concatenate(outputs, 0), jnp.concatenate(log_parts, 0))


def head_backward(items):
    queries, keys_all, values_all, grad_rows, log_totals = items
    length = queries.shape[0]
    block = min(512, length)
    scale = 1.0 / math.sqrt(queries.shape[1])
    grad_keys = jnp.zeros(keys_all.shape, F32)
    grad_values = jnp.zeros(values_all.shape, F32)
    grad_queries = []
    for index in range(length // block):
        begin = index * block
        finish = begin + block
        query_rows = queries[begin:finish]
        upstream = grad_rows[begin:finish]
        scores = (
            jnp.einsum("qd,kd->qk", query_rows, keys_all[:finish], preferred_element_type=F32)
            * scale
        )
        scores = jnp.where(causal_mask(begin, block, finish), scores, -1e30)
        probs = jnp.exp(scores - log_totals[begin:finish, None])
        grad_probs = jnp.einsum(
            "qd,kd->qk", upstream, values_all[:finish], preferred_element_type=F32
        )
        inner = jnp.sum(probs * grad_probs, -1, keepdims=True)
        grad_scores = (probs * (grad_probs - inner)).astype(BF)
        grad_queries.append(
            (jnp.dot(grad_scores, keys_all[:finish], preferred_element_type=F32) * scale).astype(BF)
        )
        grad_keys = grad_keys.at[:finish].add(
            jnp.einsum("qk,qd->kd", grad_scores, query_rows, preferred_element_type=F32) * scale
        )
        grad_values = grad_values.at[:finish].add(
            jnp.einsum("qk,qd->kd", probs.astype(BF), upstream, preferred_element_type=F32)
        )
    return (
        jnp.concatenate(grad_queries, 0),
        grad_keys.astype(BF),
        grad_values.astype(BF),
    )


class Group:
    def __init__(self, mesh):
        self.seqs = mesh.shape["seq"]
        self.chips = mesh.shape["fsdp"] // 2
        self.seq = lax.axis_index("seq")
        place = lax.axis_index("fsdp")
        self.chip = place // 2
        self.core = place % 2

    def across(self, value, step):
        return lax.ppermute(value, "seq", [(s, s ^ step) for s in range(self.seqs)])

    def sibling(self, value):
        return lax.ppermute(value, "fsdp", [(f, f ^ 1) for f in range(2 * self.chips)])

    def onward(self, value):
        count = 2 * self.chips
        return lax.ppermute(value, "fsdp", [(f, (f + 2) % count) for f in range(count)])

    def gather_seq(self, value):
        whole = jnp.zeros((self.seqs,) + value.shape, value.dtype)
        parts = [value] + [self.across(value, step) for step in range(1, self.seqs)]
        for step, part in enumerate(parts):
            whole = lax.dynamic_update_index_in_dim(whole, part, self.seq ^ step, 0)
        return whole

    def swap_seq(self, blocks, axis):
        whole = jnp.zeros_like(blocks)
        for step in range(self.seqs):
            part = lax.dynamic_index_in_dim(blocks, self.seq ^ step, axis, keepdims=True)
            if step:
                part = self.across(part, step)
            start = [0] * blocks.ndim
            start[axis] = self.seq ^ step
            whole = lax.dynamic_update_slice(whole, part, start)
        return whole

    def sum_seq(self, blocks):
        total = lax.dynamic_index_in_dim(blocks, self.seq, 0, keepdims=False)
        sent = blocks.astype(BF)
        for step in range(1, self.seqs):
            part = lax.dynamic_index_in_dim(sent, self.seq ^ step, 0, keepdims=False)
            total = total + self.across(part, step).astype(F32)
        return total


class Line:
    def __init__(self, group):
        self.group = group
        self.flying = []

    def onward(self, value):
        if len(self.flying) >= 2:
            value = after(value, self.flying[-2])
        got = self.group.onward(value)
        self.flying.append(got)
        return got

    def gather(self, pieces):
        group = self.group
        wholes = []
        for piece in pieces:
            seqs, rows, cols = piece.shape
            wholes.append(jnp.zeros((seqs, group.chips, 2, rows, cols), piece.dtype))
        current = list(pieces)
        for hop in range(group.chips):
            for i in range(len(pieces)):
                if hop:
                    current[i] = self.onward(current[i])
                other = group.sibling(current[i])
                origin = (group.chip - hop) % group.chips
                for part, core in ((current[i], group.core), (other, 1 - group.core)):
                    wholes[i] = lax.dynamic_update_slice(
                        wholes[i], part[:, None, None], (0, origin, core, 0, 0)
                    )
        return [w.reshape(-1, w.shape[-1]) for w in wholes]

    def reduce(self, terms, rows):
        group = self.group
        held = []
        for term in terms:
            split = term.reshape(group.seqs, group.chips, 2, rows, term.shape[-1])
            given = lax.dynamic_index_in_dim(split, 1 - group.core, 2, keepdims=False)
            kept = lax.dynamic_index_in_dim(split, group.core, 2, keepdims=False)
            got = group.sibling(given)
            held.append((kept.astype(F32) + got.astype(F32)).astype(BF))

        def block(value, hop):
            return lax.dynamic_index_in_dim(
                value, (group.chip - 1 - hop) % group.chips, 1, keepdims=False
            )

        totals = [block(value, 0) for value in held]
        for hop in range(1, group.chips):
            for i in range(len(terms)):
                got = self.onward(totals[i].astype(BF))
                totals[i] = got.astype(F32) + block(held[i], hop).astype(F32)
        return totals


def dot(left, right):
    return jnp.dot(left, right, preferred_element_type=F32)


def dot_rows(left, right):
    return jnp.einsum("tn,tc->nc", left, right, preferred_element_type=F32)


def dot_cols(left, right):
    return jnp.einsum("tc,nc->tn", left, right, preferred_element_type=F32)


def per_device(
    mesh, tokens, positions, w_qkv, w_out, gain_attn, w_gate_up, w_down, gain_mlp, cotangent
):
    group = Group(mesh)
    line = Line(group)
    seqs = group.seqs
    inputs = tokens[0].astype(F32)
    token_count, width = inputs.shape
    length = token_count * seqs
    ff_width = w_down.shape[1]
    rows = w_qkv.shape[0]
    head_cols = width // seqs
    ff_cols = ff_width // seqs

    gain_one = gain_attn.astype(F32)[:, None]
    gain_two = gain_mlp.astype(F32)[:, None]
    qkv_scaled = (w_qkv.astype(F32) * gain_one).astype(BF).reshape(rows, 3, seqs, head_cols)
    gate_up_scaled = (w_gate_up.astype(F32) * gain_two).astype(BF).reshape(rows, 2, seqs, ff_cols)

    def to_columns(weights):
        return group.swap_seq(jnp.moveaxis(weights, 1, 0), 0)

    qkv_mine = to_columns(jnp.moveaxis(qkv_scaled, 1, 2).reshape(rows, seqs, 3 * head_cols))
    out_mine = to_columns(w_out.reshape(rows, seqs, head_cols))
    gate_mine = to_columns(gate_up_scaled[:, 0])
    up_mine = to_columns(gate_up_scaled[:, 1])
    down_mine = to_columns(w_down.reshape(rows, seqs, ff_cols))

    half = 3 * head_cols // 2
    qkv_a, qkv_b = line.gather([qkv_mine[..., :half], qkv_mine[..., half:]])
    qkv_whole = jnp.concatenate([qkv_a, qkv_b], 1)
    (out_whole,) = line.gather([out_mine])
    gate_whole, up_whole = line.gather([gate_mine, up_mine])
    half = ff_cols // 2
    down_a, down_b = line.gather([down_mine[..., :half], down_mine[..., half:]])

    inv_one = lax.rsqrt(jnp.mean(inputs * inputs, -1, keepdims=True) + EPS)
    normed = inputs * inv_one
    acts = group.gather_seq(normed.astype(BF)).reshape(length, width)
    places = group.gather_seq(positions[0]).reshape(length)
    upstream_own = cotangent[0]
    upstream = group.gather_seq(upstream_own).reshape(length, width)

    mixed = dot(acts, qkv_whole)
    cosine, sine = rope_tables(places, HEAD_DIM)
    queries = rotate(mixed[:, :head_cols], cosine, sine, 1.0).astype(BF)
    keys_rot = rotate(mixed[:, head_cols : 2 * head_cols], cosine, sine, 1.0).astype(BF)
    values_all = mixed[:, 2 * head_cols :].astype(BF)

    def by_head(block):
        return jnp.moveaxis(block.reshape(length, -1, HEAD_DIM), 1, 0)

    def by_token(block):
        return jnp.moveaxis(block, 0, 1).reshape(length, -1)

    stacked = (by_head(queries), by_head(keys_rot), by_head(values_all))
    head_out, log_totals = lax.map(head_forward, stacked)
    attended = by_token(head_out)

    def own_sum(terms):
        return group.sum_seq(terms.reshape(seqs, token_count, width))

    middle = inputs + own_sum(dot_cols(attended, out_whole))
    inv_two = lax.rsqrt(jnp.mean(middle * middle, -1, keepdims=True) + EPS)
    normed_mid = middle * inv_two
    acts_mid = group.gather_seq(normed_mid.astype(BF)).reshape(length, width)

    gate = dot(acts_mid, gate_whole)
    up = dot(acts_mid, up_whole)
    sigma = jax.nn.sigmoid(gate)
    hidden = (gate * sigma * up).astype(BF)
    half = ff_cols // 2
    down_terms = [
        dot_rows(upstream, hidden[:, :half]).astype(BF),
        dot_rows(upstream, hidden[:, half:]).astype(BF),
    ]
    down_sums = line.reduce(down_terms, rows)

    grad_hidden = jnp.concatenate([dot(upstream, down_a), dot(upstream, down_b)], 1)
    grad_gate = (grad_hidden * up * sigma * (1.0 + gate * (1.0 - sigma))).astype(BF)
    grad_up = (grad_hidden * gate * sigma).astype(BF)
    grad_norm_mid = own_sum(dot_cols(grad_gate, gate_whole) + dot_cols(grad_up, up_whole))
    gate_up_terms = [
        dot_rows(acts_mid, grad_gate).astype(BF),
        dot_rows(acts_mid, grad_up).astype(BF),
    ]
    gate_up_sums = line.reduce(gate_up_terms, rows)

    outcome = (
        middle + own_sum(dot_cols(hidden[:, :half], down_a) + dot_cols(hidden[:, half:], down_b))
    ).astype(BF)

    grad_middle = upstream_own.astype(F32) + inv_two * (
        grad_norm_mid - normed_mid * jnp.mean(grad_norm_mid * normed_mid, -1, keepdims=True)
    )
    grad_branch = group.gather_seq(grad_middle.astype(BF)).reshape(length, width)
    out_sums = line.reduce([dot_rows(grad_branch, attended).astype(BF)], rows)

    grad_attended = dot(grad_branch, out_whole).astype(BF)
    grad_hq, grad_hk, grad_hv = lax.map(
        head_backward, stacked + (by_head(grad_attended), log_totals)
    )
    grad_mixed = jnp.concatenate(
        [
            rotate(by_token(grad_hq).astype(F32), cosine, sine, -1.0).astype(BF),
            rotate(by_token(grad_hk).astype(F32), cosine, sine, -1.0).astype(BF),
            by_token(grad_hv),
        ],
        1,
    )
    half = 3 * head_cols // 2
    qkv_terms = [
        dot_rows(acts, grad_mixed[:, :half]).astype(BF),
        dot_rows(acts, grad_mixed[:, half:]).astype(BF),
    ]
    qkv_sums = line.reduce(qkv_terms, rows)
    grad_norm = own_sum(dot_cols(grad_mixed, qkv_whole))
    grad_inputs = grad_middle + inv_one * (
        grad_norm - normed * jnp.mean(grad_norm * normed, -1, keepdims=True)
    )

    def to_rows(sums):
        return jnp.moveaxis(group.swap_seq(sums.astype(BF), 0), 0, 1).astype(F32)

    grad_qkv = to_rows(jnp.concatenate(qkv_sums, 2)).reshape(rows, seqs, 3, head_cols)
    grad_qkv = jnp.moveaxis(grad_qkv, 2, 1).reshape(rows, 3 * width)
    grad_out = to_rows(out_sums[0]).reshape(rows, width)
    grad_gate_up = jnp.concatenate(
        [to_rows(part).reshape(rows, ff_width) for part in gate_up_sums], 1
    )
    grad_down = to_rows(jnp.concatenate(down_sums, 2)).reshape(rows, ff_width)
    gain_one_sum = jnp.sum(grad_qkv * w_qkv.astype(F32), 1)
    gain_two_sum = jnp.sum(grad_gate_up * w_gate_up.astype(F32), 1)
    return (
        outcome[None],
        grad_inputs[None],
        grad_qkv * gain_one,
        grad_out,
        gain_one_sum,
        grad_gate_up * gain_two,
        grad_down,
        gain_two_sum,
    )


def solution(mesh):
    tokens = P("fsdp", "seq", None)
    matrix = P(("seq", "fsdp"), None)
    vector = P(("seq", "fsdp"))

    def step(*arrays):
        return per_device(mesh, *arrays)

    return jax.shard_map(
        step,
        mesh=mesh,
        in_specs=(
            tokens,
            P("fsdp", "seq"),
            matrix,
            matrix,
            vector,
            matrix,
            matrix,
            vector,
            tokens,
        ),
        out_specs=(tokens, tokens, matrix, matrix, vector, matrix, matrix, vector),
        check_vma=False,
    )
```

```python
import functools
import math

import jax
import jax.numpy as jnp
from jax import lax
from jax.experimental import pallas as pl
from jax.experimental.pallas import tpu as pltpu
from jax.sharding import Mesh, PartitionSpec as P

HEAD_DIM = 64
PAIR = 2 * HEAD_DIM
BLOCK = 256
EPS = 1e-05
ROPE_BASE = 130000.0
BF = jnp.bfloat16
F32 = jnp.float32
VMEM_LIMIT = 48 << 20
CHUNKS = 2


def kernel_call(body, name, **spec):
    return pl.pallas_call(
        body,
        name=name,
        compiler_params=pltpu.CompilerParams(vmem_limit_bytes=VMEM_LIMIT),
        **spec,
    )


def blank(shape, dtype):
    return pl.pallas_call(
        lambda out: None,
        name="blank",
        out_shape=jax.ShapeDtypeStruct(shape, dtype),
        out_specs=pl.BlockSpec(memory_space=pl.ANY),
    )()


def turn(x, cosine, sine):
    half = HEAD_DIM // 2
    lane = lax.broadcasted_iota(jnp.int32, x.shape, 1)
    swapped = jnp.where(
        lane % HEAD_DIM < half, pltpu.roll(x, PAIR - half, 1), pltpu.roll(x, half, 1)
    )
    return x * cosine + swapped * sine


def nt(left, right):
    return lax.dot_general(left, right, (((1,), (1,)), ((), ())), preferred_element_type=F32)


def tn(left, right):
    return lax.dot_general(left, right, (((0,), (0,)), ((), ())), preferred_element_type=F32)


def nn(left, right):
    return lax.dot_general(left, right, (((1,), (0,)), ((), ())), preferred_element_type=F32)


def masked_scores(queries, keys, block):
    scores = nt(queries, keys)
    rows = lax.broadcasted_iota(jnp.int32, (BLOCK, BLOCK), 0)
    cols = lax.broadcasted_iota(jnp.int32, (BLOCK, BLOCK), 1)
    last = jnp.where(cols <= rows, scores[:, block * BLOCK :], -1e30)
    return jnp.concatenate([scores[:, : block * BLOCK], last], 1) if block else last


def attend_kernel(mixed, cosine, sine, qkv, out, logs):
    length = mixed.shape[0]
    qkv[:, :PAIR] = turn(mixed[:, :PAIR], cosine[...], sine[...]).astype(BF)
    qkv[:, PAIR : 2 * PAIR] = turn(mixed[:, PAIR : 2 * PAIR], cosine[...], sine[...]).astype(BF)
    qkv[:, 2 * PAIR :] = mixed[:, 2 * PAIR :].astype(BF)
    scale = jnp.asarray(1.0 / math.sqrt(HEAD_DIM), BF)
    for block in range(length // BLOCK):
        at = pl.ds(block * BLOCK, BLOCK)
        seen = (block + 1) * BLOCK
        outs = []
        totals = []
        for low in (0, HEAD_DIM):
            high = low + HEAD_DIM
            queries = qkv[at, low:high] * scale
            scores = masked_scores(queries, qkv[:seen, PAIR + low : PAIR + high], block)
            highest = jnp.max(scores, -1, keepdims=True)
            weights = jnp.exp(scores - highest)
            summed = jnp.sum(weights, -1, keepdims=True)
            probs = (weights * (1.0 / summed)).astype(BF)
            outs.append(nn(probs, qkv[:seen, 2 * PAIR + low : 2 * PAIR + high]))
            totals.append(jnp.broadcast_to(highest + jnp.log(summed), (BLOCK, HEAD_DIM)))
        out[at, :] = jnp.concatenate(outs, 1).astype(BF)
        logs[at, :] = jnp.concatenate(totals, 1)


def attend_back_kernel(qkv, grad, logs, cosine, sine, grad_qkv, grad_keys, grad_values):
    length = qkv.shape[0]
    scale = 1.0 / math.sqrt(HEAD_DIM)
    last = length // BLOCK - 1
    for block in range(last, -1, -1):
        at = pl.ds(block * BLOCK, BLOCK)
        seen = (block + 1) * BLOCK
        grad_queries = []
        for low in (0, HEAD_DIM):
            high = low + HEAD_DIM
            queries = qkv[at, low:high] * jnp.asarray(scale, BF)
            keys = qkv[:seen, PAIR + low : PAIR + high]
            upstream = grad[at, low:high]
            scores = masked_scores(queries, keys, block)
            probs = jnp.exp(scores - logs[at, low : low + 1])
            grad_probs = nt(upstream, qkv[:seen, 2 * PAIR + low : 2 * PAIR + high])
            inner = jnp.sum(probs * grad_probs, -1, keepdims=True)
            grad_scores = (probs * (grad_probs - inner)).astype(BF)
            grad_queries.append(nn(grad_scores, keys))
            for_keys = tn(grad_scores, queries)
            for_values = tn(probs.astype(BF), upstream)
            if block == last:
                grad_keys[:, low:high] = for_keys
                grad_values[:, low:high] = for_values
            else:
                grad_keys[:seen, low:high] += for_keys
                grad_values[:seen, low:high] += for_values
        rounded = (jnp.concatenate(grad_queries, 1) * scale).astype(BF).astype(F32)
        grad_qkv[at, :PAIR] = turn(rounded, cosine[at, :], -sine[at, :]).astype(BF)
    rounded = grad_keys[...].astype(BF).astype(F32)
    grad_qkv[:, PAIR : 2 * PAIR] = turn(rounded, cosine[...], -sine[...]).astype(BF)
    grad_qkv[:, 2 * PAIR :] = grad_values[...].astype(BF)


def head_specs(length):
    wide = pl.BlockSpec((length, 3 * PAIR), lambda s, i: (s, i))
    one = pl.BlockSpec((length, PAIR), lambda s, i: (s, i))
    table = pl.BlockSpec((length, PAIR), lambda s, i: (s, 0))
    return wide, one, table


def attend(mixed, cosine, sine, count):
    tokens, cols = mixed.shape
    wide, one, table = head_specs(tokens // count)
    return kernel_call(
        attend_kernel,
        "attend",
        grid=(count, cols // (3 * PAIR)),
        in_specs=[wide, table, table],
        out_specs=[wide, one, one],
        out_shape=[
            jax.ShapeDtypeStruct((tokens, cols), BF),
            jax.ShapeDtypeStruct((tokens, cols // 3), BF),
            jax.ShapeDtypeStruct((tokens, cols // 3), F32),
        ],
    )(mixed, cosine, sine)


def attend_back(qkv, grad, logs, cosine, sine, count):
    tokens, cols = qkv.shape
    length = tokens // count
    wide, one, table = head_specs(length)
    return kernel_call(
        attend_back_kernel,
        "attend_back",
        grid=(count, cols // (3 * PAIR)),
        in_specs=[wide, one, one, table, table],
        out_specs=wide,
        out_shape=jax.ShapeDtypeStruct((tokens, cols), BF),
        scratch_shapes=[pltpu.VMEM((length, PAIR), F32)] * 2,
    )(qkv, grad, logs, cosine, sine)


def qkv_columns(owners, cols):
    for owner in range(owners):
        for pair in range(cols // PAIR):
            for kind in range(3):
                there = (pair * 3 + kind) * PAIR
                yield owner, there, (kind * owners + owner) * cols + pair * PAIR


def gate_up_columns(owners, cols, chunk):
    part = cols // CHUNKS
    for owner in range(owners):
        for kind in range(2):
            yield owner, kind * part, (kind * owners + owner) * cols + chunk * part


def cut(weights, gain, places, width, owners):
    rows = weights.shape[0]

    def body(*refs):
        source, outs = refs[0], refs[-len(places) :]
        for out, (listed, cols) in zip(outs, places):
            for owner, there, here in listed:
                part = source[:, here : here + width]
                if gain is not None:
                    part = (part.astype(F32) * refs[1][...]).astype(BF)
                out[owner, :, there : there + width] = part

    return kernel_call(
        body,
        "cut",
        out_shape=[jax.ShapeDtypeStruct((owners, rows, cols), BF) for _, cols in places],
    )(*((weights,) if gain is None else (weights, gain)))


def join(sums, weights, gain, places, width, total_width):
    rows = sums[0].shape[1]

    def body(*refs):
        count = len(sums)
        out = refs[-2] if gain is not None else refs[-1]
        total = jnp.zeros((rows, PAIR), F32)
        for source, listed in zip(refs[:count], places):
            for owner, there, here in listed:
                for step in range(0, width, PAIR):
                    part = source[owner, :, there + step : there + step + PAIR].astype(F32)
                    at = slice(here + step, here + step + PAIR)
                    if gain is not None:
                        total += part * refs[count][:, at].astype(F32)
                        part = part * refs[count + 1][...]
                    out[:, at] = part
        if gain is not None:
            refs[-1][...] = jnp.sum(total, 1, keepdims=True)

    shapes = [jax.ShapeDtypeStruct((rows, total_width), F32)]
    extra = ()
    if gain is not None:
        shapes.append(jax.ShapeDtypeStruct((rows, 1), F32))
        extra = (weights, gain)
    return kernel_call(body, "join", out_shape=shapes)(*sums, *extra)


MESH = pl.DeviceIdType.MESH
ANYWHERE = pl.BlockSpec(memory_space=pl.ANY)
LOCAL = pl.BlockSpec(memory_space=pltpu.VMEM)


def flip(index, offset):
    weight = 1
    while weight <= offset:
        if offset & weight:
            index = index + weight - 2 * weight * ((index // weight) % 2)
        weight *= 2
    return index


def greet(partners):
    barrier = pltpu.get_barrier_semaphore()
    for partner in partners:
        pl.semaphore_signal(barrier, inc=1, device_id=partner, device_id_type=MESH)
    pl.semaphore_wait(barrier, len(partners))


def here():
    return lax.axis_index("seq"), lax.axis_index("core")


def bits_of(seqs):
    return [1 << bit for bit in range(seqs.bit_length() - 1)]


def cube_partners(seqs):
    me, core = here()
    partners = [{"seq": flip(me, bit), "core": core} for bit in bits_of(seqs)]
    return partners + [{"seq": me, "core": 1 - core}]


def all_partners(seqs):
    me, core = here()
    return [
        {"seq": flip(me, step), "core": core if same else 1 - core}
        for step in range(seqs)
        for same in (True, False)
        if step or not same
    ]


def orders_of(seqs):
    bits = bits_of(seqs)
    return [bits, bits[1:] + bits[:1]]


def push(source, target, sems, at, device):
    copy = pltpu.make_async_remote_copy(
        src_ref=source,
        dst_ref=target,
        send_sem=sems[0].at[at],
        recv_sem=sems[1].at[at],
        device_id=device,
        device_id_type=MESH,
    )
    copy.start()
    return copy


def pair_sems(*shape):
    return [pltpu.SemaphoreType.DMA(shape)] * 2


def spread_scratch(seqs):
    return pair_sems(2, seqs) + pair_sems(2, seqs) + [pltpu.SemaphoreType.DMA]


def spread(own, out, scratch):
    across, aside, local = scratch[0:2], scratch[2:4], scratch[4]
    seqs, _, width = out.shape[1:]
    half = width // 2
    me, core = here()
    sibling = {"seq": me, "core": 1 - core}
    kept = pltpu.make_async_copy(own, out.at[core, me], local)
    kept.start()
    started = []

    def columns(ref, stream):
        return ref.at[:, pl.ds(stream * half, half)]

    def block(offset, stream):
        if offset == 0:
            return columns(own, stream)
        return columns(out.at[core, flip(me, offset)], stream)

    def place(offset, stream):
        return columns(out.at[core, flip(me, offset)], stream)

    def give_sibling(offset, stream):
        started.append(
            push(block(offset, stream), place(offset, stream), aside, (stream, offset), sibling)
        )

    orders = orders_of(seqs)
    have = [[0], [0]]
    swapped = []
    for phase in range(len(orders[0])):
        coming = []
        for stream in range(2):
            bit = orders[stream][phase]
            partner = {"seq": flip(me, bit), "core": core}
            for offset in have[stream]:
                copy = push(
                    block(offset, stream),
                    place(offset, stream),
                    across,
                    (stream, offset + bit),
                    partner,
                )
                coming.append((copy, offset + bit, stream))
        if phase == 0:
            for stream in range(2):
                give_sibling(0, stream)
        for copy, offset, stream in coming:
            copy.wait_recv()
            have[stream].append(offset)
            give_sibling(offset, stream)
        swapped += coming
    for copy in started:
        copy.wait()
    for copy, _, _ in swapped:
        copy.wait_send()
    kept.wait()


def fold_scratch(seqs, tokens, width):
    return [
        pltpu.VMEM((seqs, tokens, width), BF),
        pltpu.VMEM((2, seqs, tokens, width // 2), BF),
    ] + pair_sems(seqs) + pair_sems(2, seqs)


def fold(terms, scratch):
    total, got, aside, across = scratch[0], scratch[1], scratch[2:4], scratch[4:6]
    seqs, tokens, width = total.shape
    half = width // 2
    step = min(32, tokens)
    me, core = here()
    sibling = {"seq": me, "core": 1 - core}
    orders = orders_of(seqs)
    offsets = list(range(seqs - 1, -1, -1))
    given = {}
    for offset in offsets:
        at = flip(me, offset)
        given[offset] = push(terms.at[1 - core, at], total.at[at], aside, (offset,), sibling)
    started = []

    def send(stream, phase, offset):
        bit = orders[stream][phase]
        columns = pl.ds(stream * half, half)
        copy = push(
            total.at[flip(me, offset), :, columns],
            got.at[stream, offset],
            across,
            (stream, offset),
            {"seq": flip(me, bit), "core": core},
        )
        started.append(copy)
        return copy

    coming = [[], []]
    for offset in offsets:
        given[offset].wait_recv()
        at = flip(me, offset)

        def add_sibling(i, carry, at=at):
            rows = pl.ds(pl.multiple_of(i * step, step), step)
            both = total[at, rows, :].astype(F32) + terms[core, at, rows, :].astype(F32)
            total[at, rows, :] = both.astype(BF)
            return carry

        lax.fori_loop(0, tokens // step, add_sibling, 0)
        for stream in range(2):
            if offset & orders[stream][0]:
                coming[stream].append((send(stream, 0, offset), offset))
    for phase in range(len(orders[0])):
        for stream in range(2):
            bit = orders[stream][phase]
            for copy, offset in coming[stream]:
                copy.wait_recv()
                at = flip(me, offset - bit)

                def add_got(i, carry, at=at, stream=stream, offset=offset):
                    rows = pl.ds(pl.multiple_of(i * step, step), step)
                    columns = pl.ds(stream * half, half)
                    both = total[at, rows, columns].astype(F32) + got[
                        stream, offset, rows, :
                    ].astype(F32)
                    total[at, rows, columns] = both.astype(BF)
                    return carry

                lax.fori_loop(0, tokens // step, add_got, 0)
            if phase + 1 < len(orders[0]):
                done = sum(orders[stream][: phase + 1])
                following = orders[stream][phase + 1]
                coming[stream] = [
                    (send(stream, phase + 1, offset), offset)
                    for offset in offsets
                    if offset & following and not offset & done
                ]
    for copy in list(given.values()) + started:
        copy.wait_send()
    return total.at[me]


def by_rows(count, work):
    step = min(32, count)

    def one(i, carry):
        work(pl.ds(pl.multiple_of(i * step, step), step))
        return carry

    lax.fori_loop(0, count // step, one, 0)


def reaching_call(body, name, number, **spec):
    return pl.pallas_call(
        body,
        name=name,
        compiler_params=pltpu.CompilerParams(
            vmem_limit_bytes=VMEM_LIMIT, collective_id=number, has_side_effects=True
        ),
        **spec,
    )


def deal_copies(pieces, outs, sems, locals_):
    me, core = here()
    copies = []
    kept = []
    seqs = pieces[0].shape[0]
    for i, (piece, out) in enumerate(zip(pieces, outs)):
        own = pltpu.make_async_copy(piece.at[me, core], out.at[me, core], locals_.at[i])
        own.start()
        kept.append(own)
        for step in range(seqs):
            for same in (True, False):
                if step or not same:
                    to_seq, to_core = flip(me, step), core if same else 1 - core
                    copies.append(
                        push(
                            piece.at[to_seq, to_core],
                            out.at[me, core],
                            sems,
                            (i, 2 * step + (0 if same else 1)),
                            {"seq": to_seq, "core": to_core},
                        )
                    )
    return kept, copies


def deal(pieces, number):
    count = len(pieces)
    seqs = pieces[0].shape[0]

    def body(*refs):
        greet(all_partners(seqs))
        sems, locals_ = refs[2 * count : 2 * count + 2], refs[2 * count + 2]
        kept, copies = deal_copies(refs[:count], refs[count : 2 * count], sems, locals_)
        for copy in copies:
            copy.wait()
        for copy in kept:
            copy.wait()

    return reaching_call(
        body,
        "deal",
        number,
        in_specs=[ANYWHERE] * count,
        out_specs=[ANYWHERE] * count,
        out_shape=[jax.ShapeDtypeStruct(piece.shape, BF) for piece in pieces],
        scratch_shapes=pair_sems(count, 2 * seqs) + [pltpu.SemaphoreType.DMA((count,))],
    )(*pieces)


def first_acts(tokens, pieces, seqs, number):
    count, width = tokens.shape
    pieces_count = len(pieces)

    def body(*refs):
        source, given = refs[0], refs[1 : 1 + pieces_count]
        out, outs = refs[1 + pieces_count], refs[2 + pieces_count : 2 + 2 * pieces_count]
        own, *sems = refs[2 + 2 * pieces_count :]
        greet(all_partners(seqs))
        kept, copies = deal_copies(given, outs, sems[:2], sems[2])

        def norm(rows):
            values = source[rows, :].astype(F32)
            own[rows, :] = (values * norm_scale(values)).astype(BF)

        by_rows(count, norm)
        spread(own, out, sems[3:])
        for copy in copies:
            copy.wait()
        for copy in kept:
            copy.wait()

    return reaching_call(
        body,
        "first_acts",
        number,
        in_specs=[LOCAL] + [ANYWHERE] * pieces_count,
        out_specs=[ANYWHERE] * (1 + pieces_count),
        out_shape=[jax.ShapeDtypeStruct((2, seqs, count, width), BF)]
        + [jax.ShapeDtypeStruct(piece.shape, BF) for piece in pieces],
        scratch_shapes=[pltpu.VMEM((count, width), BF)]
        + pair_sems(pieces_count, 2 * seqs)
        + [pltpu.SemaphoreType.DMA((pieces_count,))]
        + spread_scratch(seqs),
    )(tokens, *pieces)


def middle_acts(terms, tokens, number):
    _, seqs, count, width = terms.shape

    def body(given, source, middle, out, own, *scratch):
        greet(cube_partners(seqs))
        total = fold(given, scratch[:6])

        def norm(rows):
            values = source[rows, :].astype(F32) + total[rows, :].astype(F32)
            middle[rows, :] = values
            own[rows, :] = (values * norm_scale(values)).astype(BF)

        by_rows(count, norm)
        spread(own, out, scratch[6:])

    return reaching_call(
        body,
        "middle_acts",
        number,
        in_specs=[LOCAL, LOCAL],
        out_specs=[LOCAL, ANYWHERE],
        out_shape=[
            jax.ShapeDtypeStruct((count, width), F32),
            jax.ShapeDtypeStruct(terms.shape, BF),
        ],
        scratch_shapes=[pltpu.VMEM((count, width), BF)]
        + fold_scratch(seqs, count, width)
        + spread_scratch(seqs),
    )(terms, tokens)


def middle_grad(terms, cotangent, middle, number):
    _, seqs, count, width = terms.shape

    def body(given, upstream, values, grad, out, own, *scratch):
        greet(cube_partners(seqs))
        total = fold(given, scratch[:6])

        def back(rows):
            held = values[rows, :]
            scale = norm_scale(held)
            result = upstream[rows, :].astype(F32) + norm_back(
                total[rows, :].astype(F32), held * scale, scale
            )
            grad[rows, :] = result
            own[rows, :] = result.astype(BF)

        by_rows(count, back)
        spread(own, out, scratch[6:])

    return reaching_call(
        body,
        "middle_grad",
        number,
        in_specs=[LOCAL] * 3,
        out_specs=[LOCAL, ANYWHERE],
        out_shape=[
            jax.ShapeDtypeStruct((count, width), F32),
            jax.ShapeDtypeStruct(terms.shape, BF),
        ],
        scratch_shapes=[pltpu.VMEM((count, width), BF)]
        + fold_scratch(seqs, count, width)
        + spread_scratch(seqs),
    )(terms, cotangent, middle)


def input_grad(terms, tokens, grad_middle, number):
    _, seqs, count, width = terms.shape

    def body(given, source, held, out, *scratch):
        greet(cube_partners(seqs))
        total = fold(given, scratch)

        def back(rows):
            values = source[rows, :].astype(F32)
            scale = norm_scale(values)
            out[rows, :] = held[rows, :] + norm_back(
                total[rows, :].astype(F32), values * scale, scale
            )

        by_rows(count, back)

    return reaching_call(
        body,
        "input_grad",
        number,
        in_specs=[LOCAL] * 3,
        out_specs=LOCAL,
        out_shape=jax.ShapeDtypeStruct((count, width), F32),
        scratch_shapes=fold_scratch(seqs, count, width),
    )(terms, tokens, grad_middle)


class Order:
    def __init__(self):
        self.latest = None

    def enter(self, values):
        if self.latest is None:
            return values
        return lax.optimization_barrier((values, self.latest))[0]

    def run(self, work, *values):
        result = work(*self.enter(values))
        self.latest = jax.tree.leaves(result)[0]
        return result

    def take(self, values):
        if self.latest is not None:
            values = lax.optimization_barrier((values, self.latest))[0]
        self.latest = jax.tree.leaves(values)[0]
        return values


class Group:
    def __init__(self, mesh, order):
        self.order = order
        self.seqs = mesh.shape["seq"]
        self.chips = mesh.shape["z"]
        self.seq = lax.axis_index("seq")
        self.chip = lax.axis_index("z")
        self.core = lax.axis_index("core")

    def across(self, value, step):
        return lax.ppermute(value, "seq", [(s, s ^ step) for s in range(self.seqs)])

    def sibling(self, value):
        return lax.ppermute(value, "core", [(0, 1), (1, 0)])

    def onward(self, value):
        return lax.ppermute(value, "z", [(f, (f + 1) % self.chips) for f in range(self.chips)])


class Gather:
    def __init__(self, group, piece):
        self.group = group
        self.piece = piece
        self.whole = blank((group.chips,) + piece.shape, piece.dtype)
        self.hop = 0
        self.flying = None
        self.place()

    def place(self):
        origin = (self.group.chip - self.hop) % self.group.chips
        self.whole = lax.dynamic_update_index_in_dim(self.whole, self.piece, origin, 0)

    def send(self):
        if self.flying is None and self.hop < self.group.chips - 1:
            self.flying = self.group.onward(self.group.order.enter(self.piece))

    def take(self):
        if self.flying is not None:
            self.piece = self.group.order.take(self.flying)
            self.flying = None
            self.hop += 1
            self.place()

    def rows(self):
        while self.hop < self.group.chips - 1:
            self.send()
            self.take()
        self.group.order.latest = self.whole
        return self.whole.reshape(-1, self.whole.shape[-1])


class Reduce:
    def __init__(self, group, term):
        self.group = group
        self.term = term.reshape(group.chips, group.seqs, -1, term.shape[-1])
        self.total = self.block(0)
        self.flying = None
        self.hop = 0

    def block(self, hop):
        at = (self.group.chip - 1 - hop) % self.group.chips
        return lax.dynamic_index_in_dim(self.term, at, 0, keepdims=False)

    def send(self):
        if self.flying is None and self.hop < self.group.chips - 1:
            self.flying = self.group.onward(self.group.order.enter(self.total))

    def take(self):
        if self.flying is not None:
            self.hop += 1
            got = self.group.order.take(self.flying).astype(F32)
            self.flying = None
            self.total = (got + self.block(self.hop).astype(F32)).astype(BF)
            self.group.order.latest = self.total

    def sums(self):
        while self.hop < self.group.chips - 1:
            self.send()
            self.take()
        return self.total


def rope_tables(places):
    half = HEAD_DIM // 2
    inverse = ROPE_BASE ** (-2.0 * jnp.arange(half).astype(F32) / HEAD_DIM)
    angles = places.astype(F32)[:, None] * inverse[None, :]
    cosine, sine = jnp.cos(angles), jnp.sin(angles)
    return jnp.concatenate([cosine] * 4, 1), jnp.concatenate([-sine, sine] * 2, 1)


def norm_scale(values):
    return lax.rsqrt(jnp.mean(values * values, -1, keepdims=True) + EPS)


def norm_back(grad, normed, scale):
    return scale * (grad - normed * jnp.mean(grad * normed, -1, keepdims=True))


def per_device(
    mesh, tokens, positions, w_qkv, w_out, gain_attn, w_gate_up, w_down, gain_mlp, cotangent
):
    order = Order()
    group = Group(mesh, order)
    seqs, chips = group.seqs, group.chips
    owners = 2 * seqs
    token_count, width = tokens.shape[1:]
    ff_width = w_down.shape[1]
    rows = w_qkv.shape[0]
    head_cols = width // owners
    ff_cols = ff_width // owners
    part = ff_cols // CHUNKS
    gain_one = gain_attn.astype(F32)[:, None]
    gain_two = gain_mlp.astype(F32)[:, None]

    def inside(values):
        split = values.reshape(token_count, seqs, chips, 2 * rows)
        return jnp.moveaxis(split, 2, 1).reshape(token_count, width)

    def outside(values):
        split = values.reshape(token_count, chips, seqs, 2 * rows)
        return jnp.moveaxis(split, 2, 1).reshape(token_count, width)

    def by_place(piece):
        return piece.reshape(seqs, 2, rows, -1)

    def to_gather(piece):
        return piece.reshape(seqs, 2 * rows, -1)

    def all_rows(piece):
        gathered = lax.all_gather(piece, "z", axis=0, tiled=False)
        return gathered

    def flat(gathered):
        return order.take(gathered).reshape(width, -1)

    def summed(term):
        split = order.enter(term).reshape(chips, seqs, 2 * rows, -1)
        return lax.psum_scatter(split, "z", scatter_dimension=0, tiled=False)

    qkv_places = list(qkv_columns(owners, head_cols))
    (qkv_cut,) = order.run(
        lambda w, g: cut(w, g, [(qkv_places, 3 * head_cols)], PAIR, owners), w_qkv, gain_one
    )
    (qkv_piece,) = order.run(lambda a: deal([a], 1), by_place(qkv_cut))
    qkv_gathered = all_rows(order.enter(to_gather(qkv_piece)))
    places_sent = [order.enter(positions[0])]
    places_sent += [group.across(places_sent[0], step) for step in range(1, seqs)]

    gate_up_places = [
        (list(gate_up_columns(owners, ff_cols, chunk)), 2 * part) for chunk in range(CHUNKS)
    ]
    down_places = [
        ([(o, 0, o * ff_cols + chunk * part) for o in range(owners)], part)
        for chunk in range(CHUNKS)
    ]
    out_places = [([(o, 0, o * head_cols) for o in range(owners)], head_cols)]
    gate_up_cut = order.run(
        lambda w, g: cut(w, g, gate_up_places, part, owners), w_gate_up, gain_two
    )
    out_cut = order.run(lambda w: cut(w, None, out_places, head_cols, owners), w_out)
    down_cut = order.run(lambda w: cut(w, None, down_places, part, owners), w_down)
    tokens_in, upstream_own = order.run(
        lambda a, b: (inside(a), inside(b)), tokens[0], cotangent[0]
    )
    acts, *pieces = order.run(
        lambda x, *given: first_acts(x, given, seqs, 2),
        tokens_in,
        *[by_place(p) for p in gate_up_cut + out_cut + down_cut],
    )
    acts = acts.reshape(-1, width)
    pieces = [to_gather(p) for p in pieces]
    gate_up_gathered = [all_rows(order.enter(pieces[i])) for i in range(CHUNKS)]
    out_all = Gather(group, pieces[CHUNKS])
    down_all = [Gather(group, p) for p in pieces[CHUNKS + 1 :]]
    out_all.send()
    upstream_sent = [order.enter(upstream_own)]
    upstream_sent += [group.across(upstream_sent[0], step) for step in range(1, seqs)]

    places = blank((2, seqs, token_count), jnp.int32)
    for step in range(seqs):
        got = order.take(places_sent[step])
        places = lax.dynamic_update_slice(
            places, got[None, None], (group.core, group.seq ^ step, 0)
        )
        other = order.take(group.sibling(got))
        places = lax.dynamic_update_slice(
            places, other[None, None], (1 - group.core, group.seq ^ step, 0)
        )
    cosine, sine = order.run(rope_tables, places.reshape(-1))

    qkv_whole = flat(qkv_gathered)
    mixed = order.run(nn, acts, qkv_whole)
    out_all.take()
    out_all.send()
    down_all[0].send()
    qkv, attended, logs = order.run(
        lambda m, c, s: attend(m, c, s, 2), mixed, cosine, sine
    )
    out_all.take()
    out_all.send()
    down_all[0].take()
    down_all[0].send()
    out_all.take()
    out_whole = out_all.rows()

    def terms_of(total):
        return total.astype(BF).reshape(2, seqs, token_count, width)

    branch = order.run(lambda a, w: terms_of(nt(a, w)), attended, out_whole)
    down_all[1].send()
    middle, acts_mid = order.run(lambda a, b: middle_acts(a, b, 3), branch, tokens_in)
    acts_mid = acts_mid.reshape(-1, width)
    down_all[0].take()
    down_all[0].send()
    down_all[1].take()
    down_all[1].send()

    upstream = blank((2, seqs, token_count, width), BF)
    for step in range(seqs):
        got = order.take(upstream_sent[step])
        upstream = lax.dynamic_update_slice(
            upstream, got[None, None], (group.core, group.seq ^ step, 0, 0)
        )
        upstream_sent[step] = group.sibling(order.enter(got))
    for step in range(seqs):
        got = order.take(upstream_sent[step])
        upstream = lax.dynamic_update_slice(
            upstream, got[None, None], (1 - group.core, group.seq ^ step, 0, 0)
        )
    order.latest = upstream
    upstream = upstream.reshape(-1, width)

    def feed(acts_mid, weights):
        return nn(acts_mid, weights)

    def feed_hidden(both):
        gate, up = both[:, :part], both[:, part:]
        return (gate * jax.nn.sigmoid(gate) * up).astype(BF)

    def feed_back(grad_hidden, both):
        gate, up = both[:, :part], both[:, part:]
        sigma = jax.nn.sigmoid(gate)
        grad_gate = grad_hidden * up * sigma * (1.0 + gate * (1.0 - sigma))
        grad_up = grad_hidden * gate * sigma
        return jnp.concatenate([grad_gate.astype(BF), grad_up.astype(BF)], 1)

    hidden, grad_both, down_whole = [], [], []
    gate_up_sums, down_sums = [], []
    norm_mid_terms = None
    for chunk in range(CHUNKS):
        gate_up_whole = flat(gate_up_gathered[chunk])
        both = order.run(feed, acts_mid, gate_up_whole)
        hidden.append(order.run(feed_hidden, both))
        for each in down_all:
            each.take()
            each.send()
        down_whole.append(down_all[chunk].rows())
        grad_hidden = order.run(nn, upstream, down_whole[chunk])
        grad_both.append(order.run(feed_back, grad_hidden, both))
        if chunk == 0:
            norm_mid_terms = order.run(
                lambda a, b: nt(a, b).astype(BF), grad_both[chunk], gate_up_whole
            )
        else:
            norm_mid_terms = order.run(
                lambda a, b, c: (nt(a, b) + c.astype(F32)).astype(BF),
                grad_both[chunk],
                gate_up_whole,
                norm_mid_terms,
            )
        term = order.run(lambda a, b: tn(a, b).astype(BF), acts_mid, grad_both[chunk])
        gate_up_sums.append(summed(term))
        term = order.run(lambda a, b: tn(a, b).astype(BF), upstream, hidden[chunk])
        down_sums.append(Reduce(group, term))
        for each in down_sums:
            each.take()
            each.send()

    grad_middle, grad_branch = order.run(
        lambda a, b, c: middle_grad(a, b, c, 4),
        norm_mid_terms.reshape(2, seqs, token_count, width),
        upstream_own,
        middle,
    )
    grad_branch = grad_branch.reshape(-1, width)
    for each in down_sums:
        each.take()
        each.send()

    gate_up_sums[0] = order.take(gate_up_sums[0])

    grad_attended = order.run(lambda a, b: nn(a, b).astype(BF), grad_branch, out_whole)
    grad_mixed = order.run(
        lambda *a: attend_back(*a, 2), qkv, grad_attended, logs, cosine, sine
    )
    gate_up_sums[1:] = [order.take(value) for value in gate_up_sums[1:]]
    for each in down_sums:
        each.take()
        each.send()
    qkv_term = order.run(lambda a, b: tn(a, b).astype(BF), acts, grad_mixed)
    qkv_sum = summed(qkv_term)
    norm_terms = order.run(lambda a, b: terms_of(nt(a, b)), grad_mixed, qkv_whole)
    out_term = order.run(lambda a, b: tn(a, b).astype(BF), grad_branch, attended)
    out_sum = Reduce(group, out_term)
    out_sum.send()
    grad_inputs = order.run(
        lambda a, b, c: input_grad(a, b, c, 5), norm_terms, tokens_in, grad_middle
    )
    out_sum.take()
    out_sum.send()

    outcome_terms = order.run(
        lambda a, b, c, d: terms_of(nt(a, c) + nt(b, d)), *hidden, *down_whole
    )
    given = lax.dynamic_index_in_dim(outcome_terms, 1 - group.core, 0, keepdims=False)
    kept = lax.dynamic_index_in_dim(outcome_terms, group.core, 0, keepdims=False)
    given_sent = group.sibling(order.enter(given))
    down_rows = [each.sums() for each in down_sums]
    got = order.take(given_sent)
    both = order.run(lambda a, b: (a.astype(F32) + b.astype(F32)).astype(BF), kept, got)
    outcome_sent = [
        order.enter(lax.dynamic_index_in_dim(both, group.seq ^ step, 0, keepdims=False))
        for step in range(seqs)
    ]
    outcome_sent[1:] = [group.across(outcome_sent[step], step) for step in range(1, seqs)]

    out_sum.take()
    out_sum.send()
    dealt = order.run(
        lambda *a: deal(a, 6), *[by_place(value) for value in down_rows + gate_up_sums]
    )
    down_dealt = [to_owner.reshape(owners, rows, -1) for to_owner in dealt[:CHUNKS]]
    gate_up_dealt = [to_owner.reshape(owners, rows, -1) for to_owner in dealt[CHUNKS:]]
    (grad_down,) = order.run(
        lambda *a: join(a, None, None, [p for p, _ in down_places], part, ff_width), *down_dealt
    )
    grad_gate_up, gain_two_sum = order.run(
        lambda w, g, *a: join(a, w, g, [p for p, _ in gate_up_places], part, 2 * ff_width),
        w_gate_up,
        gain_two,
        *gate_up_dealt,
    )
    outcome_got = order.take(outcome_sent)
    outcome = order.run(
        lambda m, parts: (m + sum(p.astype(F32) for p in parts)).astype(BF), middle, outcome_got
    )
    outcome, grad_inputs = order.run(lambda a, b: (outside(a), outside(b)), outcome, grad_inputs)
    out_rows = out_sum.sums()
    qkv_rows = order.take(qkv_sum)
    dealt = order.run(lambda *a: deal(a, 7), by_place(out_rows), by_place(qkv_rows))
    out_dealt, qkv_dealt = [value.reshape(owners, rows, -1) for value in dealt]
    grad_qkv, gain_one_sum = order.run(
        lambda w, g, a: join([a], w, g, [qkv_places], PAIR, 3 * width), w_qkv, gain_one, qkv_dealt
    )
    (grad_out,) = order.run(
        lambda a: join([a], None, None, [p for p, _ in out_places], head_cols, width), out_dealt
    )
    return (
        outcome[None],
        grad_inputs[None],
        grad_qkv,
        grad_out,
        gain_one_sum[:, 0],
        grad_gate_up,
        grad_down,
        gain_two_sum[:, 0],
    )


def solution(mesh):
    seqs, devices = mesh.shape["seq"], mesh.shape["fsdp"]
    parted = Mesh(mesh.devices.reshape(seqs, devices // 2, 2), ("seq", "z", "core"))
    tokens = P(("z", "core"), "seq", None)
    matrix = P(("seq", "z", "core"), None)
    vector = P(("seq", "z", "core"))
    return jax.shard_map(
        functools.partial(per_device, parted),
        mesh=parted,
        in_specs=(
            tokens,
            P(("z", "core"), "seq"),
            matrix,
            matrix,
            vector,
            matrix,
            matrix,
            vector,
            tokens,
        ),
        out_specs=(tokens, tokens, matrix, matrix, vector, matrix, matrix, vector),
        check_vma=False,
    )
```

```python
import functools
import math

import jax
import jax.numpy as jnp
from jax import lax
from jax.experimental import pallas as pl
from jax.experimental.pallas import tpu as pltpu
from jax.sharding import Mesh, PartitionSpec as P

HEAD_DIM = 64
PAIR = 2 * HEAD_DIM
BLOCK = 256
EPS = 1e-05
ROPE_BASE = 130000.0
BF = jnp.bfloat16
F32 = jnp.float32
VMEM_LIMIT = 48 << 20
MESH = pl.DeviceIdType.MESH
ANYWHERE = pl.BlockSpec(memory_space=pl.ANY)
LOCAL = pl.BlockSpec(memory_space=pltpu.VMEM)


def kernel_call(body, name, **spec):
    return pl.pallas_call(
        body,
        name=name,
        compiler_params=pltpu.CompilerParams(vmem_limit_bytes=VMEM_LIMIT),
        **spec,
    )


def turn(x, cosine, sine):
    half = HEAD_DIM // 2
    lane = lax.broadcasted_iota(jnp.int32, x.shape, 1)
    swapped = jnp.where(
        lane % HEAD_DIM < half, pltpu.roll(x, PAIR - half, 1), pltpu.roll(x, half, 1)
    )
    return x * cosine + swapped * sine


def nt(left, right):
    return lax.dot_general(left, right, (((1,), (1,)), ((), ())), preferred_element_type=F32)


def tn(left, right):
    return lax.dot_general(left, right, (((0,), (0,)), ((), ())), preferred_element_type=F32)


def nn(left, right):
    return lax.dot_general(left, right, (((1,), (0,)), ((), ())), preferred_element_type=F32)


def masked_scores(queries, keys, block):
    scores = nt(queries, keys)
    rows = lax.broadcasted_iota(jnp.int32, (BLOCK, BLOCK), 0)
    cols = lax.broadcasted_iota(jnp.int32, (BLOCK, BLOCK), 1)
    last = jnp.where(cols <= rows, scores[:, block * BLOCK :], -1e30)
    return jnp.concatenate([scores[:, : block * BLOCK], last], 1) if block else last


def unpack(table):
    half = HEAD_DIM // 2
    cosine, sine = table[:, :half], table[:, half:HEAD_DIM]
    return (
        jnp.concatenate([cosine] * 4, 1),
        jnp.concatenate([-sine, sine] * 2, 1),
    )


def attend_body(mixed, table, qkv, out, logs):
    length = mixed.shape[0]
    cosine, sine = unpack(table[...])
    qkv[:, :PAIR] = turn(mixed[:, :PAIR], cosine, sine).astype(BF)
    qkv[:, PAIR : 2 * PAIR] = turn(mixed[:, PAIR : 2 * PAIR], cosine, sine).astype(BF)
    qkv[:, 2 * PAIR :] = mixed[:, 2 * PAIR :].astype(BF)
    scale = jnp.asarray(1.0 / math.sqrt(HEAD_DIM), BF)
    for block in range(length // BLOCK):
        at = pl.ds(block * BLOCK, BLOCK)
        seen = (block + 1) * BLOCK
        outs = []
        totals = []
        for low in (0, HEAD_DIM):
            high = low + HEAD_DIM
            queries = qkv[at, low:high] * scale
            scores = masked_scores(queries, qkv[:seen, PAIR + low : PAIR + high], block)
            highest = jnp.max(scores, -1, keepdims=True)
            weights = jnp.exp(scores - highest)
            summed = jnp.sum(weights, -1, keepdims=True)
            probs = (weights * (1.0 / summed)).astype(BF)
            outs.append(nn(probs, qkv[:seen, 2 * PAIR + low : 2 * PAIR + high]))
            totals.append(jnp.broadcast_to(highest + jnp.log(summed), (BLOCK, HEAD_DIM)))
        out[at, :] = jnp.concatenate(outs, 1).astype(BF)
        logs[at, :] = jnp.concatenate(totals, 1)


def attend_back_body(qkv, grad, logs, table, grad_qkv, grad_keys, grad_values):
    length = qkv.shape[0]
    scale = 1.0 / math.sqrt(HEAD_DIM)
    cosine, sine = unpack(table[...])
    last = length // BLOCK - 1
    for block in range(last, -1, -1):
        at = pl.ds(block * BLOCK, BLOCK)
        seen = (block + 1) * BLOCK
        rows = slice(block * BLOCK, seen)
        grad_queries = []
        for low in (0, HEAD_DIM):
            high = low + HEAD_DIM
            queries = qkv[at, low:high] * jnp.asarray(scale, BF)
            keys = qkv[:seen, PAIR + low : PAIR + high]
            upstream = grad[at, low:high]
            scores = masked_scores(queries, keys, block)
            probs = jnp.exp(scores - logs[at, low : low + 1])
            grad_probs = nt(upstream, qkv[:seen, 2 * PAIR + low : 2 * PAIR + high])
            inner = jnp.sum(probs * grad_probs, -1, keepdims=True)
            grad_scores = (probs * (grad_probs - inner)).astype(BF)
            grad_queries.append(nn(grad_scores, keys))
            for_keys = tn(grad_scores, queries)
            for_values = tn(probs.astype(BF), upstream)
            if block == last:
                grad_keys[:, low:high] = for_keys
                grad_values[:, low:high] = for_values
            else:
                grad_keys[:seen, low:high] += for_keys
                grad_values[:seen, low:high] += for_values
        rounded = (jnp.concatenate(grad_queries, 1) * scale).astype(BF).astype(F32)
        grad_qkv[at, :PAIR] = turn(rounded, cosine[rows], -sine[rows]).astype(BF)
    rounded = grad_keys[...].astype(BF).astype(F32)
    grad_qkv[:, PAIR : 2 * PAIR] = turn(rounded, cosine, -sine).astype(BF)
    grad_qkv[:, 2 * PAIR :] = grad_values[...].astype(BF)


def heads_call(body, name, arrays, kinds, outs, out_kinds, count, beside, number, scratch):
    tokens = arrays[0].shape[0]
    length = tokens // count
    pairs = arrays[0].shape[1] // (3 * PAIR)
    specs = {
        "wide": pl.BlockSpec((length, 3 * PAIR), lambda s, i: (s, i)),
        "one": pl.BlockSpec((length, PAIR), lambda s, i: (s, i)),
        "table": pl.BlockSpec((length, PAIR), lambda s, i: (s, 0)),
    }
    n_in, n_out = len(arrays), len(outs)
    more_in, more_out = len(beside.arrays), len(beside.outs)

    def whole(*refs):
        ins, given = refs[:n_in], refs[n_in : n_in + more_in]
        rest = refs[n_in + more_in :]
        results, made = rest[:n_out], rest[n_out : n_out + more_out]
        rest = rest[n_out + more_out :]
        room, held = rest[: len(beside.scratch)], rest[len(beside.scratch) :]
        step = pl.program_id(0) * pairs + pl.program_id(1)
        last = count * pairs - 1
        acts = beside.acts(given, made, room)
        when = [min(2 * i, last + 1) for i in range(len(acts) - 1)] + [last + 1]
        for i, act in enumerate(acts):
            if when[i] <= last:
                pl.when(step == when[i])(act)
        body(*ins, *results, *held)

        @pl.when(step == last)
        def _():
            for i, act in enumerate(acts):
                if when[i] > last:
                    act()

    return reaching_call(
        whole,
        name,
        number,
        grid=(count, pairs),
        in_specs=[specs[kind] for kind in kinds] + [ANYWHERE] * more_in,
        out_specs=[specs[kind] for kind in out_kinds] + [ANYWHERE] * more_out,
        out_shape=list(outs) + list(beside.outs),
        scratch_shapes=list(beside.scratch) + scratch(length),
    )(*arrays, *beside.arrays)


class Beside:
    def __init__(self, seqs, own=None, pieces=()):
        self.seqs = seqs
        self.spreads = own is not None
        self.arrays = ([own] if self.spreads else []) + list(pieces)
        self.outs = [jax.ShapeDtypeStruct(piece.shape, BF) for piece in pieces]
        self.scratch = deal_scratch(pieces, seqs) if pieces else []
        self.first = len(self.scratch)
        if self.spreads:
            self.outs.insert(0, jax.ShapeDtypeStruct((2, seqs) + own.shape, BF))
            self.scratch += [pltpu.VMEM(own.shape, BF), pltpu.SemaphoreType.DMA]
            self.scratch += spread_scratch(seqs)

    def acts(self, given, made, room):
        at = 1 if self.spreads else 0
        place = room[self.first :]

        def dealing():
            return Deal(given[at:], made[at:], room[: self.first])

        def spreading():
            return Spread(place[0], made[0], place[2:])

        def begin():
            if self.spreads:
                copy = pltpu.make_async_copy(given[0], place[0], place[1])
                copy.start()
            greet(all_partners(self.seqs))
            if self.spreads:
                copy.wait()
                spreading().begin()
            if self.first:
                dealing().begin()

        def finish():
            if self.spreads:
                spreading().finish()
            if self.first:
                dealing().finish()

        def step(phase):
            return lambda: spreading().step(phase)

        phases = len(bits_of(self.seqs)) if self.spreads else 1
        return [begin] + [step(i) for i in range(1, phases)] + [finish]


def attend(mixed, table, beside, count, number):
    tokens, cols = mixed.shape
    outs = [
        jax.ShapeDtypeStruct((tokens, cols), BF),
        jax.ShapeDtypeStruct((tokens, cols // 3), BF),
        jax.ShapeDtypeStruct((tokens, cols // 3), F32),
    ]
    return heads_call(
        attend_body,
        "attend",
        [mixed, table],
        ["wide", "table"],
        outs,
        ["wide", "one", "one"],
        count,
        beside,
        number,
        lambda length: [],
    )


def attend_back(qkv, grad, logs, table, beside, count, number):
    return heads_call(
        attend_back_body,
        "attend_back",
        [qkv, grad, logs, table],
        ["wide", "one", "one", "table"],
        [jax.ShapeDtypeStruct(qkv.shape, BF)],
        ["wide"],
        count,
        beside,
        number,
        lambda length: [pltpu.VMEM((length, PAIR), F32)] * 2,
    )


def qkv_columns(owners, cols):
    for owner in range(owners):
        for pair in range(cols // PAIR):
            for kind in range(3):
                there = (pair * 3 + kind) * PAIR
                yield owner, there, (kind * owners + owner) * cols + pair * PAIR, PAIR


def chunk_widths(cols):
    units = cols // PAIR
    first = max(1, (5 * units) // 8)
    return [n * PAIR for n in (first, units - first) if n]


def ff_columns(owners, cols):
    begin = 0
    gate_up, down = [], []
    for part in chunk_widths(cols):
        gate_up.append(
            [
                (owner, kind * part, (kind * owners + owner) * cols + begin, part)
                for owner in range(owners)
                for kind in range(2)
            ]
        )
        down.append([(owner, 2 * part, owner * cols + begin, part) for owner in range(owners)])
        begin += part
    return gate_up, down


def cut(weights, gains, plan, cols, owners):
    rows = weights[0].shape[0]
    scaled = [gain is not None for gain in gains]
    arrays = list(weights) + [gain for gain in gains if gain is not None]
    gain_at = [len(weights) + sum(scaled[:i]) for i in range(len(weights))]

    def body(*refs):
        for out, parts in zip(refs[len(arrays) :], plan):
            for which, places in parts:
                for owner, there, here, width in places:
                    part = refs[which][:, here : here + width]
                    if scaled[which]:
                        part = (part.astype(F32) * refs[gain_at[which]][...]).astype(BF)
                    out[owner, :, there : there + width] = part

    return kernel_call(
        body,
        "cut",
        out_shape=[jax.ShapeDtypeStruct((owners, rows, n), BF) for n in cols],
    )(*arrays)


def side_by_side(left, right):
    def body(one, two, out, sems):
        cut = left.shape[1]
        copies = [
            pltpu.make_async_copy(one, out.at[:, pl.ds(0, cut)], sems.at[0]),
            pltpu.make_async_copy(two, out.at[:, pl.ds(cut, right.shape[1])], sems.at[1]),
        ]
        for copy in copies:
            copy.start()
        for copy in copies:
            copy.wait()

    return kernel_call(
        body,
        "side_by_side",
        in_specs=[LOCAL, LOCAL],
        out_specs=ANYWHERE,
        out_shape=jax.ShapeDtypeStruct((left.shape[0], left.shape[1] + right.shape[1]), BF),
        scratch_shapes=[pltpu.SemaphoreType.DMA((2,))],
    )(left, right)


def blocks_in(rows, seqs, chips):
    return [
        ((s * chips + z) * 2 * rows, (z * seqs + s) * 2 * rows, 2 * rows)
        for z in range(chips)
        for s in range(seqs)
    ]


def inside(arrays, blocks):
    def body(*refs):
        for source, out in zip(refs[: len(arrays)], refs[len(arrays) :]):
            for outer, inner, width in blocks:
                out[:, inner : inner + width] = source[:, outer : outer + width]

    return kernel_call(
        body, "inside", out_shape=[jax.ShapeDtypeStruct(a.shape, a.dtype) for a in arrays]
    )(*arrays)


def join_ff(sums, w_gate_up, gain, gate_up_places, down_places):
    rows, total_width = w_gate_up.shape
    count = len(sums)

    def body(*refs):
        weights, gains, out, out_gain, out_down = refs[count:]
        total = jnp.zeros((rows, PAIR), F32)
        for source, listed in zip(refs[:count], gate_up_places):
            for owner, there, here, width in listed:
                for step in range(0, width, PAIR):
                    part = source[owner, :, there + step : there + step + PAIR].astype(F32)
                    at = slice(here + step, here + step + PAIR)
                    total += part * weights[:, at].astype(F32)
                    out[:, at] = part * gains[...]
        for source, listed in zip(refs[:count], down_places):
            for owner, there, here, width in listed:
                out_down[:, here : here + width] = source[owner, :, there : there + width].astype(
                    F32
                )
        out_gain[...] = jnp.sum(total, 1, keepdims=True)

    return kernel_call(
        body,
        "join_ff",
        out_shape=[
            jax.ShapeDtypeStruct((rows, total_width), F32),
            jax.ShapeDtypeStruct((rows, 1), F32),
            jax.ShapeDtypeStruct((rows, total_width // 2), F32),
        ],
    )(*sums, w_gate_up, gain)


def join_attend(sums, w_qkv, gain, qkv_places, out_places):
    rows, total_width = w_qkv.shape

    def body(source, weights, gains, out, out_gain, out_out):
        total = jnp.zeros((rows, PAIR), F32)
        for owner, there, here, width in qkv_places:
            part = source[owner, :, there : there + width].astype(F32)
            total += part * weights[:, here : here + width].astype(F32)
            out[:, here : here + width] = part * gains[...]
        for owner, there, here, width in out_places:
            out_out[:, here : here + width] = source[owner, :, there : there + width].astype(F32)
        out_gain[...] = jnp.sum(total, 1, keepdims=True)

    return kernel_call(
        body,
        "join_attend",
        out_shape=[
            jax.ShapeDtypeStruct((rows, total_width), F32),
            jax.ShapeDtypeStruct((rows, 1), F32),
            jax.ShapeDtypeStruct((rows, total_width // 3), F32),
        ],
    )(sums, w_qkv, gain)


def flip(index, offset):
    weight = 1
    while weight <= offset:
        if offset & weight:
            index = index + weight - 2 * weight * ((index // weight) % 2)
        weight *= 2
    return index


def greet(partners):
    barrier = pltpu.get_barrier_semaphore()
    for partner in partners:
        pl.semaphore_signal(barrier, inc=1, device_id=partner, device_id_type=MESH)
    pl.semaphore_wait(barrier, len(partners))


def here():
    return lax.axis_index("seq"), lax.axis_index("core")


def bits_of(seqs):
    return [1 << bit for bit in range(seqs.bit_length() - 1)]


def cube_partners(seqs):
    me, core = here()
    partners = [{"seq": flip(me, bit), "core": core} for bit in bits_of(seqs)]
    return partners + [{"seq": me, "core": 1 - core}]


def all_partners(seqs):
    me, core = here()
    return [
        {"seq": flip(me, step), "core": core if same else 1 - core}
        for step in range(seqs)
        for same in (True, False)
        if step or not same
    ]


def orders_of(seqs):
    bits = bits_of(seqs)
    return [bits, bits[1:] + bits[:1]]


def remote(source, target, sems, at, device):
    return pltpu.make_async_remote_copy(
        src_ref=source,
        dst_ref=target,
        send_sem=sems[0].at[at],
        recv_sem=sems[1].at[at],
        device_id=device,
        device_id_type=MESH,
    )


def push(*where):
    copy = remote(*where)
    copy.start()
    return copy


def pair_sems(*shape):
    return [pltpu.SemaphoreType.DMA(shape)] * 2


def spread_scratch(seqs):
    return pair_sems(2, seqs) + pair_sems(2, seqs) + [pltpu.SemaphoreType.DMA]


class Spread:
    def __init__(self, own, out, scratch):
        self.own, self.out = own, out
        self.across, self.aside, self.local = scratch[0:2], scratch[2:4], scratch[4]
        self.me, self.core = here()
        self.half = out.shape[-1] // 2
        self.orders = orders_of(out.shape[1])
        self.phases = len(self.orders[0])

    def columns(self, ref, stream):
        return ref.at[:, pl.ds(stream * self.half, self.half)]

    def place(self, offset, stream):
        return self.columns(self.out.at[self.core, flip(self.me, offset)], stream)

    def block(self, offset, stream):
        return self.place(offset, stream) if offset else self.columns(self.own, stream)

    def kept(self):
        return pltpu.make_async_copy(self.own, self.out.at[self.core, self.me], self.local)

    def swap(self, offset, stream):
        sibling = {"seq": self.me, "core": 1 - self.core}
        return remote(
            self.block(offset, stream),
            self.place(offset, stream),
            self.aside,
            (stream, offset),
            sibling,
        )

    def held(self, phase, stream):
        offsets = [0]
        for bit in self.orders[stream][:phase]:
            offsets += [offset + bit for offset in offsets]
        return offsets

    def moves(self, phase):
        found = []
        for stream in range(2):
            bit = self.orders[stream][phase]
            partner = {"seq": flip(self.me, bit), "core": self.core}
            for offset in self.held(phase, stream):
                copy = remote(
                    self.block(offset, stream),
                    self.place(offset, stream),
                    self.across,
                    (stream, offset + bit),
                    partner,
                )
                found.append((copy, offset + bit, stream))
        return found

    def begin(self):
        self.kept().start()
        for copy, _, _ in self.moves(0):
            copy.start()
        for stream in range(2):
            self.swap(0, stream).start()

    def arrive(self, phase):
        for copy, offset, stream in self.moves(phase):
            copy.wait_recv()
            self.swap(offset, stream).start()

    def step(self, phase):
        self.arrive(phase - 1)
        for copy, _, _ in self.moves(phase):
            copy.start()

    def finish(self):
        self.arrive(self.phases - 1)
        for phase in range(self.phases):
            for copy, _, _ in self.moves(phase):
                copy.wait_send()
        for stream in range(2):
            for offset in self.held(self.phases, stream):
                self.swap(offset, stream).wait()
        self.kept().wait()


def spread(own, out, scratch):
    work = Spread(own, out, scratch)
    work.begin()
    for phase in range(1, work.phases):
        work.step(phase)
    work.finish()


def fold_scratch(seqs, tokens, width):
    return [
        pltpu.VMEM((seqs, tokens, width), BF),
        pltpu.VMEM((2, seqs, tokens, width // 2), BF),
    ] + pair_sems(seqs) + pair_sems(2, seqs)


def fold(terms, scratch):
    total, got, aside, across = scratch[0], scratch[1], scratch[2:4], scratch[4:6]
    seqs, tokens, width = total.shape
    half = width // 2
    step = min(32, tokens)
    me, core = here()
    sibling = {"seq": me, "core": 1 - core}
    orders = orders_of(seqs)
    offsets = list(range(seqs - 1, -1, -1))
    given = {}
    for offset in offsets:
        at = flip(me, offset)
        given[offset] = push(terms.at[1 - core, at], total.at[at], aside, (offset,), sibling)
    started = []

    def send(stream, phase, offset):
        bit = orders[stream][phase]
        columns = pl.ds(stream * half, half)
        copy = push(
            total.at[flip(me, offset), :, columns],
            got.at[stream, offset],
            across,
            (stream, offset),
            {"seq": flip(me, bit), "core": core},
        )
        started.append(copy)
        return copy

    coming = [[], []]
    for offset in offsets:
        given[offset].wait_recv()
        at = flip(me, offset)

        def add_sibling(i, carry, at=at):
            rows = pl.ds(pl.multiple_of(i * step, step), step)
            both = total[at, rows, :].astype(F32) + terms[core, at, rows, :].astype(F32)
            total[at, rows, :] = both.astype(BF)
            return carry

        lax.fori_loop(0, tokens // step, add_sibling, 0)
        for stream in range(2):
            if offset & orders[stream][0]:
                coming[stream].append((send(stream, 0, offset), offset))
    for phase in range(len(orders[0])):
        for stream in range(2):
            bit = orders[stream][phase]
            for copy, offset in coming[stream]:
                copy.wait_recv()
                at = flip(me, offset - bit)

                def add_got(i, carry, at=at, stream=stream, offset=offset):
                    rows = pl.ds(pl.multiple_of(i * step, step), step)
                    columns = pl.ds(stream * half, half)
                    both = total[at, rows, columns].astype(F32) + got[
                        stream, offset, rows, :
                    ].astype(F32)
                    total[at, rows, columns] = both.astype(BF)
                    return carry

                lax.fori_loop(0, tokens // step, add_got, 0)
            if phase + 1 < len(orders[0]):
                done = sum(orders[stream][: phase + 1])
                following = orders[stream][phase + 1]
                coming[stream] = [
                    (send(stream, phase + 1, offset), offset)
                    for offset in offsets
                    if offset & following and not offset & done
                ]
    for copy in list(given.values()) + started:
        copy.wait_send()
    return total.at[me]


def by_rows(count, work):
    step = min(32, count)

    def one(i, carry):
        work(pl.ds(pl.multiple_of(i * step, step), step))
        return carry

    lax.fori_loop(0, count // step, one, 0)


def reaching_call(body, name, number, **spec):
    return pl.pallas_call(
        body,
        name=name,
        compiler_params=pltpu.CompilerParams(
            vmem_limit_bytes=VMEM_LIMIT, collective_id=number, has_side_effects=True
        ),
        **spec,
    )


def deal_scratch(pieces, seqs):
    blocks = [piece.shape[-2:] for piece in pieces]
    return (
        pair_sems(len(pieces), 2 * seqs)
        + [pltpu.SemaphoreType.DMA((2, len(pieces)))]
        + [pltpu.VMEM(block, piece.dtype) for block, piece in zip(blocks, pieces)]
    )


class Deal:
    def __init__(self, pieces, outs, scratch):
        self.pieces, self.outs = pieces, outs
        self.sems, self.local, self.rooms = scratch[:2], scratch[2], scratch[3:]
        self.me, self.core = here()

    def cut_up(self, i):
        return len(self.pieces[i].shape) == len(self.outs[i].shape)

    def copies(self):
        found = []
        for i, (piece, out) in enumerate(zip(self.pieces, self.outs)):
            for step in range(out.shape[0]):
                for same in (True, False):
                    if step or not same:
                        to_seq = flip(self.me, step)
                        to_core = self.core if same else 1 - self.core
                        found.append(
                            remote(
                                piece.at[to_seq, to_core] if self.cut_up(i) else piece,
                                out.at[self.me, self.core],
                                self.sems,
                                (i, 2 * step + (0 if same else 1)),
                                {"seq": to_seq, "core": to_core},
                            )
                        )
        return found

    def entering(self):
        return [
            pltpu.make_async_copy(
                piece.at[self.me, self.core] if self.cut_up(i) else piece,
                self.rooms[i],
                self.local.at[0, i],
            )
            for i, piece in enumerate(self.pieces)
        ]

    def leaving(self):
        return [
            pltpu.make_async_copy(
                self.rooms[i], out.at[self.me, self.core], self.local.at[1, i]
            )
            for i, out in enumerate(self.outs)
        ]

    def begin(self):
        for copy in self.copies() + self.entering():
            copy.start()
        for copy in self.entering():
            copy.wait()
        for copy in self.leaving():
            copy.start()

    def finish(self):
        for copy in self.copies() + self.leaving():
            copy.wait()


def deal(pieces, number):
    count = len(pieces)
    seqs = pieces[0].shape[0]

    def body(*refs):
        greet(all_partners(seqs))
        work = Deal(refs[:count], refs[count : 2 * count], refs[2 * count :])
        work.begin()
        work.finish()

    return reaching_call(
        body,
        "deal",
        number,
        in_specs=[ANYWHERE] * count,
        out_specs=[ANYWHERE] * count,
        out_shape=[jax.ShapeDtypeStruct(piece.shape, BF) for piece in pieces],
        scratch_shapes=deal_scratch(pieces, seqs),
    )(*pieces)


def first_acts(tokens, table, pieces, seqs, number):
    count, width = tokens.shape
    pieces = list(pieces) + [table]
    n = len(pieces)
    shapes = [piece.shape for piece in pieces[:-1]] + [(seqs, 2) + table.shape]

    def body(*refs):
        source, given = refs[0], refs[1 : 1 + n]
        out, outs = refs[1 + n], refs[2 + n : 2 + 2 * n]
        own, *scratch = refs[2 + 2 * n :]
        greet(all_partners(seqs))

        def norm(rows):
            values = source[rows, :].astype(F32)
            own[rows, :] = (values * norm_scale(values)).astype(BF)

        by_rows(count, norm)
        dealing = Deal(given, outs, scratch[5:])
        dealing.begin()
        spread(own, out, scratch[:5])
        dealing.finish()

    return reaching_call(
        body,
        "first_acts",
        number,
        in_specs=[LOCAL] + [ANYWHERE] * n,
        out_specs=[ANYWHERE] * (1 + n),
        out_shape=[jax.ShapeDtypeStruct((2, seqs, count, width), BF)]
        + [jax.ShapeDtypeStruct(shape, p.dtype) for shape, p in zip(shapes, pieces)],
        scratch_shapes=[pltpu.VMEM((count, width), BF)]
        + spread_scratch(seqs)
        + deal_scratch(pieces, seqs),
    )(tokens, *pieces)


def middle_acts(terms, tokens, number):
    _, seqs, count, width = terms.shape

    def body(given, source, middle, out, own, *scratch):
        greet(cube_partners(seqs))
        total = fold(given, scratch[:6])

        def norm(rows):
            values = source[rows, :].astype(F32) + total[rows, :].astype(F32)
            middle[rows, :] = values
            own[rows, :] = (values * norm_scale(values)).astype(BF)

        by_rows(count, norm)
        spread(own, out, scratch[6:])

    return reaching_call(
        body,
        "middle_acts",
        number,
        in_specs=[LOCAL, LOCAL],
        out_specs=[LOCAL, ANYWHERE],
        out_shape=[
            jax.ShapeDtypeStruct((count, width), F32),
            jax.ShapeDtypeStruct(terms.shape, BF),
        ],
        scratch_shapes=[pltpu.VMEM((count, width), BF)]
        + fold_scratch(seqs, count, width)
        + spread_scratch(seqs),
    )(terms, tokens)


def middle_grad(terms, cotangent, middle, number):
    _, seqs, count, width = terms.shape

    def body(given, upstream, values, grad, out, own, *scratch):
        greet(cube_partners(seqs))
        total = fold(given, scratch[:6])

        def back(rows):
            held = values[rows, :]
            scale = norm_scale(held)
            result = upstream[rows, :].astype(F32) + norm_back(
                total[rows, :].astype(F32), held * scale, scale
            )
            grad[rows, :] = result
            own[rows, :] = result.astype(BF)

        by_rows(count, back)
        spread(own, out, scratch[6:])

    return reaching_call(
        body,
        "middle_grad",
        number,
        in_specs=[LOCAL] * 3,
        out_specs=[LOCAL, ANYWHERE],
        out_shape=[
            jax.ShapeDtypeStruct((count, width), F32),
            jax.ShapeDtypeStruct(terms.shape, BF),
        ],
        scratch_shapes=[pltpu.VMEM((count, width), BF)]
        + fold_scratch(seqs, count, width)
        + spread_scratch(seqs),
    )(terms, cotangent, middle)


def input_grad(terms, tokens, grad_middle, blocks, number):
    _, seqs, count, width = terms.shape

    def body(given, source, held, out, *scratch):
        greet(cube_partners(seqs))
        total = fold(given, scratch)

        def back(rows):
            values = source[rows, :].astype(F32)
            scale = norm_scale(values)
            result = held[rows, :] + norm_back(total[rows, :].astype(F32), values * scale, scale)
            for outer, inner, size in blocks:
                out[rows, outer : outer + size] = result[:, inner : inner + size]

        by_rows(count, back)

    return reaching_call(
        body,
        "input_grad",
        number,
        in_specs=[LOCAL] * 3,
        out_specs=LOCAL,
        out_shape=jax.ShapeDtypeStruct((count, width), F32),
        scratch_shapes=fold_scratch(seqs, count, width),
    )(terms, tokens, grad_middle)


def block_output(terms, middle, blocks, pieces, number):
    _, seqs, count, width = terms.shape
    n = len(pieces)

    def body(given, held, *refs):
        out = refs[n]
        scratch = refs[1 + 2 * n :]
        greet(all_partners(seqs))
        dealing = Deal(refs[:n], refs[1 + n : 1 + 2 * n], scratch[6:])
        if n:
            dealing.begin()
        total = fold(given, scratch[:6])

        def add(rows):
            result = held[rows, :] + total[rows, :].astype(F32)
            for outer, inner, size in blocks:
                out[rows, outer : outer + size] = result[:, inner : inner + size].astype(BF)

        by_rows(count, add)
        if n:
            dealing.finish()

    return reaching_call(
        body,
        "block_output",
        number,
        in_specs=[LOCAL] * 2 + [ANYWHERE] * n,
        out_specs=[LOCAL] + [ANYWHERE] * n,
        out_shape=[jax.ShapeDtypeStruct((count, width), BF)]
        + [jax.ShapeDtypeStruct(piece.shape, BF) for piece in pieces],
        scratch_shapes=fold_scratch(seqs, count, width)
        + (deal_scratch(pieces, seqs) if n else []),
    )(terms, middle, *pieces)


class Order:
    def __init__(self):
        self.latest = None

    def enter(self, values):
        if self.latest is None:
            return values
        return lax.optimization_barrier((values, self.latest))[0]

    def run(self, work, *values):
        result = work(*self.enter(values))
        self.latest = jax.tree.leaves(result)[0]
        return result

    def take(self, values):
        if self.latest is not None:
            values = lax.optimization_barrier((values, self.latest))[0]
        self.latest = jax.tree.leaves(values)[0]
        return values


def rope_table(places):
    half = HEAD_DIM // 2
    inverse = ROPE_BASE ** (-2.0 * jnp.arange(half).astype(F32) / HEAD_DIM)
    angles = places.astype(F32)[:, None] * inverse[None, :]
    return jnp.concatenate([jnp.cos(angles), jnp.sin(angles)] * 2, 1)


def norm_scale(values):
    return lax.rsqrt(jnp.mean(values * values, -1, keepdims=True) + EPS)


def norm_back(grad, normed, scale):
    return scale * (grad - normed * jnp.mean(grad * normed, -1, keepdims=True))


def per_device(
    mesh, tokens, positions, w_qkv, w_out, gain_attn, w_gate_up, w_down, gain_mlp, cotangent
):
    order = Order()
    seqs, chips = mesh.shape["seq"], mesh.shape["z"]
    owners = 2 * seqs
    token_count, width = tokens.shape[1:]
    ff_width = w_down.shape[1]
    rows = w_qkv.shape[0]
    head_cols = width // owners
    ff_cols = ff_width // owners
    parts = chunk_widths(ff_cols)
    last = len(parts) - 1
    blocks = blocks_in(rows, seqs, chips)
    gain_one = gain_attn.astype(F32)[:, None]
    gain_two = gain_mlp.astype(F32)[:, None]

    def by_place(piece):
        return piece.reshape(seqs, 2, rows, -1)

    def gathered(piece):
        piece = order.enter(piece).reshape(seqs, 2 * rows, -1)
        return lax.all_gather(piece, "z", axis=0, tiled=False)

    def flat(value):
        return order.take(value).reshape(width, -1)

    def summed(term):
        split = order.enter(term).reshape(chips, seqs, 2 * rows, -1)
        return lax.psum_scatter(split, "z", scatter_dimension=0, tiled=False)

    def rounded(left, right):
        return tn(left, right).astype(BF)

    def terms_of(total):
        return total.astype(BF).reshape(2, seqs, token_count, width)

    qkv_places = list(qkv_columns(owners, head_cols))
    out_places = [(o, 3 * head_cols, o * head_cols, head_cols) for o in range(owners)]
    gate_up_places, down_places = ff_columns(owners, ff_cols)
    (attend_cut,) = order.run(
        lambda a, b, g: cut(
            [a, b], [g, None], [[(0, qkv_places), (1, out_places)]], [4 * head_cols], owners
        ),
        w_qkv,
        w_out,
        gain_one,
    )
    (attend_piece,) = order.run(lambda a: deal([a], 1), by_place(attend_cut))
    attend_coming = gathered(attend_piece)
    ff_cut = order.run(
        lambda a, b, g: cut(
            [a, b],
            [g, None],
            [[(0, pair), (1, single)] for pair, single in zip(gate_up_places, down_places)],
            [3 * part for part in parts],
            owners,
        ),
        w_gate_up,
        w_down,
        gain_two,
    )
    table_own = order.run(rope_table, positions[0])
    tokens_in, upstream_own = order.run(
        lambda a, b: inside([a, b], blocks), tokens[0], cotangent[0]
    )
    acts, ff_piece, table = order.run(
        lambda x, t, a: first_acts(x, t, [a], seqs, 2), tokens_in, table_own, by_place(ff_cut[0])
    )
    acts = acts.reshape(-1, width)
    table = jnp.moveaxis(table, 1, 0).reshape(-1, PAIR)
    ff_coming = [gathered(ff_piece)]

    qkv_cols = 3 * head_cols
    attend_whole = flat(attend_coming)
    mixed = order.run(lambda a, w: nn(a, w[:, :qkv_cols]), acts, attend_whole)
    qkv, attended, logs, upstream, *ff_pieces = order.run(
        lambda m, t, u, *given: attend(m, t, Beside(seqs, u, given), 2, 3),
        mixed,
        table,
        upstream_own,
        *[by_place(piece) for piece in ff_cut[1:]],
    )
    ff_coming += [gathered(piece) for piece in ff_pieces]
    upstream = upstream.reshape(-1, width)
    branch = order.run(lambda a, w: terms_of(nt(a, w[:, qkv_cols:])), attended, attend_whole)
    middle, acts_mid = order.run(lambda a, b: middle_acts(a, b, 4), branch, tokens_in)
    acts_mid = acts_mid.reshape(-1, width)

    def feed_hidden(both):
        part = both.shape[1] // 2
        gate, up = both[:, :part], both[:, part:]
        return (gate * jax.nn.sigmoid(gate) * up).astype(BF)

    def feed_back(grad_hidden, both):
        part = both.shape[1] // 2
        gate, up = both[:, :part], both[:, part:]
        sigma = jax.nn.sigmoid(gate)
        grad_gate = grad_hidden * up * sigma * (1.0 + gate * (1.0 - sigma))
        grad_up = grad_hidden * gate * sigma
        return jnp.concatenate([grad_gate.astype(BF), grad_up.astype(BF)], 1)

    def both_terms(left, right, left_two, right_two):
        return side_by_side(rounded(left, right), rounded(left_two, right_two))

    def add_nt(left, right, total=None):
        result = nt(left, right)
        return (result if total is None else result + total.astype(F32)).astype(BF)

    ff_sums = []
    norm_mid_terms, outcome_terms = (), ()
    for chunk, part in enumerate(parts):
        cols = 2 * part
        whole = flat(ff_coming[chunk])
        both = order.run(lambda a, w: nn(a, w[:, :cols]), acts_mid, whole)
        hidden = order.run(feed_hidden, both)
        grad_hidden = order.run(lambda a, w: nn(a, w[:, cols:]), upstream, whole)
        grad_both = order.run(feed_back, grad_hidden, both)
        norm_mid_terms = (
            order.run(lambda a, w, *t: add_nt(a, w[:, :cols], *t), grad_both, whole, *norm_mid_terms),
        )
        term = order.run(both_terms, acts_mid, grad_both, upstream, hidden)
        ff_sums.append(summed(term))
        if chunk < len(parts) - 1:
            outcome_terms = (
                order.run(lambda a, w, *t: add_nt(a, w[:, cols:], *t), hidden, whole, *outcome_terms),
            )

    grad_middle, grad_branch = order.run(
        lambda a, b, c: middle_grad(a, b, c, 5),
        norm_mid_terms[0].reshape(2, seqs, token_count, width),
        upstream_own,
        middle,
    )
    grad_branch = grad_branch.reshape(-1, width)

    grad_attended = order.run(
        lambda a, w: nn(a, w[:, qkv_cols:]).astype(BF), grad_branch, attend_whole
    )
    ff_sums[0] = order.take(ff_sums[0])
    grad_mixed, *ff_dealt = order.run(
        lambda *a: attend_back(*a[:4], Beside(seqs, None, a[4:]), 2, 6),
        qkv,
        grad_attended,
        logs,
        table,
        by_place(ff_sums[0]),
    )
    term = order.run(both_terms, acts, grad_mixed, grad_branch, attended)
    attend_sum = summed(term)
    norm_terms = order.run(lambda a, w: terms_of(nt(a, w[:, :qkv_cols])), grad_mixed, attend_whole)
    grad_inputs = order.run(
        lambda a, b, c: input_grad(a, b, c, blocks, 7), norm_terms, tokens_in, grad_middle
    )
    outcome_terms = order.run(
        lambda a, w, *t: add_nt(a, w[:, cols:], *t), hidden, whole, *outcome_terms
    )

    ff_rows = [by_place(order.take(value)) for value in ff_sums[1:]]
    outcome, *received = order.run(
        lambda a, b, *given: block_output(a, b, blocks, given, 8),
        outcome_terms.reshape(2, seqs, token_count, width),
        middle,
        *ff_rows,
    )
    grad_gate_up, gain_two_sum, grad_down = order.run(
        lambda w, g, *a: join_ff(a, w, g, gate_up_places, down_places),
        w_gate_up,
        gain_two,
        *[value.reshape(owners, rows, -1) for value in ff_dealt + received],
    )
    attend_rows = order.take(attend_sum)
    (attend_dealt,) = order.run(lambda a: deal([a], 9), by_place(attend_rows))
    grad_qkv, gain_one_sum, grad_out = order.run(
        lambda w, g, a: join_attend(a, w, g, qkv_places, out_places),
        w_qkv,
        gain_one,
        attend_dealt.reshape(owners, rows, -1),
    )
    return (
        outcome[None],
        grad_inputs[None],
        grad_qkv,
        grad_out,
        gain_one_sum[:, 0],
        grad_gate_up,
        grad_down,
        gain_two_sum[:, 0],
    )


def solution(mesh):
    seqs, devices = mesh.shape["seq"], mesh.shape["fsdp"]
    parted = Mesh(mesh.devices.reshape(seqs, devices // 2, 2), ("seq", "z", "core"))
    tokens = P(("z", "core"), "seq", None)
    matrix = P(("seq", "z", "core"), None)
    vector = P(("seq", "z", "core"))
    return jax.shard_map(
        functools.partial(per_device, parted),
        mesh=parted,
        in_specs=(
            tokens,
            P(("z", "core"), "seq"),
            matrix,
            matrix,
            vector,
            matrix,
            matrix,
            vector,
            tokens,
        ),
        out_specs=(tokens, tokens, matrix, matrix, vector, matrix, matrix, vector),
        check_vma=False,
    )
```

```python
import functools
import math

import jax
import jax.numpy as jnp
from jax import lax
from jax.experimental import pallas as pl
from jax.experimental.pallas import tpu as pltpu
from jax.sharding import Mesh, PartitionSpec as P

HEAD_DIM = 64
PAIR = 2 * HEAD_DIM
BLOCK = 256
EPS = 1e-05
ROPE_BASE = 130000.0
BF = jnp.bfloat16
F32 = jnp.float32
VMEM_MOST = 58 << 20
MESH = pl.DeviceIdType.MESH
ANYWHERE = pl.BlockSpec(memory_space=pltpu.HBM)
LOCAL = pl.BlockSpec(memory_space=pltpu.VMEM)


def room_for(spec, arrays):
    total = 8 << 20
    for room in spec.get("scratch_shapes", ()):
        if hasattr(room, "shape") and room.dtype in (BF, F32):
            total += math.prod(room.shape) * jnp.dtype(room.dtype).itemsize
    outs = spec["out_shape"] if isinstance(spec["out_shape"], list) else [spec["out_shape"]]
    specs = spec.get("out_specs", LOCAL), spec.get("in_specs", LOCAL)
    for values, given in zip((outs, arrays), specs):
        given = given if isinstance(given, list) else [given] * len(values)
        for value, where in zip(values, given):
            if where.block_shape is not None:
                total += 2 * math.prod(where.block_shape) * value.dtype.itemsize
            elif where is not ANYWHERE:
                total += math.prod(value.shape) * value.dtype.itemsize
    return min(total, VMEM_MOST)


def kernel_call(body, name, arrays, number=None, **spec):
    params = {"vmem_limit_bytes": room_for(spec, arrays)}
    if number is not None:
        params.update(vmem_limit_bytes=VMEM_MOST, collective_id=number, has_side_effects=True)
    return pl.pallas_call(
        body, name=name, compiler_params=pltpu.CompilerParams(**params), **spec
    )(*arrays)


def turn(x, cosine, sine):
    half = HEAD_DIM // 2
    lane = lax.broadcasted_iota(jnp.int32, x.shape, 1)
    swapped = jnp.where(
        lane % HEAD_DIM < half, pltpu.roll(x, PAIR - half, 1), pltpu.roll(x, half, 1)
    )
    return x * cosine + swapped * sine


def nt(left, right):
    return lax.dot_general(left, right, (((1,), (1,)), ((), ())), preferred_element_type=F32)


def tn(left, right):
    return lax.dot_general(left, right, (((0,), (0,)), ((), ())), preferred_element_type=F32)


def nn(left, right):
    return lax.dot_general(left, right, (((1,), (0,)), ((), ())), preferred_element_type=F32)


def masked_scores(queries, keys, block):
    scores = nt(queries, keys)
    rows = lax.broadcasted_iota(jnp.int32, (BLOCK, BLOCK), 0)
    cols = lax.broadcasted_iota(jnp.int32, (BLOCK, BLOCK), 1)
    last = jnp.where(cols <= rows, scores[:, block * BLOCK :], -1e30)
    return jnp.concatenate([scores[:, : block * BLOCK], last], 1) if block else last


def unpack(table):
    half = HEAD_DIM // 2
    cosine, sine = table[:, :half], table[:, half:HEAD_DIM]
    return (
        jnp.concatenate([cosine] * 4, 1),
        jnp.concatenate([-sine, sine] * 2, 1),
    )


def attend_body(mixed, table, qkv, out, logs):
    length = mixed.shape[0]
    cosine, sine = unpack(table[...])
    qkv[:, :PAIR] = turn(mixed[:, :PAIR], cosine, sine).astype(BF)
    qkv[:, PAIR : 2 * PAIR] = turn(mixed[:, PAIR : 2 * PAIR], cosine, sine).astype(BF)
    qkv[:, 2 * PAIR :] = mixed[:, 2 * PAIR :].astype(BF)
    scale = jnp.asarray(1.0 / math.sqrt(HEAD_DIM), BF)
    for block in range(length // BLOCK):
        at = pl.ds(block * BLOCK, BLOCK)
        seen = (block + 1) * BLOCK
        outs = []
        totals = []
        for low in (0, HEAD_DIM):
            high = low + HEAD_DIM
            queries = qkv[at, low:high] * scale
            scores = masked_scores(queries, qkv[:seen, PAIR + low : PAIR + high], block)
            highest = jnp.max(scores, -1, keepdims=True)
            weights = jnp.exp(scores - highest)
            summed = jnp.sum(weights, -1, keepdims=True)
            probs = (weights * (1.0 / summed)).astype(BF)
            outs.append(nn(probs, qkv[:seen, 2 * PAIR + low : 2 * PAIR + high]))
            totals.append(jnp.broadcast_to(highest + jnp.log(summed), (BLOCK, HEAD_DIM)))
        out[at, :] = jnp.concatenate(outs, 1).astype(BF)
        logs[at, :] = jnp.concatenate(totals, 1)


def attend_back_body(qkv, grad, logs, table, grad_qkv, grad_keys, grad_values):
    length = qkv.shape[0]
    scale = 1.0 / math.sqrt(HEAD_DIM)
    cosine, sine = unpack(table[...])
    last = length // BLOCK - 1
    for block in range(last, -1, -1):
        at = pl.ds(block * BLOCK, BLOCK)
        seen = (block + 1) * BLOCK
        rows = slice(block * BLOCK, seen)
        grad_queries = []
        for low in (0, HEAD_DIM):
            high = low + HEAD_DIM
            queries = qkv[at, low:high] * jnp.asarray(scale, BF)
            keys = qkv[:seen, PAIR + low : PAIR + high]
            upstream = grad[at, low:high]
            scores = masked_scores(queries, keys, block)
            probs = jnp.exp(scores - logs[at, low : low + 1])
            grad_probs = nt(upstream, qkv[:seen, 2 * PAIR + low : 2 * PAIR + high])
            inner = jnp.sum(probs * grad_probs, -1, keepdims=True)
            grad_scores = (probs * (grad_probs - inner)).astype(BF)
            grad_queries.append(nn(grad_scores, keys))
            for_keys = tn(grad_scores, queries)
            for_values = tn(probs.astype(BF), upstream)
            if block == last:
                grad_keys[:, low:high] = for_keys
                grad_values[:, low:high] = for_values
            else:
                grad_keys[:seen, low:high] += for_keys
                grad_values[:seen, low:high] += for_values
        rounded = (jnp.concatenate(grad_queries, 1) * scale).astype(BF).astype(F32)
        grad_qkv[at, :PAIR] = turn(rounded, cosine[rows], -sine[rows]).astype(BF)
    rounded = grad_keys[...].astype(BF).astype(F32)
    grad_qkv[:, PAIR : 2 * PAIR] = turn(rounded, cosine, -sine).astype(BF)
    grad_qkv[:, 2 * PAIR :] = grad_values[...].astype(BF)


def heads_call(body, name, arrays, kinds, outs, out_kinds, count, beside, number, scratch):
    tokens = arrays[0].shape[0]
    length = tokens // count
    pairs = arrays[0].shape[1] // (3 * PAIR)
    specs = {
        "wide": pl.BlockSpec((length, 3 * PAIR), lambda s, i: (s, i)),
        "one": pl.BlockSpec((length, PAIR), lambda s, i: (s, i)),
        "table": pl.BlockSpec((length, PAIR), lambda s, i: (s, 0)),
    }
    n_in, n_out = len(arrays), len(outs)
    more_in, more_out = len(beside.arrays), len(beside.outs)

    def whole(*refs):
        ins, given = refs[:n_in], refs[n_in : n_in + more_in]
        rest = refs[n_in + more_in :]
        results, made = rest[:n_out], rest[n_out : n_out + more_out]
        rest = rest[n_out + more_out :]
        room, held = rest[: len(beside.scratch)], rest[len(beside.scratch) :]
        step = pl.program_id(0) * pairs + pl.program_id(1)
        last = count * pairs - 1
        acts = beside.acts(given, made, room)
        when = [(2 * i * (last + 1) + len(acts) - 1) // (2 * len(acts) - 2) for i in range(len(acts))]
        for i, act in enumerate(acts):
            if when[i] <= last:
                pl.when(step == when[i])(act)
        body(*ins, *results, *held)

        @pl.when(step == last)
        def _():
            for i, act in enumerate(acts):
                if when[i] > last:
                    act()

    return kernel_call(
        whole,
        name,
        list(arrays) + list(beside.arrays),
        number,
        grid=(count, pairs),
        in_specs=[specs[kind] for kind in kinds] + [ANYWHERE] * more_in,
        out_specs=[specs[kind] for kind in out_kinds] + [ANYWHERE] * more_out,
        out_shape=list(outs) + list(beside.outs),
        scratch_shapes=list(beside.scratch) + scratch(length),
    )


class SpreadBeside:
    def __init__(self, seqs, own, pieces):
        self.seqs = seqs
        self.arrays = [own] + list(pieces)
        self.outs = [jax.ShapeDtypeStruct((2, seqs) + own.shape, BF)]
        self.outs += [jax.ShapeDtypeStruct(piece.shape, BF) for piece in pieces]
        self.scratch = [pltpu.VMEM(own.shape, BF), pltpu.SemaphoreType.DMA]
        self.scratch += spread_scratch(seqs)
        self.first = len(self.scratch)
        self.scratch += deal_scratch(pieces, seqs) if pieces else []

    def acts(self, given, made, room):
        def dealing():
            return Deal(given[1:], made[1:], room[self.first :])

        def spreading():
            return Spread(room[0], made[0], room[2:])

        def begin():
            copy = pltpu.make_async_copy(given[0], room[0], room[1])
            copy.start()
            greet(all_partners(self.seqs))
            copy.wait()
            spreading().begin()
            if given[1:]:
                dealing().begin()

        def finish():
            spreading().finish()
            if given[1:]:
                dealing().finish()

        def step(phase):
            return lambda: spreading().step(phase)

        return [begin] + [step(i) for i in range(1, len(bits_of(self.seqs)))] + [finish]


class OutputBeside:
    def __init__(self, seqs, terms, middle, pieces):
        self.seqs = seqs
        self.arrays = [terms, middle] + list(pieces)
        self.outs = [jax.ShapeDtypeStruct(middle.shape, BF)]
        self.outs += [jax.ShapeDtypeStruct(piece.shape, BF) for piece in pieces]
        self.scratch = [
            pltpu.VMEM(middle.shape, F32),
            pltpu.VMEM(middle.shape, BF),
            pltpu.SemaphoreType.DMA((2,)),
        ]
        self.scratch += fold_rooms(seqs, *middle.shape, False) + fold_sems(seqs)
        self.first = len(self.scratch)
        self.scratch += deal_scratch(pieces, seqs)

    def acts(self, given, made, room):
        held, rounded, sems = room[:3]

        def dealing():
            return Deal(given[2:], made[1:], room[self.first :])

        def folding():
            return Fold(given[0], room[3:7], room[7:12], pl.ds(0, held.shape[0]))

        def entering():
            return pltpu.make_async_copy(given[1], held, sems.at[0])

        def begin():
            entering().start()
            folding().load()
            greet(all_partners(self.seqs))
            folding().begin()

        def first():
            folding().first()
            dealing().begin()

        def finish():
            fold = folding()
            fold.last()
            entering().wait()

            def add(rows):
                rounded[rows, :] = (held[rows, :] + fold.result(rows)).astype(BF)

            fold.add(add)
            leaving = pltpu.make_async_copy(rounded, made[0], sems.at[1])
            leaving.start()
            fold.settle()
            dealing().finish()
            leaving.wait()

        def step(phase):
            return lambda: folding().step(phase)

        phases = len(bits_of(self.seqs))
        return [begin, first] + [step(i) for i in range(1, phases)] + [finish]


def attend(mixed, table, beside, count, number):
    tokens, cols = mixed.shape
    outs = [
        jax.ShapeDtypeStruct((tokens, cols), BF),
        jax.ShapeDtypeStruct((tokens, cols // 3), BF),
        jax.ShapeDtypeStruct((tokens, cols // 3), F32),
    ]
    return heads_call(
        attend_body,
        "attend",
        [mixed, table],
        ["wide", "table"],
        outs,
        ["wide", "one", "one"],
        count,
        beside,
        number,
        lambda length: [],
    )


def attend_back(qkv, grad, logs, table, beside, count, number):
    return heads_call(
        attend_back_body,
        "attend_back",
        [qkv, grad, logs, table],
        ["wide", "one", "one", "table"],
        [jax.ShapeDtypeStruct(qkv.shape, BF)],
        ["wide"],
        count,
        beside,
        number,
        lambda length: [pltpu.VMEM((length, PAIR), F32)] * 2,
    )


def qkv_columns(owners, cols):
    for owner in range(owners):
        for pair in range(cols // PAIR):
            for kind in range(3):
                there = (pair * 3 + kind) * PAIR
                yield owner, there, (kind * owners + owner) * cols + pair * PAIR, PAIR


def chunk_widths(cols):
    units = cols // PAIR
    first = max(1, (5 * units) // 8)
    return [n * PAIR for n in (first, units - first) if n]


def ff_columns(owners, cols):
    begin = 0
    gate_up, down = [], []
    for part in chunk_widths(cols):
        gate_up.append(
            [
                (owner, kind * part, (kind * owners + owner) * cols + begin, part)
                for owner in range(owners)
                for kind in range(2)
            ]
        )
        down.append([(owner, 2 * part, owner * cols + begin, part) for owner in range(owners)])
        begin += part
    return gate_up, down


def cut(weights, gains, plan, cols, owners):
    rows = weights[0].shape[0]
    scaled = [gain is not None for gain in gains]
    arrays = list(weights) + [gain for gain in gains if gain is not None]
    gain_at = [len(weights) + sum(scaled[:i]) for i in range(len(weights))]

    def body(*refs):
        for out, parts in zip(refs[len(arrays) :], plan):
            for which, places in parts:
                for owner, there, here, width in places:
                    part = refs[which][:, here : here + width]
                    if scaled[which]:
                        part = (part.astype(F32) * refs[gain_at[which]][...]).astype(BF)
                    out[owner, :, there : there + width] = part

    return kernel_call(
        body,
        "cut",
        [*arrays],
        out_shape=[jax.ShapeDtypeStruct((owners, rows, n), BF) for n in cols],
    )


def side_by_side(left, right):
    def body(one, two, out, sems):
        cut = left.shape[1]
        copies = [
            pltpu.make_async_copy(one, out.at[:, pl.ds(0, cut)], sems.at[0]),
            pltpu.make_async_copy(two, out.at[:, pl.ds(cut, right.shape[1])], sems.at[1]),
        ]
        for copy in copies:
            copy.start()
        for copy in copies:
            copy.wait()

    return kernel_call(
        body,
        "side_by_side",
        [left, right],
        in_specs=[LOCAL, LOCAL],
        out_specs=ANYWHERE,
        out_shape=jax.ShapeDtypeStruct((left.shape[0], left.shape[1] + right.shape[1]), BF),
        scratch_shapes=[pltpu.SemaphoreType.DMA((2,))],
    )


def blocks_in(rows, seqs, chips):
    return [
        ((s * chips + z) * 2 * rows, (z * seqs + s) * 2 * rows, 2 * rows)
        for z in range(chips)
        for s in range(seqs)
    ]


def inside(arrays, blocks):
    def body(*refs):
        for source, out in zip(refs[: len(arrays)], refs[len(arrays) :]):
            for outer, inner, width in blocks:
                out[:, inner : inner + width] = source[:, outer : outer + width]

    return kernel_call(
        body,
        "inside",
        arrays,
        out_shape=[jax.ShapeDtypeStruct(a.shape, a.dtype) for a in arrays],
    )


def outside(arrays, blocks):
    return inside(arrays, [(inner, outer, width) for outer, inner, width in blocks])


def join_ff(sums, w_gate_up, gain, gate_up_places, down_places):
    rows, total_width = w_gate_up.shape
    count = len(sums)

    def body(*refs):
        weights, gains, out, out_gain, out_down = refs[count:]
        total = jnp.zeros((rows, PAIR), F32)
        for source, listed in zip(refs[:count], gate_up_places):
            for owner, there, here, width in listed:
                for step in range(0, width, PAIR):
                    part = source[owner, :, there + step : there + step + PAIR].astype(F32)
                    at = slice(here + step, here + step + PAIR)
                    total += part * weights[:, at].astype(F32)
                    out[:, at] = part * gains[...]
        for source, listed in zip(refs[:count], down_places):
            for owner, there, here, width in listed:
                out_down[:, here : here + width] = source[owner, :, there : there + width].astype(
                    F32
                )
        out_gain[...] = jnp.sum(total, 1, keepdims=True)

    return kernel_call(
        body,
        "join_ff",
        [*sums, w_gate_up, gain],
        out_shape=[
            jax.ShapeDtypeStruct((rows, total_width), F32),
            jax.ShapeDtypeStruct((rows, 1), F32),
            jax.ShapeDtypeStruct((rows, total_width // 2), F32),
        ],
    )


def join_attend(sums, w_qkv, gain, qkv_places, out_places):
    rows, total_width = w_qkv.shape

    def body(source, weights, gains, out, out_gain, out_out):
        total = jnp.zeros((rows, PAIR), F32)
        for owner, there, here, width in qkv_places:
            part = source[owner, :, there : there + width].astype(F32)
            total += part * weights[:, here : here + width].astype(F32)
            out[:, here : here + width] = part * gains[...]
        for owner, there, here, width in out_places:
            out_out[:, here : here + width] = source[owner, :, there : there + width].astype(F32)
        out_gain[...] = jnp.sum(total, 1, keepdims=True)

    return kernel_call(
        body,
        "join_attend",
        [sums, w_qkv, gain],
        out_shape=[
            jax.ShapeDtypeStruct((rows, total_width), F32),
            jax.ShapeDtypeStruct((rows, 1), F32),
            jax.ShapeDtypeStruct((rows, total_width // 3), F32),
        ],
    )


def flip(index, offset):
    weight = 1
    while weight <= offset:
        if offset & weight:
            index = index + weight - 2 * weight * ((index // weight) % 2)
        weight *= 2
    return index


def greet(partners):
    barrier = pltpu.get_barrier_semaphore()
    for partner in partners:
        pl.semaphore_signal(barrier, inc=1, device_id=partner, device_id_type=MESH)
    pl.semaphore_wait(barrier, len(partners))


def here():
    return lax.axis_index("seq"), lax.axis_index("core")


def bits_of(seqs):
    return [1 << bit for bit in range(seqs.bit_length() - 1)]


def cube_partners(seqs):
    me, core = here()
    partners = [{"seq": flip(me, bit), "core": core} for bit in bits_of(seqs)]
    return partners + [{"seq": me, "core": 1 - core}]


def all_partners(seqs):
    me, core = here()
    return [
        {"seq": flip(me, step), "core": core if same else 1 - core}
        for step in range(seqs)
        for same in (True, False)
        if step or not same
    ]


def orders_of(seqs):
    bits = bits_of(seqs)
    return [bits, bits[1:] + bits[:1]]


def remote(source, target, sems, at, device):
    return pltpu.make_async_remote_copy(
        src_ref=source,
        dst_ref=target,
        send_sem=sems[0].at[at],
        recv_sem=sems[1].at[at],
        device_id=device,
        device_id_type=MESH,
    )


def push(*where):
    copy = remote(*where)
    copy.start()
    return copy


def loads(sources, rooms, sems):
    copies = []
    for i, (source, room) in enumerate(zip(sources, rooms)):
        if isinstance(source, tuple):
            source = source[0].at[:, pl.ds(source[1], source[2])]
        copies.append(pltpu.make_async_copy(source, room, sems.at[i]))
    return copies


def like(*arrays):
    return [pltpu.VMEM(array.shape, array.dtype) for array in arrays]


def pair_sems(*shape):
    return [pltpu.SemaphoreType.DMA(shape)] * 2


def spread_scratch(seqs):
    return pair_sems(2, seqs) + pair_sems(2, seqs) + [pltpu.SemaphoreType.DMA]


class Spread:
    def __init__(self, own, out, scratch, rows=None):
        self.own, self.out = own, out
        self.rows = rows or pl.ds(0, own.shape[0])
        self.across, self.aside, self.local = scratch[0:2], scratch[2:4], scratch[4]
        self.me, self.core = here()
        self.half = out.shape[-1] // 2
        self.orders = orders_of(out.shape[1])
        self.phases = len(self.orders[0])

    def columns(self, ref, stream):
        return ref.at[self.rows, pl.ds(stream * self.half, self.half)]

    def place(self, offset, stream):
        return self.columns(self.out.at[self.core, flip(self.me, offset)], stream)

    def block(self, offset, stream):
        return self.place(offset, stream) if offset else self.columns(self.own, stream)

    def kept(self):
        return pltpu.make_async_copy(
            self.own.at[self.rows], self.out.at[self.core, self.me, self.rows], self.local
        )

    def swap(self, offset, stream):
        sibling = {"seq": self.me, "core": 1 - self.core}
        return remote(
            self.block(offset, stream),
            self.place(offset, stream),
            self.aside,
            (stream, offset),
            sibling,
        )

    def held(self, phase, stream):
        offsets = [0]
        for bit in self.orders[stream][:phase]:
            offsets += [offset + bit for offset in offsets]
        return offsets

    def moves(self, phase):
        found = []
        for stream in range(2):
            bit = self.orders[stream][phase]
            partner = {"seq": flip(self.me, bit), "core": self.core}
            for offset in self.held(phase, stream):
                copy = remote(
                    self.block(offset, stream),
                    self.place(offset, stream),
                    self.across,
                    (stream, offset + bit),
                    partner,
                )
                found.append((copy, offset + bit, stream))
        return found

    def begin(self):
        self.kept().start()
        for copy, _, _ in self.moves(0):
            copy.start()
        for stream in range(2):
            self.swap(0, stream).start()

    def arrive(self, phase):
        for copy, offset, stream in self.moves(phase):
            copy.wait_recv()
            self.swap(offset, stream).start()

    def step(self, phase):
        self.arrive(phase - 1)
        for copy, _, _ in self.moves(phase):
            copy.start()

    def finish(self):
        self.arrive(self.phases - 1)
        for phase in range(self.phases):
            for copy, _, _ in self.moves(phase):
                copy.wait_send()
        for stream in range(2):
            for offset in self.held(self.phases, stream):
                self.swap(offset, stream).wait()
        self.kept().wait()


def fold_rooms(seqs, tokens, width, made=True):
    return [
        pltpu.VMEM((seqs, tokens, width), BF),
        pltpu.VMEM((seqs, tokens, width) if made else (16, PAIR), BF),
        pltpu.VMEM((seqs, tokens, width), BF),
        pltpu.VMEM((2, seqs, tokens, width // 2), BF),
    ]


def fold_sems(seqs):
    return [pltpu.SemaphoreType.DMA((2,))] + pair_sems(seqs) + pair_sems(2, seqs)


class Fold:
    def __init__(self, terms, rooms, sems, rows, make=None):
        self.terms, self.make = terms, make
        self.own, self.give, self.total, self.got = rooms
        self.local, self.aside, self.across = sems[0], sems[1:3], sems[3:5]
        self.rows = rows
        self.me, self.core = here()
        self.seqs = self.total.shape[0]
        self.half = self.total.shape[-1] // 2
        self.orders = orders_of(self.seqs)
        self.phases = len(self.orders[0])

    def taken(self, mine):
        core, room = (self.core, self.own) if mine else (1 - self.core, self.give)
        return pltpu.make_async_copy(
            self.terms.at[core, :, self.rows],
            room.at[:, self.rows],
            self.local.at[1 if mine else 0],
        )

    def fill(self, room, core, at):
        width = room.shape[-1]
        tile = min(2 * BLOCK, width)

        def one(j, carry):
            columns = pl.ds(pl.multiple_of(j * tile, tile), tile)
            value = self.make(core, at, self.rows, columns)
            if self.terms is not None:
                value = value + room[at, self.rows, columns].astype(F32)
            room[at, self.rows, columns] = value.astype(BF)
            return carry

        lax.fori_loop(0, width // tile, one, 0)

    def swap(self, offset):
        at = flip(self.me, offset)
        source = self.give.at[at] if self.make else self.terms.at[1 - self.core, at]
        return remote(
            source.at[self.rows],
            self.total.at[at, self.rows],
            self.aside,
            (offset,),
            {"seq": self.me, "core": 1 - self.core},
        )

    def columns(self, stream):
        return pl.ds(stream * self.half, self.half)

    def moves(self, phase, stream, only=None):
        bit = self.orders[stream][phase]
        done = sum(self.orders[stream][:phase])
        partner = {"seq": flip(self.me, bit), "core": self.core}
        return [
            (
                remote(
                    self.total.at[flip(self.me, offset), self.rows, self.columns(stream)],
                    self.got.at[stream, offset, self.rows],
                    self.across,
                    (stream, offset),
                    partner,
                ),
                offset,
            )
            for offset in range(self.seqs - 1, -1, -1)
            if offset & bit and not offset & done and only in (None, offset)
        ]

    def add(self, work):
        count = self.rows.size
        step = min(32, count)

        def one(i, carry):
            work(pl.ds(pl.multiple_of(self.rows.start + i * step, step), step))
            return carry

        lax.fori_loop(0, count // step, one, 0)

    def load(self):
        if self.terms is not None:
            if self.make:
                self.taken(False).start()
            self.taken(True).start()

    def begin(self):
        if self.make and self.terms is not None:
            self.taken(False).wait()
        for offset in range(self.seqs - 1, -1, -1):
            if self.make:
                self.fill(self.give, 1 - self.core, flip(self.me, offset))
            self.swap(offset).start()

    def first(self):
        if self.terms is not None:
            self.taken(True).wait()
        for offset in range(self.seqs - 1, -1, -1):
            at = flip(self.me, offset)
            if self.make:
                self.fill(self.own, self.core, at)
            self.swap(offset).wait_recv()

            def add_sibling(rows, at=at):
                both = self.total[at, rows, :].astype(F32) + self.own[at, rows, :].astype(F32)
                self.total[at, rows, :] = both.astype(BF)

            self.add(add_sibling)
            for stream in range(2):
                for copy, _ in self.moves(0, stream, offset):
                    copy.start()

    def receive(self, phase, stream):
        bit = self.orders[stream][phase]
        for copy, offset in self.moves(phase, stream):
            copy.wait_recv()
            at = flip(self.me, offset - bit)

            def add_got(rows, at=at, offset=offset):
                columns = self.columns(stream)
                both = self.total[at, rows, columns].astype(F32) + self.got[
                    stream, offset, rows, :
                ].astype(F32)
                self.total[at, rows, columns] = both.astype(BF)

            self.add(add_got)

    def step(self, phase):
        for stream in range(2):
            self.receive(phase - 1, stream)
            for copy, _ in self.moves(phase, stream):
                copy.start()

    def last(self):
        for stream in range(2):
            self.receive(self.phases - 1, stream)

    def result(self, rows):
        return self.total[self.me, rows, :].astype(F32)

    def settle(self):
        for offset in range(self.seqs):
            self.swap(offset).wait_send()
        for phase in range(self.phases):
            for stream in range(2):
                for copy, _ in self.moves(phase, stream):
                    copy.wait_send()


def halves(count):
    return [pl.ds(i * (count // 2), count // 2) for i in range(2)]


def fold_then_spread(folds, spreads, work, aside=lambda: None):
    phases = folds[0].phases
    for fold in folds:
        fold.begin()
        fold.first()
    aside()
    for phase in range(1, phases):
        for fold in folds:
            fold.step(phase)
            aside()
    for fold, spread in zip(folds, spreads):
        fold.last()
        fold.add(work)
        spread.begin()
        aside()
    for phase in range(1, phases):
        for spread in spreads:
            spread.step(phase)
            aside()
    for spread in spreads:
        spread.finish()
    for fold in folds:
        fold.settle()


def by_rows(count, work):
    step = min(32, count)

    def one(i, carry):
        work(pl.ds(pl.multiple_of(i * step, step), step))
        return carry

    lax.fori_loop(0, count // step, one, 0)


def deal_scratch(pieces, seqs):
    blocks = [piece.shape[-2:] for piece in pieces]
    return (
        pair_sems(len(pieces), 2 * seqs)
        + [pltpu.SemaphoreType.DMA((2, len(pieces)))]
        + [pltpu.VMEM(block, piece.dtype) for block, piece in zip(blocks, pieces)]
    )


class Deal:
    def __init__(self, pieces, outs, scratch):
        self.pieces, self.outs = pieces, outs
        self.sems, self.local, self.rooms = scratch[:2], scratch[2], scratch[3:]
        self.me, self.core = here()

    def cut_up(self, i):
        return len(self.pieces[i].shape) == len(self.outs[i].shape)

    def copies(self):
        found = []
        for i, (piece, out) in enumerate(zip(self.pieces, self.outs)):
            for step in range(out.shape[0]):
                for same in (True, False):
                    if step or not same:
                        to_seq = flip(self.me, step)
                        to_core = self.core if same else 1 - self.core
                        found.append(
                            remote(
                                piece.at[to_seq, to_core] if self.cut_up(i) else piece,
                                out.at[self.me, self.core],
                                self.sems,
                                (i, 2 * step + (0 if same else 1)),
                                {"seq": to_seq, "core": to_core},
                            )
                        )
        return found

    def entering(self):
        return [
            pltpu.make_async_copy(
                piece.at[self.me, self.core] if self.cut_up(i) else piece,
                self.rooms[i],
                self.local.at[0, i],
            )
            for i, piece in enumerate(self.pieces)
        ]

    def leaving(self):
        return [
            pltpu.make_async_copy(
                self.rooms[i], out.at[self.me, self.core], self.local.at[1, i]
            )
            for i, out in enumerate(self.outs)
        ]

    def begin(self):
        for copy in self.copies() + self.entering():
            copy.start()
        for copy in self.entering():
            copy.wait()
        for copy in self.leaving():
            copy.start()

    def finish(self):
        for copy in self.copies() + self.leaving():
            copy.wait()


def deal(pieces, number, alike=()):
    seqs = pieces[0].shape[0]
    shapes = [piece.shape for piece in pieces] + [(seqs, 2) + one.shape for one in alike]
    pieces = list(pieces) + list(alike)
    count = len(pieces)

    def body(*refs):
        greet(all_partners(seqs))
        work = Deal(refs[:count], refs[count : 2 * count], refs[2 * count :])
        work.begin()
        work.finish()

    return kernel_call(
        body,
        "deal",
        [*pieces],
        number,
        in_specs=[ANYWHERE] * count,
        out_specs=[ANYWHERE] * count,
        out_shape=[
            jax.ShapeDtypeStruct(shape, piece.dtype) for shape, piece in zip(shapes, pieces)
        ],
        scratch_shapes=deal_scratch(pieces, seqs),
    )


def first_acts(tokens, pieces, seqs, number):
    count, width = tokens.shape
    n = len(pieces)

    def body(*refs):
        given = refs[1 : 1 + n]
        out, outs = refs[1 + n], refs[2 + n : 2 + 2 * n]
        source, sem, own, *scratch = refs[2 + 2 * n :]
        (entering,) = loads(refs[:1], [source], sem)
        entering.start()
        greet(all_partners(seqs))
        entering.wait()

        def norm(rows):
            values = source[rows, :].astype(F32)
            own[rows, :] = (values * norm_scale(values)).astype(BF)

        by_rows(count, norm)
        spreading = Spread(own, out, scratch[:5])
        dealing = Deal(given, outs, scratch[5:])
        spreading.begin()
        dealing.begin()
        for phase in range(1, spreading.phases):
            spreading.step(phase)
        spreading.finish()
        dealing.finish()

    return kernel_call(
        body,
        "first_acts",
        [tokens, *pieces],
        number,
        in_specs=[ANYWHERE] * (1 + n),
        out_specs=[ANYWHERE] * (1 + n),
        out_shape=[jax.ShapeDtypeStruct((2, seqs, count, width), BF)]
        + [jax.ShapeDtypeStruct(piece.shape, BF) for piece in pieces],
        scratch_shapes=like(tokens)
        + [pltpu.SemaphoreType.DMA((1,)), pltpu.VMEM((count, width), BF)]
        + spread_scratch(seqs)
        + deal_scratch(pieces, seqs),
    )


def two_way_scratch(seqs, count, width):
    return (
        [pltpu.VMEM((count, width), BF)]
        + fold_rooms(seqs, count, width)
        + fold_sems(seqs) * 2
        + spread_scratch(seqs) * 2
    )


def two_way(given, out, scratch, make):
    own, rooms, sems = scratch[0], scratch[1:5], scratch[5:]
    parts = halves(own.shape[0])
    folds = [
        Fold(given, rooms, sems[5 * i : 5 * i + 5], rows, make) for i, rows in enumerate(parts)
    ]
    sems = sems[10:]
    spreads = [Spread(own, out, sems[5 * i : 5 * i + 5], rows) for i, rows in enumerate(parts)]
    for fold in folds:
        fold.load()
    return folds, spreads, own


def product(left, right, seqs, count):
    def make(core, at, rows, columns):
        begin = pl.multiple_of((core * seqs + at) * count + rows.start, rows.size)
        return nt(left[pl.ds(begin, rows.size), :], right[columns, :])

    return make


def middle_acts(attended, weights, tokens, seqs, number):
    count, width = tokens.shape
    cols = attended.shape[1]
    begin = weights.shape[1] - cols

    def body(left_in, given, source_in, middle, out, left, right, source, sems, *scratch):
        coming = loads([left_in, (given, begin, cols), source_in], [left, right, source], sems)
        for copy in coming:
            copy.start()
        folds, spreads, own = two_way(None, out, scratch, product(left, right, seqs, count))
        greet(cube_partners(seqs))
        for copy in coming:
            copy.wait()

        def norm(rows):
            values = source[rows, :].astype(F32) + folds[0].result(rows)
            middle[rows, :] = values
            own[rows, :] = (values * norm_scale(values)).astype(BF)

        fold_then_spread(folds, spreads, norm)

    return kernel_call(
        body,
        "middle_acts",
        [attended, weights, tokens],
        number,
        in_specs=[ANYWHERE] * 3,
        out_specs=[LOCAL, ANYWHERE],
        out_shape=[
            jax.ShapeDtypeStruct((count, width), F32),
            jax.ShapeDtypeStruct((2, seqs, count, width), BF),
        ],
        scratch_shapes=like(attended)
        + [pltpu.VMEM((width, cols), BF)]
        + like(tokens)
        + [pltpu.SemaphoreType.DMA((3,))]
        + two_way_scratch(seqs, count, width),
    )


def middle_grad(terms, grad_both, cotangent, middle, hidden, weights, number):
    _, seqs, count, width = terms.shape
    tokens = hidden[0].shape[0]
    n = len(hidden)
    block = min(BLOCK, tokens)
    tile = min(2 * BLOCK, width)
    blocks = tokens // block
    parts = [h.shape[1] for h in hidden]

    def body(given, *refs):
        sources, down = refs[: 3 + n], refs[3 + n : 3 + 2 * n]
        grad, out, products = refs[3 + 2 * n : 6 + 2 * n]
        scratch = refs[6 + 2 * n :]
        left, upstream, values = scratch[:3]
        units, room, right = scratch[3 : 3 + n], scratch[3 + n : 3 + 2 * n], scratch[3 + 2 * n]
        stage, sems, leaving = scratch[4 + 2 * n : 7 + 2 * n]
        columns = [(down[i], 2 * parts[i], parts[i]) for i in range(n)]
        coming = loads(
            [sources[0], (down[-1], 0, 2 * parts[-1]), *sources[3:], *columns, *sources[1:3]],
            [left, right, *units, *room, upstream, values],
            sems,
        )
        for copy in coming[:2]:
            copy.start()
        make = product(left, right, seqs, count)
        folds, spreads, own = two_way(given, out, scratch[7 + 2 * n :], make)
        for copy in coming[2:]:
            copy.start()
        greet(cube_partners(seqs))
        for copy in coming[:2]:
            copy.wait()

        def leave(i):
            rows = pl.ds(i * block, block)
            return pltpu.make_async_copy(stage.at[i % 2], products.at[rows], leaving.at[i % 2])

        def multiply(i):
            if i == 0:
                for copy in coming[2:]:
                    copy.wait()
            if i >= 2:
                leave(i - 2).wait()

            def one(j, carry):
                columns = pl.ds(pl.multiple_of(j * tile, tile), tile)
                total = sum(
                    nt(units[k][pl.ds(i * block, block), :], room[k][columns, :])
                    for k in range(n)
                )
                stage[i % 2, :, columns] = total.astype(BF)
                return carry

            lax.fori_loop(0, width // tile, one, 0)
            leave(i).start()

        left_over = list(range(blocks))

        def aside():
            for _ in range(2 if len(left_over) == blocks else max(1, blocks // 8)):
                if left_over:
                    multiply(left_over.pop(0))

        def back(rows):
            held = values[rows, :]
            scale = norm_scale(held)
            result = upstream[rows, :].astype(F32) + norm_back(
                folds[0].result(rows), held * scale, scale
            )
            grad[rows, :] = result
            own[rows, :] = result.astype(BF)

        fold_then_spread(folds, spreads, back, aside)
        while left_over:
            multiply(left_over.pop(0))
        for i in range(max(0, blocks - 2), blocks):
            leave(i).wait()

    return kernel_call(
        body,
        "middle_grad",
        [terms, grad_both, cotangent, middle, *hidden, *weights],
        number,
        in_specs=[ANYWHERE] * (4 + 2 * n),
        out_specs=[LOCAL, ANYWHERE, ANYWHERE],
        out_shape=[
            jax.ShapeDtypeStruct((count, width), F32),
            jax.ShapeDtypeStruct(terms.shape, BF),
            jax.ShapeDtypeStruct((tokens, width), BF),
        ],
        scratch_shapes=like(grad_both, cotangent, middle, *hidden)
        + [pltpu.VMEM((width, part), BF) for part in parts]
        + [pltpu.VMEM((width, 2 * parts[-1]), BF), pltpu.VMEM((2, block, width), BF)]
        + [pltpu.SemaphoreType.DMA((4 + 2 * n,)), pltpu.SemaphoreType.DMA((2,))]
        + two_way_scratch(seqs, count, width),
    )


def input_grad(grad_mixed, weights, tokens, grad_middle, pieces, seqs, number):
    count, width = tokens.shape
    n = len(pieces)
    cols = grad_mixed.shape[1]

    def body(*refs):
        left_in, given, source_in, held_in = refs[:4]
        out = refs[4 + n]
        left, right, source, held, sems, *scratch = refs[5 + 2 * n :]
        coming = loads(
            [left_in, (given, 0, cols), source_in, held_in], [left, right, source, held], sems
        )
        for copy in coming:
            copy.start()
        make = product(left, right, seqs, count)
        fold = Fold(None, scratch[:4], scratch[4:9], pl.ds(0, count), make)
        greet(all_partners(seqs))
        for copy in coming:
            copy.wait()
        fold.begin()
        fold.first()
        if n:
            dealing = Deal(refs[4 : 4 + n], refs[5 + n : 5 + 2 * n], scratch[9:])
            dealing.begin()
        for phase in range(1, fold.phases):
            fold.step(phase)
        fold.last()

        def back(rows):
            values = source[rows, :].astype(F32)
            scale = norm_scale(values)
            out[rows, :] = held[rows, :] + norm_back(fold.result(rows), values * scale, scale)

        fold.add(back)
        fold.settle()
        if n:
            dealing.finish()

    return kernel_call(
        body,
        "input_grad",
        [grad_mixed, weights, tokens, grad_middle, *pieces],
        number,
        in_specs=[ANYWHERE] * (4 + n),
        out_specs=[LOCAL] + [ANYWHERE] * n,
        out_shape=[jax.ShapeDtypeStruct((count, width), F32)]
        + [jax.ShapeDtypeStruct(piece.shape, BF) for piece in pieces],
        scratch_shapes=like(grad_mixed)
        + [pltpu.VMEM((width, cols), BF)]
        + like(tokens, grad_middle)
        + [pltpu.SemaphoreType.DMA((4,))]
        + fold_rooms(seqs, count, width)
        + fold_sems(seqs)
        + (deal_scratch(pieces, seqs) if n else []),
    )


class Order:
    def __init__(self):
        self.latest = None

    def enter(self, values):
        if self.latest is None:
            return values
        return lax.optimization_barrier((values, self.latest))[0]

    def run(self, work, *values):
        result = work(*self.enter(values))
        self.latest = jax.tree.leaves(result)[0]
        return result

    def take(self, values):
        if self.latest is not None:
            values = lax.optimization_barrier((values, self.latest))[0]
        self.latest = jax.tree.leaves(values)[0]
        return values


def rope_table(places):
    half = HEAD_DIM // 2
    inverse = ROPE_BASE ** (-2.0 * jnp.arange(half).astype(F32) / HEAD_DIM)
    angles = places.astype(F32)[:, None] * inverse[None, :]
    return jnp.concatenate([jnp.cos(angles), jnp.sin(angles)] * 2, 1)


def norm_scale(values):
    return lax.rsqrt(jnp.mean(values * values, -1, keepdims=True) + EPS)


def norm_back(grad, normed, scale):
    return scale * (grad - normed * jnp.mean(grad * normed, -1, keepdims=True))


def per_device(
    mesh, tokens, positions, w_qkv, w_out, gain_attn, w_gate_up, w_down, gain_mlp, cotangent
):
    order = Order()
    seqs, chips = mesh.shape["seq"], mesh.shape["z"]
    owners = 2 * seqs
    token_count, width = tokens.shape[1:]
    ff_width = w_down.shape[1]
    rows = w_qkv.shape[0]
    head_cols = width // owners
    ff_cols = ff_width // owners
    parts = chunk_widths(ff_cols)
    last = len(parts) - 1
    blocks = blocks_in(rows, seqs, chips)
    gain_one = gain_attn.astype(F32)[:, None]
    gain_two = gain_mlp.astype(F32)[:, None]

    def by_place(piece):
        return piece.reshape(seqs, 2, rows, -1)

    def gathered(piece):
        piece = order.enter(piece).reshape(seqs, 2 * rows, -1)
        return lax.all_gather(piece, "z", axis=0, tiled=False)

    def flat(value):
        return order.take(value).reshape(width, -1)

    def summed(term):
        split = order.enter(term).reshape(chips, seqs, 2 * rows, -1)
        return lax.psum_scatter(split, "z", scatter_dimension=0, tiled=False)

    def rounded(left, right):
        return tn(left, right).astype(BF)

    qkv_places = list(qkv_columns(owners, head_cols))
    out_places = [(o, 3 * head_cols, o * head_cols, head_cols) for o in range(owners)]
    gate_up_places, down_places = ff_columns(owners, ff_cols)
    (attend_cut,) = order.run(
        lambda a, b, g: cut(
            [a, b], [g, None], [[(0, qkv_places), (1, out_places)]], [4 * head_cols], owners
        ),
        w_qkv,
        w_out,
        gain_one,
    )
    attend_piece, places = order.run(
        lambda a, p: deal([a], 1, [jnp.broadcast_to(p, (8, token_count))]),
        by_place(attend_cut),
        positions,
    )
    attend_coming = gathered(attend_piece)
    ff_cut = order.run(
        lambda a, b, g: cut(
            [a, b],
            [g, None],
            [[(0, pair), (1, single)] for pair, single in zip(gate_up_places, down_places)],
            [3 * part for part in parts],
            owners,
        ),
        w_gate_up,
        w_down,
        gain_two,
    )
    table = order.run(
        lambda p: rope_table(jnp.moveaxis(p[:, :, 0], 1, 0).reshape(-1)), places
    )
    tokens_in, upstream_own = order.run(
        lambda a, b: inside([a, b], blocks), tokens[0], cotangent[0]
    )
    acts, ff_piece = order.run(
        lambda x, a: first_acts(x, [a], seqs, 2), tokens_in, by_place(ff_cut[0])
    )
    acts = acts.reshape(-1, width)
    ff_coming = [gathered(ff_piece)]

    qkv_cols = 3 * head_cols
    attend_whole = flat(attend_coming)
    mixed = order.run(lambda a, w: nn(a, w[:, :qkv_cols]), acts, attend_whole)
    qkv, attended, logs, upstream, *ff_pieces = order.run(
        lambda m, t, u, *given: attend(m, t, SpreadBeside(seqs, u, given), 2, 3),
        mixed,
        table,
        upstream_own,
        *[by_place(piece) for piece in ff_cut[1:]],
    )
    ff_coming += [gathered(piece) for piece in ff_pieces]
    upstream = upstream.reshape(-1, width)
    middle, acts_mid = order.run(
        lambda a, w, x: middle_acts(a, w, x, seqs, 4), attended, attend_whole, tokens_in
    )
    acts_mid = acts_mid.reshape(-1, width)

    def feed_hidden(both):
        part = both.shape[1] // 2
        gate, up = both[:, :part], both[:, part:]
        return (gate * jax.nn.sigmoid(gate) * up).astype(BF)

    def feed_back(grad_hidden, both):
        part = both.shape[1] // 2
        gate, up = both[:, :part], both[:, part:]
        sigma = jax.nn.sigmoid(gate)
        grad_gate = grad_hidden * up * sigma * (1.0 + gate * (1.0 - sigma))
        grad_up = grad_hidden * gate * sigma
        return jnp.concatenate([grad_gate.astype(BF), grad_up.astype(BF)], 1)

    def both_terms(left, right, left_two, right_two):
        return side_by_side(rounded(left, right), rounded(left_two, right_two))

    def add_nt(left, right, total=None):
        result = nt(left, right)
        return (result if total is None else result + total.astype(F32)).astype(BF)

    ff_sums, hiddens, wholes = [], [], []
    norm_mid_terms = ()
    for chunk, part in enumerate(parts):
        cols = 2 * part
        whole = flat(ff_coming[chunk])
        both = order.run(lambda a, w: nn(a, w[:, :cols]), acts_mid, whole)
        hidden = order.run(feed_hidden, both)
        hiddens.append(hidden)
        wholes.append(whole)
        grad_hidden = order.run(lambda a, w: nn(a, w[:, cols:]), upstream, whole)
        grad_both = order.run(feed_back, grad_hidden, both)
        term = order.run(both_terms, acts_mid, grad_both, upstream, hidden)
        ff_sums.append(summed(term))
        if chunk < len(parts) - 1:
            norm_mid_terms = (
                order.run(
                    lambda a, w, *t: add_nt(a, w[:, :cols], *t), grad_both, whole, *norm_mid_terms
                ),
            )

    grad_middle, grad_branch, outcome_terms = order.run(
        lambda a, b, c, d, e, f: middle_grad(a, b, c, d, e, f, 5),
        norm_mid_terms[0].reshape(2, seqs, token_count, width),
        grad_both,
        upstream_own,
        middle,
        hiddens,
        wholes,
    )
    grad_branch = grad_branch.reshape(-1, width)

    grad_attended = order.run(
        lambda a, w: nn(a, w[:, qkv_cols:]).astype(BF), grad_branch, attend_whole
    )
    ff_sums[0] = order.take(ff_sums[0])
    grad_mixed, outcome, *ff_dealt = order.run(
        lambda a, b, c, d, e, f, *given: attend_back(
            a, b, c, d, OutputBeside(seqs, e, f, given), 2, 6
        ),
        qkv,
        grad_attended,
        logs,
        table,
        outcome_terms.reshape(2, seqs, token_count, width),
        middle,
        by_place(ff_sums[0]),
    )
    term = order.run(both_terms, acts, grad_mixed, grad_branch, attended)
    attend_sum = summed(term)

    (grad_inputs,) = order.run(
        lambda a, w, b, c: input_grad(a, w, b, c, [], seqs, 7),
        grad_mixed,
        attend_whole,
        tokens_in,
        grad_middle,
    )
    (grad_inputs,) = order.run(lambda a: outside([a], blocks), grad_inputs)
    (outcome,) = order.run(lambda a: outside([a], blocks), outcome)
    ff_rows = [by_place(order.take(value)) for value in ff_sums[1:]]
    if ff_rows:
        ff_dealt += order.run(lambda *a: deal(a, 8), *ff_rows)
    grad_gate_up, gain_two_sum, grad_down = order.run(
        lambda w, g, *a: join_ff(a, w, g, gate_up_places, down_places),
        w_gate_up,
        gain_two,
        *[value.reshape(owners, rows, -1) for value in ff_dealt],
    )
    attend_rows = order.take(attend_sum)
    (attend_dealt,) = order.run(lambda a: deal([a], 9), by_place(attend_rows))
    grad_qkv, gain_one_sum, grad_out = order.run(
        lambda w, g, a: join_attend(a, w, g, qkv_places, out_places),
        w_qkv,
        gain_one,
        attend_dealt.reshape(owners, rows, -1),
    )
    return (
        outcome[None],
        grad_inputs[None],
        grad_qkv,
        grad_out,
        gain_one_sum[:, 0],
        grad_gate_up,
        grad_down,
        gain_two_sum[:, 0],
    )


def solution(mesh):
    seqs, devices = mesh.shape["seq"], mesh.shape["fsdp"]
    parted = Mesh(mesh.devices.reshape(seqs, devices // 2, 2), ("seq", "z", "core"))
    tokens = P(("z", "core"), "seq", None)
    matrix = P(("seq", "z", "core"), None)
    vector = P(("seq", "z", "core"))
    return jax.shard_map(
        functools.partial(per_device, parted),
        mesh=parted,
        in_specs=(
            tokens,
            P(("z", "core"), "seq"),
            matrix,
            matrix,
            vector,
            matrix,
            matrix,
            vector,
            tokens,
        ),
        out_specs=(tokens, tokens, matrix, matrix, vector, matrix, matrix, vector),
        check_vma=False,
    )
```

```python
import functools
import math

import jax
import jax.numpy as jnp
from jax import lax
from jax.experimental import pallas as pl
from jax.experimental.pallas import tpu as pltpu
from jax.sharding import Mesh, PartitionSpec as P

HEAD_DIM = 64
PAIR = 2 * HEAD_DIM
BLOCK = 256
EPS = 1e-05
ROPE_BASE = 130000.0
BF = jnp.bfloat16
F32 = jnp.float32
VMEM_MOST = 58 << 20
MESH = pl.DeviceIdType.MESH
ANYWHERE = pl.BlockSpec(memory_space=pltpu.HBM)
LOCAL = pl.BlockSpec(memory_space=pltpu.VMEM)


def room_for(spec, arrays):
    total = 8 << 20
    for room in spec.get("scratch_shapes", ()):
        if hasattr(room, "shape") and room.dtype in (BF, F32):
            total += math.prod(room.shape) * jnp.dtype(room.dtype).itemsize
    outs = spec["out_shape"] if isinstance(spec["out_shape"], list) else [spec["out_shape"]]
    specs = spec.get("out_specs", LOCAL), spec.get("in_specs", LOCAL)
    for values, given in zip((outs, arrays), specs):
        given = given if isinstance(given, list) else [given] * len(values)
        for value, where in zip(values, given):
            if where.block_shape is not None:
                total += 2 * math.prod(where.block_shape) * value.dtype.itemsize
            elif where is not ANYWHERE:
                total += math.prod(value.shape) * value.dtype.itemsize
    return min(total, VMEM_MOST)


def kernel_call(body, name, arrays, number=None, **spec):
    params = {"vmem_limit_bytes": room_for(spec, arrays)}
    if number is not None:
        params.update(vmem_limit_bytes=VMEM_MOST, collective_id=number, has_side_effects=True)
    return pl.pallas_call(
        body, name=name, compiler_params=pltpu.CompilerParams(**params), **spec
    )(*arrays)


def turn(x, cosine, sine):
    half = HEAD_DIM // 2
    lane = lax.broadcasted_iota(jnp.int32, x.shape, 1)
    swapped = jnp.where(
        lane % HEAD_DIM < half, pltpu.roll(x, PAIR - half, 1), pltpu.roll(x, half, 1)
    )
    return x * cosine + swapped * sine


def nt(left, right):
    return lax.dot_general(left, right, (((1,), (1,)), ((), ())), preferred_element_type=F32)


def tn(left, right):
    return lax.dot_general(left, right, (((0,), (0,)), ((), ())), preferred_element_type=F32)


def nn(left, right):
    return lax.dot_general(left, right, (((1,), (0,)), ((), ())), preferred_element_type=F32)


def masked_scores(queries, keys, block):
    scores = nt(queries, keys)
    rows = lax.broadcasted_iota(jnp.int32, (BLOCK, BLOCK), 0)
    cols = lax.broadcasted_iota(jnp.int32, (BLOCK, BLOCK), 1)
    last = jnp.where(cols <= rows, scores[:, block * BLOCK :], -1e30)
    return jnp.concatenate([scores[:, : block * BLOCK], last], 1) if block else last


def unpack(table):
    half = HEAD_DIM // 2
    cosine, sine = table[:, :half], table[:, half:HEAD_DIM]
    return (
        jnp.concatenate([cosine] * 4, 1),
        jnp.concatenate([-sine, sine] * 2, 1),
    )


def attend_body(mixed, table, qkv, out, logs):
    length = mixed.shape[0]
    cosine, sine = unpack(table[...])
    qkv[:, :PAIR] = turn(mixed[:, :PAIR], cosine, sine).astype(BF)
    qkv[:, PAIR : 2 * PAIR] = turn(mixed[:, PAIR : 2 * PAIR], cosine, sine).astype(BF)
    qkv[:, 2 * PAIR :] = mixed[:, 2 * PAIR :].astype(BF)
    scale = jnp.asarray(1.0 / math.sqrt(HEAD_DIM), BF)
    for block in range(length // BLOCK):
        at = pl.ds(block * BLOCK, BLOCK)
        seen = (block + 1) * BLOCK
        outs = []
        totals = []
        for low in (0, HEAD_DIM):
            high = low + HEAD_DIM
            queries = qkv[at, low:high] * scale
            scores = masked_scores(queries, qkv[:seen, PAIR + low : PAIR + high], block)
            highest = jnp.max(scores, -1, keepdims=True)
            weights = jnp.exp(scores - highest)
            summed = jnp.sum(weights, -1, keepdims=True)
            probs = (weights * (1.0 / summed)).astype(BF)
            outs.append(nn(probs, qkv[:seen, 2 * PAIR + low : 2 * PAIR + high]))
            totals.append(jnp.broadcast_to(highest + jnp.log(summed), (BLOCK, HEAD_DIM)))
        out[at, :] = jnp.concatenate(outs, 1).astype(BF)
        logs[at, :] = jnp.concatenate(totals, 1)


def attend_back_body(qkv, grad, logs, table, grad_qkv, grad_keys, grad_values):
    length = qkv.shape[0]
    scale = 1.0 / math.sqrt(HEAD_DIM)
    cosine, sine = unpack(table[...])
    last = length // BLOCK - 1
    for block in range(last, -1, -1):
        at = pl.ds(block * BLOCK, BLOCK)
        seen = (block + 1) * BLOCK
        rows = slice(block * BLOCK, seen)
        grad_queries = []
        for low in (0, HEAD_DIM):
            high = low + HEAD_DIM
            queries = qkv[at, low:high] * jnp.asarray(scale, BF)
            keys = qkv[:seen, PAIR + low : PAIR + high]
            upstream = grad[at, low:high]
            scores = masked_scores(queries, keys, block)
            probs = jnp.exp(scores - logs[at, low : low + 1])
            grad_probs = nt(upstream, qkv[:seen, 2 * PAIR + low : 2 * PAIR + high])
            inner = jnp.sum(probs * grad_probs, -1, keepdims=True)
            grad_scores = (probs * (grad_probs - inner)).astype(BF)
            grad_queries.append(nn(grad_scores, keys))
            for_keys = tn(grad_scores, queries)
            for_values = tn(probs.astype(BF), upstream)
            if block == last:
                grad_keys[:, low:high] = for_keys
                grad_values[:, low:high] = for_values
            else:
                grad_keys[:seen, low:high] += for_keys
                grad_values[:seen, low:high] += for_values
        rounded = (jnp.concatenate(grad_queries, 1) * scale).astype(BF).astype(F32)
        grad_qkv[at, :PAIR] = turn(rounded, cosine[rows], -sine[rows]).astype(BF)
    rounded = grad_keys[...].astype(BF).astype(F32)
    grad_qkv[:, PAIR : 2 * PAIR] = turn(rounded, cosine, -sine).astype(BF)
    grad_qkv[:, 2 * PAIR :] = grad_values[...].astype(BF)


def heads_call(body, name, arrays, kinds, outs, out_kinds, count, beside, number, scratch):
    tokens = arrays[0].shape[0]
    length = tokens // count
    pairs = arrays[0].shape[1] // (3 * PAIR)
    specs = {
        "wide": pl.BlockSpec((length, 3 * PAIR), lambda s, i: (s, i)),
        "one": pl.BlockSpec((length, PAIR), lambda s, i: (s, i)),
        "table": pl.BlockSpec((length, PAIR), lambda s, i: (s, 0)),
    }
    n_in, n_out = len(arrays), len(outs)
    more_in, more_out = len(beside.arrays), len(beside.outs)

    def whole(*refs):
        ins, given = refs[:n_in], refs[n_in : n_in + more_in]
        rest = refs[n_in + more_in :]
        results, made = rest[:n_out], rest[n_out : n_out + more_out]
        rest = rest[n_out + more_out :]
        room, held = rest[: len(beside.scratch)], rest[len(beside.scratch) :]
        step = pl.program_id(0) * pairs + pl.program_id(1)
        last = count * pairs - 1
        acts = beside.acts(given, made, room)
        when = [(2 * i * (last + 1) + len(acts) - 1) // (2 * len(acts) - 2) for i in range(len(acts))]
        for i, act in enumerate(acts):
            if when[i] <= last:
                pl.when(step == when[i])(act)
        body(*ins, *results, *held)

        @pl.when(step == last)
        def _():
            for i, act in enumerate(acts):
                if when[i] > last:
                    act()

    return kernel_call(
        whole,
        name,
        list(arrays) + list(beside.arrays),
        number,
        grid=(count, pairs),
        in_specs=[specs[kind] for kind in kinds] + [ANYWHERE] * more_in,
        out_specs=[specs[kind] for kind in out_kinds] + [ANYWHERE] * more_out,
        out_shape=list(outs) + list(beside.outs),
        scratch_shapes=list(beside.scratch) + scratch(length),
    )


class SpreadBeside:
    def __init__(self, seqs, own, pieces):
        self.seqs = seqs
        self.arrays = [own] + list(pieces)
        self.outs = [jax.ShapeDtypeStruct((2, seqs) + own.shape, BF)]
        self.outs += [jax.ShapeDtypeStruct(piece.shape, BF) for piece in pieces]
        self.scratch = [pltpu.VMEM(own.shape, BF), pltpu.SemaphoreType.DMA]
        self.scratch += spread_scratch(seqs)
        self.first = len(self.scratch)
        self.scratch += deal_scratch(pieces, seqs) if pieces else []

    def acts(self, given, made, room):
        def dealing():
            return Deal(given[1:], made[1:], room[self.first :])

        def spreading():
            return Spread(room[0], made[0], room[2:])

        def begin():
            copy = pltpu.make_async_copy(given[0], room[0], room[1])
            copy.start()
            greet(all_partners(self.seqs))
            copy.wait()
            spreading().begin()
            if given[1:]:
                dealing().begin()

        def finish():
            spreading().finish()
            if given[1:]:
                dealing().finish()

        def step(phase):
            return lambda: spreading().step(phase)

        return [begin] + [step(i) for i in range(1, len(bits_of(self.seqs)))] + [finish]


class OutputBeside:
    def __init__(self, seqs, terms, middle, pieces):
        self.seqs = seqs
        self.arrays = [terms, middle] + list(pieces)
        self.outs = [jax.ShapeDtypeStruct(middle.shape, BF)]
        self.outs += [jax.ShapeDtypeStruct(piece.shape, BF) for piece in pieces]
        self.scratch = [
            pltpu.VMEM(middle.shape, F32),
            pltpu.VMEM(middle.shape, BF),
            pltpu.SemaphoreType.DMA((2,)),
        ]
        self.scratch += fold_rooms(seqs, *middle.shape, False) + fold_sems(seqs)
        self.first = len(self.scratch)
        self.scratch += deal_scratch(pieces, seqs)

    def acts(self, given, made, room):
        held, rounded, sems = room[:3]

        def dealing():
            return Deal(given[2:], made[1:], room[self.first :])

        def folding():
            return Fold(given[0], room[3:7], room[7:12], pl.ds(0, held.shape[0]))

        def entering():
            return pltpu.make_async_copy(given[1], held, sems.at[0])

        def begin():
            entering().start()
            folding().load()
            greet(all_partners(self.seqs))
            folding().begin()

        def first():
            folding().first()
            dealing().begin()

        def finish():
            fold = folding()
            fold.last()
            entering().wait()

            def add(rows):
                rounded[rows, :] = (held[rows, :] + fold.result(rows)).astype(BF)

            fold.add(add)
            leaving = pltpu.make_async_copy(rounded, made[0], sems.at[1])
            leaving.start()
            fold.settle()
            dealing().finish()
            leaving.wait()

        def step(phase):
            return lambda: folding().step(phase)

        phases = len(bits_of(self.seqs))
        return [begin, first] + [step(i) for i in range(1, phases)] + [finish]


def attend(mixed, table, beside, count, number):
    tokens, cols = mixed.shape
    outs = [
        jax.ShapeDtypeStruct((tokens, cols), BF),
        jax.ShapeDtypeStruct((tokens, cols // 3), BF),
        jax.ShapeDtypeStruct((tokens, cols // 3), F32),
    ]
    return heads_call(
        attend_body,
        "attend",
        [mixed, table],
        ["wide", "table"],
        outs,
        ["wide", "one", "one"],
        count,
        beside,
        number,
        lambda length: [],
    )


def attend_back(qkv, grad, logs, table, beside, count, number):
    return heads_call(
        attend_back_body,
        "attend_back",
        [qkv, grad, logs, table],
        ["wide", "one", "one", "table"],
        [jax.ShapeDtypeStruct(qkv.shape, BF)],
        ["wide"],
        count,
        beside,
        number,
        lambda length: [pltpu.VMEM((length, PAIR), F32)] * 2,
    )


def qkv_columns(owners, cols):
    for owner in range(owners):
        for pair in range(cols // PAIR):
            for kind in range(3):
                there = (pair * 3 + kind) * PAIR
                yield owner, there, (kind * owners + owner) * cols + pair * PAIR, PAIR


def chunk_widths(cols):
    units = cols // PAIR
    first = max(1, (5 * units) // 8)
    return [n * PAIR for n in (first, units - first) if n]


def ff_columns(owners, cols):
    begin = 0
    gate_up, down = [], []
    for part in chunk_widths(cols):
        gate_up.append(
            [
                (owner, kind * part, (kind * owners + owner) * cols + begin, part)
                for owner in range(owners)
                for kind in range(2)
            ]
        )
        down.append([(owner, 2 * part, owner * cols + begin, part) for owner in range(owners)])
        begin += part
    return gate_up, down


def side_by_side(parts):
    begins = [sum(part.shape[1] for part in parts[:i]) for i in range(len(parts))]

    def body(*refs):
        out, sems = refs[-2:]
        copies = [
            pltpu.make_async_copy(
                refs[i], out.at[:, pl.ds(begins[i], part.shape[1])], sems.at[i]
            )
            for i, part in enumerate(parts)
        ]
        for copy in copies:
            copy.start()
        for copy in copies:
            copy.wait()

    total = sum(part.shape[1] for part in parts)
    return kernel_call(
        body,
        "side_by_side",
        [*parts],
        in_specs=[LOCAL] * len(parts),
        out_specs=ANYWHERE,
        out_shape=jax.ShapeDtypeStruct((parts[0].shape[0], total), BF),
        scratch_shapes=[pltpu.SemaphoreType.DMA((len(parts),))],
    )


def blocks_in(rows, seqs, chips):
    return [
        ((s * chips + z) * 2 * rows, (z * seqs + s) * 2 * rows, 2 * rows)
        for z in range(chips)
        for s in range(seqs)
    ]


def inside(arrays, blocks):
    def body(*refs):
        for source, out in zip(refs[: len(arrays)], refs[len(arrays) :]):
            for outer, inner, width in blocks:
                out[:, inner : inner + width] = source[:, outer : outer + width]

    return kernel_call(
        body,
        "inside",
        arrays,
        out_shape=[jax.ShapeDtypeStruct(a.shape, a.dtype) for a in arrays],
    )


def outside(arrays, blocks):
    return inside(arrays, [(inner, outer, width) for outer, inner, width in blocks])


def join_ff(sums, w_gate_up, gain, gate_up_places, down_places, out_places):
    rows, total_width = w_gate_up.shape
    count = len(sums)

    def body(*refs):
        weights, gains, out, out_gain, out_down, out_out = refs[count:]
        total = jnp.zeros((rows, PAIR), F32)
        for source, listed in zip(refs[:count], gate_up_places):
            for owner, there, here, width in listed:
                for step in range(0, width, PAIR):
                    part = source[owner, :, there + step : there + step + PAIR].astype(F32)
                    at = slice(here + step, here + step + PAIR)
                    total += part * weights[:, at].astype(F32)
                    out[:, at] = part * gains[...]
        for source, listed in zip(refs[:count], down_places):
            for owner, there, here, width in listed:
                part = source[owner, :, there : there + width].astype(F32)
                out_down[:, here : here + width] = part
        for owner, there, here, width in out_places:
            part = refs[count - 1][owner, :, there : there + width].astype(F32)
            out_out[:, here : here + width] = part
        out_gain[...] = jnp.sum(total, 1, keepdims=True)

    return kernel_call(
        body,
        "join_ff",
        [*sums, w_gate_up, gain],
        out_shape=[
            jax.ShapeDtypeStruct((rows, total_width), F32),
            jax.ShapeDtypeStruct((rows, 1), F32),
            jax.ShapeDtypeStruct((rows, total_width // 2), F32),
            jax.ShapeDtypeStruct((rows, sum(p[3] for p in out_places)), F32),
        ],
    )


def join_qkv(sums, w_qkv, gain, qkv_places):
    rows, total_width = w_qkv.shape

    def body(source, weights, gains, out, out_gain):
        total = jnp.zeros((rows, PAIR), F32)
        for owner, there, here, width in qkv_places:
            part = source[owner, :, there : there + width].astype(F32)
            total += part * weights[:, here : here + width].astype(F32)
            out[:, here : here + width] = part * gains[...]
        out_gain[...] = jnp.sum(total, 1, keepdims=True)

    return kernel_call(
        body,
        "join_qkv",
        [sums, w_qkv, gain],
        out_shape=[
            jax.ShapeDtypeStruct((rows, total_width), F32),
            jax.ShapeDtypeStruct((rows, 1), F32),
        ],
    )


def flip(index, offset):
    weight = 1
    while weight <= offset:
        if offset & weight:
            index = index + weight - 2 * weight * ((index // weight) % 2)
        weight *= 2
    return index


def greet(partners):
    barrier = pltpu.get_barrier_semaphore()
    for partner in partners:
        pl.semaphore_signal(barrier, inc=1, device_id=partner, device_id_type=MESH)
    pl.semaphore_wait(barrier, len(partners))


def here():
    return lax.axis_index("seq"), lax.axis_index("core")


def bits_of(seqs):
    return [1 << bit for bit in range(seqs.bit_length() - 1)]


def cube_partners(seqs):
    me, core = here()
    partners = [{"seq": flip(me, bit), "core": core} for bit in bits_of(seqs)]
    return partners + [{"seq": me, "core": 1 - core}]


def all_partners(seqs):
    me, core = here()
    return [
        {"seq": flip(me, step), "core": core if same else 1 - core}
        for step in range(seqs)
        for same in (True, False)
        if step or not same
    ]


def orders_of(seqs):
    bits = bits_of(seqs)
    return [bits, bits[1:] + bits[:1]]


def remote(source, target, sems, at, device):
    return pltpu.make_async_remote_copy(
        src_ref=source,
        dst_ref=target,
        send_sem=sems[0].at[at],
        recv_sem=sems[1].at[at],
        device_id=device,
        device_id_type=MESH,
    )


def push(*where):
    copy = remote(*where)
    copy.start()
    return copy


def loads(sources, rooms, sems):
    copies = []
    for i, (source, room) in enumerate(zip(sources, rooms)):
        if isinstance(source, tuple):
            source = source[0].at[:, pl.ds(source[1], source[2])]
        copies.append(pltpu.make_async_copy(source, room, sems.at[i]))
    return copies


def like(*arrays):
    return [pltpu.VMEM(array.shape, array.dtype) for array in arrays]


def pair_sems(*shape):
    return [pltpu.SemaphoreType.DMA(shape)] * 2


def spread_scratch(seqs):
    return pair_sems(2, seqs) + pair_sems(2, seqs) + [pltpu.SemaphoreType.DMA]


class Spread:
    def __init__(self, own, out, scratch, rows=None):
        self.own, self.out = own, out
        self.rows = rows or pl.ds(0, own.shape[0])
        self.across, self.aside, self.local = scratch[0:2], scratch[2:4], scratch[4]
        self.me, self.core = here()
        self.half = out.shape[-1] // 2
        self.orders = orders_of(out.shape[1])
        self.phases = len(self.orders[0])

    def columns(self, ref, stream):
        return ref.at[self.rows, pl.ds(stream * self.half, self.half)]

    def place(self, offset, stream):
        return self.columns(self.out.at[self.core, flip(self.me, offset)], stream)

    def block(self, offset, stream):
        return self.place(offset, stream) if offset else self.columns(self.own, stream)

    def kept(self):
        return pltpu.make_async_copy(
            self.own.at[self.rows], self.out.at[self.core, self.me, self.rows], self.local
        )

    def swap(self, offset, stream):
        sibling = {"seq": self.me, "core": 1 - self.core}
        return remote(
            self.block(offset, stream),
            self.place(offset, stream),
            self.aside,
            (stream, offset),
            sibling,
        )

    def held(self, phase, stream):
        offsets = [0]
        for bit in self.orders[stream][:phase]:
            offsets += [offset + bit for offset in offsets]
        return offsets

    def moves(self, phase):
        found = []
        for stream in range(2):
            bit = self.orders[stream][phase]
            partner = {"seq": flip(self.me, bit), "core": self.core}
            for offset in self.held(phase, stream):
                copy = remote(
                    self.block(offset, stream),
                    self.place(offset, stream),
                    self.across,
                    (stream, offset + bit),
                    partner,
                )
                found.append((copy, offset + bit, stream))
        return found

    def begin(self):
        self.kept().start()
        for copy, _, _ in self.moves(0):
            copy.start()
        for stream in range(2):
            self.swap(0, stream).start()

    def arrive(self, phase):
        for copy, offset, stream in self.moves(phase):
            copy.wait_recv()
            self.swap(offset, stream).start()

    def step(self, phase):
        self.arrive(phase - 1)
        for copy, _, _ in self.moves(phase):
            copy.start()

    def finish(self):
        self.arrive(self.phases - 1)
        for phase in range(self.phases):
            for copy, _, _ in self.moves(phase):
                copy.wait_send()
        for stream in range(2):
            for offset in self.held(self.phases, stream):
                self.swap(offset, stream).wait()
        self.kept().wait()


def fold_rooms(seqs, tokens, width, made=True):
    return [
        pltpu.VMEM((seqs, tokens, width), BF),
        pltpu.VMEM((seqs, tokens, width) if made else (16, PAIR), BF),
        pltpu.VMEM((seqs, tokens, width), BF),
        pltpu.VMEM((2, seqs, tokens, width // 2), BF),
    ]


def fold_sems(seqs):
    return [pltpu.SemaphoreType.DMA((2,))] + pair_sems(seqs) + pair_sems(2, seqs)


class Fold:
    def __init__(self, terms, rooms, sems, rows, make=None):
        self.terms, self.make = terms, make
        self.own, self.give, self.total, self.got = rooms
        self.local, self.aside, self.across = sems[0], sems[1:3], sems[3:5]
        self.rows = rows
        self.me, self.core = here()
        self.seqs = self.total.shape[0]
        self.half = self.total.shape[-1] // 2
        self.orders = orders_of(self.seqs)
        self.phases = len(self.orders[0])

    def taken(self, mine):
        core, room = (self.core, self.own) if mine else (1 - self.core, self.give)
        return pltpu.make_async_copy(
            self.terms.at[core, :, self.rows],
            room.at[:, self.rows],
            self.local.at[1 if mine else 0],
        )

    def fill(self, room, core, at):
        width = room.shape[-1]
        tile = min(2 * BLOCK, width)

        def one(j, carry):
            columns = pl.ds(pl.multiple_of(j * tile, tile), tile)
            value = self.make(core, at, self.rows, columns)
            if self.terms is not None:
                value = value + room[at, self.rows, columns].astype(F32)
            room[at, self.rows, columns] = value.astype(BF)
            return carry

        lax.fori_loop(0, width // tile, one, 0)

    def swap(self, offset):
        at = flip(self.me, offset)
        source = self.give.at[at] if self.make else self.terms.at[1 - self.core, at]
        return remote(
            source.at[self.rows],
            self.total.at[at, self.rows],
            self.aside,
            (offset,),
            {"seq": self.me, "core": 1 - self.core},
        )

    def columns(self, stream):
        return pl.ds(stream * self.half, self.half)

    def moves(self, phase, stream, only=None):
        bit = self.orders[stream][phase]
        done = sum(self.orders[stream][:phase])
        partner = {"seq": flip(self.me, bit), "core": self.core}
        return [
            (
                remote(
                    self.total.at[flip(self.me, offset), self.rows, self.columns(stream)],
                    self.got.at[stream, offset, self.rows],
                    self.across,
                    (stream, offset),
                    partner,
                ),
                offset,
            )
            for offset in range(self.seqs - 1, -1, -1)
            if offset & bit and not offset & done and only in (None, offset)
        ]

    def add(self, work):
        count = self.rows.size
        step = min(32, count)

        def one(i, carry):
            work(pl.ds(pl.multiple_of(self.rows.start + i * step, step), step))
            return carry

        lax.fori_loop(0, count // step, one, 0)

    def load(self):
        if self.terms is not None:
            if self.make:
                self.taken(False).start()
            self.taken(True).start()

    def begin(self):
        if self.make and self.terms is not None:
            self.taken(False).wait()
        for offset in range(self.seqs - 1, -1, -1):
            if self.make:
                self.fill(self.give, 1 - self.core, flip(self.me, offset))
            self.swap(offset).start()

    def first(self):
        if self.terms is not None:
            self.taken(True).wait()
        for offset in range(self.seqs - 1, -1, -1):
            at = flip(self.me, offset)
            if self.make:
                self.fill(self.own, self.core, at)
            self.swap(offset).wait_recv()

            def add_sibling(rows, at=at):
                both = self.total[at, rows, :].astype(F32) + self.own[at, rows, :].astype(F32)
                self.total[at, rows, :] = both.astype(BF)

            self.add(add_sibling)
            for stream in range(2):
                for copy, _ in self.moves(0, stream, offset):
                    copy.start()

    def receive(self, phase, stream):
        bit = self.orders[stream][phase]
        for copy, offset in self.moves(phase, stream):
            copy.wait_recv()
            at = flip(self.me, offset - bit)

            def add_got(rows, at=at, offset=offset):
                columns = self.columns(stream)
                both = self.total[at, rows, columns].astype(F32) + self.got[
                    stream, offset, rows, :
                ].astype(F32)
                self.total[at, rows, columns] = both.astype(BF)

            self.add(add_got)

    def step(self, phase):
        for stream in range(2):
            self.receive(phase - 1, stream)
            for copy, _ in self.moves(phase, stream):
                copy.start()

    def last(self):
        for stream in range(2):
            self.receive(self.phases - 1, stream)

    def result(self, rows):
        return self.total[self.me, rows, :].astype(F32)

    def settle(self):
        for offset in range(self.seqs):
            self.swap(offset).wait_send()
        for phase in range(self.phases):
            for stream in range(2):
                for copy, _ in self.moves(phase, stream):
                    copy.wait_send()


def halves(count):
    return [pl.ds(i * (count // 2), count // 2) for i in range(2)]


def fold_then_spread(folds, spreads, work, aside=lambda: None):
    phases = folds[0].phases
    for fold in folds:
        fold.begin()
        fold.first()
    aside()
    for phase in range(1, phases):
        for fold in folds:
            fold.step(phase)
            aside()
    for fold, spread in zip(folds, spreads):
        fold.last()
        fold.add(work)
        spread.begin()
        aside()
    for phase in range(1, phases):
        for spread in spreads:
            spread.step(phase)
            aside()
    for spread in spreads:
        spread.finish()
    for fold in folds:
        fold.settle()


def by_rows(count, work):
    step = min(32, count)

    def one(i, carry):
        work(pl.ds(pl.multiple_of(i * step, step), step))
        return carry

    lax.fori_loop(0, count // step, one, 0)


def deal_scratch(pieces, seqs):
    blocks = [piece.shape[-2:] for piece in pieces]
    return (
        pair_sems(len(pieces), 2 * seqs)
        + [pltpu.SemaphoreType.DMA((2, len(pieces)))]
        + [pltpu.VMEM(block, piece.dtype) for block, piece in zip(blocks, pieces)]
    )


class Deal:
    def __init__(self, pieces, outs, scratch, core_first=False):
        self.pieces, self.outs = pieces, outs
        self.sems, self.local, self.rooms = scratch[:2], scratch[2], scratch[3:]
        self.me, self.core = here()
        self.core_first = core_first
        self.seqs = outs[0].shape[1 if core_first else 0]

    def piece(self, i, seq, core):
        piece, out = self.pieces[i], self.outs[i]
        return piece.at[seq, core] if len(piece.shape) == len(out.shape) else piece

    def place(self, i):
        out = self.outs[i]
        return out.at[self.core, self.me] if self.core_first else out.at[self.me, self.core]

    def copy(self, i, step, same):
        to_seq = flip(self.me, step)
        to_core = self.core if same else 1 - self.core
        return remote(
            self.piece(i, to_seq, to_core),
            self.place(i),
            self.sems,
            (i, 2 * step + (0 if same else 1)),
            {"seq": to_seq, "core": to_core},
        )

    def copies(self):
        return [
            self.copy(i, step, same)
            for i in range(len(self.pieces))
            for step in range(self.seqs)
            for same in (True, False)
            if step or not same
        ]

    def entering(self):
        return [
            pltpu.make_async_copy(
                self.piece(i, self.me, self.core), self.rooms[i], self.local.at[0, i]
            )
            for i in range(len(self.rooms))
        ]

    def leaving(self):
        return [
            pltpu.make_async_copy(
                self.rooms[i] if self.rooms else self.piece(i, self.me, self.core),
                self.place(i),
                self.local.at[1, i],
            )
            for i in range(len(self.outs))
        ]

    def begin(self):
        for copy in self.copies() + self.entering():
            copy.start()
        for copy in self.entering():
            copy.wait()
        for copy in self.leaving():
            copy.start()

    def arrive_from(self, step):
        if step:
            self.copy(0, step, True).wait_recv()
        else:
            for copy in self.leaving():
                copy.wait()
        self.copy(0, step, False).wait_recv()

    def arrive(self):
        for copy in self.copies():
            copy.wait_recv()
        for copy in self.leaving():
            copy.wait()

    def settle(self):
        for copy in self.copies():
            copy.wait_send()

    def finish(self):
        self.arrive()
        self.settle()


class Ring:
    def __init__(self, whole, sems, part):
        self.whole, self.sems, self.part = whole, sems, part
        self.count = whole.shape[0]
        self.chip = lax.axis_index("z")

    def hop(self, i):
        block = self.whole.at[lax.rem(self.chip + self.count - i, self.count), self.part]
        following = lax.rem(self.chip + 1, self.count)
        return remote(block, block, self.sems, (i,), {"z": following})

    def preceding(self):
        return {"z": lax.rem(self.chip + self.count - 1, self.count)}

    def begin(self):
        self.hop(0).start()

    def step(self, i):
        self.hop(i - 1).wait_recv()
        if i < self.count - 1:
            self.hop(i).start()

    def settle(self):
        for i in range(self.count - 1):
            self.hop(i).wait_send()


def deal(pieces, number):
    count = len(pieces)
    seqs = pieces[0].shape[0]

    def body(*refs):
        greet(all_partners(seqs))
        work = Deal(refs[:count], refs[count : 2 * count], refs[2 * count :])
        work.begin()
        work.finish()

    return kernel_call(
        body,
        "deal",
        [*pieces],
        number,
        in_specs=[ANYWHERE] * count,
        out_specs=[ANYWHERE] * count,
        out_shape=[jax.ShapeDtypeStruct(piece.shape, BF) for piece in pieces],
        scratch_shapes=deal_scratch(pieces, seqs),
    )


def cut_into(out, parts):
    for source, gain, places in parts:
        for owner, there, begin, width in places:
            part = source[:, begin : begin + width]
            if gain is not None:
                part = (part.astype(F32) * gain).astype(BF)
            out[owner // 2, owner % 2, :, there : there + width] = part


def start(arrays, gains, table, plans, blocks, seqs, chips, number):
    tokens, w_qkv = arrays[0], arrays[2]
    count, width = tokens.shape
    rows = w_qkv.shape[0]
    (qkv_places, out_places, attend_cols), chunks = plans
    shape = (seqs, 2, rows)
    cuts = [shape + (cols,) for _, _, cols in chunks]
    more = len(chunks) - 1

    def body(*refs):
        sources, gains_in, table_in = refs[:6], refs[6], refs[7]
        acts, whole, piece, tables, *moved = refs[8:14]
        cut_out = refs[14 : 14 + more]
        scratch = refs[14 + more :]
        gain_one, gain_two = gains_in[:, :1], gains_in[:, 1:]
        rooms, (sem, attend_cut), scratch = scratch[:6], scratch[6:8], scratch[8:]
        ff_cut, scratch = scratch[: 1 + more], scratch[1 + more :]
        turned, own, scratch = scratch[:2], scratch[2], scratch[3:]
        out_sem, ring_sems, scratch = scratch[0], scratch[1 : 1 + 2 * seqs], scratch[1 + 2 * seqs :]
        deal_sems, spread_sems, table_room = scratch[:9], scratch[9:14], scratch[14:]
        coming = loads(sources, rooms, sem)
        for i in (2, 3, 0, 4, 5, 1):
            coming[i].start()
        me_chip = lax.axis_index("z")
        rings = [
            Ring(whole, ring_sems[2 * i : 2 * i + 2], flip(lax.axis_index("seq"), i))
            for i in range(seqs)
        ]
        greet(all_partners(seqs) + [rings[0].preceding()])
        coming[2].wait()
        coming[3].wait()
        cut_into(
            attend_cut, [(rooms[2], gain_one, qkv_places), (rooms[3], None, out_places)]
        )
        attend_deal = Deal([attend_cut], [whole.at[me_chip]], deal_sems[:3])
        attend_deal.begin()
        attend_deal.arrive_from(0)
        rings[0].begin()
        coming[0].wait()
        for outer, inner, size in blocks:
            turned[0][:, inner : inner + size] = rooms[0][:, outer : outer + size]

        def norm(at):
            values = turned[0][at, :].astype(F32)
            own[at, :] = (values * norm_scale(values)).astype(BF)

        by_rows(count, norm)
        coming[4].wait()
        coming[5].wait()
        for out, (pair, single, _) in zip(ff_cut, chunks):
            cut_into(out, [(rooms[4], gain_two, pair), (rooms[5], None, single)])
        coming[1].wait()
        for outer, inner, size in blocks:
            turned[1][:, inner : inner + size] = rooms[1][:, outer : outer + size]
        going = loads(list(turned) + list(ff_cut[1:]), list(moved) + list(cut_out), out_sem)
        for copy in going:
            copy.start()
        for step in range(1, seqs):
            attend_deal.arrive_from(step)
            rings[step].begin()
        spreading = Spread(own, acts, spread_sems)
        spreading.begin()
        table_deal = Deal([table_in], [tables], deal_sems[3:6] + table_room, True)
        table_deal.begin()
        for phase in range(1, spreading.phases):
            spreading.step(phase)
        ff_deal = Deal([ff_cut[0]], [piece], deal_sems[6:9])
        ff_deal.begin()
        for ring in rings:
            ring.step(1)
        for i in range(2, chips):
            for ring in rings:
                ring.step(i)
            if i == 2:
                spreading.finish()
        for ring in rings:
            ring.settle()
        attend_deal.settle()
        table_deal.finish()
        ff_deal.finish()
        for copy in going:
            copy.wait()

    like_tokens = jax.ShapeDtypeStruct((count, width), BF)
    deal_sem = pair_sems(1, 2 * seqs) + [pltpu.SemaphoreType.DMA((2, 1))]
    return kernel_call(
        body,
        "start",
        [*arrays, gains, table],
        number,
        in_specs=[ANYWHERE] * 6 + [LOCAL, ANYWHERE],
        out_specs=[ANYWHERE] * (6 + more),
        out_shape=[
            jax.ShapeDtypeStruct((2, seqs, count, width), BF),
            jax.ShapeDtypeStruct((chips,) + shape + (attend_cols,), BF),
            jax.ShapeDtypeStruct(cuts[0], BF),
            jax.ShapeDtypeStruct((2, seqs) + table.shape, F32),
            like_tokens,
            like_tokens,
        ]
        + [jax.ShapeDtypeStruct(cut, BF) for cut in cuts[1:]],
        scratch_shapes=like(*arrays)
        + [pltpu.SemaphoreType.DMA((6,)), pltpu.VMEM(shape + (attend_cols,), BF)]
        + [pltpu.VMEM(cut, BF) for cut in cuts]
        + [pltpu.VMEM((count, width), BF)] * 3
        + [pltpu.SemaphoreType.DMA((2 + more,))]
        + pair_sems(chips) * seqs
        + deal_sem * 3
        + spread_scratch(seqs)
        + like(table),
    )


def two_way_scratch(seqs, count, width):
    return (
        [pltpu.VMEM((count, width), BF)]
        + fold_rooms(seqs, count, width)
        + fold_sems(seqs) * 2
        + spread_scratch(seqs) * 2
    )


def two_way(given, out, scratch, make):
    own, rooms, sems = scratch[0], scratch[1:5], scratch[5:]
    parts = halves(own.shape[0])
    folds = [
        Fold(given, rooms, sems[5 * i : 5 * i + 5], rows, make) for i, rows in enumerate(parts)
    ]
    sems = sems[10:]
    spreads = [Spread(own, out, sems[5 * i : 5 * i + 5], rows) for i, rows in enumerate(parts)]
    for fold in folds:
        fold.load()
    return folds, spreads, own


def product(left, right, seqs, count):
    def make(core, at, rows, columns):
        begin = pl.multiple_of((core * seqs + at) * count + rows.start, rows.size)
        return nt(left[pl.ds(begin, rows.size), :], right[columns, :])

    return make


def middle_acts(attended, weights, tokens, seqs, number):
    count, width = tokens.shape
    cols = attended.shape[1]
    begin = weights.shape[1] - cols

    def body(left_in, given, source_in, middle, out, left, right, source, sems, *scratch):
        coming = loads([left_in, (given, begin, cols), source_in], [left, right, source], sems)
        for copy in coming:
            copy.start()
        folds, spreads, own = two_way(None, out, scratch, product(left, right, seqs, count))
        greet(cube_partners(seqs))
        for copy in coming:
            copy.wait()

        def norm(rows):
            values = source[rows, :].astype(F32) + folds[0].result(rows)
            middle[rows, :] = values
            own[rows, :] = (values * norm_scale(values)).astype(BF)

        fold_then_spread(folds, spreads, norm)

    return kernel_call(
        body,
        "middle_acts",
        [attended, weights, tokens],
        number,
        in_specs=[ANYWHERE] * 3,
        out_specs=[LOCAL, ANYWHERE],
        out_shape=[
            jax.ShapeDtypeStruct((count, width), F32),
            jax.ShapeDtypeStruct((2, seqs, count, width), BF),
        ],
        scratch_shapes=like(attended)
        + [pltpu.VMEM((width, cols), BF)]
        + like(tokens)
        + [pltpu.SemaphoreType.DMA((3,))]
        + two_way_scratch(seqs, count, width),
    )


def middle_grad(terms, grad_both, cotangent, middle, hidden, weights, number):
    _, seqs, count, width = terms.shape
    tokens = hidden[0].shape[0]
    n = len(hidden)
    block = min(BLOCK, tokens)
    tile = min(2 * BLOCK, width)
    blocks = tokens // block
    parts = [h.shape[1] for h in hidden]

    def body(given, *refs):
        sources, down = refs[: 3 + n], refs[3 + n : 3 + 2 * n]
        grad, out, products = refs[3 + 2 * n : 6 + 2 * n]
        scratch = refs[6 + 2 * n :]
        left, upstream, values = scratch[:3]
        units, room, right = scratch[3 : 3 + n], scratch[3 + n : 3 + 2 * n], scratch[3 + 2 * n]
        stage, sems, leaving = scratch[4 + 2 * n : 7 + 2 * n]
        columns = [(down[i], 2 * parts[i], parts[i]) for i in range(n)]
        coming = loads(
            [sources[0], (down[-1], 0, 2 * parts[-1]), *sources[3:], *columns, *sources[1:3]],
            [left, right, *units, *room, upstream, values],
            sems,
        )
        for copy in coming[:2]:
            copy.start()
        make = product(left, right, seqs, count)
        folds, spreads, own = two_way(given, out, scratch[7 + 2 * n :], make)
        for copy in coming[2:]:
            copy.start()
        greet(cube_partners(seqs))
        for copy in coming[:2]:
            copy.wait()

        def leave(i):
            rows = pl.ds(i * block, block)
            return pltpu.make_async_copy(stage.at[i % 2], products.at[rows], leaving.at[i % 2])

        def multiply(i):
            if i == 0:
                for copy in coming[2:]:
                    copy.wait()
            if i >= 2:
                leave(i - 2).wait()

            def one(j, carry):
                columns = pl.ds(pl.multiple_of(j * tile, tile), tile)
                total = sum(
                    nt(units[k][pl.ds(i * block, block), :], room[k][columns, :])
                    for k in range(n)
                )
                stage[i % 2, :, columns] = total.astype(BF)
                return carry

            lax.fori_loop(0, width // tile, one, 0)
            leave(i).start()

        left_over = list(range(blocks))

        def aside():
            for _ in range(2 if len(left_over) == blocks else max(1, blocks // 8)):
                if left_over:
                    multiply(left_over.pop(0))

        def back(rows):
            held = values[rows, :]
            scale = norm_scale(held)
            result = upstream[rows, :].astype(F32) + norm_back(
                folds[0].result(rows), held * scale, scale
            )
            grad[rows, :] = result
            own[rows, :] = result.astype(BF)

        fold_then_spread(folds, spreads, back, aside)
        while left_over:
            multiply(left_over.pop(0))
        for i in range(max(0, blocks - 2), blocks):
            leave(i).wait()

    return kernel_call(
        body,
        "middle_grad",
        [terms, grad_both, cotangent, middle, *hidden, *weights],
        number,
        in_specs=[ANYWHERE] * (4 + 2 * n),
        out_specs=[LOCAL, ANYWHERE, ANYWHERE],
        out_shape=[
            jax.ShapeDtypeStruct((count, width), F32),
            jax.ShapeDtypeStruct(terms.shape, BF),
            jax.ShapeDtypeStruct((tokens, width), BF),
        ],
        scratch_shapes=like(grad_both, cotangent, middle, *hidden)
        + [pltpu.VMEM((width, part), BF) for part in parts]
        + [pltpu.VMEM((width, 2 * parts[-1]), BF), pltpu.VMEM((2, block, width), BF)]
        + [pltpu.SemaphoreType.DMA((4 + 2 * n,)), pltpu.SemaphoreType.DMA((2,))]
        + two_way_scratch(seqs, count, width),
    )


def input_grad(grad_mixed, weights, tokens, grad_middle, seqs, number):
    count, width = tokens.shape
    cols = grad_mixed.shape[1]

    def body(*refs):
        left_in, given, source_in, held_in, out, left, right, source, held, sems, *scratch = refs
        coming = loads(
            [left_in, (given, 0, cols), source_in, held_in], [left, right, source, held], sems
        )
        for copy in coming:
            copy.start()
        make = product(left, right, seqs, count)
        sems = scratch[4:]
        folds = [
            Fold(None, scratch[:4], sems[5 * i : 5 * i + 5], rows, make)
            for i, rows in enumerate(halves(count))
        ]
        greet(cube_partners(seqs))
        for copy in coming:
            copy.wait()
        for fold in folds:
            fold.begin()
            fold.first()
        for phase in range(1, folds[0].phases):
            for fold in folds:
                fold.step(phase)

        def back(rows):
            values = source[rows, :].astype(F32)
            scale = norm_scale(values)
            out[rows, :] = held[rows, :] + norm_back(folds[0].result(rows), values * scale, scale)

        for fold in folds:
            fold.last()
            fold.add(back)
        for fold in folds:
            fold.settle()

    return kernel_call(
        body,
        "input_grad",
        [grad_mixed, weights, tokens, grad_middle],
        number,
        in_specs=[ANYWHERE] * 4,
        out_specs=LOCAL,
        out_shape=jax.ShapeDtypeStruct((count, width), F32),
        scratch_shapes=like(grad_mixed)
        + [pltpu.VMEM((width, cols), BF)]
        + like(tokens, grad_middle)
        + [pltpu.SemaphoreType.DMA((4,))]
        + fold_rooms(seqs, count, width)
        + fold_sems(seqs) * 2,
    )


class Order:
    def __init__(self):
        self.latest = None

    def enter(self, values):
        if self.latest is None:
            return values
        return lax.optimization_barrier((values, self.latest))[0]

    def run(self, work, *values):
        result = work(*self.enter(values))
        self.latest = jax.tree.leaves(result)
        return result

    def take(self, values):
        if self.latest is not None:
            values = lax.optimization_barrier((values, self.latest))[0]
        self.latest = jax.tree.leaves(values)
        return values


def rope_table(places):
    half = HEAD_DIM // 2
    inverse = ROPE_BASE ** (-2.0 * jnp.arange(half).astype(F32) / HEAD_DIM)
    angles = places.astype(F32)[:, None] * inverse[None, :]
    return jnp.concatenate([jnp.cos(angles), jnp.sin(angles)] * 2, 1)


def norm_scale(values):
    return lax.rsqrt(jnp.mean(values * values, -1, keepdims=True) + EPS)


def norm_back(grad, normed, scale):
    return scale * (grad - normed * jnp.mean(grad * normed, -1, keepdims=True))


def per_device(
    mesh, tokens, positions, w_qkv, w_out, gain_attn, w_gate_up, w_down, gain_mlp, cotangent
):
    order = Order()
    seqs, chips = mesh.shape["seq"], mesh.shape["z"]
    owners = 2 * seqs
    token_count, width = tokens.shape[1:]
    ff_width = w_down.shape[1]
    rows = w_qkv.shape[0]
    head_cols = width // owners
    ff_cols = ff_width // owners
    parts = chunk_widths(ff_cols)
    last = len(parts) - 1
    blocks = blocks_in(rows, seqs, chips)
    gain_one = gain_attn.astype(F32)[:, None]
    gain_two = gain_mlp.astype(F32)[:, None]

    def by_place(piece):
        return piece.reshape(seqs, 2, rows, -1)

    def gathered(piece):
        piece = order.enter(piece).reshape(seqs, 2 * rows, -1)
        return lax.all_gather(piece, "z", axis=0, tiled=False)

    def flat(value):
        return order.take(value).reshape(width, -1)

    def summed(term):
        split = order.enter(term).reshape(chips, seqs, 2 * rows, -1)
        return lax.psum_scatter(split, "z", scatter_dimension=0, tiled=False)

    def rounded(left, right):
        return tn(left, right).astype(BF)

    qkv_places = list(qkv_columns(owners, head_cols))
    out_places = [(o, 3 * head_cols, o * head_cols, head_cols) for o in range(owners)]
    gate_up_places, down_places = ff_columns(owners, ff_cols)
    chunks = [
        (pair, single, 3 * part) for pair, single, part in zip(gate_up_places, down_places, parts)
    ]
    table_own = rope_table(positions[0])
    acts, attend_whole, ff_piece, table, tokens_in, upstream_own, *ff_cut = order.run(
        lambda t, *a: start(
            a[:6],
            a[6],
            t,
            ((qkv_places, out_places, 4 * head_cols), chunks),
            blocks,
            seqs,
            chips,
            1,
        ),
        table_own,
        tokens[0],
        cotangent[0],
        w_qkv,
        w_out,
        w_gate_up,
        w_down,
        jnp.stack([gain_attn, gain_mlp], 1).astype(F32),
    )
    acts = acts.reshape(-1, width)
    attend_whole = attend_whole.reshape(width, -1)
    table = table.reshape(-1, PAIR)
    ff_coming = [gathered(ff_piece)]

    qkv_cols = 3 * head_cols
    mixed = order.run(lambda a, w: nn(a, w[:, :qkv_cols]), acts, attend_whole)
    qkv, attended, logs, upstream, *ff_pieces = order.run(
        lambda m, t, u, *given: attend(m, t, SpreadBeside(seqs, u, given), 2, 3),
        mixed,
        table,
        upstream_own,
        *ff_cut,
    )
    ff_coming += [gathered(piece) for piece in ff_pieces]
    upstream = upstream.reshape(-1, width)
    middle, acts_mid = order.run(
        lambda a, w, x: middle_acts(a, w, x, seqs, 4), attended, attend_whole, tokens_in
    )
    acts_mid = acts_mid.reshape(-1, width)

    def feed_hidden(both):
        part = both.shape[1] // 2
        gate, up = both[:, :part], both[:, part:]
        return (gate * jax.nn.sigmoid(gate) * up).astype(BF)

    def feed_back(grad_hidden, both):
        part = both.shape[1] // 2
        gate, up = both[:, :part], both[:, part:]
        sigma = jax.nn.sigmoid(gate)
        grad_gate = grad_hidden * up * sigma * (1.0 + gate * (1.0 - sigma))
        grad_up = grad_hidden * gate * sigma
        return jnp.concatenate([grad_gate.astype(BF), grad_up.astype(BF)], 1)

    def both_terms(left, right, left_two, right_two):
        return [rounded(left, right), rounded(left_two, right_two)]

    def add_nt(left, right, total=None):
        result = nt(left, right)
        return (result if total is None else result + total.astype(F32)).astype(BF)

    ff_sums, hiddens, wholes = [], [], []
    norm_mid_terms = ()
    for chunk, part in enumerate(parts):
        cols = 2 * part
        whole = flat(ff_coming[chunk])
        both = order.run(lambda a, w: nn(a, w[:, :cols]), acts_mid, whole)
        hidden = order.run(feed_hidden, both)
        hiddens.append(hidden)
        wholes.append(whole)
        grad_hidden = order.run(lambda a, w: nn(a, w[:, cols:]), upstream, whole)
        grad_both = order.run(feed_back, grad_hidden, both)
        terms = order.run(both_terms, acts_mid, grad_both, upstream, hidden)
        if chunk < len(parts) - 1:
            ff_sums.append(summed(order.run(side_by_side, terms)))
        if chunk < len(parts) - 1:
            norm_mid_terms = (
                order.run(
                    lambda a, w, *t: add_nt(a, w[:, :cols], *t), grad_both, whole, *norm_mid_terms
                ),
            )

    grad_middle, grad_branch, outcome_terms = order.run(
        lambda a, b, c, d, e, f: middle_grad(a, b, c, d, e, f, 5),
        norm_mid_terms[0].reshape(2, seqs, token_count, width),
        grad_both,
        upstream_own,
        middle,
        hiddens,
        wholes,
    )
    grad_branch = grad_branch.reshape(-1, width)

    terms.append(order.run(rounded, grad_branch, attended))
    ff_sums.append(summed(order.run(side_by_side, terms)))
    grad_attended = order.run(
        lambda a, w: nn(a, w[:, qkv_cols:]).astype(BF), grad_branch, attend_whole
    )
    first_rows = [by_place(order.take(value)) for value in ff_sums[:-1]]
    grad_mixed, outcome, *ff_dealt = order.run(
        lambda a, b, c, d, e, f, *given: attend_back(
            a, b, c, d, OutputBeside(seqs, e, f, given), 2, 6
        ),
        qkv,
        grad_attended,
        logs,
        table,
        outcome_terms.reshape(2, seqs, token_count, width),
        middle,
        *first_rows,
    )
    qkv_sum = summed(order.run(rounded, acts, grad_mixed))

    grad_inputs = order.run(
        lambda a, w, b, c: input_grad(a, w, b, c, seqs, 7),
        grad_mixed,
        attend_whole,
        tokens_in,
        grad_middle,
    )
    grad_inputs, outcome = order.run(lambda *a: outside(a, blocks), grad_inputs, outcome)
    last_rows = by_place(order.take(ff_sums[-1]))
    ff_dealt += order.run(lambda a: deal([a], 8), last_rows)
    last_places = [(o, 3 * parts[-1], o * head_cols, head_cols) for o in range(owners)]
    grad_gate_up, gain_two_sum, grad_down, grad_out = order.run(
        lambda w, g, *a: join_ff(a, w, g, gate_up_places, down_places, last_places),
        w_gate_up,
        gain_two,
        *[value.reshape(owners, rows, -1) for value in ff_dealt],
    )
    qkv_rows = order.take(qkv_sum)
    (qkv_dealt,) = order.run(lambda a: deal([a], 9), by_place(qkv_rows))
    grad_qkv, gain_one_sum = order.run(
        lambda w, g, a: join_qkv(a, w, g, qkv_places),
        w_qkv,
        gain_one,
        qkv_dealt.reshape(owners, rows, -1),
    )
    return (
        outcome[None],
        grad_inputs[None],
        grad_qkv,
        grad_out,
        gain_one_sum[:, 0],
        grad_gate_up,
        grad_down,
        gain_two_sum[:, 0],
    )


def solution(mesh):
    seqs, devices = mesh.shape["seq"], mesh.shape["fsdp"]
    parted = Mesh(mesh.devices.reshape(seqs, devices // 2, 2), ("seq", "z", "core"))
    tokens = P(("z", "core"), "seq", None)
    matrix = P(("seq", "z", "core"), None)
    vector = P(("seq", "z", "core"))
    return jax.shard_map(
        functools.partial(per_device, parted),
        mesh=parted,
        in_specs=(
            tokens,
            P(("z", "core"), "seq"),
            matrix,
            matrix,
            vector,
            matrix,
            matrix,
            vector,
            tokens,
        ),
        out_specs=(tokens, tokens, matrix, matrix, vector, matrix, matrix, vector),
        check_vma=False,
    )
```

```python
import functools
import math

import jax
import jax.numpy as jnp
import numpy as np
from jax import lax
from jax.experimental import pallas as pl
from jax.experimental.pallas import tpu as pltpu
from jax.sharding import Mesh, PartitionSpec as P

HEAD_DIM = 64
PAIR = 2 * HEAD_DIM
BLOCK = 256
EPS = 1e-05
ROPE_BASE = 130000.0
BF = jnp.bfloat16
F32 = jnp.float32
VMEM_MOST = 58 << 20
MESH = pl.DeviceIdType.MESH
ANYWHERE = pl.BlockSpec(memory_space=pltpu.HBM)
LOCAL = pl.BlockSpec(memory_space=pltpu.VMEM)


def room_for(spec, arrays):
    total = 8 << 20
    for room in spec.get("scratch_shapes", ()):
        if hasattr(room, "shape") and room.dtype in (BF, F32):
            total += math.prod(room.shape) * jnp.dtype(room.dtype).itemsize
    outs = spec["out_shape"] if isinstance(spec["out_shape"], list) else [spec["out_shape"]]
    specs = spec.get("out_specs", LOCAL), spec.get("in_specs", LOCAL)
    for values, given in zip((outs, arrays), specs):
        given = given if isinstance(given, list) else [given] * len(values)
        for value, where in zip(values, given):
            if where.block_shape is not None:
                total += 2 * math.prod(where.block_shape) * value.dtype.itemsize
            elif where is not ANYWHERE:
                total += math.prod(value.shape) * value.dtype.itemsize
    return min(total, VMEM_MOST)


def kernel_call(body, name, arrays, number=None, **spec):
    params = {"vmem_limit_bytes": room_for(spec, arrays)}
    if number is not None:
        params.update(vmem_limit_bytes=VMEM_MOST, collective_id=number, has_side_effects=True)
    return pl.pallas_call(
        body, name=name, compiler_params=pltpu.CompilerParams(**params), **spec
    )(*arrays)


def turn(x, cosine, sine):
    half = HEAD_DIM // 2
    lane = lax.broadcasted_iota(jnp.int32, x.shape, 1)
    swapped = jnp.where(
        lane % HEAD_DIM < half, pltpu.roll(x, PAIR - half, 1), pltpu.roll(x, half, 1)
    )
    return x * cosine + swapped * sine


def nt(left, right):
    return lax.dot_general(left, right, (((1,), (1,)), ((), ())), preferred_element_type=F32)


def tn(left, right):
    return lax.dot_general(left, right, (((0,), (0,)), ((), ())), preferred_element_type=F32)


def nn(left, right):
    return lax.dot_general(left, right, (((1,), (0,)), ((), ())), preferred_element_type=F32)


def masked_scores(queries, keys, block):
    scores = nt(queries, keys)
    rows = lax.broadcasted_iota(jnp.int32, (BLOCK, BLOCK), 0)
    cols = lax.broadcasted_iota(jnp.int32, (BLOCK, BLOCK), 1)
    last = jnp.where(cols <= rows, scores[:, block * BLOCK :], -1e30)
    return jnp.concatenate([scores[:, : block * BLOCK], last], 1) if block else last


def unpack(table):
    half = HEAD_DIM // 2
    cosine, sine = table[:, :half], table[:, half:HEAD_DIM]
    return (
        jnp.concatenate([cosine] * 4, 1),
        jnp.concatenate([-sine, sine] * 2, 1),
    )


def attend_body(mixed, table, qkv, out, logs):
    length = mixed.shape[0]
    cosine, sine = unpack(table[...])
    qkv[:, :PAIR] = turn(mixed[:, :PAIR], cosine, sine).astype(BF)
    qkv[:, PAIR : 2 * PAIR] = turn(mixed[:, PAIR : 2 * PAIR], cosine, sine).astype(BF)
    qkv[:, 2 * PAIR :] = mixed[:, 2 * PAIR :].astype(BF)
    scale = jnp.asarray(1.0 / math.sqrt(HEAD_DIM), BF)
    for block in range(length // BLOCK):
        at = pl.ds(block * BLOCK, BLOCK)
        seen = (block + 1) * BLOCK
        outs = []
        totals = []
        for low in (0, HEAD_DIM):
            high = low + HEAD_DIM
            queries = qkv[at, low:high] * scale
            scores = masked_scores(queries, qkv[:seen, PAIR + low : PAIR + high], block)
            highest = jnp.max(scores, -1, keepdims=True)
            weights = jnp.exp(scores - highest)
            summed = jnp.sum(weights, -1, keepdims=True)
            probs = (weights * (1.0 / summed)).astype(BF)
            outs.append(nn(probs, qkv[:seen, 2 * PAIR + low : 2 * PAIR + high]))
            totals.append(jnp.broadcast_to(highest + jnp.log(summed), (BLOCK, HEAD_DIM)))
        out[at, :] = jnp.concatenate(outs, 1).astype(BF)
        logs[at, :] = jnp.concatenate(totals, 1)


def attend_back_body(qkv, grad, logs, table, grad_qkv, grad_keys, grad_values):
    length = qkv.shape[0]
    scale = 1.0 / math.sqrt(HEAD_DIM)
    cosine, sine = unpack(table[...])
    last = length // BLOCK - 1
    for block in range(last, -1, -1):
        at = pl.ds(block * BLOCK, BLOCK)
        seen = (block + 1) * BLOCK
        rows = slice(block * BLOCK, seen)
        grad_queries = []
        for low in (0, HEAD_DIM):
            high = low + HEAD_DIM
            queries = qkv[at, low:high] * jnp.asarray(scale, BF)
            keys = qkv[:seen, PAIR + low : PAIR + high]
            upstream = grad[at, low:high]
            scores = masked_scores(queries, keys, block)
            probs = jnp.exp(scores - logs[at, low : low + 1])
            grad_probs = nt(upstream, qkv[:seen, 2 * PAIR + low : 2 * PAIR + high])
            inner = jnp.sum(probs * grad_probs, -1, keepdims=True)
            grad_scores = (probs * (grad_probs - inner)).astype(BF)
            grad_queries.append(nn(grad_scores, keys))
            for_keys = tn(grad_scores, queries)
            for_values = tn(probs.astype(BF), upstream)
            if block == last:
                grad_keys[:, low:high] = for_keys
                grad_values[:, low:high] = for_values
            else:
                grad_keys[:seen, low:high] += for_keys
                grad_values[:seen, low:high] += for_values
        rounded = (jnp.concatenate(grad_queries, 1) * scale).astype(BF).astype(F32)
        grad_qkv[at, :PAIR] = turn(rounded, cosine[rows], -sine[rows]).astype(BF)
    rounded = grad_keys[...].astype(BF).astype(F32)
    grad_qkv[:, PAIR : 2 * PAIR] = turn(rounded, cosine, -sine).astype(BF)
    grad_qkv[:, 2 * PAIR :] = grad_values[...].astype(BF)


def heads_call(body, name, arrays, kinds, outs, out_kinds, count, beside, number, scratch):
    tokens = arrays[0].shape[0]
    length = tokens // count
    pairs = arrays[0].shape[1] // (3 * PAIR)
    specs = {
        "wide": pl.BlockSpec((length, 3 * PAIR), lambda s, i: (s, i)),
        "one": pl.BlockSpec((length, PAIR), lambda s, i: (s, i)),
        "table": pl.BlockSpec((length, PAIR), lambda s, i: (s, 0)),
    }
    n_in, n_out = len(arrays), len(outs)
    more_in, more_out = len(beside.arrays), len(beside.outs)

    def whole(*refs):
        ins, given = refs[:n_in], refs[n_in : n_in + more_in]
        rest = refs[n_in + more_in :]
        results, made = rest[:n_out], rest[n_out : n_out + more_out]
        rest = rest[n_out + more_out :]
        room, held = rest[: len(beside.scratch)], rest[len(beside.scratch) :]
        step = pl.program_id(0) * pairs + pl.program_id(1)
        last = count * pairs - 1
        acts = beside.acts(given, made, room)
        when = [(2 * i * (last + 1) + len(acts) - 1) // (2 * len(acts) - 2) for i in range(len(acts))]
        for i, act in enumerate(acts):
            if when[i] <= last:
                pl.when(step == when[i])(act)
        body(*ins, *results, *held)

        @pl.when(step == last)
        def _():
            for i, act in enumerate(acts):
                if when[i] > last:
                    act()

    return kernel_call(
        whole,
        name,
        list(arrays) + list(beside.arrays),
        number,
        grid=(count, pairs),
        in_specs=[specs[kind] for kind in kinds] + [ANYWHERE] * more_in,
        out_specs=[specs[kind] for kind in out_kinds] + [ANYWHERE] * more_out,
        out_shape=list(outs) + list(beside.outs),
        scratch_shapes=list(beside.scratch) + scratch(length),
    )


class SpreadBeside:
    def __init__(self, seqs, own, pieces):
        self.seqs = seqs
        self.arrays = [own] + list(pieces)
        self.outs = [jax.ShapeDtypeStruct((2, seqs) + own.shape, BF)]
        self.outs += [jax.ShapeDtypeStruct(piece.shape, BF) for piece in pieces]
        self.scratch = [pltpu.VMEM(own.shape, BF), pltpu.SemaphoreType.DMA]
        self.scratch += spread_scratch(seqs)
        self.first = len(self.scratch)
        self.scratch += deal_scratch(pieces, seqs) if pieces else []

    def acts(self, given, made, room):
        def dealing():
            return Deal(given[1:], made[1:], room[self.first :])

        def spreading():
            return Spread(room[0], made[0], room[2:])

        def begin():
            copy = pltpu.make_async_copy(given[0], room[0], room[1])
            copy.start()
            greet(all_partners(self.seqs))
            copy.wait()
            spreading().begin()
            if given[1:]:
                dealing().begin()

        def finish():
            spreading().finish()
            if given[1:]:
                dealing().finish()

        def step(phase):
            return lambda: spreading().step(phase)

        return [begin] + [step(i) for i in range(1, len(bits_of(self.seqs)))] + [finish]


class OutputBeside:
    def __init__(self, seqs, terms, middle, pieces):
        self.seqs = seqs
        self.arrays = [terms, middle] + list(pieces)
        self.outs = [jax.ShapeDtypeStruct(middle.shape, BF)]
        self.outs += [jax.ShapeDtypeStruct(piece.shape, BF) for piece in pieces]
        self.scratch = [
            pltpu.VMEM(middle.shape, F32),
            pltpu.VMEM(middle.shape, BF),
            pltpu.SemaphoreType.DMA((2,)),
        ]
        self.scratch += fold_rooms(seqs, *middle.shape, False) + fold_sems(seqs)
        self.first = len(self.scratch)
        self.scratch += deal_scratch(pieces, seqs)

    def acts(self, given, made, room):
        held, rounded, sems = room[:3]

        def dealing():
            return Deal(given[2:], made[1:], room[self.first :])

        def folding():
            return Fold(given[0], room[3:7], room[7:12], pl.ds(0, held.shape[0]))

        def entering():
            return pltpu.make_async_copy(given[1], held, sems.at[0])

        def begin():
            entering().start()
            folding().load()
            greet(all_partners(self.seqs))
            folding().begin()
            dealing().begin()

        def finish():
            fold = folding()
            fold.last()
            entering().wait()

            def add(rows):
                rounded[rows, :] = (held[rows, :] + fold.result(rows)).astype(BF)

            fold.add(add)
            leaving = pltpu.make_async_copy(rounded, made[0], sems.at[1])
            leaving.start()
            fold.settle()
            dealing().finish()
            leaving.wait()

        def step(phase):
            return lambda: folding().step(phase)

        phases = len(bits_of(self.seqs))
        return [begin, lambda: folding().first()] + [step(i) for i in range(1, phases)] + [finish]


def attend(mixed, table, beside, count, number):
    tokens, cols = mixed.shape
    outs = [
        jax.ShapeDtypeStruct((tokens, cols), BF),
        jax.ShapeDtypeStruct((tokens, cols // 3), BF),
        jax.ShapeDtypeStruct((tokens, cols // 3), F32),
    ]
    return heads_call(
        attend_body,
        "attend",
        [mixed, table],
        ["wide", "table"],
        outs,
        ["wide", "one", "one"],
        count,
        beside,
        number,
        lambda length: [],
    )


def attend_back(qkv, grad, logs, table, beside, count, number):
    return heads_call(
        attend_back_body,
        "attend_back",
        [qkv, grad, logs, table],
        ["wide", "one", "one", "table"],
        [jax.ShapeDtypeStruct(qkv.shape, BF)],
        ["wide"],
        count,
        beside,
        number,
        lambda length: [pltpu.VMEM((length, PAIR), F32)] * 2,
    )


def qkv_columns(owners, cols):
    for owner in range(owners):
        for pair in range(cols // PAIR):
            for kind in range(3):
                there = (pair * 3 + kind) * PAIR
                yield owner, there, (kind * owners + owner) * cols + pair * PAIR, PAIR


def chunk_widths(cols):
    units = cols // PAIR
    first = max(1, (5 * units) // 8)
    return [n * PAIR for n in (first, units - first) if n]


def ff_columns(owners, cols):
    begin = 0
    gate_up, down = [], []
    for part in chunk_widths(cols):
        gate_up.append(
            [
                (owner, kind * part, (kind * owners + owner) * cols + begin, part)
                for owner in range(owners)
                for kind in range(2)
            ]
        )
        down.append([(owner, 2 * part, owner * cols + begin, part) for owner in range(owners)])
        begin += part
    return gate_up, down


def side_by_side(parts):
    begins = [sum(part.shape[1] for part in parts[:i]) for i in range(len(parts))]

    def body(*refs):
        out, sems = refs[-2:]
        copies = [
            pltpu.make_async_copy(
                refs[i], out.at[:, pl.ds(begins[i], part.shape[1])], sems.at[i]
            )
            for i, part in enumerate(parts)
        ]
        for copy in copies:
            copy.start()
        for copy in copies:
            copy.wait()

    total = sum(part.shape[1] for part in parts)
    return kernel_call(
        body,
        "side_by_side",
        [*parts],
        in_specs=[LOCAL] * len(parts),
        out_specs=ANYWHERE,
        out_shape=jax.ShapeDtypeStruct((parts[0].shape[0], total), BF),
        scratch_shapes=[pltpu.SemaphoreType.DMA((len(parts),))],
    )


def blocks_in(rows, seqs, chips):
    return [
        ((s * chips + z) * 2 * rows, (z * seqs + s) * 2 * rows, 2 * rows)
        for z in range(chips)
        for s in range(seqs)
    ]


def inside(arrays, blocks):
    n = len(arrays)

    def body(*refs):
        rooms, sems = refs[2 * n : 3 * n], refs[3 * n]
        coming = loads(refs[:n], rooms, sems)
        for copy in coming:
            copy.start()
        for copy, source, out in zip(coming, rooms, refs[n : 2 * n]):
            copy.wait()
            for outer, inner, width in blocks:
                out[:, inner : inner + width] = source[:, outer : outer + width]

    return kernel_call(
        body,
        "inside",
        arrays,
        in_specs=[ANYWHERE] * n,
        out_shape=[jax.ShapeDtypeStruct(a.shape, a.dtype) for a in arrays],
        scratch_shapes=like(*arrays) + [pltpu.SemaphoreType.DMA((n,))],
    )


def outside(arrays, blocks):
    return inside(arrays, [(inner, outer, width) for outer, inner, width in blocks])


def join_ff(sums, w_gate_up, gain, gate_up_places, down_places, out_places):
    rows, total_width = w_gate_up.shape
    count = len(sums)

    def body(*refs):
        weights, gain_in, out, out_gain, out_down, out_out = refs[count:]
        gains = column(gain_in[...])
        total = jnp.zeros((rows, PAIR), F32)
        for source, listed in zip(refs[:count], gate_up_places):
            for owner, there, here, width in listed:
                for step in range(0, width, PAIR):
                    part = source[owner, :, there + step : there + step + PAIR].astype(F32)
                    at = slice(here + step, here + step + PAIR)
                    total += part * weights[:, at].astype(F32)
                    out[:, at] = part * gains
        for source, listed in zip(refs[:count], down_places):
            for owner, there, here, width in listed:
                part = source[owner, :, there : there + width].astype(F32)
                out_down[:, here : here + width] = part
        for owner, there, here, width in out_places:
            part = refs[count - 1][owner, :, there : there + width].astype(F32)
            out_out[:, here : here + width] = part
        out_gain[...] = row(jnp.sum(total, 1, keepdims=True))

    return kernel_call(
        body,
        "join_ff",
        [*sums, w_gate_up, gain],
        out_shape=[
            jax.ShapeDtypeStruct((rows, total_width), F32),
            jax.ShapeDtypeStruct((1, rows), F32),
            jax.ShapeDtypeStruct((rows, total_width // 2), F32),
            jax.ShapeDtypeStruct((rows, sum(p[3] for p in out_places)), F32),
        ],
    )


def join_qkv(sums, w_qkv, gain, qkv_places):
    rows, total_width = w_qkv.shape

    def body(source, weights, gain_in, out, out_gain):
        gains = column(gain_in[...])
        total = jnp.zeros((rows, PAIR), F32)
        for owner, there, here, width in qkv_places:
            part = source[owner, :, there : there + width].astype(F32)
            total += part * weights[:, here : here + width].astype(F32)
            out[:, here : here + width] = part * gains
        out_gain[...] = row(jnp.sum(total, 1, keepdims=True))

    return kernel_call(
        body,
        "join_qkv",
        [sums, w_qkv, gain],
        out_shape=[
            jax.ShapeDtypeStruct((rows, total_width), F32),
            jax.ShapeDtypeStruct((1, rows), F32),
        ],
    )


def flip(index, offset):
    weight = 1
    while weight <= offset:
        if offset & weight:
            index = index + weight - 2 * weight * ((index // weight) % 2)
        weight *= 2
    return index


def greet(partners):
    barrier = pltpu.get_barrier_semaphore()
    for partner in partners:
        pl.semaphore_signal(barrier, inc=1, device_id=partner, device_id_type=MESH)
    pl.semaphore_wait(barrier, len(partners))


def here():
    return lax.axis_index("seq"), lax.axis_index("core")


def bits_of(seqs):
    return [1 << bit for bit in range(seqs.bit_length() - 1)]


def cube_partners(seqs):
    me, core = here()
    partners = [{"seq": flip(me, bit), "core": core} for bit in bits_of(seqs)]
    return partners + [{"seq": me, "core": 1 - core}]


def all_partners(seqs):
    me, core = here()
    return [
        {"seq": flip(me, step), "core": core if same else 1 - core}
        for step in range(seqs)
        for same in (True, False)
        if step or not same
    ]


def orders_of(seqs):
    bits = bits_of(seqs)
    return [bits, bits[1:] + bits[:1]]


def remote(source, target, sems, at, device):
    return pltpu.make_async_remote_copy(
        src_ref=source,
        dst_ref=target,
        send_sem=sems[0].at[at],
        recv_sem=sems[1].at[at],
        device_id=device,
        device_id_type=MESH,
    )


def push(*where):
    copy = remote(*where)
    copy.start()
    return copy


def loads(sources, rooms, sems):
    copies = []
    for i, (source, room) in enumerate(zip(sources, rooms)):
        if isinstance(source, tuple):
            source = source[0].at[:, pl.ds(source[1], source[2])]
        copies.append(pltpu.make_async_copy(source, room, sems.at[i]))
    return copies


def like(*arrays):
    return [pltpu.VMEM(array.shape, array.dtype) for array in arrays]


def pair_sems(*shape):
    return [pltpu.SemaphoreType.DMA(shape)] * 2


def spread_scratch(seqs):
    return pair_sems(2, seqs) + pair_sems(2, seqs) + [pltpu.SemaphoreType.DMA]


class Spread:
    def __init__(self, own, out, scratch, rows=None):
        self.own, self.out = own, out
        self.rows = rows or pl.ds(0, own.shape[0])
        self.across, self.aside, self.local = scratch[0:2], scratch[2:4], scratch[4]
        self.me, self.core = here()
        self.half = out.shape[-1] // 2
        self.orders = orders_of(out.shape[1])
        self.phases = len(self.orders[0])

    def columns(self, ref, stream):
        return ref.at[self.rows, pl.ds(stream * self.half, self.half)]

    def place(self, offset, stream):
        return self.columns(self.out.at[self.core, flip(self.me, offset)], stream)

    def block(self, offset, stream):
        return self.place(offset, stream) if offset else self.columns(self.own, stream)

    def kept(self):
        return pltpu.make_async_copy(
            self.own.at[self.rows], self.out.at[self.core, self.me, self.rows], self.local
        )

    def swap(self, offset, stream):
        sibling = {"seq": self.me, "core": 1 - self.core}
        return remote(
            self.block(offset, stream),
            self.place(offset, stream),
            self.aside,
            (stream, offset),
            sibling,
        )

    def held(self, phase, stream):
        offsets = [0]
        for bit in self.orders[stream][:phase]:
            offsets += [offset + bit for offset in offsets]
        return offsets

    def moves(self, phase):
        found = []
        for stream in range(2):
            bit = self.orders[stream][phase]
            partner = {"seq": flip(self.me, bit), "core": self.core}
            for offset in self.held(phase, stream):
                copy = remote(
                    self.block(offset, stream),
                    self.place(offset, stream),
                    self.across,
                    (stream, offset + bit),
                    partner,
                )
                found.append((copy, offset + bit, stream))
        return found

    def begin(self):
        self.kept().start()
        for copy, _, _ in self.moves(0):
            copy.start()
        for stream in range(2):
            self.swap(0, stream).start()

    def arrive(self, phase):
        for copy, offset, stream in self.moves(phase):
            copy.wait_recv()
            self.swap(offset, stream).start()

    def step(self, phase):
        self.arrive(phase - 1)
        for copy, _, _ in self.moves(phase):
            copy.start()

    def finish(self):
        self.arrive(self.phases - 1)
        for phase in range(self.phases):
            for copy, _, _ in self.moves(phase):
                copy.wait_send()
        for stream in range(2):
            for offset in self.held(self.phases, stream):
                self.swap(offset, stream).wait()
        self.kept().wait()


def fold_rooms(seqs, tokens, width, made=True):
    return [
        pltpu.VMEM((seqs, tokens, width), BF),
        pltpu.VMEM((seqs, tokens, width) if made else (16, PAIR), BF),
        pltpu.VMEM((seqs, tokens, width), BF),
        pltpu.VMEM((2, seqs, tokens, width // 2), BF),
    ]


def fold_sems(seqs):
    return [pltpu.SemaphoreType.DMA((2,))] + pair_sems(seqs) + pair_sems(2, seqs)


class Fold:
    def __init__(self, terms, rooms, sems, rows, make=None):
        self.terms, self.make = terms, make
        self.own, self.give, self.total, self.got = rooms
        self.local, self.aside, self.across = sems[0], sems[1:3], sems[3:5]
        self.rows = rows
        self.me, self.core = here()
        self.seqs = self.total.shape[0]
        self.half = self.total.shape[-1] // 2
        self.orders = orders_of(self.seqs)
        self.phases = len(self.orders[0])

    def taken(self, mine):
        core, room = (self.core, self.own) if mine else (1 - self.core, self.give)
        return pltpu.make_async_copy(
            self.terms.at[core, :, self.rows],
            room.at[:, self.rows],
            self.local.at[1 if mine else 0],
        )

    def fill(self, room, core, at):
        width = room.shape[-1]
        tile = min(2 * BLOCK, width)

        def one(j, carry):
            columns = pl.ds(pl.multiple_of(j * tile, tile), tile)
            value = self.make(core, at, self.rows, columns)
            if self.terms is not None:
                value = value + room[at, self.rows, columns].astype(F32)
            room[at, self.rows, columns] = value.astype(BF)
            return carry

        lax.fori_loop(0, width // tile, one, 0)

    def swap(self, offset):
        at = flip(self.me, offset)
        source = self.give.at[at] if self.make else self.terms.at[1 - self.core, at]
        return remote(
            source.at[self.rows],
            self.total.at[at, self.rows],
            self.aside,
            (offset,),
            {"seq": self.me, "core": 1 - self.core},
        )

    def columns(self, stream):
        return pl.ds(stream * self.half, self.half)

    def moves(self, phase, stream, only=None):
        bit = self.orders[stream][phase]
        done = sum(self.orders[stream][:phase])
        partner = {"seq": flip(self.me, bit), "core": self.core}
        return [
            (
                remote(
                    self.total.at[flip(self.me, offset), self.rows, self.columns(stream)],
                    self.got.at[stream, offset, self.rows],
                    self.across,
                    (stream, offset),
                    partner,
                ),
                offset,
            )
            for offset in range(self.seqs - 1, -1, -1)
            if offset & bit and not offset & done and only in (None, offset)
        ]

    def add(self, work):
        count = self.rows.size
        step = min(32, count)

        def one(i, carry):
            work(pl.ds(pl.multiple_of(self.rows.start + i * step, step), step))
            return carry

        lax.fori_loop(0, count // step, one, 0)

    def load(self):
        if self.terms is not None:
            if self.make:
                self.taken(False).start()
            self.taken(True).start()

    def begin(self):
        if self.make and self.terms is not None:
            self.taken(False).wait()
        for offset in range(self.seqs - 1, -1, -1):
            if self.make:
                self.fill(self.give, 1 - self.core, flip(self.me, offset))
            self.swap(offset).start()

    def first(self):
        if self.terms is not None:
            self.taken(True).wait()
        for offset in range(self.seqs - 1, -1, -1):
            at = flip(self.me, offset)
            if self.make:
                self.fill(self.own, self.core, at)
            self.swap(offset).wait_recv()

            def add_sibling(rows, at=at):
                both = self.total[at, rows, :].astype(F32) + self.own[at, rows, :].astype(F32)
                self.total[at, rows, :] = both.astype(BF)

            self.add(add_sibling)
            for stream in range(2):
                for copy, _ in self.moves(0, stream, offset):
                    copy.start()

    def receive(self, phase, stream):
        bit = self.orders[stream][phase]
        for copy, offset in self.moves(phase, stream):
            copy.wait_recv()
            at = flip(self.me, offset - bit)

            def add_got(rows, at=at, offset=offset):
                columns = self.columns(stream)
                both = self.total[at, rows, columns].astype(F32) + self.got[
                    stream, offset, rows, :
                ].astype(F32)
                self.total[at, rows, columns] = both.astype(BF)

            self.add(add_got)

    def step(self, phase):
        for stream in range(2):
            self.receive(phase - 1, stream)
            for copy, _ in self.moves(phase, stream):
                copy.start()

    def last(self):
        for stream in range(2):
            self.receive(self.phases - 1, stream)

    def result(self, rows):
        return self.total[self.me, rows, :].astype(F32)

    def settle(self):
        for offset in range(self.seqs):
            self.swap(offset).wait_send()
        for phase in range(self.phases):
            for stream in range(2):
                for copy, _ in self.moves(phase, stream):
                    copy.wait_send()


def halves(count):
    return [pl.ds(i * (count // 2), count // 2) for i in range(2)]


def fold_then_spread(folds, spreads, work, aside=lambda: None):
    phases = folds[0].phases
    for fold in folds:
        fold.begin()
        fold.first()
    aside()
    for phase in range(1, phases):
        for fold in folds:
            fold.step(phase)
            aside()
    for fold, spread in zip(folds, spreads):
        fold.last()
        fold.add(work)
        spread.begin()
        aside()
    for phase in range(1, phases):
        for spread in spreads:
            spread.step(phase)
            aside()
    for spread in spreads:
        spread.finish()
    for fold in folds:
        fold.settle()


def by_rows(count, work):
    step = min(32, count)

    def one(i, carry):
        work(pl.ds(pl.multiple_of(i * step, step), step))
        return carry

    lax.fori_loop(0, count // step, one, 0)


def deal_scratch(pieces, seqs):
    blocks = [piece.shape[-2:] for piece in pieces]
    return (
        pair_sems(len(pieces), 2 * seqs)
        + [pltpu.SemaphoreType.DMA((2, len(pieces)))]
        + [pltpu.VMEM(block, piece.dtype) for block, piece in zip(blocks, pieces)]
    )


class Deal:
    def __init__(self, pieces, outs, scratch, core_first=False):
        self.pieces, self.outs = pieces, outs
        self.sems, self.local, self.rooms = scratch[:2], scratch[2], scratch[3:]
        self.me, self.core = here()
        self.core_first = core_first
        self.seqs = outs[0].shape[1 if core_first else 0]

    def piece(self, i, seq, core):
        piece, out = self.pieces[i], self.outs[i]
        return piece.at[seq, core] if len(piece.shape) == len(out.shape) else piece

    def place(self, i):
        out = self.outs[i]
        return out.at[self.core, self.me] if self.core_first else out.at[self.me, self.core]

    def copy(self, i, step, same):
        to_seq = flip(self.me, step)
        to_core = self.core if same else 1 - self.core
        return remote(
            self.piece(i, to_seq, to_core),
            self.place(i),
            self.sems,
            (i, 2 * step + (0 if same else 1)),
            {"seq": to_seq, "core": to_core},
        )

    def copies(self):
        return [
            self.copy(i, step, same)
            for i in range(len(self.pieces))
            for step in range(self.seqs)
            for same in (True, False)
            if step or not same
        ]

    def entering(self):
        return [
            pltpu.make_async_copy(
                self.piece(i, self.me, self.core), self.rooms[i], self.local.at[0, i]
            )
            for i in range(len(self.rooms))
        ]

    def leaving(self):
        return [
            pltpu.make_async_copy(
                self.rooms[i] if self.rooms else self.piece(i, self.me, self.core),
                self.place(i),
                self.local.at[1, i],
            )
            for i in range(len(self.outs))
        ]

    def begin(self):
        for copy in self.copies() + self.entering():
            copy.start()
        for copy in self.entering():
            copy.wait()
        for copy in self.leaving():
            copy.start()

    def arrive_from(self, step):
        if step:
            self.copy(0, step, True).wait_recv()
        else:
            for copy in self.leaving():
                copy.wait()
        self.copy(0, step, False).wait_recv()

    def arrive(self):
        for copy in self.copies():
            copy.wait_recv()
        for copy in self.leaving():
            copy.wait()

    def settle(self):
        for copy in self.copies():
            copy.wait_send()

    def finish(self):
        self.arrive()
        self.settle()


class Ring:
    def __init__(self, whole, sems, part):
        self.whole, self.sems, self.part = whole, sems, part
        self.count = whole.shape[0]
        self.chip = lax.axis_index("z")

    def hop(self, i):
        block = self.whole.at[lax.rem(self.chip + self.count - i, self.count), self.part]
        following = lax.rem(self.chip + 1, self.count)
        return remote(block, block, self.sems, (i,), {"z": following})

    def preceding(self):
        return {"z": lax.rem(self.chip + self.count - 1, self.count)}

    def begin(self):
        self.hop(0).start()

    def step(self, i):
        self.hop(i - 1).wait_recv()
        if i < self.count - 1:
            self.hop(i).start()

    def settle(self):
        for i in range(self.count - 1):
            self.hop(i).wait_send()


def deal(pieces, number):
    count = len(pieces)
    seqs = pieces[0].shape[0]

    def body(*refs):
        greet(all_partners(seqs))
        work = Deal(refs[:count], refs[count : 2 * count], refs[2 * count :])
        work.begin()
        work.finish()

    return kernel_call(
        body,
        "deal",
        [*pieces],
        number,
        in_specs=[ANYWHERE] * count,
        out_specs=[ANYWHERE] * count,
        out_shape=[jax.ShapeDtypeStruct(piece.shape, BF) for piece in pieces],
        scratch_shapes=deal_scratch(pieces, seqs),
    )


def cut_into(out, parts):
    for source, gain, places in parts:
        for owner, there, begin, width in places:
            part = source[:, begin : begin + width]
            if gain is not None:
                part = (part.astype(F32) * gain).astype(BF)
            out[owner // 2, owner % 2, :, there : there + width] = part


def column(row):
    count = row.shape[1]
    shape = (count, count)
    wide = jnp.broadcast_to(row.astype(F32), shape)
    same = lax.broadcasted_iota(jnp.int32, shape, 0) == lax.broadcasted_iota(jnp.int32, shape, 1)
    return jnp.sum(jnp.where(same, wide, 0.0), 1, keepdims=True)


def row(values):
    count = values.shape[0]
    shape = (count, count)
    wide = jnp.broadcast_to(values, shape)
    same = lax.broadcasted_iota(jnp.int32, shape, 0) == lax.broadcasted_iota(jnp.int32, shape, 1)
    return jnp.sum(jnp.where(same, wide, 0.0), 0, keepdims=True)


def frequencies():
    half = HEAD_DIM // 2
    inverse = ROPE_BASE ** (-2.0 * np.arange(half) / HEAD_DIM)
    return np.tile(inverse.astype(np.float32), (8, PAIR // half))


def start(arrays, gains, positions, plans, blocks, seqs, chips, number):
    tokens, w_qkv = arrays[0], arrays[2]
    count, width = tokens.shape
    rows = w_qkv.shape[0]
    (qkv_places, out_places, attend_cols), chunks = plans
    shape = (seqs, 2, rows)
    cuts = [shape + (cols,) for _, _, cols in chunks]
    more = len(chunks) - 1

    def body(*refs):
        sources, places, inverse = refs[:6], refs[8], refs[9]
        acts, whole, piece, tables, *moved = refs[10:16]
        cut_out = refs[16 : 16 + more]
        scratch = refs[16 + more :]
        gain_one, gain_two = column(refs[6][...]), column(refs[7][...])
        rooms, (sem, attend_cut), scratch = scratch[:6], scratch[6:8], scratch[8:]
        ff_cut, scratch = scratch[: 1 + more], scratch[1 + more :]
        turned, own, scratch = scratch[:2], scratch[2], scratch[3:]
        out_sem, ring_sems, scratch = scratch[0], scratch[1 : 1 + 2 * seqs], scratch[1 + 2 * seqs :]
        deal_sems, spread_sems, table = scratch[:9], scratch[9:14], scratch[14]
        coming = loads(sources, rooms, sem)
        for i in (2, 3, 0, 4, 5, 1):
            coming[i].start()
        me_chip = lax.axis_index("z")
        rings = [
            Ring(whole, ring_sems[2 * i : 2 * i + 2], flip(lax.axis_index("seq"), i))
            for i in range(seqs)
        ]
        greet(all_partners(seqs) + [rings[0].preceding()])
        coming[2].wait()
        coming[3].wait()
        cut_into(
            attend_cut, [(rooms[2], gain_one, qkv_places), (rooms[3], None, out_places)]
        )
        attend_deal = Deal([attend_cut], [whole.at[me_chip]], deal_sems[:3])
        attend_deal.begin()
        attend_deal.arrive_from(0)
        rings[0].begin()
        coming[0].wait()
        for outer, inner, size in blocks:
            turned[0][:, inner : inner + size] = rooms[0][:, outer : outer + size]

        def norm(at):
            values = turned[0][at, :].astype(F32)
            own[at, :] = (values * norm_scale(values)).astype(BF)

        by_rows(count, norm)
        coming[4].wait()
        coming[5].wait()
        for out, (pair, single, _) in zip(ff_cut, chunks):
            cut_into(out, [(rooms[4], gain_two, pair), (rooms[5], None, single)])
        coming[1].wait()
        for outer, inner, size in blocks:
            turned[1][:, inner : inner + size] = rooms[1][:, outer : outer + size]
        going = loads(list(turned) + list(ff_cut[1:]), list(moved) + list(cut_out), out_sem)
        for copy in going:
            copy.start()
        for step in range(1, seqs):
            attend_deal.arrive_from(step)
            rings[step].begin()
        spreading = Spread(own, acts, spread_sems)
        spreading.begin()
        angles = column(places[...]) * inverse[:1, :]
        lane = lax.broadcasted_iota(jnp.int32, angles.shape, 1)
        table[...] = jnp.where(
            lane % HEAD_DIM < HEAD_DIM // 2, jnp.cos(angles), jnp.sin(angles)
        )
        table_deal = Deal([table], [tables], deal_sems[3:6], True)
        table_deal.begin()
        for phase in range(1, spreading.phases):
            spreading.step(phase)
        ff_deal = Deal([ff_cut[0]], [piece], deal_sems[6:9])
        ff_deal.begin()
        for ring in rings:
            ring.step(1)
        for i in range(2, chips):
            for ring in rings:
                ring.step(i)
            if i == 2:
                spreading.finish()
        for ring in rings:
            ring.settle()
        attend_deal.settle()
        table_deal.finish()
        ff_deal.finish()
        for copy in going:
            copy.wait()

    like_tokens = jax.ShapeDtypeStruct((count, width), BF)
    deal_sem = pair_sems(1, 2 * seqs) + [pltpu.SemaphoreType.DMA((2, 1))]
    return kernel_call(
        body,
        "start",
        [*arrays, *gains, positions, frequencies()],
        number,
        in_specs=[ANYWHERE] * 6 + [LOCAL] * 4,
        out_specs=[ANYWHERE] * (6 + more),
        out_shape=[
            jax.ShapeDtypeStruct((2, seqs, count, width), BF),
            jax.ShapeDtypeStruct((chips,) + shape + (attend_cols,), BF),
            jax.ShapeDtypeStruct(cuts[0], BF),
            jax.ShapeDtypeStruct((2, seqs, count, PAIR), F32),
            like_tokens,
            like_tokens,
        ]
        + [jax.ShapeDtypeStruct(cut, BF) for cut in cuts[1:]],
        scratch_shapes=like(*arrays)
        + [pltpu.SemaphoreType.DMA((6,)), pltpu.VMEM(shape + (attend_cols,), BF)]
        + [pltpu.VMEM(cut, BF) for cut in cuts]
        + [pltpu.VMEM((count, width), BF)] * 3
        + [pltpu.SemaphoreType.DMA((2 + more,))]
        + pair_sems(chips) * seqs
        + deal_sem * 3
        + spread_scratch(seqs)
        + [pltpu.VMEM((count, PAIR), F32)],
    )


def two_way_scratch(seqs, count, width):
    return (
        [pltpu.VMEM((count, width), BF)]
        + fold_rooms(seqs, count, width)
        + fold_sems(seqs) * 2
        + spread_scratch(seqs) * 2
    )


def two_way(given, out, scratch, make):
    own, rooms, sems = scratch[0], scratch[1:5], scratch[5:]
    parts = halves(own.shape[0])
    folds = [
        Fold(given, rooms, sems[5 * i : 5 * i + 5], rows, make) for i, rows in enumerate(parts)
    ]
    sems = sems[10:]
    spreads = [Spread(own, out, sems[5 * i : 5 * i + 5], rows) for i, rows in enumerate(parts)]
    for fold in folds:
        fold.load()
    return folds, spreads, own


def product(left, right, seqs, count):
    def make(core, at, rows, columns):
        begin = pl.multiple_of((core * seqs + at) * count + rows.start, rows.size)
        return nt(left[pl.ds(begin, rows.size), :], right[columns, :])

    return make


def middle_acts(attended, weights, tokens, seqs, number):
    count, width = tokens.shape
    cols = attended.shape[1]
    begin = weights.shape[1] - cols

    def body(left_in, given, source_in, middle, out, left, right, source, sems, *scratch):
        coming = loads([left_in, (given, begin, cols), source_in], [left, right, source], sems)
        for copy in coming:
            copy.start()
        folds, spreads, own = two_way(None, out, scratch, product(left, right, seqs, count))
        greet(cube_partners(seqs))
        for copy in coming:
            copy.wait()

        def norm(rows):
            values = source[rows, :].astype(F32) + folds[0].result(rows)
            middle[rows, :] = values
            own[rows, :] = (values * norm_scale(values)).astype(BF)

        fold_then_spread(folds, spreads, norm)

    return kernel_call(
        body,
        "middle_acts",
        [attended, weights, tokens],
        number,
        in_specs=[ANYWHERE] * 3,
        out_specs=[LOCAL, ANYWHERE],
        out_shape=[
            jax.ShapeDtypeStruct((count, width), F32),
            jax.ShapeDtypeStruct((2, seqs, count, width), BF),
        ],
        scratch_shapes=like(attended)
        + [pltpu.VMEM((width, cols), BF)]
        + like(tokens)
        + [pltpu.SemaphoreType.DMA((3,))]
        + two_way_scratch(seqs, count, width),
    )


def middle_grad(terms, grad_both, cotangent, middle, hidden, weights, number):
    _, seqs, count, width = terms.shape
    tokens = hidden[0].shape[0]
    n = len(hidden)
    block = min(BLOCK, tokens)
    tile = min(2 * BLOCK, width)
    blocks = tokens // block
    parts = [h.shape[1] for h in hidden]

    def body(given, *refs):
        sources, down = refs[: 3 + n], refs[3 + n : 3 + 2 * n]
        grad, out, products = refs[3 + 2 * n : 6 + 2 * n]
        scratch = refs[6 + 2 * n :]
        left, upstream, values = scratch[:3]
        units, room, right = scratch[3 : 3 + n], scratch[3 + n : 3 + 2 * n], scratch[3 + 2 * n]
        stage, sems, leaving = scratch[4 + 2 * n : 7 + 2 * n]
        columns = [(down[i], 2 * parts[i], parts[i]) for i in range(n)]
        coming = loads(
            [sources[0], (down[-1], 0, 2 * parts[-1]), *sources[3:], *columns, *sources[1:3]],
            [left, right, *units, *room, upstream, values],
            sems,
        )
        for copy in coming[:2]:
            copy.start()
        make = product(left, right, seqs, count)
        folds, spreads, own = two_way(given, out, scratch[7 + 2 * n :], make)
        for copy in coming[2:]:
            copy.start()
        greet(cube_partners(seqs))
        for copy in coming[:2]:
            copy.wait()

        def leave(i):
            rows = pl.ds(i * block, block)
            return pltpu.make_async_copy(stage.at[i % 2], products.at[rows], leaving.at[i % 2])

        def multiply(i):
            if i == 0:
                for copy in coming[2:]:
                    copy.wait()
            if i >= 2:
                leave(i - 2).wait()

            def one(j, carry):
                columns = pl.ds(pl.multiple_of(j * tile, tile), tile)
                total = sum(
                    nt(units[k][pl.ds(i * block, block), :], room[k][columns, :])
                    for k in range(n)
                )
                stage[i % 2, :, columns] = total.astype(BF)
                return carry

            lax.fori_loop(0, width // tile, one, 0)
            leave(i).start()

        left_over = list(range(blocks))

        def aside():
            for _ in range(2 if len(left_over) == blocks else max(1, blocks // 8)):
                if left_over:
                    multiply(left_over.pop(0))

        def back(rows):
            held = values[rows, :]
            scale = norm_scale(held)
            result = upstream[rows, :].astype(F32) + norm_back(
                folds[0].result(rows), held * scale, scale
            )
            grad[rows, :] = result
            own[rows, :] = result.astype(BF)

        fold_then_spread(folds, spreads, back, aside)
        while left_over:
            multiply(left_over.pop(0))
        for i in range(max(0, blocks - 2), blocks):
            leave(i).wait()

    return kernel_call(
        body,
        "middle_grad",
        [terms, grad_both, cotangent, middle, *hidden, *weights],
        number,
        in_specs=[ANYWHERE] * (4 + 2 * n),
        out_specs=[LOCAL, ANYWHERE, ANYWHERE],
        out_shape=[
            jax.ShapeDtypeStruct((count, width), F32),
            jax.ShapeDtypeStruct(terms.shape, BF),
            jax.ShapeDtypeStruct((tokens, width), BF),
        ],
        scratch_shapes=like(grad_both, cotangent, middle, *hidden)
        + [pltpu.VMEM((width, part), BF) for part in parts]
        + [pltpu.VMEM((width, 2 * parts[-1]), BF), pltpu.VMEM((2, block, width), BF)]
        + [pltpu.SemaphoreType.DMA((4 + 2 * n,)), pltpu.SemaphoreType.DMA((2,))]
        + two_way_scratch(seqs, count, width),
    )


def input_grad(grad_mixed, weights, tokens, grad_middle, seqs, number):
    count, width = tokens.shape
    cols = grad_mixed.shape[1]

    def body(left_in, given, source_in, held_in, out, left, right, source, held, sems, *scratch):
        coming = loads(
            [left_in, (given, 0, cols), source_in, held_in], [left, right, source, held], sems
        )
        for copy in coming:
            copy.start()
        make = product(left, right, seqs, count)
        sems = scratch[4:]
        folds = [
            Fold(None, scratch[:4], sems[5 * i : 5 * i + 5], rows, make)
            for i, rows in enumerate(halves(count))
        ]
        greet(cube_partners(seqs))
        for copy in coming:
            copy.wait()
        for fold in folds:
            fold.begin()
            fold.first()
        for phase in range(1, folds[0].phases):
            for fold in folds:
                fold.step(phase)

        def back(rows):
            values = source[rows, :].astype(F32)
            scale = norm_scale(values)
            out[rows, :] = held[rows, :] + norm_back(folds[0].result(rows), values * scale, scale)

        for fold in folds:
            fold.last()
            fold.add(back)
        for fold in folds:
            fold.settle()

    return kernel_call(
        body,
        "input_grad",
        [grad_mixed, weights, tokens, grad_middle],
        number,
        in_specs=[ANYWHERE] * 4,
        out_specs=LOCAL,
        out_shape=jax.ShapeDtypeStruct((count, width), F32),
        scratch_shapes=like(grad_mixed)
        + [pltpu.VMEM((width, cols), BF)]
        + like(tokens, grad_middle)
        + [pltpu.SemaphoreType.DMA((4,))]
        + fold_rooms(seqs, count, width)
        + fold_sems(seqs) * 2,
    )


class Order:
    def __init__(self):
        self.latest = None

    def enter(self, values):
        if self.latest is None:
            return values
        return lax.optimization_barrier((values, self.latest))[0]

    def run(self, work, *values):
        result = work(*self.enter(values))
        self.latest = jax.tree.leaves(result)
        return result

    def take(self, values):
        if self.latest is not None:
            values = lax.optimization_barrier((values, self.latest))[0]
        self.latest = jax.tree.leaves(values)
        return values


def norm_scale(values):
    return lax.rsqrt(jnp.mean(values * values, -1, keepdims=True) + EPS)


def norm_back(grad, normed, scale):
    return scale * (grad - normed * jnp.mean(grad * normed, -1, keepdims=True))


def per_device(
    mesh, tokens, positions, w_qkv, w_out, gain_attn, w_gate_up, w_down, gain_mlp, cotangent
):
    order = Order()
    seqs, chips = mesh.shape["seq"], mesh.shape["z"]
    owners = 2 * seqs
    token_count, width = tokens.shape[1:]
    ff_width = w_down.shape[1]
    rows = w_qkv.shape[0]
    head_cols = width // owners
    ff_cols = ff_width // owners
    parts = chunk_widths(ff_cols)
    last = len(parts) - 1
    blocks = blocks_in(rows, seqs, chips)

    def by_place(piece):
        return piece.reshape(seqs, 2, rows, -1)

    def gathered(piece):
        piece = order.enter(piece).reshape(seqs, 2 * rows, -1)
        return lax.all_gather(piece, "z", axis=0, tiled=False)

    def flat(value):
        return order.take(value).reshape(width, -1)

    def summed(term):
        split = order.enter(term).reshape(chips, seqs, 2 * rows, -1)
        return lax.psum_scatter(split, "z", scatter_dimension=0, tiled=False)

    def rounded(left, right):
        return tn(left, right).astype(BF)

    qkv_places = list(qkv_columns(owners, head_cols))
    out_places = [(o, 3 * head_cols, o * head_cols, head_cols) for o in range(owners)]
    gate_up_places, down_places = ff_columns(owners, ff_cols)
    chunks = [
        (pair, single, 3 * part) for pair, single, part in zip(gate_up_places, down_places, parts)
    ]
    acts, attend_whole, ff_piece, table, tokens_in, upstream_own, *ff_cut = order.run(
        lambda *a: start(
            a[:6],
            a[6:8],
            a[8],
            ((qkv_places, out_places, 4 * head_cols), chunks),
            blocks,
            seqs,
            chips,
            1,
        ),
        tokens[0],
        cotangent[0],
        w_qkv,
        w_out,
        w_gate_up,
        w_down,
        gain_attn[None],
        gain_mlp[None],
        positions,
    )
    acts = acts.reshape(-1, width)
    attend_whole = attend_whole.reshape(width, -1)
    table = table.reshape(-1, PAIR)
    ff_coming = [gathered(ff_piece)]

    qkv_cols = 3 * head_cols
    mixed = order.run(lambda a, w: nn(a, w[:, :qkv_cols]), acts, attend_whole)
    qkv, attended, logs, upstream, *ff_pieces = order.run(
        lambda m, t, u, *given: attend(m, t, SpreadBeside(seqs, u, given), 2, 3),
        mixed,
        table,
        upstream_own,
        *ff_cut,
    )
    ff_coming += [gathered(piece) for piece in ff_pieces]
    upstream = upstream.reshape(-1, width)
    middle, acts_mid = order.run(
        lambda a, w, x: middle_acts(a, w, x, seqs, 4), attended, attend_whole, tokens_in
    )
    acts_mid = acts_mid.reshape(-1, width)

    def feed_hidden(both):
        part = both.shape[1] // 2
        gate, up = both[:, :part], both[:, part:]
        return (gate * jax.nn.sigmoid(gate) * up).astype(BF)

    def feed_back(grad_hidden, both):
        part = both.shape[1] // 2
        gate, up = both[:, :part], both[:, part:]
        sigma = jax.nn.sigmoid(gate)
        grad_gate = grad_hidden * up * sigma * (1.0 + gate * (1.0 - sigma))
        grad_up = grad_hidden * gate * sigma
        return jnp.concatenate([grad_gate.astype(BF), grad_up.astype(BF)], 1)

    def both_terms(left, right, left_two, right_two):
        return [rounded(left, right), rounded(left_two, right_two)]

    def add_nt(left, right, total=None):
        result = nt(left, right)
        return (result if total is None else result + total.astype(F32)).astype(BF)

    ff_sums, hiddens, wholes = [], [], []
    norm_mid_terms = ()
    for chunk, part in enumerate(parts):
        cols = 2 * part
        whole = flat(ff_coming[chunk])
        both = order.run(lambda a, w: nn(a, w[:, :cols]), acts_mid, whole)
        hidden = order.run(feed_hidden, both)
        hiddens.append(hidden)
        wholes.append(whole)
        grad_hidden = order.run(lambda a, w: nn(a, w[:, cols:]), upstream, whole)
        grad_both = order.run(feed_back, grad_hidden, both)
        terms = order.run(both_terms, acts_mid, grad_both, upstream, hidden)
        if chunk < len(parts) - 1:
            ff_sums.append(summed(order.run(side_by_side, terms)))
        if chunk < len(parts) - 1:
            norm_mid_terms = (
                order.run(
                    lambda a, w, *t: add_nt(a, w[:, :cols], *t), grad_both, whole, *norm_mid_terms
                ),
            )

    grad_middle, grad_branch, outcome_terms = order.run(
        lambda a, b, c, d, e, f: middle_grad(a, b, c, d, e, f, 5),
        norm_mid_terms[0].reshape(2, seqs, token_count, width),
        grad_both,
        upstream_own,
        middle,
        hiddens,
        wholes,
    )
    grad_branch = grad_branch.reshape(-1, width)

    terms.append(order.run(rounded, grad_branch, attended))
    ff_sums.append(summed(order.run(side_by_side, terms)))
    grad_attended = order.run(
        lambda a, w: nn(a, w[:, qkv_cols:]).astype(BF), grad_branch, attend_whole
    )
    first_rows = [by_place(order.take(value)) for value in ff_sums[:-1]]
    grad_mixed, outcome, *ff_dealt = order.run(
        lambda a, b, c, d, e, f, *given: attend_back(
            a, b, c, d, OutputBeside(seqs, e, f, given), 2, 6
        ),
        qkv,
        grad_attended,
        logs,
        table,
        outcome_terms.reshape(2, seqs, token_count, width),
        middle,
        *first_rows,
    )
    qkv_sum = summed(order.run(rounded, acts, grad_mixed))

    grad_inputs = order.run(
        lambda a, w, b, c: input_grad(a, w, b, c, seqs, 7),
        grad_mixed,
        attend_whole,
        tokens_in,
        grad_middle,
    )
    last_rows = by_place(order.take(ff_sums[-1]))
    ff_dealt += order.run(lambda a: deal([a], 8), last_rows)
    out_at = [(o, 3 * parts[-1], o * head_cols, head_cols) for o in range(owners)]
    grad_gate_up, gain_two_sum, grad_down, grad_out = order.run(
        lambda w, g, *a: join_ff(a, w, g, gate_up_places, down_places, out_at),
        w_gate_up,
        gain_mlp[None],
        *[value.reshape(owners, rows, -1) for value in ff_dealt],
    )
    grad_inputs, outcome = order.run(lambda *a: outside(a, blocks), grad_inputs, outcome)
    qkv_rows = order.take(qkv_sum)
    (qkv_dealt,) = order.run(lambda a: deal([a], 9), by_place(qkv_rows))
    grad_qkv, gain_one_sum = order.run(
        lambda w, g, a: join_qkv(a, w, g, qkv_places),
        w_qkv,
        gain_attn[None],
        qkv_dealt.reshape(owners, rows, -1),
    )
    return (
        outcome[None],
        grad_inputs[None],
        grad_qkv,
        grad_out,
        gain_one_sum[0],
        grad_gate_up,
        grad_down,
        gain_two_sum[0],
    )


def solution(mesh):
    seqs, devices = mesh.shape["seq"], mesh.shape["fsdp"]
    parted = Mesh(mesh.devices.reshape(seqs, devices // 2, 2), ("seq", "z", "core"))
    tokens = P(("z", "core"), "seq", None)
    matrix = P(("seq", "z", "core"), None)
    vector = P(("seq", "z", "core"))
    return jax.shard_map(
        functools.partial(per_device, parted),
        mesh=parted,
        in_specs=(
            tokens,
            P(("z", "core"), "seq"),
            matrix,
            matrix,
            vector,
            matrix,
            matrix,
            vector,
            tokens,
        ),
        out_specs=(tokens, tokens, matrix, matrix, vector, matrix, matrix, vector),
        check_vma=False,
    )
```

```python
import functools
import math

import jax
import jax.numpy as jnp
import numpy as np
from jax import lax
from jax.experimental import pallas as pl
from jax.experimental.pallas import tpu as pltpu
from jax.sharding import Mesh, PartitionSpec as P

HEAD_DIM = 64
PAIR = 2 * HEAD_DIM
BLOCK = 256
EPS = 1e-05
ROPE_BASE = 130000.0
BF = jnp.bfloat16
F32 = jnp.float32
VMEM_MOST = 58 << 20
MESH = pl.DeviceIdType.MESH
ANYWHERE = pl.BlockSpec(memory_space=pltpu.HBM)
LOCAL = pl.BlockSpec(memory_space=pltpu.VMEM)


def room_for(spec, arrays):
    total = 8 << 20
    for room in spec.get("scratch_shapes", ()):
        if hasattr(room, "shape") and room.dtype in (BF, F32):
            total += math.prod(room.shape) * jnp.dtype(room.dtype).itemsize
    outs = spec["out_shape"] if isinstance(spec["out_shape"], list) else [spec["out_shape"]]
    specs = spec.get("out_specs", LOCAL), spec.get("in_specs", LOCAL)
    for values, given in zip((outs, arrays), specs):
        given = given if isinstance(given, list) else [given] * len(values)
        for value, where in zip(values, given):
            if where.block_shape is not None:
                total += 2 * math.prod(where.block_shape) * value.dtype.itemsize
            elif where is not ANYWHERE:
                total += math.prod(value.shape) * value.dtype.itemsize
    return min(total, VMEM_MOST)


def kernel_call(body, name, arrays, number=None, **spec):
    params = {"vmem_limit_bytes": room_for(spec, arrays)}
    if number is not None:
        params.update(vmem_limit_bytes=VMEM_MOST, collective_id=number, has_side_effects=True)
    return pl.pallas_call(
        body, name=name, compiler_params=pltpu.CompilerParams(**params), **spec
    )(*arrays)


def turn(x, cosine, sine):
    half = HEAD_DIM // 2
    lane = lax.broadcasted_iota(jnp.int32, x.shape, 1)
    swapped = jnp.where(
        lane % HEAD_DIM < half, pltpu.roll(x, PAIR - half, 1), pltpu.roll(x, half, 1)
    )
    return x * cosine + swapped * sine


def nt(left, right):
    return lax.dot_general(left, right, (((1,), (1,)), ((), ())), preferred_element_type=F32)


def tn(left, right):
    return lax.dot_general(left, right, (((0,), (0,)), ((), ())), preferred_element_type=F32)


def nn(left, right):
    return lax.dot_general(left, right, (((1,), (0,)), ((), ())), preferred_element_type=F32)


def masked_scores(queries, keys, block):
    scores = nt(queries, keys)
    rows = lax.broadcasted_iota(jnp.int32, (BLOCK, BLOCK), 0)
    cols = lax.broadcasted_iota(jnp.int32, (BLOCK, BLOCK), 1)
    last = jnp.where(cols <= rows, scores[:, block * BLOCK :], -1e30)
    return jnp.concatenate([scores[:, : block * BLOCK], last], 1) if block else last


def unpack(table):
    half = HEAD_DIM // 2
    cosine, sine = table[:, :half], table[:, half:HEAD_DIM]
    return (
        jnp.concatenate([cosine] * 4, 1),
        jnp.concatenate([-sine, sine] * 2, 1),
    )


def attend_body(mixed, table, qkv, out, logs):
    length = mixed.shape[0]
    cosine, sine = unpack(table[...])
    qkv[:, :PAIR] = turn(mixed[:, :PAIR], cosine, sine).astype(BF)
    qkv[:, PAIR : 2 * PAIR] = turn(mixed[:, PAIR : 2 * PAIR], cosine, sine).astype(BF)
    qkv[:, 2 * PAIR :] = mixed[:, 2 * PAIR :].astype(BF)
    scale = jnp.asarray(1.0 / math.sqrt(HEAD_DIM), BF)
    for block in range(length // BLOCK):
        at = pl.ds(block * BLOCK, BLOCK)
        seen = (block + 1) * BLOCK
        outs = []
        totals = []
        for low in (0, HEAD_DIM):
            high = low + HEAD_DIM
            queries = qkv[at, low:high] * scale
            scores = masked_scores(queries, qkv[:seen, PAIR + low : PAIR + high], block)
            highest = jnp.max(scores, -1, keepdims=True)
            weights = jnp.exp(scores - highest)
            summed = jnp.sum(weights, -1, keepdims=True)
            probs = (weights * (1.0 / summed)).astype(BF)
            outs.append(nn(probs, qkv[:seen, 2 * PAIR + low : 2 * PAIR + high]))
            totals.append(jnp.broadcast_to(highest + jnp.log(summed), (BLOCK, HEAD_DIM)))
        out[at, :] = jnp.concatenate(outs, 1).astype(BF)
        logs[at, :] = jnp.concatenate(totals, 1)


def attend_back_body(qkv, grad, logs, table, grad_qkv, grad_keys, grad_values):
    length = qkv.shape[0]
    scale = 1.0 / math.sqrt(HEAD_DIM)
    cosine, sine = unpack(table[...])
    last = length // BLOCK - 1
    for block in range(last, -1, -1):
        at = pl.ds(block * BLOCK, BLOCK)
        seen = (block + 1) * BLOCK
        rows = slice(block * BLOCK, seen)
        grad_queries = []
        for low in (0, HEAD_DIM):
            high = low + HEAD_DIM
            queries = qkv[at, low:high] * jnp.asarray(scale, BF)
            keys = qkv[:seen, PAIR + low : PAIR + high]
            upstream = grad[at, low:high]
            scores = masked_scores(queries, keys, block)
            probs = jnp.exp(scores - logs[at, low : low + 1])
            grad_probs = nt(upstream, qkv[:seen, 2 * PAIR + low : 2 * PAIR + high])
            inner = jnp.sum(probs * grad_probs, -1, keepdims=True)
            grad_scores = (probs * (grad_probs - inner)).astype(BF)
            grad_queries.append(nn(grad_scores, keys))
            for_keys = tn(grad_scores, queries)
            for_values = tn(probs.astype(BF), upstream)
            if block == last:
                grad_keys[:, low:high] = for_keys
                grad_values[:, low:high] = for_values
            else:
                grad_keys[:seen, low:high] += for_keys
                grad_values[:seen, low:high] += for_values
        rounded = (jnp.concatenate(grad_queries, 1) * scale).astype(BF).astype(F32)
        grad_qkv[at, :PAIR] = turn(rounded, cosine[rows], -sine[rows]).astype(BF)
    rounded = grad_keys[...].astype(BF).astype(F32)
    grad_qkv[:, PAIR : 2 * PAIR] = turn(rounded, cosine, -sine).astype(BF)
    grad_qkv[:, 2 * PAIR :] = grad_values[...].astype(BF)


def heads_call(body, name, arrays, kinds, outs, out_kinds, count, beside, number, scratch):
    tokens = arrays[0].shape[0]
    length = tokens // count
    pairs = arrays[0].shape[1] // (3 * PAIR)
    specs = {
        "wide": pl.BlockSpec((length, 3 * PAIR), lambda s, i: (s, i)),
        "one": pl.BlockSpec((length, PAIR), lambda s, i: (s, i)),
        "table": pl.BlockSpec((length, PAIR), lambda s, i: (s, 0)),
    }
    n_in, n_out = len(arrays), len(outs)
    more_in, more_out = len(beside.arrays), len(beside.outs)

    def whole(*refs):
        ins, given = refs[:n_in], refs[n_in : n_in + more_in]
        rest = refs[n_in + more_in :]
        results, made = rest[:n_out], rest[n_out : n_out + more_out]
        rest = rest[n_out + more_out :]
        room, held = rest[: len(beside.scratch)], rest[len(beside.scratch) :]
        step = pl.program_id(0) * pairs + pl.program_id(1)
        last = count * pairs - 1
        acts = beside.acts(given, made, room)
        when = [(2 * i * (last + 1) + len(acts) - 1) // (2 * len(acts) - 2) for i in range(len(acts))]
        for i, act in enumerate(acts):
            if when[i] <= last:
                pl.when(step == when[i])(act)
        body(*ins, *results, *held)

        @pl.when(step == last)
        def _():
            for i, act in enumerate(acts):
                if when[i] > last:
                    act()

    return kernel_call(
        whole,
        name,
        list(arrays) + list(beside.arrays),
        number,
        grid=(count, pairs),
        in_specs=[specs[kind] for kind in kinds] + [ANYWHERE] * more_in,
        out_specs=[specs[kind] for kind in out_kinds] + [ANYWHERE] * more_out,
        out_shape=list(outs) + list(beside.outs),
        scratch_shapes=list(beside.scratch) + scratch(length),
    )


class SpreadBeside:
    def __init__(self, seqs, own, pieces):
        self.seqs = seqs
        self.arrays = [own] + list(pieces)
        self.outs = [jax.ShapeDtypeStruct((2, seqs) + own.shape, BF)]
        self.outs += [jax.ShapeDtypeStruct(piece.shape, BF) for piece in pieces]
        self.scratch = [pltpu.VMEM(own.shape, BF), pltpu.SemaphoreType.DMA]
        self.scratch += spread_scratch(seqs)
        self.first = len(self.scratch)
        self.scratch += deal_scratch(pieces, seqs) if pieces else []

    def acts(self, given, made, room):
        def dealing():
            return Deal(given[1:], made[1:], room[self.first :])

        def spreading():
            return Spread(room[0], made[0], room[2:])

        def begin():
            copy = pltpu.make_async_copy(given[0], room[0], room[1])
            copy.start()
            greet(all_partners(self.seqs))
            copy.wait()
            spreading().begin()
            if given[1:]:
                dealing().begin()

        def finish():
            spreading().finish()
            if given[1:]:
                dealing().finish()

        def step(phase):
            return lambda: spreading().step(phase)

        return [begin] + [step(i) for i in range(1, len(bits_of(self.seqs)))] + [finish]


class OutputBeside:
    def __init__(self, seqs, terms, middle, pieces):
        self.seqs = seqs
        self.arrays = [terms, middle] + list(pieces)
        self.outs = [jax.ShapeDtypeStruct(middle.shape, BF)]
        self.outs += [jax.ShapeDtypeStruct(piece.shape, BF) for piece in pieces]
        self.scratch = [
            pltpu.VMEM(middle.shape, F32),
            pltpu.VMEM(middle.shape, BF),
            pltpu.SemaphoreType.DMA((2,)),
        ]
        self.scratch += fold_rooms(seqs, *middle.shape, False) + fold_sems(seqs)
        self.first = len(self.scratch)
        self.scratch += deal_scratch(pieces, seqs)

    def acts(self, given, made, room):
        held, rounded, sems = room[:3]

        def dealing():
            return Deal(given[2:], made[1:], room[self.first :])

        def folding():
            return Fold(given[0], room[3:7], room[7:12], pl.ds(0, held.shape[0]))

        def entering():
            return pltpu.make_async_copy(given[1], held, sems.at[0])

        def begin():
            entering().start()
            folding().load()
            greet(all_partners(self.seqs))
            folding().begin()
            dealing().begin()

        def finish():
            fold = folding()
            fold.last()
            entering().wait()

            def add(rows):
                rounded[rows, :] = (held[rows, :] + fold.result(rows)).astype(BF)

            fold.add(add)
            leaving = pltpu.make_async_copy(rounded, made[0], sems.at[1])
            leaving.start()
            fold.settle()
            dealing().finish()
            leaving.wait()

        def step(phase):
            return lambda: folding().step(phase)

        phases = len(bits_of(self.seqs))
        return [begin, lambda: folding().first()] + [step(i) for i in range(1, phases)] + [finish]


def attend(mixed, table, beside, count, number):
    tokens, cols = mixed.shape
    outs = [
        jax.ShapeDtypeStruct((tokens, cols), BF),
        jax.ShapeDtypeStruct((tokens, cols // 3), BF),
        jax.ShapeDtypeStruct((tokens, cols // 3), F32),
    ]
    return heads_call(
        attend_body,
        "attend",
        [mixed, table],
        ["wide", "table"],
        outs,
        ["wide", "one", "one"],
        count,
        beside,
        number,
        lambda length: [],
    )


def attend_back(qkv, grad, logs, table, beside, count, number):
    return heads_call(
        attend_back_body,
        "attend_back",
        [qkv, grad, logs, table],
        ["wide", "one", "one", "table"],
        [jax.ShapeDtypeStruct(qkv.shape, BF)],
        ["wide"],
        count,
        beside,
        number,
        lambda length: [pltpu.VMEM((length, PAIR), F32)] * 2,
    )


def qkv_columns(owners, cols):
    for owner in range(owners):
        for pair in range(cols // PAIR):
            for kind in range(3):
                there = (pair * 3 + kind) * PAIR
                yield owner, there, (kind * owners + owner) * cols + pair * PAIR, PAIR


def chunk_widths(cols):
    units = cols // PAIR
    first = max(1, (5 * units) // 8)
    return [n * PAIR for n in (first, units - first) if n]


def ff_columns(owners, cols):
    begin = 0
    gate_up, down = [], []
    for part in chunk_widths(cols):
        gate_up.append(
            [
                (owner, kind * part, (kind * owners + owner) * cols + begin, part)
                for owner in range(owners)
                for kind in range(2)
            ]
        )
        down.append([(owner, 2 * part, owner * cols + begin, part) for owner in range(owners)])
        begin += part
    return gate_up, down


def side_by_side(parts):
    begins = [sum(part.shape[1] for part in parts[:i]) for i in range(len(parts))]

    def body(*refs):
        out, sems = refs[-2:]
        copies = [
            pltpu.make_async_copy(
                refs[i], out.at[:, pl.ds(begins[i], part.shape[1])], sems.at[i]
            )
            for i, part in enumerate(parts)
        ]
        for copy in copies:
            copy.start()
        for copy in copies:
            copy.wait()

    total = sum(part.shape[1] for part in parts)
    return kernel_call(
        body,
        "side_by_side",
        [*parts],
        in_specs=[LOCAL] * len(parts),
        out_specs=ANYWHERE,
        out_shape=jax.ShapeDtypeStruct((parts[0].shape[0], total), BF),
        scratch_shapes=[pltpu.SemaphoreType.DMA((len(parts),))],
    )


def blocks_in(rows, seqs, chips):
    return [
        ((s * chips + z) * 2 * rows, (z * seqs + s) * 2 * rows, 2 * rows)
        for z in range(chips)
        for s in range(seqs)
    ]


def inside(arrays, blocks):
    n = len(arrays)

    def body(*refs):
        rooms, sems = refs[2 * n : 3 * n], refs[3 * n]
        coming = loads(refs[:n], rooms, sems)
        for copy in coming:
            copy.start()
        for copy, source, out in zip(coming, rooms, refs[n : 2 * n]):
            copy.wait()
            for outer, inner, width in blocks:
                out[:, inner : inner + width] = source[:, outer : outer + width]

    return kernel_call(
        body,
        "inside",
        arrays,
        in_specs=[ANYWHERE] * n,
        out_shape=[jax.ShapeDtypeStruct(a.shape, a.dtype) for a in arrays],
        scratch_shapes=like(*arrays) + [pltpu.SemaphoreType.DMA((n,))],
    )


def outside(arrays, blocks):
    return inside(arrays, [(inner, outer, width) for outer, inner, width in blocks])


def join_ff(sums, w_gate_up, gain, gate_up_places, down_places, out_places):
    rows, total_width = w_gate_up.shape
    count = len(sums)

    def body(*refs):
        weights, gain_in, out, out_gain, out_down, out_out = refs[count:]
        gains = column(gain_in[...])
        total = jnp.zeros((rows, PAIR), F32)
        for source, listed in zip(refs[:count], gate_up_places):
            for owner, there, here, width in listed:
                for step in range(0, width, PAIR):
                    part = source[owner, :, there + step : there + step + PAIR].astype(F32)
                    at = slice(here + step, here + step + PAIR)
                    total += part * weights[:, at].astype(F32)
                    out[:, at] = part * gains
        for source, listed in zip(refs[:count], down_places):
            for owner, there, here, width in listed:
                part = source[owner, :, there : there + width].astype(F32)
                out_down[:, here : here + width] = part
        for owner, there, here, width in out_places:
            part = refs[count - 1][owner, :, there : there + width].astype(F32)
            out_out[:, here : here + width] = part
        out_gain[...] = row(jnp.sum(total, 1, keepdims=True))

    return kernel_call(
        body,
        "join_ff",
        [*sums, w_gate_up, gain],
        out_shape=[
            jax.ShapeDtypeStruct((rows, total_width), F32),
            jax.ShapeDtypeStruct((1, rows), F32),
            jax.ShapeDtypeStruct((rows, total_width // 2), F32),
            jax.ShapeDtypeStruct((rows, sum(p[3] for p in out_places)), F32),
        ],
    )


def join_qkv(sums, w_qkv, gain, qkv_places):
    rows, total_width = w_qkv.shape

    def body(source, weights, gain_in, out, out_gain):
        gains = column(gain_in[...])
        total = jnp.zeros((rows, PAIR), F32)
        for owner, there, here, width in qkv_places:
            part = source[owner, :, there : there + width].astype(F32)
            total += part * weights[:, here : here + width].astype(F32)
            out[:, here : here + width] = part * gains
        out_gain[...] = row(jnp.sum(total, 1, keepdims=True))

    return kernel_call(
        body,
        "join_qkv",
        [sums, w_qkv, gain],
        out_shape=[
            jax.ShapeDtypeStruct((rows, total_width), F32),
            jax.ShapeDtypeStruct((1, rows), F32),
        ],
    )


def flip(index, offset):
    weight = 1
    while weight <= offset:
        if offset & weight:
            index = index + weight - 2 * weight * ((index // weight) % 2)
        weight *= 2
    return index


def greet(partners):
    barrier = pltpu.get_barrier_semaphore()
    for partner in partners:
        pl.semaphore_signal(barrier, inc=1, device_id=partner, device_id_type=MESH)
    pl.semaphore_wait(barrier, len(partners))


def here():
    return lax.axis_index("seq"), lax.axis_index("core")


def bits_of(seqs):
    return [1 << bit for bit in range(seqs.bit_length() - 1)]


def cube_partners(seqs):
    me, core = here()
    partners = [{"seq": flip(me, bit), "core": core} for bit in bits_of(seqs)]
    return partners + [{"seq": me, "core": 1 - core}]


def all_partners(seqs):
    me, core = here()
    return [
        {"seq": flip(me, step), "core": core if same else 1 - core}
        for step in range(seqs)
        for same in (True, False)
        if step or not same
    ]


def orders_of(seqs):
    bits = bits_of(seqs)
    return [bits, bits[1:] + bits[:1]]


def remote(source, target, sems, at, device):
    return pltpu.make_async_remote_copy(
        src_ref=source,
        dst_ref=target,
        send_sem=sems[0].at[at],
        recv_sem=sems[1].at[at],
        device_id=device,
        device_id_type=MESH,
    )


def push(*where):
    copy = remote(*where)
    copy.start()
    return copy


def loads(sources, rooms, sems):
    copies = []
    for i, (source, room) in enumerate(zip(sources, rooms)):
        if isinstance(source, tuple):
            source = source[0].at[:, pl.ds(source[1], source[2])]
        copies.append(pltpu.make_async_copy(source, room, sems.at[i]))
    return copies


def like(*arrays):
    return [pltpu.VMEM(array.shape, array.dtype) for array in arrays]


def pair_sems(*shape):
    return [pltpu.SemaphoreType.DMA(shape)] * 2


def spread_scratch(seqs):
    return pair_sems(2, seqs) + pair_sems(2, seqs) + [pltpu.SemaphoreType.DMA]


class Spread:
    def __init__(self, own, out, scratch, rows=None):
        self.own, self.out = own, out
        self.rows = rows or pl.ds(0, own.shape[0])
        self.across, self.aside, self.local = scratch[0:2], scratch[2:4], scratch[4]
        self.me, self.core = here()
        self.half = out.shape[-1] // 2
        self.orders = orders_of(out.shape[1])
        self.phases = len(self.orders[0])

    def columns(self, ref, stream):
        return ref.at[self.rows, pl.ds(stream * self.half, self.half)]

    def place(self, offset, stream):
        return self.columns(self.out.at[self.core, flip(self.me, offset)], stream)

    def block(self, offset, stream):
        return self.place(offset, stream) if offset else self.columns(self.own, stream)

    def kept(self):
        return pltpu.make_async_copy(
            self.own.at[self.rows], self.out.at[self.core, self.me, self.rows], self.local
        )

    def swap(self, offset, stream):
        sibling = {"seq": self.me, "core": 1 - self.core}
        return remote(
            self.block(offset, stream),
            self.place(offset, stream),
            self.aside,
            (stream, offset),
            sibling,
        )

    def held(self, phase, stream):
        offsets = [0]
        for bit in self.orders[stream][:phase]:
            offsets += [offset + bit for offset in offsets]
        return offsets

    def moves(self, phase):
        found = []
        for stream in range(2):
            bit = self.orders[stream][phase]
            partner = {"seq": flip(self.me, bit), "core": self.core}
            for offset in self.held(phase, stream):
                copy = remote(
                    self.block(offset, stream),
                    self.place(offset, stream),
                    self.across,
                    (stream, offset + bit),
                    partner,
                )
                found.append((copy, offset + bit, stream))
        return found

    def begin(self):
        self.kept().start()
        for copy, _, _ in self.moves(0):
            copy.start()
        for stream in range(2):
            self.swap(0, stream).start()

    def arrive(self, phase):
        for copy, offset, stream in self.moves(phase):
            copy.wait_recv()
            self.swap(offset, stream).start()

    def step(self, phase):
        self.arrive(phase - 1)
        for copy, _, _ in self.moves(phase):
            copy.start()

    def finish(self):
        self.arrive(self.phases - 1)
        for phase in range(self.phases):
            for copy, _, _ in self.moves(phase):
                copy.wait_send()
        for stream in range(2):
            for offset in self.held(self.phases, stream):
                self.swap(offset, stream).wait()
        self.kept().wait()


def fold_rooms(seqs, tokens, width, made=True):
    return [
        pltpu.VMEM((seqs, tokens, width), BF),
        pltpu.VMEM((seqs, tokens, width) if made else (16, PAIR), BF),
        pltpu.VMEM((seqs, tokens, width), BF),
        pltpu.VMEM((2, seqs, tokens, width // 2), BF),
    ]


def fold_sems(seqs):
    return [pltpu.SemaphoreType.DMA((2,))] + pair_sems(seqs) + pair_sems(2, seqs)


class Fold:
    def __init__(self, terms, rooms, sems, rows, make=None):
        self.terms, self.make = terms, make
        self.own, self.give, self.total, self.got = rooms
        self.local, self.aside, self.across = sems[0], sems[1:3], sems[3:5]
        self.rows = rows
        self.me, self.core = here()
        self.seqs = self.total.shape[0]
        self.half = self.total.shape[-1] // 2
        self.orders = orders_of(self.seqs)
        self.phases = len(self.orders[0])

    def taken(self, mine):
        core, room = (self.core, self.own) if mine else (1 - self.core, self.give)
        return pltpu.make_async_copy(
            self.terms.at[core, :, self.rows],
            room.at[:, self.rows],
            self.local.at[1 if mine else 0],
        )

    def fill(self, room, core, at):
        width = room.shape[-1]
        tile = min(2 * BLOCK, width)

        def one(j, carry):
            columns = pl.ds(pl.multiple_of(j * tile, tile), tile)
            value = self.make(core, at, self.rows, columns)
            if self.terms is not None:
                value = value + room[at, self.rows, columns].astype(F32)
            room[at, self.rows, columns] = value.astype(BF)
            return carry

        lax.fori_loop(0, width // tile, one, 0)

    def swap(self, offset):
        at = flip(self.me, offset)
        source = self.give.at[at] if self.make else self.terms.at[1 - self.core, at]
        return remote(
            source.at[self.rows],
            self.total.at[at, self.rows],
            self.aside,
            (offset,),
            {"seq": self.me, "core": 1 - self.core},
        )

    def columns(self, stream):
        return pl.ds(stream * self.half, self.half)

    def moves(self, phase, stream, only=None):
        bit = self.orders[stream][phase]
        done = sum(self.orders[stream][:phase])
        partner = {"seq": flip(self.me, bit), "core": self.core}
        return [
            (
                remote(
                    self.total.at[flip(self.me, offset), self.rows, self.columns(stream)],
                    self.got.at[stream, offset, self.rows],
                    self.across,
                    (stream, offset),
                    partner,
                ),
                offset,
            )
            for offset in range(self.seqs - 1, -1, -1)
            if offset & bit and not offset & done and only in (None, offset)
        ]

    def add(self, work):
        count = self.rows.size
        step = min(32, count)

        def one(i, carry):
            work(pl.ds(pl.multiple_of(self.rows.start + i * step, step), step))
            return carry

        lax.fori_loop(0, count // step, one, 0)

    def load(self):
        if self.terms is not None:
            if self.make:
                self.taken(False).start()
            self.taken(True).start()

    def begin(self):
        if self.make and self.terms is not None:
            self.taken(False).wait()
        for offset in range(self.seqs - 1, -1, -1):
            if self.make:
                self.fill(self.give, 1 - self.core, flip(self.me, offset))
            self.swap(offset).start()

    def first(self):
        if self.terms is not None:
            self.taken(True).wait()
        for offset in range(self.seqs - 1, -1, -1):
            at = flip(self.me, offset)
            if self.make:
                self.fill(self.own, self.core, at)
            self.swap(offset).wait_recv()

            def add_sibling(rows, at=at):
                both = self.total[at, rows, :].astype(F32) + self.own[at, rows, :].astype(F32)
                self.total[at, rows, :] = both.astype(BF)

            self.add(add_sibling)
            for stream in range(2):
                for copy, _ in self.moves(0, stream, offset):
                    copy.start()

    def receive(self, phase, stream):
        bit = self.orders[stream][phase]
        for copy, offset in self.moves(phase, stream):
            copy.wait_recv()
            at = flip(self.me, offset - bit)

            def add_got(rows, at=at, offset=offset):
                columns = self.columns(stream)
                both = self.total[at, rows, columns].astype(F32) + self.got[
                    stream, offset, rows, :
                ].astype(F32)
                self.total[at, rows, columns] = both.astype(BF)

            self.add(add_got)

    def step(self, phase):
        for stream in range(2):
            self.receive(phase - 1, stream)
            for copy, _ in self.moves(phase, stream):
                copy.start()

    def last(self):
        for stream in range(2):
            self.receive(self.phases - 1, stream)

    def result(self, rows):
        return self.total[self.me, rows, :].astype(F32)

    def settle(self):
        for offset in range(self.seqs):
            self.swap(offset).wait_send()
        for phase in range(self.phases):
            for stream in range(2):
                for copy, _ in self.moves(phase, stream):
                    copy.wait_send()


def halves(count):
    return [pl.ds(i * (count // 2), count // 2) for i in range(2)]


def fold_then_spread(folds, spreads, work, aside=lambda: None):
    phases = folds[0].phases
    for fold in folds:
        fold.begin()
        fold.first()
    aside()
    for phase in range(1, phases):
        for fold in folds:
            fold.step(phase)
            aside()
    for fold, spread in zip(folds, spreads):
        fold.last()
        fold.add(work)
        spread.begin()
        aside()
    for phase in range(1, phases):
        for spread in spreads:
            spread.step(phase)
            aside()
    for spread in spreads:
        spread.finish()
    for fold in folds:
        fold.settle()


def by_rows(count, work):
    step = min(32, count)

    def one(i, carry):
        work(pl.ds(pl.multiple_of(i * step, step), step))
        return carry

    lax.fori_loop(0, count // step, one, 0)


def deal_scratch(pieces, seqs):
    blocks = [piece.shape[-2:] for piece in pieces]
    return (
        pair_sems(len(pieces), 2 * seqs)
        + [pltpu.SemaphoreType.DMA((2, len(pieces)))]
        + [pltpu.VMEM(block, piece.dtype) for block, piece in zip(blocks, pieces)]
    )


class Deal:
    def __init__(self, pieces, outs, scratch, core_first=False):
        self.pieces, self.outs = pieces, outs
        self.sems, self.local, self.rooms = scratch[:2], scratch[2], scratch[3:]
        self.me, self.core = here()
        self.core_first = core_first
        self.seqs = outs[0].shape[1 if core_first else 0]

    def piece(self, i, seq, core):
        piece, out = self.pieces[i], self.outs[i]
        return piece.at[seq, core] if len(piece.shape) == len(out.shape) else piece

    def place(self, i):
        out = self.outs[i]
        return out.at[self.core, self.me] if self.core_first else out.at[self.me, self.core]

    def copy(self, i, step, same):
        to_seq = flip(self.me, step)
        to_core = self.core if same else 1 - self.core
        return remote(
            self.piece(i, to_seq, to_core),
            self.place(i),
            self.sems,
            (i, 2 * step + (0 if same else 1)),
            {"seq": to_seq, "core": to_core},
        )

    def copies(self):
        return [
            self.copy(i, step, same)
            for i in range(len(self.pieces))
            for step in range(self.seqs)
            for same in (True, False)
            if step or not same
        ]

    def entering(self):
        return [
            pltpu.make_async_copy(
                self.piece(i, self.me, self.core), self.rooms[i], self.local.at[0, i]
            )
            for i in range(len(self.rooms))
        ]

    def leaving(self):
        return [
            pltpu.make_async_copy(
                self.rooms[i] if self.rooms else self.piece(i, self.me, self.core),
                self.place(i),
                self.local.at[1, i],
            )
            for i in range(len(self.outs))
        ]

    def begin(self):
        for copy in self.copies() + self.entering():
            copy.start()
        for copy in self.entering():
            copy.wait()
        for copy in self.leaving():
            copy.start()

    def arrive_from(self, step):
        if step:
            self.copy(0, step, True).wait_recv()
        else:
            for copy in self.leaving():
                copy.wait()
        self.copy(0, step, False).wait_recv()

    def arrive(self):
        for copy in self.copies():
            copy.wait_recv()
        for copy in self.leaving():
            copy.wait()

    def settle(self):
        for copy in self.copies():
            copy.wait_send()

    def finish(self):
        self.arrive()
        self.settle()


class Ring:
    def __init__(self, whole, sems, part):
        self.whole, self.sems, self.part = whole, sems, part
        self.count = whole.shape[0]
        self.chip = lax.axis_index("z")

    def hop(self, i):
        block = self.whole.at[lax.rem(self.chip + self.count - i, self.count), self.part]
        following = lax.rem(self.chip + 1, self.count)
        return remote(block, block, self.sems, (i,), {"z": following})

    def preceding(self):
        return {"z": lax.rem(self.chip + self.count - 1, self.count)}

    def begin(self):
        self.hop(0).start()

    def step(self, i):
        self.hop(i - 1).wait_recv()
        if i < self.count - 1:
            self.hop(i).start()

    def settle(self):
        for i in range(self.count - 1):
            self.hop(i).wait_send()


def deal(pieces, number):
    count = len(pieces)
    seqs = pieces[0].shape[0]

    def body(*refs):
        greet(all_partners(seqs))
        work = Deal(refs[:count], refs[count : 2 * count], refs[2 * count :])
        work.begin()
        work.finish()

    return kernel_call(
        body,
        "deal",
        [*pieces],
        number,
        in_specs=[ANYWHERE] * count,
        out_specs=[ANYWHERE] * count,
        out_shape=[jax.ShapeDtypeStruct(piece.shape, BF) for piece in pieces],
        scratch_shapes=deal_scratch(pieces, seqs),
    )


def cut_into(out, parts):
    for source, gain, places in parts:
        for owner, there, begin, width in places:
            part = source[:, begin : begin + width]
            if gain is not None:
                part = (part.astype(F32) * gain).astype(BF)
            out[owner // 2, owner % 2, :, there : there + width] = part


def column(row):
    count = row.shape[1]
    shape = (count, count)
    wide = jnp.broadcast_to(row.astype(F32), shape)
    same = lax.broadcasted_iota(jnp.int32, shape, 0) == lax.broadcasted_iota(jnp.int32, shape, 1)
    return jnp.sum(jnp.where(same, wide, 0.0), 1, keepdims=True)


def row(values):
    count = values.shape[0]
    shape = (count, count)
    wide = jnp.broadcast_to(values, shape)
    same = lax.broadcasted_iota(jnp.int32, shape, 0) == lax.broadcasted_iota(jnp.int32, shape, 1)
    return jnp.sum(jnp.where(same, wide, 0.0), 0, keepdims=True)


def frequencies():
    half = HEAD_DIM // 2
    inverse = ROPE_BASE ** (-2.0 * np.arange(half) / HEAD_DIM)
    return np.tile(inverse.astype(np.float32), (8, PAIR // half))


def start(arrays, gains, positions, plans, blocks, seqs, chips, number):
    tokens, w_qkv = arrays[0], arrays[2]
    count, width = tokens.shape
    rows = w_qkv.shape[0]
    (qkv_places, out_places, attend_cols), chunks = plans
    shape = (seqs, 2, rows)
    cuts = [shape + (cols,) for _, _, cols in chunks]
    more = len(chunks) - 1

    def body(*refs):
        sources, places, inverse = refs[:6], refs[8], refs[9]
        acts, whole, piece, tables, *moved = refs[10:16]
        cut_out = refs[16 : 16 + more]
        scratch = refs[16 + more :]
        gain_one, gain_two = column(refs[6][...]), column(refs[7][...])
        rooms, (sem, attend_cut), scratch = scratch[:6], scratch[6:8], scratch[8:]
        ff_cut, scratch = scratch[: 1 + more], scratch[1 + more :]
        turned, own, scratch = scratch[:2], scratch[2], scratch[3:]
        out_sem, ring_sems, scratch = scratch[0], scratch[1 : 1 + 2 * seqs], scratch[1 + 2 * seqs :]
        deal_sems, spread_sems = scratch[:9], scratch[9:14]
        own_places, all_places, all_tables = scratch[14:]
        coming = loads(sources, rooms, sem)
        for i in (2, 3, 0, 4, 5, 1):
            coming[i].start()
        own_places[...] = jnp.broadcast_to(places[...], own_places.shape)
        me_chip = lax.axis_index("z")
        rings = [
            Ring(whole, ring_sems[2 * i : 2 * i + 2], flip(lax.axis_index("seq"), i))
            for i in range(seqs)
        ]
        greet(all_partners(seqs) + [rings[0].preceding()])
        coming[2].wait()
        coming[3].wait()
        cut_into(
            attend_cut, [(rooms[2], gain_one, qkv_places), (rooms[3], None, out_places)]
        )
        attend_deal = Deal([attend_cut], [whole.at[me_chip]], deal_sems[:3])
        attend_deal.begin()
        place_deal = Deal([own_places], [all_places], deal_sems[3:6], True)
        place_deal.begin()
        attend_deal.arrive_from(0)
        rings[0].begin()
        coming[0].wait()
        for outer, inner, size in blocks:
            turned[0][:, inner : inner + size] = rooms[0][:, outer : outer + size]

        def norm(at):
            values = turned[0][at, :].astype(F32)
            own[at, :] = (values * norm_scale(values)).astype(BF)

        by_rows(count, norm)
        for step in range(1, seqs):
            attend_deal.arrive_from(step)
            rings[step].begin()
        spreading = Spread(own, acts, spread_sems)
        spreading.begin()
        coming[4].wait()
        coming[5].wait()
        for out, (pair, single, _) in zip(ff_cut, chunks):
            cut_into(out, [(rooms[4], gain_two, pair), (rooms[5], None, single)])
        coming[1].wait()
        for outer, inner, size in blocks:
            turned[1][:, inner : inner + size] = rooms[1][:, outer : outer + size]
        going = loads(list(turned) + list(ff_cut[1:]), list(moved) + list(cut_out), out_sem)
        for copy in going:
            copy.start()
        for phase in range(1, spreading.phases):
            spreading.step(phase)
        ff_deal = Deal([ff_cut[0]], [piece], deal_sems[6:9])
        ff_deal.begin()
        place_deal.arrive()

        def table(i, carry):
            at, seq = lax.div(i, seqs), lax.rem(i, seqs)
            angles = column(all_places[at, seq][:1]) * inverse[:1, :]
            lane = lax.broadcasted_iota(jnp.int32, angles.shape, 1)
            cosine = lane % HEAD_DIM < HEAD_DIM // 2
            all_tables[at, seq] = jnp.where(cosine, jnp.cos(angles), jnp.sin(angles))
            return carry

        for i in range(1, chips):
            for ring in rings:
                ring.step(i)
            if i <= 2:
                lax.fori_loop((i - 1) * seqs, i * seqs, table, 0)
            if i == 2:
                spreading.finish()
        leaving = pltpu.make_async_copy(all_tables, tables, out_sem.at[2 + more])
        leaving.start()
        for ring in rings:
            ring.settle()
        attend_deal.settle()
        place_deal.settle()
        ff_deal.finish()
        for copy in going:
            copy.wait()
        leaving.wait()

    like_tokens = jax.ShapeDtypeStruct((count, width), BF)
    deal_sem = pair_sems(1, 2 * seqs) + [pltpu.SemaphoreType.DMA((2, 1))]
    return kernel_call(
        body,
        "start",
        [*arrays, *gains, positions, frequencies()],
        number,
        in_specs=[ANYWHERE] * 6 + [LOCAL] * 4,
        out_specs=[ANYWHERE] * (6 + more),
        out_shape=[
            jax.ShapeDtypeStruct((2, seqs, count, width), BF),
            jax.ShapeDtypeStruct((chips,) + shape + (attend_cols,), BF),
            jax.ShapeDtypeStruct(cuts[0], BF),
            jax.ShapeDtypeStruct((2, seqs, count, PAIR), F32),
            like_tokens,
            like_tokens,
        ]
        + [jax.ShapeDtypeStruct(cut, BF) for cut in cuts[1:]],
        scratch_shapes=like(*arrays)
        + [pltpu.SemaphoreType.DMA((6,)), pltpu.VMEM(shape + (attend_cols,), BF)]
        + [pltpu.VMEM(cut, BF) for cut in cuts]
        + [pltpu.VMEM((count, width), BF)] * 3
        + [pltpu.SemaphoreType.DMA((3 + more,))]
        + pair_sems(chips) * seqs
        + deal_sem * 3
        + spread_scratch(seqs)
        + [pltpu.VMEM((8, count), jnp.int32), pltpu.VMEM((2, seqs, 8, count), jnp.int32)]
        + [pltpu.VMEM((2, seqs, count, PAIR), F32)],
    )


def two_way_scratch(seqs, count, width):
    return (
        [pltpu.VMEM((count, width), BF)]
        + fold_rooms(seqs, count, width)
        + fold_sems(seqs) * 2
        + spread_scratch(seqs) * 2
    )


def two_way(given, out, scratch, make):
    own, rooms, sems = scratch[0], scratch[1:5], scratch[5:]
    parts = halves(own.shape[0])
    folds = [
        Fold(given, rooms, sems[5 * i : 5 * i + 5], rows, make) for i, rows in enumerate(parts)
    ]
    sems = sems[10:]
    spreads = [Spread(own, out, sems[5 * i : 5 * i + 5], rows) for i, rows in enumerate(parts)]
    for fold in folds:
        fold.load()
    return folds, spreads, own


def product(left, right, seqs, count):
    def make(core, at, rows, columns):
        begin = pl.multiple_of((core * seqs + at) * count + rows.start, rows.size)
        return nt(left[pl.ds(begin, rows.size), :], right[columns, :])

    return make


def middle_acts(attended, weights, tokens, seqs, number):
    count, width = tokens.shape
    cols = attended.shape[1]
    begin = weights.shape[1] - cols

    def body(left_in, given, source_in, middle, out, left, right, source, sems, *scratch):
        coming = loads([left_in, (given, begin, cols), source_in], [left, right, source], sems)
        for copy in coming:
            copy.start()
        folds, spreads, own = two_way(None, out, scratch, product(left, right, seqs, count))
        greet(cube_partners(seqs))
        for copy in coming:
            copy.wait()

        def norm(rows):
            values = source[rows, :].astype(F32) + folds[0].result(rows)
            middle[rows, :] = values
            own[rows, :] = (values * norm_scale(values)).astype(BF)

        fold_then_spread(folds, spreads, norm)

    return kernel_call(
        body,
        "middle_acts",
        [attended, weights, tokens],
        number,
        in_specs=[ANYWHERE] * 3,
        out_specs=[LOCAL, ANYWHERE],
        out_shape=[
            jax.ShapeDtypeStruct((count, width), F32),
            jax.ShapeDtypeStruct((2, seqs, count, width), BF),
        ],
        scratch_shapes=like(attended)
        + [pltpu.VMEM((width, cols), BF)]
        + like(tokens)
        + [pltpu.SemaphoreType.DMA((3,))]
        + two_way_scratch(seqs, count, width),
    )


def middle_grad(terms, grad_both, cotangent, middle, hidden, weights, number):
    _, seqs, count, width = terms.shape
    tokens = hidden[0].shape[0]
    n = len(hidden)
    block = min(BLOCK, tokens)
    tile = min(2 * BLOCK, width)
    blocks = tokens // block
    parts = [h.shape[1] for h in hidden]

    def body(given, *refs):
        sources, down = refs[: 3 + n], refs[3 + n : 3 + 2 * n]
        grad, out, products = refs[3 + 2 * n : 6 + 2 * n]
        scratch = refs[6 + 2 * n :]
        left, upstream, values = scratch[:3]
        units, room, right = scratch[3 : 3 + n], scratch[3 + n : 3 + 2 * n], scratch[3 + 2 * n]
        stage, sems, leaving = scratch[4 + 2 * n : 7 + 2 * n]
        columns = [(down[i], 2 * parts[i], parts[i]) for i in range(n)]
        coming = loads(
            [sources[0], (down[-1], 0, 2 * parts[-1]), *sources[3:], *columns, *sources[1:3]],
            [left, right, *units, *room, upstream, values],
            sems,
        )
        for copy in coming[:2]:
            copy.start()
        make = product(left, right, seqs, count)
        folds, spreads, own = two_way(given, out, scratch[7 + 2 * n :], make)
        for copy in coming[2:]:
            copy.start()
        greet(cube_partners(seqs))
        for copy in coming[:2]:
            copy.wait()

        def leave(i):
            rows = pl.ds(i * block, block)
            return pltpu.make_async_copy(stage.at[i % 2], products.at[rows], leaving.at[i % 2])

        def multiply(i):
            if i == 0:
                for copy in coming[2:]:
                    copy.wait()
            if i >= 2:
                leave(i - 2).wait()

            def one(j, carry):
                columns = pl.ds(pl.multiple_of(j * tile, tile), tile)
                total = sum(
                    nt(units[k][pl.ds(i * block, block), :], room[k][columns, :])
                    for k in range(n)
                )
                stage[i % 2, :, columns] = total.astype(BF)
                return carry

            lax.fori_loop(0, width // tile, one, 0)
            leave(i).start()

        left_over = list(range(blocks))

        def aside():
            for _ in range(2 if len(left_over) == blocks else max(1, blocks // 8)):
                if left_over:
                    multiply(left_over.pop(0))

        def back(rows):
            held = values[rows, :]
            scale = norm_scale(held)
            result = upstream[rows, :].astype(F32) + norm_back(
                folds[0].result(rows), held * scale, scale
            )
            grad[rows, :] = result
            own[rows, :] = result.astype(BF)

        fold_then_spread(folds, spreads, back, aside)
        while left_over:
            multiply(left_over.pop(0))
        for i in range(max(0, blocks - 2), blocks):
            leave(i).wait()

    return kernel_call(
        body,
        "middle_grad",
        [terms, grad_both, cotangent, middle, *hidden, *weights],
        number,
        in_specs=[ANYWHERE] * (4 + 2 * n),
        out_specs=[LOCAL, ANYWHERE, ANYWHERE],
        out_shape=[
            jax.ShapeDtypeStruct((count, width), F32),
            jax.ShapeDtypeStruct(terms.shape, BF),
            jax.ShapeDtypeStruct((tokens, width), BF),
        ],
        scratch_shapes=like(grad_both, cotangent, middle, *hidden)
        + [pltpu.VMEM((width, part), BF) for part in parts]
        + [pltpu.VMEM((width, 2 * parts[-1]), BF), pltpu.VMEM((2, block, width), BF)]
        + [pltpu.SemaphoreType.DMA((4 + 2 * n,)), pltpu.SemaphoreType.DMA((2,))]
        + two_way_scratch(seqs, count, width),
    )


def input_grad(grad_mixed, weights, tokens, grad_middle, seqs, number):
    count, width = tokens.shape
    cols = grad_mixed.shape[1]

    def body(left_in, given, source_in, held_in, out, left, right, source, held, sems, *scratch):
        coming = loads(
            [left_in, (given, 0, cols), source_in, held_in], [left, right, source, held], sems
        )
        for copy in coming:
            copy.start()
        make = product(left, right, seqs, count)
        sems = scratch[4:]
        folds = [
            Fold(None, scratch[:4], sems[5 * i : 5 * i + 5], rows, make)
            for i, rows in enumerate(halves(count))
        ]
        greet(cube_partners(seqs))
        for copy in coming:
            copy.wait()
        for fold in folds:
            fold.begin()
            fold.first()
        for phase in range(1, folds[0].phases):
            for fold in folds:
                fold.step(phase)

        def back(rows):
            values = source[rows, :].astype(F32)
            scale = norm_scale(values)
            out[rows, :] = held[rows, :] + norm_back(folds[0].result(rows), values * scale, scale)

        for fold in folds:
            fold.last()
            fold.add(back)
        for fold in folds:
            fold.settle()

    return kernel_call(
        body,
        "input_grad",
        [grad_mixed, weights, tokens, grad_middle],
        number,
        in_specs=[ANYWHERE] * 4,
        out_specs=LOCAL,
        out_shape=jax.ShapeDtypeStruct((count, width), F32),
        scratch_shapes=like(grad_mixed)
        + [pltpu.VMEM((width, cols), BF)]
        + like(tokens, grad_middle)
        + [pltpu.SemaphoreType.DMA((4,))]
        + fold_rooms(seqs, count, width)
        + fold_sems(seqs) * 2,
    )


class Order:
    def __init__(self):
        self.latest = None

    def enter(self, values):
        if self.latest is None:
            return values
        return lax.optimization_barrier((values, self.latest))[0]

    def run(self, work, *values):
        result = work(*self.enter(values))
        self.latest = jax.tree.leaves(result)
        return result

    def take(self, values):
        if self.latest is not None:
            values = lax.optimization_barrier((values, self.latest))[0]
        self.latest = jax.tree.leaves(values)
        return values


def norm_scale(values):
    return lax.rsqrt(jnp.mean(values * values, -1, keepdims=True) + EPS)


def norm_back(grad, normed, scale):
    return scale * (grad - normed * jnp.mean(grad * normed, -1, keepdims=True))


def per_device(
    mesh, tokens, positions, w_qkv, w_out, gain_attn, w_gate_up, w_down, gain_mlp, cotangent
):
    order = Order()
    seqs, chips = mesh.shape["seq"], mesh.shape["z"]
    owners = 2 * seqs
    token_count, width = tokens.shape[1:]
    ff_width = w_down.shape[1]
    rows = w_qkv.shape[0]
    head_cols = width // owners
    ff_cols = ff_width // owners
    parts = chunk_widths(ff_cols)
    last = len(parts) - 1
    blocks = blocks_in(rows, seqs, chips)

    def by_place(piece):
        return piece.reshape(seqs, 2, rows, -1)

    def gathered(piece):
        piece = order.enter(piece).reshape(seqs, 2 * rows, -1)
        return lax.all_gather(piece, "z", axis=0, tiled=False)

    def flat(value):
        return order.take(value).reshape(width, -1)

    def summed(term):
        split = order.enter(term).reshape(chips, seqs, 2 * rows, -1)
        return lax.psum_scatter(split, "z", scatter_dimension=0, tiled=False)

    def rounded(left, right):
        return tn(left, right).astype(BF)

    qkv_places = list(qkv_columns(owners, head_cols))
    out_places = [(o, 3 * head_cols, o * head_cols, head_cols) for o in range(owners)]
    gate_up_places, down_places = ff_columns(owners, ff_cols)
    chunks = [
        (pair, single, 3 * part) for pair, single, part in zip(gate_up_places, down_places, parts)
    ]
    acts, attend_whole, ff_piece, table, tokens_in, upstream_own, *ff_cut = order.run(
        lambda *a: start(
            a[:6],
            a[6:8],
            a[8],
            ((qkv_places, out_places, 4 * head_cols), chunks),
            blocks,
            seqs,
            chips,
            1,
        ),
        tokens[0],
        cotangent[0],
        w_qkv,
        w_out,
        w_gate_up,
        w_down,
        gain_attn[None],
        gain_mlp[None],
        positions,
    )
    acts = acts.reshape(-1, width)
    attend_whole = attend_whole.reshape(width, -1)
    table = table.reshape(-1, PAIR)
    ff_coming = [gathered(ff_piece)]

    qkv_cols = 3 * head_cols
    mixed = order.run(lambda a, w: nn(a, w[:, :qkv_cols]), acts, attend_whole)
    qkv, attended, logs, upstream, *ff_pieces = order.run(
        lambda m, t, u, *given: attend(m, t, SpreadBeside(seqs, u, given), 2, 3),
        mixed,
        table,
        upstream_own,
        *ff_cut,
    )
    ff_coming += [gathered(piece) for piece in ff_pieces]
    upstream = upstream.reshape(-1, width)
    middle, acts_mid = order.run(
        lambda a, w, x: middle_acts(a, w, x, seqs, 4), attended, attend_whole, tokens_in
    )
    acts_mid = acts_mid.reshape(-1, width)

    def feed_hidden(both):
        part = both.shape[1] // 2
        gate, up = both[:, :part], both[:, part:]
        return (gate * jax.nn.sigmoid(gate) * up).astype(BF)

    def feed_back(grad_hidden, both):
        part = both.shape[1] // 2
        gate, up = both[:, :part], both[:, part:]
        sigma = jax.nn.sigmoid(gate)
        grad_gate = grad_hidden * up * sigma * (1.0 + gate * (1.0 - sigma))
        grad_up = grad_hidden * gate * sigma
        return jnp.concatenate([grad_gate.astype(BF), grad_up.astype(BF)], 1)

    def both_terms(left, right, left_two, right_two):
        return [rounded(left, right), rounded(left_two, right_two)]

    def add_nt(left, right, total=None):
        result = nt(left, right)
        return (result if total is None else result + total.astype(F32)).astype(BF)

    ff_sums, hiddens, wholes = [], [], []
    norm_mid_terms = ()
    for chunk, part in enumerate(parts):
        cols = 2 * part
        whole = flat(ff_coming[chunk])
        both = order.run(lambda a, w: nn(a, w[:, :cols]), acts_mid, whole)
        hidden = order.run(feed_hidden, both)
        hiddens.append(hidden)
        wholes.append(whole)
        grad_hidden = order.run(lambda a, w: nn(a, w[:, cols:]), upstream, whole)
        grad_both = order.run(feed_back, grad_hidden, both)
        terms = order.run(both_terms, acts_mid, grad_both, upstream, hidden)
        if chunk < len(parts) - 1:
            ff_sums.append(summed(order.run(side_by_side, terms)))
        if chunk < len(parts) - 1:
            norm_mid_terms = (
                order.run(
                    lambda a, w, *t: add_nt(a, w[:, :cols], *t), grad_both, whole, *norm_mid_terms
                ),
            )

    grad_middle, grad_branch, outcome_terms = order.run(
        lambda a, b, c, d, e, f: middle_grad(a, b, c, d, e, f, 5),
        norm_mid_terms[0].reshape(2, seqs, token_count, width),
        grad_both,
        upstream_own,
        middle,
        hiddens,
        wholes,
    )
    grad_branch = grad_branch.reshape(-1, width)

    terms.append(order.run(rounded, grad_branch, attended))
    ff_sums.append(summed(order.run(side_by_side, terms)))
    grad_attended = order.run(
        lambda a, w: nn(a, w[:, qkv_cols:]).astype(BF), grad_branch, attend_whole
    )
    first_rows = [by_place(order.take(value)) for value in ff_sums[:-1]]
    grad_mixed, outcome, *ff_dealt = order.run(
        lambda a, b, c, d, e, f, *given: attend_back(
            a, b, c, d, OutputBeside(seqs, e, f, given), 2, 6
        ),
        qkv,
        grad_attended,
        logs,
        table,
        outcome_terms.reshape(2, seqs, token_count, width),
        middle,
        *first_rows,
    )
    qkv_sum = summed(order.run(rounded, acts, grad_mixed))

    grad_inputs = order.run(
        lambda a, w, b, c: input_grad(a, w, b, c, seqs, 7),
        grad_mixed,
        attend_whole,
        tokens_in,
        grad_middle,
    )
    last_rows = by_place(order.take(ff_sums[-1]))
    ff_dealt += order.run(lambda a: deal([a], 8), last_rows)
    out_at = [(o, 3 * parts[-1], o * head_cols, head_cols) for o in range(owners)]
    grad_gate_up, gain_two_sum, grad_down, grad_out = order.run(
        lambda w, g, *a: join_ff(a, w, g, gate_up_places, down_places, out_at),
        w_gate_up,
        gain_mlp[None],
        *[value.reshape(owners, rows, -1) for value in ff_dealt],
    )
    grad_inputs, outcome = order.run(lambda *a: outside(a, blocks), grad_inputs, outcome)
    qkv_rows = order.take(qkv_sum)
    (qkv_dealt,) = order.run(lambda a: deal([a], 9), by_place(qkv_rows))
    grad_qkv, gain_one_sum = order.run(
        lambda w, g, a: join_qkv(a, w, g, qkv_places),
        w_qkv,
        gain_attn[None],
        qkv_dealt.reshape(owners, rows, -1),
    )
    return (
        outcome[None],
        grad_inputs[None],
        grad_qkv,
        grad_out,
        gain_one_sum[0],
        grad_gate_up,
        grad_down,
        gain_two_sum[0],
    )


def solution(mesh):
    seqs, devices = mesh.shape["seq"], mesh.shape["fsdp"]
    parted = Mesh(mesh.devices.reshape(seqs, devices // 2, 2), ("seq", "z", "core"))
    tokens = P(("z", "core"), "seq", None)
    matrix = P(("seq", "z", "core"), None)
    vector = P(("seq", "z", "core"))
    return jax.shard_map(
        functools.partial(per_device, parted),
        mesh=parted,
        in_specs=(
            tokens,
            P(("z", "core"), "seq"),
            matrix,
            matrix,
            vector,
            matrix,
            matrix,
            vector,
            tokens,
        ),
        out_specs=(tokens, tokens, matrix, matrix, vector, matrix, matrix, vector),
        check_vma=False,
    )
```

```python
import functools
import math

import jax
import jax.numpy as jnp
import numpy as np
from jax import lax
from jax.experimental import pallas as pl
from jax.experimental.pallas import tpu as pltpu
from jax.sharding import Mesh, PartitionSpec as P

HEAD_DIM = 64
PAIR = 2 * HEAD_DIM
BLOCK = 256
EPS = 1e-05
ROPE_BASE = 130000.0
BF = jnp.bfloat16
F32 = jnp.float32
VMEM_MOST = 58 << 20
MESH = pl.DeviceIdType.MESH
ANYWHERE = pl.BlockSpec(memory_space=pltpu.HBM)
LOCAL = pl.BlockSpec(memory_space=pltpu.VMEM)


def room_for(spec, arrays):
    total = 8 << 20
    for room in spec.get("scratch_shapes", ()):
        if hasattr(room, "shape") and room.dtype in (BF, F32):
            total += math.prod(room.shape) * jnp.dtype(room.dtype).itemsize
    outs = spec["out_shape"] if isinstance(spec["out_shape"], list) else [spec["out_shape"]]
    specs = spec.get("out_specs", LOCAL), spec.get("in_specs", LOCAL)
    for values, given in zip((outs, arrays), specs):
        given = given if isinstance(given, list) else [given] * len(values)
        for value, where in zip(values, given):
            if where.block_shape is not None:
                total += 2 * math.prod(where.block_shape) * value.dtype.itemsize
            elif where is not ANYWHERE:
                total += math.prod(value.shape) * value.dtype.itemsize
    return min(total, VMEM_MOST)


def kernel_call(body, name, arrays, number=None, **spec):
    params = {"vmem_limit_bytes": room_for(spec, arrays)}
    if number is not None:
        params.update(vmem_limit_bytes=VMEM_MOST, collective_id=number, has_side_effects=True)
    return pl.pallas_call(
        body, name=name, compiler_params=pltpu.CompilerParams(**params), **spec
    )(*arrays)


def turn(x, cosine, sine):
    half = HEAD_DIM // 2
    lane = lax.broadcasted_iota(jnp.int32, x.shape, 1)
    swapped = jnp.where(
        lane % HEAD_DIM < half, pltpu.roll(x, PAIR - half, 1), pltpu.roll(x, half, 1)
    )
    return x * cosine + swapped * sine


def nt(left, right):
    return lax.dot_general(left, right, (((1,), (1,)), ((), ())), preferred_element_type=F32)


def tn(left, right):
    return lax.dot_general(left, right, (((0,), (0,)), ((), ())), preferred_element_type=F32)


def nn(left, right):
    return lax.dot_general(left, right, (((1,), (0,)), ((), ())), preferred_element_type=F32)


def masked_scores(queries, keys, block):
    scores = nt(queries, keys)
    rows = lax.broadcasted_iota(jnp.int32, (BLOCK, BLOCK), 0)
    cols = lax.broadcasted_iota(jnp.int32, (BLOCK, BLOCK), 1)
    last = jnp.where(cols <= rows, scores[:, block * BLOCK :], -1e30)
    return jnp.concatenate([scores[:, : block * BLOCK], last], 1) if block else last


def unpack(table):
    half = HEAD_DIM // 2
    cosine, sine = table[:, :half], table[:, half:HEAD_DIM]
    return (
        jnp.concatenate([cosine] * 4, 1),
        jnp.concatenate([-sine, sine] * 2, 1),
    )


def attend_body(mixed, table, qkv, out, logs):
    length = mixed.shape[0]
    cosine, sine = unpack(table[...])
    qkv[:, :PAIR] = turn(mixed[:, :PAIR], cosine, sine).astype(BF)
    qkv[:, PAIR : 2 * PAIR] = turn(mixed[:, PAIR : 2 * PAIR], cosine, sine).astype(BF)
    qkv[:, 2 * PAIR :] = mixed[:, 2 * PAIR :].astype(BF)
    scale = jnp.asarray(1.0 / math.sqrt(HEAD_DIM), BF)
    for block in range(length // BLOCK):
        at = pl.ds(block * BLOCK, BLOCK)
        seen = (block + 1) * BLOCK
        outs = []
        totals = []
        for low in (0, HEAD_DIM):
            high = low + HEAD_DIM
            queries = qkv[at, low:high] * scale
            scores = masked_scores(queries, qkv[:seen, PAIR + low : PAIR + high], block)
            highest = jnp.max(scores, -1, keepdims=True)
            weights = jnp.exp(scores - highest)
            summed = jnp.sum(weights, -1, keepdims=True)
            probs = (weights * (1.0 / summed)).astype(BF)
            outs.append(nn(probs, qkv[:seen, 2 * PAIR + low : 2 * PAIR + high]))
            totals.append(jnp.broadcast_to(highest + jnp.log(summed), (BLOCK, HEAD_DIM)))
        out[at, :] = jnp.concatenate(outs, 1).astype(BF)
        logs[at, :] = jnp.concatenate(totals, 1)


def attend_back_body(qkv, grad, logs, table, grad_qkv, grad_keys, grad_values):
    length = qkv.shape[0]
    scale = 1.0 / math.sqrt(HEAD_DIM)
    cosine, sine = unpack(table[...])
    last = length // BLOCK - 1
    for block in range(last, -1, -1):
        at = pl.ds(block * BLOCK, BLOCK)
        seen = (block + 1) * BLOCK
        rows = slice(block * BLOCK, seen)
        grad_queries = []
        for low in (0, HEAD_DIM):
            high = low + HEAD_DIM
            queries = qkv[at, low:high] * jnp.asarray(scale, BF)
            keys = qkv[:seen, PAIR + low : PAIR + high]
            upstream = grad[at, low:high]
            scores = masked_scores(queries, keys, block)
            probs = jnp.exp(scores - logs[at, low : low + 1])
            grad_probs = nt(upstream, qkv[:seen, 2 * PAIR + low : 2 * PAIR + high])
            inner = jnp.sum(probs * grad_probs, -1, keepdims=True)
            grad_scores = (probs * (grad_probs - inner)).astype(BF)
            grad_queries.append(nn(grad_scores, keys))
            for_keys = tn(grad_scores, queries)
            for_values = tn(probs.astype(BF), upstream)
            if block == last:
                grad_keys[:, low:high] = for_keys
                grad_values[:, low:high] = for_values
            else:
                grad_keys[:seen, low:high] += for_keys
                grad_values[:seen, low:high] += for_values
        rounded = (jnp.concatenate(grad_queries, 1) * scale).astype(BF).astype(F32)
        grad_qkv[at, :PAIR] = turn(rounded, cosine[rows], -sine[rows]).astype(BF)
    rounded = grad_keys[...].astype(BF).astype(F32)
    grad_qkv[:, PAIR : 2 * PAIR] = turn(rounded, cosine, -sine).astype(BF)
    grad_qkv[:, 2 * PAIR :] = grad_values[...].astype(BF)


def heads_call(body, name, arrays, kinds, outs, out_kinds, count, beside, number, scratch):
    tokens = arrays[0].shape[0]
    length = tokens // count
    pairs = arrays[0].shape[1] // (3 * PAIR)
    specs = {
        "wide": pl.BlockSpec((length, 3 * PAIR), lambda s, i: (s, i)),
        "one": pl.BlockSpec((length, PAIR), lambda s, i: (s, i)),
        "table": pl.BlockSpec((length, PAIR), lambda s, i: (s, 0)),
    }
    n_in, n_out = len(arrays), len(outs)
    more_in, more_out = len(beside.arrays), len(beside.outs)

    def whole(*refs):
        ins, given = refs[:n_in], refs[n_in : n_in + more_in]
        rest = refs[n_in + more_in :]
        results, made = rest[:n_out], rest[n_out : n_out + more_out]
        rest = rest[n_out + more_out :]
        room, held = rest[: len(beside.scratch)], rest[len(beside.scratch) :]
        step = pl.program_id(0) * pairs + pl.program_id(1)
        last = count * pairs - 1
        acts = beside.acts(given, made, room)
        when = [(2 * i * (last + 1) + len(acts) - 1) // (2 * len(acts) - 2) for i in range(len(acts))]
        for i, act in enumerate(acts):
            if when[i] <= last:
                pl.when(step == when[i])(act)
        body(*ins, *results, *held)

        @pl.when(step == last)
        def _():
            for i, act in enumerate(acts):
                if when[i] > last:
                    act()

    return kernel_call(
        whole,
        name,
        list(arrays) + list(beside.arrays),
        number,
        grid=(count, pairs),
        in_specs=[specs[kind] for kind in kinds] + [ANYWHERE] * more_in,
        out_specs=[specs[kind] for kind in out_kinds] + [ANYWHERE] * more_out,
        out_shape=list(outs) + list(beside.outs),
        scratch_shapes=list(beside.scratch) + scratch(length),
    )


class SpreadBeside:
    def __init__(self, seqs, own, pieces):
        self.seqs = seqs
        self.arrays = [own] + list(pieces)
        self.outs = [jax.ShapeDtypeStruct((2, seqs) + own.shape, BF)]
        self.outs += [jax.ShapeDtypeStruct(piece.shape, BF) for piece in pieces]
        self.scratch = [pltpu.VMEM(own.shape, BF), pltpu.SemaphoreType.DMA]
        self.scratch += spread_scratch(seqs)
        self.first = len(self.scratch)
        self.scratch += deal_scratch(pieces, seqs) if pieces else []

    def acts(self, given, made, room):
        def dealing():
            return Deal(given[1:], made[1:], room[self.first :])

        def spreading():
            return Spread(room[0], made[0], room[2:])

        def begin():
            copy = pltpu.make_async_copy(given[0], room[0], room[1])
            copy.start()
            greet(all_partners(self.seqs))
            copy.wait()
            spreading().begin()
            if given[1:]:
                dealing().begin()

        def finish():
            spreading().finish()
            if given[1:]:
                dealing().finish()

        def step(phase):
            return lambda: spreading().step(phase)

        return [begin] + [step(i) for i in range(1, len(bits_of(self.seqs)))] + [finish]


class OutputBeside:
    def __init__(self, seqs, terms, middle, pieces):
        self.seqs = seqs
        self.arrays = [terms, middle] + list(pieces)
        self.outs = [jax.ShapeDtypeStruct(middle.shape, BF)]
        self.outs += [jax.ShapeDtypeStruct(piece.shape, BF) for piece in pieces]
        self.scratch = [
            pltpu.VMEM(middle.shape, F32),
            pltpu.VMEM(middle.shape, BF),
            pltpu.SemaphoreType.DMA((2,)),
        ]
        self.scratch += fold_rooms(seqs, *middle.shape, False) + fold_sems(seqs)
        self.first = len(self.scratch)
        self.scratch += deal_scratch(pieces, seqs)

    def acts(self, given, made, room):
        held, rounded, sems = room[:3]

        def dealing():
            return Deal(given[2:], made[1:], room[self.first :])

        def folding():
            return Fold(given[0], room[3:7], room[7:12], pl.ds(0, held.shape[0]))

        def entering():
            return pltpu.make_async_copy(given[1], held, sems.at[0])

        def begin():
            entering().start()
            folding().load()
            greet(all_partners(self.seqs))
            folding().begin()
            dealing().begin()

        def finish():
            fold = folding()
            fold.last()
            entering().wait()

            def add(rows):
                rounded[rows, :] = (held[rows, :] + fold.result(rows)).astype(BF)

            fold.add(add)
            leaving = pltpu.make_async_copy(rounded, made[0], sems.at[1])
            leaving.start()
            fold.settle()
            dealing().finish()
            leaving.wait()

        def step(phase):
            return lambda: folding().step(phase)

        phases = len(bits_of(self.seqs))
        return [begin, lambda: folding().first()] + [step(i) for i in range(1, phases)] + [finish]


def attend(mixed, table, beside, count, number):
    tokens, cols = mixed.shape
    outs = [
        jax.ShapeDtypeStruct((tokens, cols), BF),
        jax.ShapeDtypeStruct((tokens, cols // 3), BF),
        jax.ShapeDtypeStruct((tokens, cols // 3), F32),
    ]
    return heads_call(
        attend_body,
        "attend",
        [mixed, table],
        ["wide", "table"],
        outs,
        ["wide", "one", "one"],
        count,
        beside,
        number,
        lambda length: [],
    )


def attend_back(qkv, grad, logs, table, beside, count, number):
    return heads_call(
        attend_back_body,
        "attend_back",
        [qkv, grad, logs, table],
        ["wide", "one", "one", "table"],
        [jax.ShapeDtypeStruct(qkv.shape, BF)],
        ["wide"],
        count,
        beside,
        number,
        lambda length: [pltpu.VMEM((length, PAIR), F32)] * 2,
    )


def qkv_columns(owners, cols):
    for owner in range(owners):
        for pair in range(cols // PAIR):
            for kind in range(3):
                there = (pair * 3 + kind) * PAIR
                yield owner, there, (kind * owners + owner) * cols + pair * PAIR, PAIR


def chunk_widths(cols):
    units = cols // PAIR
    first = max(1, (5 * units) // 8)
    return [n * PAIR for n in (first, units - first) if n]


def ff_columns(owners, cols):
    begin = 0
    gate_up, down = [], []
    for part in chunk_widths(cols):
        gate_up.append(
            [
                (owner, kind * part, (kind * owners + owner) * cols + begin, part)
                for owner in range(owners)
                for kind in range(2)
            ]
        )
        down.append([(owner, 2 * part, owner * cols + begin, part) for owner in range(owners)])
        begin += part
    return gate_up, down


def side_by_side(parts):
    begins = [sum(part.shape[1] for part in parts[:i]) for i in range(len(parts))]

    def body(*refs):
        out, sems = refs[-2:]
        copies = [
            pltpu.make_async_copy(
                refs[i], out.at[:, pl.ds(begins[i], part.shape[1])], sems.at[i]
            )
            for i, part in enumerate(parts)
        ]
        for copy in copies:
            copy.start()
        for copy in copies:
            copy.wait()

    total = sum(part.shape[1] for part in parts)
    return kernel_call(
        body,
        "side_by_side",
        [*parts],
        in_specs=[LOCAL] * len(parts),
        out_specs=ANYWHERE,
        out_shape=jax.ShapeDtypeStruct((parts[0].shape[0], total), BF),
        scratch_shapes=[pltpu.SemaphoreType.DMA((len(parts),))],
    )


def blocks_in(rows, seqs, chips):
    return [
        ((s * chips + z) * 2 * rows, (z * seqs + s) * 2 * rows, 2 * rows)
        for z in range(chips)
        for s in range(seqs)
    ]


def inside(arrays, blocks):
    n = len(arrays)

    def body(*refs):
        rooms, sems = refs[2 * n : 3 * n], refs[3 * n]
        coming = loads(refs[:n], rooms, sems)
        for copy in coming:
            copy.start()
        for copy, source, out in zip(coming, rooms, refs[n : 2 * n]):
            copy.wait()
            for outer, inner, width in blocks:
                out[:, inner : inner + width] = source[:, outer : outer + width]

    return kernel_call(
        body,
        "inside",
        arrays,
        in_specs=[ANYWHERE] * n,
        out_shape=[jax.ShapeDtypeStruct(a.shape, a.dtype) for a in arrays],
        scratch_shapes=like(*arrays) + [pltpu.SemaphoreType.DMA((n,))],
    )


def outside(arrays, blocks):
    return inside(arrays, [(inner, outer, width) for outer, inner, width in blocks])


def join_ff(sums, w_gate_up, gain, gate_up_places, down_places, out_places):
    rows, total_width = w_gate_up.shape
    count = len(sums)

    def body(*refs):
        weights, gain, out, out_gain, out_down, out_out = refs[count:]
        total = jnp.zeros((rows, PAIR), F32)
        for source, listed in zip(refs[:count], gate_up_places):
            for owner, there, here, width in listed:
                for step in range(0, width, PAIR):
                    part = source[owner, :, there + step : there + step + PAIR].astype(F32)
                    at = slice(here + step, here + step + PAIR)
                    total += part * weights[:, at].astype(F32)
                    out[:, at] = part
        for source, listed in zip(refs[:count], down_places):
            for owner, there, here, width in listed:
                part = source[owner, :, there : there + width].astype(F32)
                out_down[:, here : here + width] = part
        for owner, there, here, width in out_places:
            part = refs[count - 1][owner, :, there : there + width].astype(F32)
            out_out[:, here : here + width] = part
        out_gain[...] = row(jnp.sum(total, 1, keepdims=True)) / gain[...].astype(F32)

    return kernel_call(
        body,
        "join_ff",
        [*sums, w_gate_up, gain],
        out_shape=[
            jax.ShapeDtypeStruct((rows, total_width), F32),
            jax.ShapeDtypeStruct((1, rows), F32),
            jax.ShapeDtypeStruct((rows, total_width // 2), F32),
            jax.ShapeDtypeStruct((rows, sum(p[3] for p in out_places)), F32),
        ],
    )


def join_qkv(sums, w_qkv, gain, qkv_places):
    rows, total_width = w_qkv.shape

    def body(source, weights, gain, out, out_gain):
        total = jnp.zeros((rows, PAIR), F32)
        for owner, there, here, width in qkv_places:
            part = source[owner, :, there : there + width].astype(F32)
            total += part * weights[:, here : here + width].astype(F32)
            out[:, here : here + width] = part
        out_gain[...] = row(jnp.sum(total, 1, keepdims=True)) / gain[...].astype(F32)

    return kernel_call(
        body,
        "join_qkv",
        [sums, w_qkv, gain],
        out_shape=[
            jax.ShapeDtypeStruct((rows, total_width), F32),
            jax.ShapeDtypeStruct((1, rows), F32),
        ],
    )


def flip(index, offset):
    weight = 1
    while weight <= offset:
        if offset & weight:
            index = index + weight - 2 * weight * ((index // weight) % 2)
        weight *= 2
    return index


def greet(partners):
    barrier = pltpu.get_barrier_semaphore()
    for partner in partners:
        pl.semaphore_signal(barrier, inc=1, device_id=partner, device_id_type=MESH)
    pl.semaphore_wait(barrier, len(partners))


def here():
    return lax.axis_index("seq"), lax.axis_index("core")


def bits_of(seqs):
    return [1 << bit for bit in range(seqs.bit_length() - 1)]


def cube_partners(seqs):
    me, core = here()
    partners = [{"seq": flip(me, bit), "core": core} for bit in bits_of(seqs)]
    return partners + [{"seq": me, "core": 1 - core}]


def all_partners(seqs):
    me, core = here()
    return [
        {"seq": flip(me, step), "core": core if same else 1 - core}
        for step in range(seqs)
        for same in (True, False)
        if step or not same
    ]


def orders_of(seqs):
    bits = bits_of(seqs)
    return [bits, bits[1:] + bits[:1]]


def remote(source, target, sems, at, device):
    return pltpu.make_async_remote_copy(
        src_ref=source,
        dst_ref=target,
        send_sem=sems[0].at[at],
        recv_sem=sems[1].at[at],
        device_id=device,
        device_id_type=MESH,
    )


def push(*where):
    copy = remote(*where)
    copy.start()
    return copy


def loads(sources, rooms, sems):
    copies = []
    for i, (source, room) in enumerate(zip(sources, rooms)):
        if isinstance(source, tuple):
            source = source[0].at[:, pl.ds(source[1], source[2])]
        copies.append(pltpu.make_async_copy(source, room, sems.at[i]))
    return copies


def like(*arrays):
    return [pltpu.VMEM(array.shape, array.dtype) for array in arrays]


def pair_sems(*shape):
    return [pltpu.SemaphoreType.DMA(shape)] * 2


def spread_scratch(seqs):
    return pair_sems(2, seqs) + pair_sems(2, seqs) + [pltpu.SemaphoreType.DMA]


class Spread:
    def __init__(self, own, out, scratch, rows=None):
        self.own, self.out = own, out
        self.rows = rows or pl.ds(0, own.shape[0])
        self.across, self.aside, self.local = scratch[0:2], scratch[2:4], scratch[4]
        self.me, self.core = here()
        self.half = out.shape[-1] // 2
        self.orders = orders_of(out.shape[1])
        self.phases = len(self.orders[0])

    def columns(self, ref, stream):
        return ref.at[self.rows, pl.ds(stream * self.half, self.half)]

    def place(self, offset, stream):
        return self.columns(self.out.at[self.core, flip(self.me, offset)], stream)

    def block(self, offset, stream):
        return self.place(offset, stream) if offset else self.columns(self.own, stream)

    def kept(self):
        return pltpu.make_async_copy(
            self.own.at[self.rows], self.out.at[self.core, self.me, self.rows], self.local
        )

    def swap(self, offset, stream):
        sibling = {"seq": self.me, "core": 1 - self.core}
        return remote(
            self.block(offset, stream),
            self.place(offset, stream),
            self.aside,
            (stream, offset),
            sibling,
        )

    def held(self, phase, stream):
        offsets = [0]
        for bit in self.orders[stream][:phase]:
            offsets += [offset + bit for offset in offsets]
        return offsets

    def moves(self, phase):
        found = []
        for stream in range(2):
            bit = self.orders[stream][phase]
            partner = {"seq": flip(self.me, bit), "core": self.core}
            for offset in self.held(phase, stream):
                copy = remote(
                    self.block(offset, stream),
                    self.place(offset, stream),
                    self.across,
                    (stream, offset + bit),
                    partner,
                )
                found.append((copy, offset + bit, stream))
        return found

    def begin(self):
        self.kept().start()
        for copy, _, _ in self.moves(0):
            copy.start()
        for stream in range(2):
            self.swap(0, stream).start()

    def arrive(self, phase):
        for copy, offset, stream in self.moves(phase):
            copy.wait_recv()
            self.swap(offset, stream).start()

    def step(self, phase):
        self.arrive(phase - 1)
        for copy, _, _ in self.moves(phase):
            copy.start()

    def finish(self):
        self.arrive(self.phases - 1)
        for phase in range(self.phases):
            for copy, _, _ in self.moves(phase):
                copy.wait_send()
        for stream in range(2):
            for offset in self.held(self.phases, stream):
                self.swap(offset, stream).wait()
        self.kept().wait()


def fold_rooms(seqs, tokens, width, made=True):
    return [
        pltpu.VMEM((seqs, tokens, width), BF),
        pltpu.VMEM((seqs, tokens, width) if made else (16, PAIR), BF),
        pltpu.VMEM((seqs, tokens, width), BF),
        pltpu.VMEM((2, seqs, tokens, width // 2), BF),
    ]


def fold_sems(seqs):
    return [pltpu.SemaphoreType.DMA((2,))] + pair_sems(seqs) + pair_sems(2, seqs)


class Fold:
    def __init__(self, terms, rooms, sems, rows, make=None):
        self.terms, self.make = terms, make
        self.own, self.give, self.total, self.got = rooms
        self.local, self.aside, self.across = sems[0], sems[1:3], sems[3:5]
        self.rows = rows
        self.me, self.core = here()
        self.seqs = self.total.shape[0]
        self.half = self.total.shape[-1] // 2
        self.orders = orders_of(self.seqs)
        self.phases = len(self.orders[0])

    def taken(self, mine):
        core, room = (self.core, self.own) if mine else (1 - self.core, self.give)
        return pltpu.make_async_copy(
            self.terms.at[core, :, self.rows],
            room.at[:, self.rows],
            self.local.at[1 if mine else 0],
        )

    def fill(self, room, core, at):
        width = room.shape[-1]
        tile = min(2 * BLOCK, width)

        def one(j, carry):
            columns = pl.ds(pl.multiple_of(j * tile, tile), tile)
            value = self.make(core, at, self.rows, columns)
            if self.terms is not None:
                value = value + room[at, self.rows, columns].astype(F32)
            room[at, self.rows, columns] = value.astype(BF)
            return carry

        lax.fori_loop(0, width // tile, one, 0)

    def swap(self, offset):
        at = flip(self.me, offset)
        source = self.give.at[at] if self.make else self.terms.at[1 - self.core, at]
        return remote(
            source.at[self.rows],
            self.total.at[at, self.rows],
            self.aside,
            (offset,),
            {"seq": self.me, "core": 1 - self.core},
        )

    def columns(self, stream):
        return pl.ds(stream * self.half, self.half)

    def moves(self, phase, stream, only=None):
        bit = self.orders[stream][phase]
        done = sum(self.orders[stream][:phase])
        partner = {"seq": flip(self.me, bit), "core": self.core}
        return [
            (
                remote(
                    self.total.at[flip(self.me, offset), self.rows, self.columns(stream)],
                    self.got.at[stream, offset, self.rows],
                    self.across,
                    (stream, offset),
                    partner,
                ),
                offset,
            )
            for offset in range(self.seqs - 1, -1, -1)
            if offset & bit and not offset & done and only in (None, offset)
        ]

    def add(self, work):
        count = self.rows.size
        step = min(32, count)

        def one(i, carry):
            work(pl.ds(pl.multiple_of(self.rows.start + i * step, step), step))
            return carry

        lax.fori_loop(0, count // step, one, 0)

    def load(self):
        if self.terms is not None:
            if self.make:
                self.taken(False).start()
            self.taken(True).start()

    def begin(self):
        if self.make and self.terms is not None:
            self.taken(False).wait()
        for offset in range(self.seqs - 1, -1, -1):
            if self.make:
                self.fill(self.give, 1 - self.core, flip(self.me, offset))
            self.swap(offset).start()

    def first(self):
        if self.terms is not None:
            self.taken(True).wait()
        for offset in range(self.seqs - 1, -1, -1):
            at = flip(self.me, offset)
            if self.make:
                self.fill(self.own, self.core, at)
            self.swap(offset).wait_recv()

            def add_sibling(rows, at=at):
                both = self.total[at, rows, :].astype(F32) + self.own[at, rows, :].astype(F32)
                self.total[at, rows, :] = both.astype(BF)

            self.add(add_sibling)
            for stream in range(2):
                for copy, _ in self.moves(0, stream, offset):
                    copy.start()

    def receive(self, phase, stream):
        bit = self.orders[stream][phase]
        for copy, offset in self.moves(phase, stream):
            copy.wait_recv()
            at = flip(self.me, offset - bit)

            def add_got(rows, at=at, offset=offset):
                columns = self.columns(stream)
                both = self.total[at, rows, columns].astype(F32) + self.got[
                    stream, offset, rows, :
                ].astype(F32)
                self.total[at, rows, columns] = both.astype(BF)

            self.add(add_got)

    def step(self, phase):
        for stream in range(2):
            self.receive(phase - 1, stream)
            for copy, _ in self.moves(phase, stream):
                copy.start()

    def last(self):
        for stream in range(2):
            self.receive(self.phases - 1, stream)

    def result(self, rows):
        return self.total[self.me, rows, :].astype(F32)

    def settle(self):
        for offset in range(self.seqs):
            self.swap(offset).wait_send()
        for phase in range(self.phases):
            for stream in range(2):
                for copy, _ in self.moves(phase, stream):
                    copy.wait_send()


def halves(count):
    return [pl.ds(i * (count // 2), count // 2) for i in range(2)]


def fold_then_spread(folds, spreads, work, aside=lambda: None):
    phases = folds[0].phases
    for fold in folds:
        fold.begin()
        fold.first()
    aside()
    for phase in range(1, phases):
        for fold in folds:
            fold.step(phase)
            aside()
    for fold, spread in zip(folds, spreads):
        fold.last()
        fold.add(work)
        spread.begin()
        aside()
    for phase in range(1, phases):
        for spread in spreads:
            spread.step(phase)
            aside()
    for spread in spreads:
        spread.finish()
    for fold in folds:
        fold.settle()


def by_rows(count, work):
    step = min(32, count)

    def one(i, carry):
        work(pl.ds(pl.multiple_of(i * step, step), step))
        return carry

    lax.fori_loop(0, count // step, one, 0)


def deal_scratch(pieces, seqs):
    blocks = [piece.shape[-2:] for piece in pieces]
    return (
        pair_sems(len(pieces), 2 * seqs)
        + [pltpu.SemaphoreType.DMA((2, len(pieces)))]
        + [pltpu.VMEM(block, piece.dtype) for block, piece in zip(blocks, pieces)]
    )


class Deal:
    def __init__(self, pieces, outs, scratch, core_first=False):
        self.pieces, self.outs = pieces, outs
        self.sems, self.local, self.rooms = scratch[:2], scratch[2], scratch[3:]
        self.me, self.core = here()
        self.core_first = core_first
        self.seqs = outs[0].shape[1 if core_first else 0]

    def piece(self, i, seq, core):
        piece, out = self.pieces[i], self.outs[i]
        return piece.at[seq, core] if len(piece.shape) == len(out.shape) else piece

    def place(self, i):
        out = self.outs[i]
        return out.at[self.core, self.me] if self.core_first else out.at[self.me, self.core]

    def copy(self, i, step, same):
        to_seq = flip(self.me, step)
        to_core = self.core if same else 1 - self.core
        return remote(
            self.piece(i, to_seq, to_core),
            self.place(i),
            self.sems,
            (i, 2 * step + (0 if same else 1)),
            {"seq": to_seq, "core": to_core},
        )

    def copies(self):
        return [
            self.copy(i, step, same)
            for i in range(len(self.pieces))
            for step in range(self.seqs)
            for same in (True, False)
            if step or not same
        ]

    def entering(self):
        return [
            pltpu.make_async_copy(
                self.piece(i, self.me, self.core), self.rooms[i], self.local.at[0, i]
            )
            for i in range(len(self.rooms))
        ]

    def leaving(self):
        return [
            pltpu.make_async_copy(
                self.rooms[i] if self.rooms else self.piece(i, self.me, self.core),
                self.place(i),
                self.local.at[1, i],
            )
            for i in range(len(self.outs))
        ]

    def begin(self):
        for copy in self.copies() + self.entering():
            copy.start()
        for copy in self.entering():
            copy.wait()
        for copy in self.leaving():
            copy.start()

    def arrive_from(self, step):
        if step:
            self.copy(0, step, True).wait_recv()
        else:
            for copy in self.leaving():
                copy.wait()
        self.copy(0, step, False).wait_recv()

    def arrive(self):
        for copy in self.copies():
            copy.wait_recv()
        for copy in self.leaving():
            copy.wait()

    def settle(self):
        for copy in self.copies():
            copy.wait_send()

    def finish(self):
        self.arrive()
        self.settle()


class Ring:
    def __init__(self, whole, sems, part):
        self.whole, self.sems, self.part = whole, sems, part
        self.count = whole.shape[0]
        self.chip = lax.axis_index("z")

    def hop(self, i):
        block = self.whole.at[lax.rem(self.chip + self.count - i, self.count)]
        block = block if self.part is None else block.at[self.part]
        following = lax.rem(self.chip + 1, self.count)
        return remote(block, block, self.sems, (i,), {"z": following})

    def preceding(self):
        return {"z": lax.rem(self.chip + self.count - 1, self.count)}

    def begin(self):
        self.hop(0).start()

    def step(self, i):
        self.hop(i - 1).wait_recv()
        if i < self.count - 1:
            self.hop(i).start()

    def settle(self):
        for i in range(self.count - 1):
            self.hop(i).wait_send()


def deal(pieces, number):
    count = len(pieces)
    seqs = pieces[0].shape[0]

    def body(*refs):
        greet(all_partners(seqs))
        work = Deal(refs[:count], refs[count : 2 * count], refs[2 * count :])
        work.begin()
        work.finish()

    return kernel_call(
        body,
        "deal",
        [*pieces],
        number,
        in_specs=[ANYWHERE] * count,
        out_specs=[ANYWHERE] * count,
        out_shape=[jax.ShapeDtypeStruct(piece.shape, BF) for piece in pieces],
        scratch_shapes=deal_scratch(pieces, seqs),
    )


def cut_into(out, parts):
    for source, places in parts:
        for owner, there, begin, width in places:
            part = source[:, begin : begin + width]
            out[owner // 2, owner % 2, :, there : there + width] = part


def column(row):
    count = row.shape[1]
    shape = (count, count)
    wide = jnp.broadcast_to(row.astype(F32), shape)
    same = lax.broadcasted_iota(jnp.int32, shape, 0) == lax.broadcasted_iota(jnp.int32, shape, 1)
    return jnp.sum(jnp.where(same, wide, 0.0), 1, keepdims=True)


def row(values):
    count = values.shape[0]
    shape = (count, count)
    wide = jnp.broadcast_to(values, shape)
    same = lax.broadcasted_iota(jnp.int32, shape, 0) == lax.broadcasted_iota(jnp.int32, shape, 1)
    return jnp.sum(jnp.where(same, wide, 0.0), 0, keepdims=True)


def frequencies():
    half = HEAD_DIM // 2
    inverse = ROPE_BASE ** (-2.0 * np.arange(half) / HEAD_DIM)
    return np.tile(inverse.astype(np.float32), (8, PAIR // half))


def start(arrays, gains, positions, plans, blocks, seqs, chips, number):
    tokens, w_qkv = arrays[0], arrays[2]
    count, width = tokens.shape
    rows = w_qkv.shape[0]
    (qkv_places, out_places, attend_cols), chunks = plans
    shape = (seqs, 2, rows)
    cuts = [shape + (cols,) for _, _, cols in chunks]
    more = len(chunks) - 1

    def body(*refs):
        sources, places, inverse = refs[:6], refs[8], refs[9]
        acts, whole, piece, tables, gains_out, *moved = refs[10:17]
        cut_out = refs[17 : 17 + more]
        scratch = refs[17 + more :]
        rooms, (sem, attend_cut), scratch = scratch[:6], scratch[6:8], scratch[8:]
        ff_cut, scratch = scratch[: 1 + more], scratch[1 + more :]
        turned, own, scratch = scratch[:2], scratch[2], scratch[3:]
        out_sem, left_sem, scratch = scratch[0], scratch[1], scratch[2:]
        ring_sems, scratch = scratch[: 2 * seqs], scratch[2 * seqs :]
        deal_sems, spread_sems, gain_sems = scratch[:12], scratch[12:17], scratch[17:19]
        own_places, all_places, all_tables, own_gains, all_gains, gain_rows = scratch[19:]
        coming = loads(sources, rooms, sem)
        for i in (2, 3, 0, 4, 5, 1):
            coming[i].start()
        own_places[...] = jnp.broadcast_to(places[...], own_places.shape)
        for i in range(2):
            one = jnp.broadcast_to(refs[6 + i][...].astype(F32), (8, rows))
            own_gains[:, i * rows : (i + 1) * rows] = one
        if 2 * rows < PAIR:
            own_gains[:, 2 * rows :] = jnp.zeros((8, PAIR - 2 * rows), F32)
        me_chip = lax.axis_index("z")
        rings = [
            Ring(whole, ring_sems[2 * i : 2 * i + 2], flip(lax.axis_index("seq"), i))
            for i in range(seqs)
        ]
        greet(all_partners(seqs) + [rings[0].preceding()])
        gain_deal = Deal([own_gains], [all_gains.at[me_chip]], deal_sems[9:12])
        gain_deal.begin()
        coming[2].wait()
        coming[3].wait()
        cut_into(attend_cut, [(rooms[2], qkv_places), (rooms[3], out_places)])
        attend_deal = Deal([attend_cut], [whole.at[me_chip]], deal_sems[:3])
        attend_deal.begin()
        place_deal = Deal([own_places], [all_places], deal_sems[3:6], True)
        place_deal.begin()
        gain_deal.arrive()
        gain_ring = Ring(all_gains, gain_sems, None)
        gain_ring.begin()
        attend_deal.arrive_from(0)
        rings[0].begin()
        coming[0].wait()
        for outer, inner, size in blocks:
            turned[0][:, inner : inner + size] = rooms[0][:, outer : outer + size]
        for i in range(1, max(seqs, chips)):
            if i < chips:
                gain_ring.step(i)
            if i < seqs:
                attend_deal.arrive_from(i)
                rings[i].begin()
        for chip in range(chips):
            for seq in range(seqs):
                for core in range(2):
                    begin = ((chip * seqs + seq) * 2 + core) * rows
                    for i in range(2):
                        gain_rows[i, :, begin : begin + rows] = all_gains[
                            chip, seq, core, :, i * rows : (i + 1) * rows
                        ]

        def norm(at):
            values = turned[0][at, :].astype(F32)
            own[at, :] = (values * norm_scale(values) * gain_rows[0, :1, :]).astype(BF)

        by_rows(count, norm)
        spreading = Spread(own, acts, spread_sems)
        spreading.begin()
        coming[4].wait()
        coming[5].wait()
        for out, (pair, single, _) in zip(ff_cut, chunks):
            cut_into(out, [(rooms[4], pair), (rooms[5], single)])
        coming[1].wait()
        for outer, inner, size in blocks:
            turned[1][:, inner : inner + size] = rooms[1][:, outer : outer + size]
        going = loads(list(turned) + list(ff_cut[1:]), list(moved) + list(cut_out), out_sem)
        for copy in going:
            copy.start()
        for phase in range(1, spreading.phases):
            spreading.step(phase)
        ff_deal = Deal([ff_cut[0]], [piece], deal_sems[6:9])
        ff_deal.begin()
        place_deal.arrive()

        def table(i, carry):
            at, seq = lax.div(i, seqs), lax.rem(i, seqs)
            angles = column(all_places[at, seq][:1]) * inverse[:1, :]
            lane = lax.broadcasted_iota(jnp.int32, angles.shape, 1)
            cosine = lane % HEAD_DIM < HEAD_DIM // 2
            all_tables[at, seq] = jnp.where(cosine, jnp.cos(angles), jnp.sin(angles))
            return carry

        for i in range(1, chips):
            for ring in rings:
                ring.step(i)
            if i <= 2:
                lax.fori_loop((i - 1) * seqs, i * seqs, table, 0)
            if i == 2:
                spreading.finish()
        leaving = loads([all_tables, gain_rows], [tables, gains_out], left_sem)
        for copy in leaving:
            copy.start()
        for ring in rings:
            ring.settle()
        attend_deal.settle()
        place_deal.settle()
        ff_deal.finish()
        gain_ring.settle()
        gain_deal.settle()
        for copy in going + leaving:
            copy.wait()

    like_tokens = jax.ShapeDtypeStruct((count, width), BF)
    deal_sem = pair_sems(1, 2 * seqs) + [pltpu.SemaphoreType.DMA((2, 1))]
    return kernel_call(
        body,
        "start",
        [*arrays, *gains, positions, frequencies()],
        number,
        in_specs=[ANYWHERE] * 6 + [LOCAL] * 4,
        out_specs=[ANYWHERE] * (7 + more),
        out_shape=[
            jax.ShapeDtypeStruct((2, seqs, count, width), BF),
            jax.ShapeDtypeStruct((chips,) + shape + (attend_cols,), BF),
            jax.ShapeDtypeStruct(cuts[0], BF),
            jax.ShapeDtypeStruct((2, seqs, count, PAIR), F32),
            jax.ShapeDtypeStruct((2, 8, width), F32),
            like_tokens,
            like_tokens,
        ]
        + [jax.ShapeDtypeStruct(cut, BF) for cut in cuts[1:]],
        scratch_shapes=like(*arrays)
        + [pltpu.SemaphoreType.DMA((6,)), pltpu.VMEM(shape + (attend_cols,), BF)]
        + [pltpu.VMEM(cut, BF) for cut in cuts]
        + [pltpu.VMEM((count, width), BF)] * 3
        + [pltpu.SemaphoreType.DMA((2 + more,)), pltpu.SemaphoreType.DMA((2,))]
        + pair_sems(chips) * seqs
        + deal_sem * 4
        + spread_scratch(seqs)
        + pair_sems(chips)
        + [pltpu.VMEM((8, count), jnp.int32), pltpu.VMEM((2, seqs, 8, count), jnp.int32)]
        + [pltpu.VMEM((2, seqs, count, PAIR), F32), pltpu.VMEM((8, PAIR), F32)]
        + [pltpu.VMEM((chips, seqs, 2, 8, PAIR), F32), pltpu.VMEM((2, 8, width), F32)],
    )


def two_way_scratch(seqs, count, width):
    return (
        [pltpu.VMEM((count, width), BF)]
        + fold_rooms(seqs, count, width)
        + fold_sems(seqs) * 2
        + spread_scratch(seqs) * 2
    )


def two_way(given, out, scratch, make):
    own, rooms, sems = scratch[0], scratch[1:5], scratch[5:]
    parts = halves(own.shape[0])
    folds = [
        Fold(given, rooms, sems[5 * i : 5 * i + 5], rows, make) for i, rows in enumerate(parts)
    ]
    sems = sems[10:]
    spreads = [Spread(own, out, sems[5 * i : 5 * i + 5], rows) for i, rows in enumerate(parts)]
    for fold in folds:
        fold.load()
    return folds, spreads, own


def product(left, right, seqs, count):
    def make(core, at, rows, columns):
        begin = pl.multiple_of((core * seqs + at) * count + rows.start, rows.size)
        return nt(left[pl.ds(begin, rows.size), :], right[columns, :])

    return make


def middle_acts(attended, weights, tokens, gains, seqs, number):
    count, width = tokens.shape
    cols = attended.shape[1]
    begin = weights.shape[1] - cols

    def body(left_in, given, source_in, gain, middle, out, left, right, source, sems, *scratch):
        coming = loads([left_in, (given, begin, cols), source_in], [left, right, source], sems)
        for copy in coming:
            copy.start()
        folds, spreads, own = two_way(None, out, scratch, product(left, right, seqs, count))
        greet(cube_partners(seqs))
        for copy in coming:
            copy.wait()

        def norm(rows):
            values = source[rows, :].astype(F32) + folds[0].result(rows)
            middle[rows, :] = values
            own[rows, :] = (values * norm_scale(values) * gain[1, :1, :]).astype(BF)

        fold_then_spread(folds, spreads, norm)

    return kernel_call(
        body,
        "middle_acts",
        [attended, weights, tokens, gains],
        number,
        in_specs=[ANYWHERE] * 3 + [LOCAL],
        out_specs=[LOCAL, ANYWHERE],
        out_shape=[
            jax.ShapeDtypeStruct((count, width), F32),
            jax.ShapeDtypeStruct((2, seqs, count, width), BF),
        ],
        scratch_shapes=like(attended)
        + [pltpu.VMEM((width, cols), BF)]
        + like(tokens)
        + [pltpu.SemaphoreType.DMA((3,))]
        + two_way_scratch(seqs, count, width),
    )


def middle_grad(terms, grad_both, cotangent, middle, hidden, weights, gains, number):
    _, seqs, count, width = terms.shape
    tokens = hidden[0].shape[0]
    n = len(hidden)
    block = min(BLOCK, tokens)
    tile = min(2 * BLOCK, width)
    blocks = tokens // block
    parts = [h.shape[1] for h in hidden]

    def body(given, *refs):
        sources, down = refs[: 3 + n], refs[3 + n : 3 + 2 * n]
        gain, grad, out, products = refs[3 + 2 * n : 7 + 2 * n]
        scratch = refs[7 + 2 * n :]
        left, upstream, values = scratch[:3]
        units, room, right = scratch[3 : 3 + n], scratch[3 + n : 3 + 2 * n], scratch[3 + 2 * n]
        stage, sems, leaving = scratch[4 + 2 * n : 7 + 2 * n]
        columns = [(down[i], 2 * parts[i], parts[i]) for i in range(n)]
        coming = loads(
            [sources[0], (down[-1], 0, 2 * parts[-1]), *sources[3:], *columns, *sources[1:3]],
            [left, right, *units, *room, upstream, values],
            sems,
        )
        for copy in coming[:2]:
            copy.start()
        make = product(left, right, seqs, count)
        folds, spreads, own = two_way(given, out, scratch[7 + 2 * n :], make)
        for copy in coming[2:]:
            copy.start()
        greet(cube_partners(seqs))
        for copy in coming[:2]:
            copy.wait()

        def leave(i):
            rows = pl.ds(i * block, block)
            return pltpu.make_async_copy(stage.at[i % 2], products.at[rows], leaving.at[i % 2])

        def multiply(i):
            if i == 0:
                for copy in coming[2:]:
                    copy.wait()
            if i >= 2:
                leave(i - 2).wait()

            def one(j, carry):
                columns = pl.ds(pl.multiple_of(j * tile, tile), tile)
                total = sum(
                    nt(units[k][pl.ds(i * block, block), :], room[k][columns, :])
                    for k in range(n)
                )
                stage[i % 2, :, columns] = total.astype(BF)
                return carry

            lax.fori_loop(0, width // tile, one, 0)
            leave(i).start()

        left_over = list(range(blocks))

        def aside():
            for _ in range(2 if len(left_over) == blocks else max(1, blocks // 8)):
                if left_over:
                    multiply(left_over.pop(0))

        def back(rows):
            held = values[rows, :]
            scale = norm_scale(held)
            result = upstream[rows, :].astype(F32) + norm_back(
                folds[0].result(rows) * gain[1, :1, :], held * scale, scale
            )
            grad[rows, :] = result
            own[rows, :] = result.astype(BF)

        fold_then_spread(folds, spreads, back, aside)
        while left_over:
            multiply(left_over.pop(0))
        for i in range(max(0, blocks - 2), blocks):
            leave(i).wait()

    return kernel_call(
        body,
        "middle_grad",
        [terms, grad_both, cotangent, middle, *hidden, *weights, gains],
        number,
        in_specs=[ANYWHERE] * (4 + 2 * n) + [LOCAL],
        out_specs=[LOCAL, ANYWHERE, ANYWHERE],
        out_shape=[
            jax.ShapeDtypeStruct((count, width), F32),
            jax.ShapeDtypeStruct(terms.shape, BF),
            jax.ShapeDtypeStruct((tokens, width), BF),
        ],
        scratch_shapes=like(grad_both, cotangent, middle, *hidden)
        + [pltpu.VMEM((width, part), BF) for part in parts]
        + [pltpu.VMEM((width, 2 * parts[-1]), BF), pltpu.VMEM((2, block, width), BF)]
        + [pltpu.SemaphoreType.DMA((4 + 2 * n,)), pltpu.SemaphoreType.DMA((2,))]
        + two_way_scratch(seqs, count, width),
    )


def input_grad(grad_mixed, weights, tokens, grad_middle, gains, seqs, number):
    count, width = tokens.shape
    cols = grad_mixed.shape[1]

    def body(left_in, given, source_in, held_in, gain, out, *scratch):
        left, right, source, held, sems, *scratch = scratch
        coming = loads(
            [left_in, (given, 0, cols), source_in, held_in], [left, right, source, held], sems
        )
        for copy in coming:
            copy.start()
        make = product(left, right, seqs, count)
        sems = scratch[4:]
        folds = [
            Fold(None, scratch[:4], sems[5 * i : 5 * i + 5], rows, make)
            for i, rows in enumerate(halves(count))
        ]
        greet(cube_partners(seqs))
        for copy in coming:
            copy.wait()
        for fold in folds:
            fold.begin()
            fold.first()
        for phase in range(1, folds[0].phases):
            for fold in folds:
                fold.step(phase)

        def back(rows):
            values = source[rows, :].astype(F32)
            scale = norm_scale(values)
            grad = folds[0].result(rows) * gain[0, :1, :]
            out[rows, :] = held[rows, :] + norm_back(grad, values * scale, scale)

        for fold in folds:
            fold.last()
            fold.add(back)
        for fold in folds:
            fold.settle()

    return kernel_call(
        body,
        "input_grad",
        [grad_mixed, weights, tokens, grad_middle, gains],
        number,
        in_specs=[ANYWHERE] * 4 + [LOCAL],
        out_specs=LOCAL,
        out_shape=jax.ShapeDtypeStruct((count, width), F32),
        scratch_shapes=like(grad_mixed)
        + [pltpu.VMEM((width, cols), BF)]
        + like(tokens, grad_middle)
        + [pltpu.SemaphoreType.DMA((4,))]
        + fold_rooms(seqs, count, width)
        + fold_sems(seqs) * 2,
    )


class Order:
    def __init__(self):
        self.latest = None

    def enter(self, values):
        if self.latest is None:
            return values
        return lax.optimization_barrier((values, self.latest))[0]

    def run(self, work, *values):
        result = work(*self.enter(values))
        self.latest = jax.tree.leaves(result)
        return result

    def take(self, values):
        if self.latest is not None:
            values = lax.optimization_barrier((values, self.latest))[0]
        self.latest = jax.tree.leaves(values)
        return values


def norm_scale(values):
    return lax.rsqrt(jnp.mean(values * values, -1, keepdims=True) + EPS)


def norm_back(grad, normed, scale):
    return scale * (grad - normed * jnp.mean(grad * normed, -1, keepdims=True))


def per_device(
    mesh, tokens, positions, w_qkv, w_out, gain_attn, w_gate_up, w_down, gain_mlp, cotangent
):
    order = Order()
    seqs, chips = mesh.shape["seq"], mesh.shape["z"]
    owners = 2 * seqs
    token_count, width = tokens.shape[1:]
    ff_width = w_down.shape[1]
    rows = w_qkv.shape[0]
    head_cols = width // owners
    ff_cols = ff_width // owners
    parts = chunk_widths(ff_cols)
    last = len(parts) - 1
    blocks = blocks_in(rows, seqs, chips)

    def by_place(piece):
        return piece.reshape(seqs, 2, rows, -1)

    def gathered(piece):
        piece = order.enter(piece).reshape(seqs, 2 * rows, -1)
        return lax.all_gather(piece, "z", axis=0, tiled=False)

    def flat(value):
        return order.take(value).reshape(width, -1)

    def summed(term):
        split = order.enter(term).reshape(chips, seqs, 2 * rows, -1)
        return lax.psum_scatter(split, "z", scatter_dimension=0, tiled=False)

    def rounded(left, right):
        return tn(left, right).astype(BF)

    qkv_places = list(qkv_columns(owners, head_cols))
    out_places = [(o, 3 * head_cols, o * head_cols, head_cols) for o in range(owners)]
    gate_up_places, down_places = ff_columns(owners, ff_cols)
    chunks = [
        (pair, single, 3 * part) for pair, single, part in zip(gate_up_places, down_places, parts)
    ]
    acts, attend_whole, ff_piece, table, gains, tokens_in, upstream_own, *ff_cut = order.run(
        lambda *a: start(
            a[:6],
            a[6:8],
            a[8],
            ((qkv_places, out_places, 4 * head_cols), chunks),
            blocks,
            seqs,
            chips,
            1,
        ),
        tokens[0],
        cotangent[0],
        w_qkv,
        w_out,
        w_gate_up,
        w_down,
        gain_attn[None],
        gain_mlp[None],
        positions,
    )
    acts = acts.reshape(-1, width)
    attend_whole = attend_whole.reshape(width, -1)
    table = table.reshape(-1, PAIR)
    ff_coming = [gathered(ff_piece)]

    qkv_cols = 3 * head_cols
    mixed = order.run(lambda a, w: nn(a, w[:, :qkv_cols]), acts, attend_whole)
    qkv, attended, logs, upstream, *ff_pieces = order.run(
        lambda m, t, u, *given: attend(m, t, SpreadBeside(seqs, u, given), 2, 3),
        mixed,
        table,
        upstream_own,
        *ff_cut,
    )
    ff_coming += [gathered(piece) for piece in ff_pieces]
    upstream = upstream.reshape(-1, width)
    middle, acts_mid = order.run(
        lambda a, w, x, g: middle_acts(a, w, x, g, seqs, 4),
        attended,
        attend_whole,
        tokens_in,
        gains,
    )
    acts_mid = acts_mid.reshape(-1, width)

    def feed_hidden(both):
        part = both.shape[1] // 2
        gate, up = both[:, :part], both[:, part:]
        return (gate * jax.nn.sigmoid(gate) * up).astype(BF)

    def feed_back(grad_hidden, both):
        part = both.shape[1] // 2
        gate, up = both[:, :part], both[:, part:]
        sigma = jax.nn.sigmoid(gate)
        grad_gate = grad_hidden * up * sigma * (1.0 + gate * (1.0 - sigma))
        grad_up = grad_hidden * gate * sigma
        return jnp.concatenate([grad_gate.astype(BF), grad_up.astype(BF)], 1)

    def both_terms(left, right, left_two, right_two):
        return [rounded(left, right), rounded(left_two, right_two)]

    def add_nt(left, right, total=None):
        result = nt(left, right)
        return (result if total is None else result + total.astype(F32)).astype(BF)

    ff_sums, hiddens, wholes = [], [], []
    norm_mid_terms = ()
    for chunk, part in enumerate(parts):
        cols = 2 * part
        whole = flat(ff_coming[chunk])
        both = order.run(lambda a, w: nn(a, w[:, :cols]), acts_mid, whole)
        hidden = order.run(feed_hidden, both)
        hiddens.append(hidden)
        wholes.append(whole)
        grad_hidden = order.run(lambda a, w: nn(a, w[:, cols:]), upstream, whole)
        grad_both = order.run(feed_back, grad_hidden, both)
        terms = order.run(both_terms, acts_mid, grad_both, upstream, hidden)
        if chunk < len(parts) - 1:
            ff_sums.append(summed(order.run(side_by_side, terms)))
        if chunk < len(parts) - 1:
            norm_mid_terms = (
                order.run(
                    lambda a, w, *t: add_nt(a, w[:, :cols], *t), grad_both, whole, *norm_mid_terms
                ),
            )

    grad_middle, grad_branch, outcome_terms = order.run(
        lambda *a: middle_grad(*a, 5),
        norm_mid_terms[0].reshape(2, seqs, token_count, width),
        grad_both,
        upstream_own,
        middle,
        hiddens,
        wholes,
        gains,
    )
    grad_branch = grad_branch.reshape(-1, width)

    terms.append(order.run(rounded, grad_branch, attended))
    ff_sums.append(summed(order.run(side_by_side, terms)))
    grad_attended = order.run(
        lambda a, w: nn(a, w[:, qkv_cols:]).astype(BF), grad_branch, attend_whole
    )
    first_rows = [by_place(order.take(value)) for value in ff_sums[:-1]]
    grad_mixed, outcome, *ff_dealt = order.run(
        lambda a, b, c, d, e, f, *given: attend_back(
            a, b, c, d, OutputBeside(seqs, e, f, given), 2, 6
        ),
        qkv,
        grad_attended,
        logs,
        table,
        outcome_terms.reshape(2, seqs, token_count, width),
        middle,
        *first_rows,
    )
    qkv_sum = summed(order.run(rounded, acts, grad_mixed))

    grad_inputs = order.run(
        lambda *a: input_grad(*a, seqs, 7),
        grad_mixed,
        attend_whole,
        tokens_in,
        grad_middle,
        gains,
    )
    last_rows = by_place(order.take(ff_sums[-1]))
    ff_dealt += order.run(lambda a: deal([a], 8), last_rows)
    out_at = [(o, 3 * parts[-1], o * head_cols, head_cols) for o in range(owners)]
    grad_gate_up, gain_two_sum, grad_down, grad_out = order.run(
        lambda w, g, *a: join_ff(a, w, g, gate_up_places, down_places, out_at),
        w_gate_up,
        gain_mlp[None],
        *[value.reshape(owners, rows, -1) for value in ff_dealt],
    )
    grad_inputs, outcome = order.run(lambda *a: outside(a, blocks), grad_inputs, outcome)
    qkv_rows = order.take(qkv_sum)
    (qkv_dealt,) = order.run(lambda a: deal([a], 9), by_place(qkv_rows))
    grad_qkv, gain_one_sum = order.run(
        lambda w, g, a: join_qkv(a, w, g, qkv_places),
        w_qkv,
        gain_attn[None],
        qkv_dealt.reshape(owners, rows, -1),
    )
    return (
        outcome[None],
        grad_inputs[None],
        grad_qkv,
        grad_out,
        gain_one_sum[0],
        grad_gate_up,
        grad_down,
        gain_two_sum[0],
    )


def solution(mesh):
    seqs, devices = mesh.shape["seq"], mesh.shape["fsdp"]
    parted = Mesh(mesh.devices.reshape(seqs, devices // 2, 2), ("seq", "z", "core"))
    tokens = P(("z", "core"), "seq", None)
    matrix = P(("seq", "z", "core"), None)
    vector = P(("seq", "z", "core"))
    return jax.shard_map(
        functools.partial(per_device, parted),
        mesh=parted,
        in_specs=(
            tokens,
            P(("z", "core"), "seq"),
            matrix,
            matrix,
            vector,
            matrix,
            matrix,
            vector,
            tokens,
        ),
        out_specs=(tokens, tokens, matrix, matrix, vector, matrix, matrix, vector),
        check_vma=False,
    )
```

```python
import functools
import math

import jax
import jax.numpy as jnp
import numpy as np
from jax import lax
from jax.experimental import pallas as pl
from jax.experimental.pallas import tpu as pltpu
from jax.sharding import Mesh, PartitionSpec as P

HEAD_DIM = 64
PAIR = 2 * HEAD_DIM
BLOCK = 256
EPS = 1e-05
ROPE_BASE = 130000.0
BF = jnp.bfloat16
F32 = jnp.float32
VMEM_MOST = 58 << 20
MESH = pl.DeviceIdType.MESH
ANYWHERE = pl.BlockSpec(memory_space=pltpu.HBM)
LOCAL = pl.BlockSpec(memory_space=pltpu.VMEM)


def room_for(spec, arrays):
    total = 8 << 20
    for room in spec.get("scratch_shapes", ()):
        if hasattr(room, "shape") and room.dtype in (BF, F32):
            total += math.prod(room.shape) * jnp.dtype(room.dtype).itemsize
    outs = spec["out_shape"] if isinstance(spec["out_shape"], list) else [spec["out_shape"]]
    specs = spec.get("out_specs", LOCAL), spec.get("in_specs", LOCAL)
    for values, given in zip((outs, arrays), specs):
        given = given if isinstance(given, list) else [given] * len(values)
        for value, where in zip(values, given):
            if where.block_shape is not None:
                total += 2 * math.prod(where.block_shape) * value.dtype.itemsize
            elif where is not ANYWHERE:
                total += math.prod(value.shape) * value.dtype.itemsize
    return min(total, VMEM_MOST)


def kernel_call(body, name, arrays, number=None, **spec):
    params = {"vmem_limit_bytes": room_for(spec, arrays)}
    if number is not None:
        params.update(vmem_limit_bytes=VMEM_MOST, collective_id=number, has_side_effects=True)
    return pl.pallas_call(
        body, name=name, compiler_params=pltpu.CompilerParams(**params), **spec
    )(*arrays)


def turn(x, cosine, sine):
    half = HEAD_DIM // 2
    lane = lax.broadcasted_iota(jnp.int32, x.shape, 1)
    swapped = jnp.where(
        lane % HEAD_DIM < half, pltpu.roll(x, PAIR - half, 1), pltpu.roll(x, half, 1)
    )
    return x * cosine + swapped * sine


def nt(left, right):
    return lax.dot_general(left, right, (((1,), (1,)), ((), ())), preferred_element_type=F32)


def tn(left, right):
    return lax.dot_general(left, right, (((0,), (0,)), ((), ())), preferred_element_type=F32)


def nn(left, right):
    return lax.dot_general(left, right, (((1,), (0,)), ((), ())), preferred_element_type=F32)


def masked_scores(queries, keys, block):
    scores = nt(queries, keys)
    rows = lax.broadcasted_iota(jnp.int32, (BLOCK, BLOCK), 0)
    cols = lax.broadcasted_iota(jnp.int32, (BLOCK, BLOCK), 1)
    last = jnp.where(cols <= rows, scores[:, block * BLOCK :], -1e30)
    return jnp.concatenate([scores[:, : block * BLOCK], last], 1) if block else last


def unpack(table):
    half = HEAD_DIM // 2
    cosine, sine = table[:, :half], table[:, half:HEAD_DIM]
    return (
        jnp.concatenate([cosine] * 4, 1),
        jnp.concatenate([-sine, sine] * 2, 1),
    )


def attend_body(mixed, table, qkv, out, logs):
    length = mixed.shape[0]
    cosine, sine = unpack(table[...])
    qkv[:, :PAIR] = turn(mixed[:, :PAIR], cosine, sine).astype(BF)
    qkv[:, PAIR : 2 * PAIR] = turn(mixed[:, PAIR : 2 * PAIR], cosine, sine).astype(BF)
    qkv[:, 2 * PAIR :] = mixed[:, 2 * PAIR :].astype(BF)
    scale = jnp.asarray(1.0 / math.sqrt(HEAD_DIM), BF)
    for block in range(length // BLOCK):
        at = pl.ds(block * BLOCK, BLOCK)
        seen = (block + 1) * BLOCK
        outs = []
        totals = []
        for low in (0, HEAD_DIM):
            high = low + HEAD_DIM
            queries = qkv[at, low:high] * scale
            scores = masked_scores(queries, qkv[:seen, PAIR + low : PAIR + high], block)
            highest = jnp.max(scores, -1, keepdims=True)
            weights = jnp.exp(scores - highest)
            summed = jnp.sum(weights, -1, keepdims=True)
            probs = (weights * (1.0 / summed)).astype(BF)
            outs.append(nn(probs, qkv[:seen, 2 * PAIR + low : 2 * PAIR + high]))
            totals.append(jnp.broadcast_to(highest + jnp.log(summed), (BLOCK, HEAD_DIM)))
        out[at, :] = jnp.concatenate(outs, 1).astype(BF)
        logs[at, :] = jnp.concatenate(totals, 1)


def attend_back_body(qkv, grad, logs, table, grad_qkv, grad_keys, grad_values):
    length = qkv.shape[0]
    scale = 1.0 / math.sqrt(HEAD_DIM)
    cosine, sine = unpack(table[...])
    last = length // BLOCK - 1
    for block in range(last, -1, -1):
        at = pl.ds(block * BLOCK, BLOCK)
        seen = (block + 1) * BLOCK
        rows = slice(block * BLOCK, seen)
        grad_queries = []
        for low in (0, HEAD_DIM):
            high = low + HEAD_DIM
            queries = qkv[at, low:high] * jnp.asarray(scale, BF)
            keys = qkv[:seen, PAIR + low : PAIR + high]
            upstream = grad[at, low:high]
            scores = masked_scores(queries, keys, block)
            probs = jnp.exp(scores - logs[at, low : low + 1])
            grad_probs = nt(upstream, qkv[:seen, 2 * PAIR + low : 2 * PAIR + high])
            inner = jnp.sum(probs * grad_probs, -1, keepdims=True)
            grad_scores = (probs * (grad_probs - inner)).astype(BF)
            grad_queries.append(nn(grad_scores, keys))
            for_keys = tn(grad_scores, queries)
            for_values = tn(probs.astype(BF), upstream)
            if block == last:
                grad_keys[:, low:high] = for_keys
                grad_values[:, low:high] = for_values
            else:
                grad_keys[:seen, low:high] += for_keys
                grad_values[:seen, low:high] += for_values
        rounded = (jnp.concatenate(grad_queries, 1) * scale).astype(BF).astype(F32)
        grad_qkv[at, :PAIR] = turn(rounded, cosine[rows], -sine[rows]).astype(BF)
    rounded = grad_keys[...].astype(BF).astype(F32)
    grad_qkv[:, PAIR : 2 * PAIR] = turn(rounded, cosine, -sine).astype(BF)
    grad_qkv[:, 2 * PAIR :] = grad_values[...].astype(BF)


def heads_call(body, name, arrays, kinds, outs, out_kinds, count, beside, number, scratch):
    tokens = arrays[0].shape[0]
    length = tokens // count
    pairs = arrays[0].shape[1] // (3 * PAIR)
    specs = {
        "wide": pl.BlockSpec((length, 3 * PAIR), lambda s, i: (s, i)),
        "one": pl.BlockSpec((length, PAIR), lambda s, i: (s, i)),
        "table": pl.BlockSpec((length, PAIR), lambda s, i: (s, 0)),
    }
    n_in, n_out = len(arrays), len(outs)
    more_in, more_out = len(beside.arrays), len(beside.outs)

    def whole(*refs):
        ins, given = refs[:n_in], refs[n_in : n_in + more_in]
        rest = refs[n_in + more_in :]
        results, made = rest[:n_out], rest[n_out : n_out + more_out]
        rest = rest[n_out + more_out :]
        room, held = rest[: len(beside.scratch)], rest[len(beside.scratch) :]
        step = pl.program_id(0) * pairs + pl.program_id(1)
        last = count * pairs - 1
        acts = beside.acts(given, made, room)
        when = [(2 * i * (last + 1) + len(acts) - 1) // (2 * len(acts) - 2) for i in range(len(acts))]
        for i, act in enumerate(acts):
            if when[i] <= last:
                pl.when(step == when[i])(act)
        body(*ins, *results, *held)

        @pl.when(step == last)
        def _():
            for i, act in enumerate(acts):
                if when[i] > last:
                    act()

    return kernel_call(
        whole,
        name,
        list(arrays) + list(beside.arrays),
        number,
        grid=(count, pairs),
        in_specs=[specs[kind] for kind in kinds] + [ANYWHERE] * more_in,
        out_specs=[specs[kind] for kind in out_kinds] + [ANYWHERE] * more_out,
        out_shape=list(outs) + list(beside.outs),
        scratch_shapes=list(beside.scratch) + scratch(length),
    )


class SpreadBeside:
    def __init__(self, seqs, own, pieces):
        self.seqs = seqs
        self.arrays = [own] + list(pieces)
        self.outs = [jax.ShapeDtypeStruct((2, seqs) + own.shape, BF)]
        self.outs += [jax.ShapeDtypeStruct(piece.shape, BF) for piece in pieces]
        self.scratch = [pltpu.VMEM(own.shape, BF), pltpu.SemaphoreType.DMA]
        self.scratch += spread_scratch(seqs)
        self.first = len(self.scratch)
        self.scratch += deal_scratch(pieces, seqs) if pieces else []

    def acts(self, given, made, room):
        def dealing():
            return Deal(given[1:], made[1:], room[self.first :])

        def spreading():
            return Spread(room[0], made[0], room[2:])

        def begin():
            copy = pltpu.make_async_copy(given[0], room[0], room[1])
            copy.start()
            greet(all_partners(self.seqs))
            copy.wait()
            spreading().begin()
            if given[1:]:
                dealing().begin()

        def finish():
            spreading().finish()
            if given[1:]:
                dealing().finish()

        def step(phase):
            return lambda: spreading().step(phase)

        return [begin] + [step(i) for i in range(1, len(bits_of(self.seqs)))] + [finish]


class OutputBeside:
    def __init__(self, seqs, terms, middle, pieces):
        self.seqs = seqs
        self.arrays = [terms, middle] + list(pieces)
        self.outs = [jax.ShapeDtypeStruct(middle.shape, BF)]
        self.outs += [jax.ShapeDtypeStruct(piece.shape, BF) for piece in pieces]
        self.scratch = [
            pltpu.VMEM(middle.shape, F32),
            pltpu.VMEM(middle.shape, BF),
            pltpu.SemaphoreType.DMA((2,)),
        ]
        self.scratch += fold_rooms(seqs, *middle.shape, False) + fold_sems(seqs)
        self.first = len(self.scratch)
        self.scratch += deal_scratch(pieces, seqs)

    def acts(self, given, made, room):
        held, rounded, sems = room[:3]

        def dealing():
            return Deal(given[2:], made[1:], room[self.first :])

        def folding():
            return Fold(given[0], room[3:7], room[7:12], pl.ds(0, held.shape[0]))

        def entering():
            return pltpu.make_async_copy(given[1], held, sems.at[0])

        def begin():
            entering().start()
            folding().load()
            greet(all_partners(self.seqs))
            folding().begin()
            dealing().begin()

        def finish():
            fold = folding()
            fold.last()
            entering().wait()

            def add(rows):
                rounded[rows, :] = (held[rows, :] + fold.result(rows)).astype(BF)

            fold.add(add)
            leaving = pltpu.make_async_copy(rounded, made[0], sems.at[1])
            leaving.start()
            fold.settle()
            dealing().finish()
            leaving.wait()

        def step(phase):
            return lambda: folding().step(phase)

        phases = len(bits_of(self.seqs))
        return [begin, lambda: folding().first()] + [step(i) for i in range(1, phases)] + [finish]


def attend(mixed, table, beside, count, number):
    tokens, cols = mixed.shape
    outs = [
        jax.ShapeDtypeStruct((tokens, cols), BF),
        jax.ShapeDtypeStruct((tokens, cols // 3), BF),
        jax.ShapeDtypeStruct((tokens, cols // 3), F32),
    ]
    return heads_call(
        attend_body,
        "attend",
        [mixed, table],
        ["wide", "table"],
        outs,
        ["wide", "one", "one"],
        count,
        beside,
        number,
        lambda length: [],
    )


def attend_back(qkv, grad, logs, table, beside, count, number):
    return heads_call(
        attend_back_body,
        "attend_back",
        [qkv, grad, logs, table],
        ["wide", "one", "one", "table"],
        [jax.ShapeDtypeStruct(qkv.shape, BF)],
        ["wide"],
        count,
        beside,
        number,
        lambda length: [pltpu.VMEM((length, PAIR), F32)] * 2,
    )


def qkv_columns(owners, cols):
    for owner in range(owners):
        for pair in range(cols // PAIR):
            for kind in range(3):
                there = (pair * 3 + kind) * PAIR
                yield owner, there, (kind * owners + owner) * cols + pair * PAIR, PAIR


def chunk_widths(cols):
    units = cols // PAIR
    first = max(1, (5 * units) // 8)
    return [n * PAIR for n in (first, units - first) if n]


def ff_columns(owners, cols):
    begin = 0
    gate_up, down = [], []
    for part in chunk_widths(cols):
        gate_up.append(
            [
                (owner, kind * part, (kind * owners + owner) * cols + begin, part)
                for owner in range(owners)
                for kind in range(2)
            ]
        )
        down.append([(owner, 2 * part, owner * cols + begin, part) for owner in range(owners)])
        begin += part
    return gate_up, down


def side_by_side(parts):
    begins = [sum(part.shape[1] for part in parts[:i]) for i in range(len(parts))]

    def body(*refs):
        out, sems = refs[-2:]
        copies = [
            pltpu.make_async_copy(
                refs[i], out.at[:, pl.ds(begins[i], part.shape[1])], sems.at[i]
            )
            for i, part in enumerate(parts)
        ]
        for copy in copies:
            copy.start()
        for copy in copies:
            copy.wait()

    total = sum(part.shape[1] for part in parts)
    return kernel_call(
        body,
        "side_by_side",
        [*parts],
        in_specs=[LOCAL] * len(parts),
        out_specs=ANYWHERE,
        out_shape=jax.ShapeDtypeStruct((parts[0].shape[0], total), BF),
        scratch_shapes=[pltpu.SemaphoreType.DMA((len(parts),))],
    )


def blocks_in(rows, seqs, chips):
    return [
        ((s * chips + z) * 2 * rows, (z * seqs + s) * 2 * rows, 2 * rows)
        for z in range(chips)
        for s in range(seqs)
    ]


def inside(arrays, blocks):
    n = len(arrays)

    def body(*refs):
        rooms, sems = refs[2 * n : 3 * n], refs[3 * n]
        coming = loads(refs[:n], rooms, sems)
        for copy in coming:
            copy.start()
        for copy, source, out in zip(coming, rooms, refs[n : 2 * n]):
            copy.wait()
            for outer, inner, width in blocks:
                out[:, inner : inner + width] = source[:, outer : outer + width]

    return kernel_call(
        body,
        "inside",
        arrays,
        in_specs=[ANYWHERE] * n,
        out_shape=[jax.ShapeDtypeStruct(a.shape, a.dtype) for a in arrays],
        scratch_shapes=like(*arrays) + [pltpu.SemaphoreType.DMA((n,))],
    )


def outside(arrays, blocks):
    return inside(arrays, [(inner, outer, width) for outer, inner, width in blocks])


def join_ff(sums, w_gate_up, gain, gate_up_places, down_places, out_places):
    rows, total_width = w_gate_up.shape
    count = len(sums)

    def body(*refs):
        weights, gain, out, out_gain, out_down, out_out = refs[count:]
        total = jnp.zeros((rows, PAIR), F32)
        for source, listed in zip(refs[:count], gate_up_places):
            for owner, there, here, width in listed:
                for step in range(0, width, PAIR):
                    part = source[owner, :, there + step : there + step + PAIR].astype(F32)
                    at = slice(here + step, here + step + PAIR)
                    total += part * weights[:, at].astype(F32)
                    out[:, at] = part
        for source, listed in zip(refs[:count], down_places):
            for owner, there, here, width in listed:
                part = source[owner, :, there : there + width].astype(F32)
                out_down[:, here : here + width] = part
        for owner, there, here, width in out_places:
            part = refs[count - 1][owner, :, there : there + width].astype(F32)
            out_out[:, here : here + width] = part
        out_gain[...] = row(jnp.sum(total, 1, keepdims=True)) / gain[...].astype(F32)

    return kernel_call(
        body,
        "join_ff",
        [*sums, w_gate_up, gain],
        out_shape=[
            jax.ShapeDtypeStruct((rows, total_width), F32),
            jax.ShapeDtypeStruct((1, rows), F32),
            jax.ShapeDtypeStruct((rows, total_width // 2), F32),
            jax.ShapeDtypeStruct((rows, sum(p[3] for p in out_places)), F32),
        ],
    )


def join_qkv(sums, w_qkv, gain, qkv_places):
    rows, total_width = w_qkv.shape

    def body(source, weights, gain, out, out_gain):
        total = jnp.zeros((rows, PAIR), F32)
        for owner, there, here, width in qkv_places:
            part = source[owner, :, there : there + width].astype(F32)
            total += part * weights[:, here : here + width].astype(F32)
            out[:, here : here + width] = part
        out_gain[...] = row(jnp.sum(total, 1, keepdims=True)) / gain[...].astype(F32)

    return kernel_call(
        body,
        "join_qkv",
        [sums, w_qkv, gain],
        out_shape=[
            jax.ShapeDtypeStruct((rows, total_width), F32),
            jax.ShapeDtypeStruct((1, rows), F32),
        ],
    )


def flip(index, offset):
    weight = 1
    while weight <= offset:
        if offset & weight:
            index = index + weight - 2 * weight * ((index // weight) % 2)
        weight *= 2
    return index


def greet(partners):
    barrier = pltpu.get_barrier_semaphore()
    for partner in partners:
        pl.semaphore_signal(barrier, inc=1, device_id=partner, device_id_type=MESH)
    pl.semaphore_wait(barrier, len(partners))


def here():
    return lax.axis_index("seq"), lax.axis_index("core")


def bits_of(seqs):
    return [1 << bit for bit in range(seqs.bit_length() - 1)]


def cube_partners(seqs):
    me, core = here()
    partners = [{"seq": flip(me, bit), "core": core} for bit in bits_of(seqs)]
    return partners + [{"seq": me, "core": 1 - core}]


def all_partners(seqs):
    me, core = here()
    return [
        {"seq": flip(me, step), "core": core if same else 1 - core}
        for step in range(seqs)
        for same in (True, False)
        if step or not same
    ]


def orders_of(seqs):
    bits = bits_of(seqs)
    return [bits, bits[1:] + bits[:1]]


def remote(source, target, sems, at, device):
    return pltpu.make_async_remote_copy(
        src_ref=source,
        dst_ref=target,
        send_sem=sems[0].at[at],
        recv_sem=sems[1].at[at],
        device_id=device,
        device_id_type=MESH,
    )


def push(*where):
    copy = remote(*where)
    copy.start()
    return copy


def loads(sources, rooms, sems):
    copies = []
    for i, (source, room) in enumerate(zip(sources, rooms)):
        if isinstance(source, tuple):
            source = source[0].at[:, pl.ds(source[1], source[2])]
        copies.append(pltpu.make_async_copy(source, room, sems.at[i]))
    return copies


def like(*arrays):
    return [pltpu.VMEM(array.shape, array.dtype) for array in arrays]


def pair_sems(*shape):
    return [pltpu.SemaphoreType.DMA(shape)] * 2


def spread_scratch(seqs):
    return pair_sems(2, seqs) + pair_sems(2, seqs) + [pltpu.SemaphoreType.DMA]


class Spread:
    def __init__(self, own, out, scratch, rows=None):
        self.own, self.out = own, out
        self.rows = rows or pl.ds(0, own.shape[0])
        self.across, self.aside, self.local = scratch[0:2], scratch[2:4], scratch[4]
        self.me, self.core = here()
        self.half = out.shape[-1] // 2
        self.orders = orders_of(out.shape[1])
        self.phases = len(self.orders[0])

    def columns(self, ref, stream):
        return ref.at[self.rows, pl.ds(stream * self.half, self.half)]

    def place(self, offset, stream):
        return self.columns(self.out.at[self.core, flip(self.me, offset)], stream)

    def block(self, offset, stream):
        return self.place(offset, stream) if offset else self.columns(self.own, stream)

    def kept(self):
        return pltpu.make_async_copy(
            self.own.at[self.rows], self.out.at[self.core, self.me, self.rows], self.local
        )

    def swap(self, offset, stream):
        sibling = {"seq": self.me, "core": 1 - self.core}
        return remote(
            self.block(offset, stream),
            self.place(offset, stream),
            self.aside,
            (stream, offset),
            sibling,
        )

    def held(self, phase, stream):
        offsets = [0]
        for bit in self.orders[stream][:phase]:
            offsets += [offset + bit for offset in offsets]
        return offsets

    def moves(self, phase):
        found = []
        for stream in range(2):
            bit = self.orders[stream][phase]
            partner = {"seq": flip(self.me, bit), "core": self.core}
            for offset in self.held(phase, stream):
                copy = remote(
                    self.block(offset, stream),
                    self.place(offset, stream),
                    self.across,
                    (stream, offset + bit),
                    partner,
                )
                found.append((copy, offset + bit, stream))
        return found

    def begin(self):
        self.kept().start()
        for copy, _, _ in self.moves(0):
            copy.start()
        for stream in range(2):
            self.swap(0, stream).start()

    def arrive(self, phase):
        for copy, offset, stream in self.moves(phase):
            copy.wait_recv()
            self.swap(offset, stream).start()

    def step(self, phase):
        self.arrive(phase - 1)
        for copy, _, _ in self.moves(phase):
            copy.start()

    def finish(self):
        self.arrive(self.phases - 1)
        for phase in range(self.phases):
            for copy, _, _ in self.moves(phase):
                copy.wait_send()
        for stream in range(2):
            for offset in self.held(self.phases, stream):
                self.swap(offset, stream).wait()
        self.kept().wait()


def fold_rooms(seqs, tokens, width, made=True):
    return [
        pltpu.VMEM((seqs, tokens, width), BF),
        pltpu.VMEM((seqs, tokens, width) if made else (16, PAIR), BF),
        pltpu.VMEM((seqs, tokens, width), BF),
        pltpu.VMEM((2, seqs, tokens, width // 2), BF),
    ]


def fold_sems(seqs):
    return [pltpu.SemaphoreType.DMA((2,))] + pair_sems(seqs) + pair_sems(2, seqs)


class Fold:
    def __init__(self, terms, rooms, sems, rows, make=None):
        self.terms, self.make = terms, make
        self.own, self.give, self.total, self.got = rooms
        self.local, self.aside, self.across = sems[0], sems[1:3], sems[3:5]
        self.rows = rows
        self.me, self.core = here()
        self.seqs = self.total.shape[0]
        self.half = self.total.shape[-1] // 2
        self.orders = orders_of(self.seqs)
        self.phases = len(self.orders[0])

    def taken(self, mine):
        core, room = (self.core, self.own) if mine else (1 - self.core, self.give)
        return pltpu.make_async_copy(
            self.terms.at[core, :, self.rows],
            room.at[:, self.rows],
            self.local.at[1 if mine else 0],
        )

    def fill(self, room, core, at):
        width = room.shape[-1]
        tile = min(2 * BLOCK, width)

        def one(j, carry):
            columns = pl.ds(pl.multiple_of(j * tile, tile), tile)
            value = self.make(core, at, self.rows, columns)
            if self.terms is not None:
                value = value + room[at, self.rows, columns].astype(F32)
            room[at, self.rows, columns] = value.astype(BF)
            return carry

        lax.fori_loop(0, width // tile, one, 0)

    def swap(self, offset):
        at = flip(self.me, offset)
        source = self.give.at[at] if self.make else self.terms.at[1 - self.core, at]
        return remote(
            source.at[self.rows],
            self.total.at[at, self.rows],
            self.aside,
            (offset,),
            {"seq": self.me, "core": 1 - self.core},
        )

    def columns(self, stream):
        return pl.ds(stream * self.half, self.half)

    def moves(self, phase, stream, only=None):
        bit = self.orders[stream][phase]
        done = sum(self.orders[stream][:phase])
        partner = {"seq": flip(self.me, bit), "core": self.core}
        return [
            (
                remote(
                    self.total.at[flip(self.me, offset), self.rows, self.columns(stream)],
                    self.got.at[stream, offset, self.rows],
                    self.across,
                    (stream, offset),
                    partner,
                ),
                offset,
            )
            for offset in range(self.seqs - 1, -1, -1)
            if offset & bit and not offset & done and only in (None, offset)
        ]

    def add(self, work):
        count = self.rows.size
        step = min(32, count)

        def one(i, carry):
            work(pl.ds(pl.multiple_of(self.rows.start + i * step, step), step))
            return carry

        lax.fori_loop(0, count // step, one, 0)

    def load(self):
        if self.terms is not None:
            if self.make:
                self.taken(False).start()
            self.taken(True).start()

    def begin(self):
        if self.make and self.terms is not None:
            self.taken(False).wait()
        for offset in range(self.seqs - 1, -1, -1):
            if self.make:
                self.fill(self.give, 1 - self.core, flip(self.me, offset))
            self.swap(offset).start()

    def first(self):
        if self.terms is not None:
            self.taken(True).wait()
        for offset in range(self.seqs - 1, -1, -1):
            at = flip(self.me, offset)
            if self.make:
                self.fill(self.own, self.core, at)
            self.swap(offset).wait_recv()

            def add_sibling(rows, at=at):
                both = self.total[at, rows, :].astype(F32) + self.own[at, rows, :].astype(F32)
                self.total[at, rows, :] = both.astype(BF)

            self.add(add_sibling)
            for stream in range(2):
                for copy, _ in self.moves(0, stream, offset):
                    copy.start()

    def receive(self, phase, stream):
        bit = self.orders[stream][phase]
        for copy, offset in self.moves(phase, stream):
            copy.wait_recv()
            at = flip(self.me, offset - bit)

            def add_got(rows, at=at, offset=offset):
                columns = self.columns(stream)
                both = self.total[at, rows, columns].astype(F32) + self.got[
                    stream, offset, rows, :
                ].astype(F32)
                self.total[at, rows, columns] = both.astype(BF)

            self.add(add_got)

    def step(self, phase):
        for stream in range(2):
            self.receive(phase - 1, stream)
            for copy, _ in self.moves(phase, stream):
                copy.start()

    def last(self):
        for stream in range(2):
            self.receive(self.phases - 1, stream)

    def result(self, rows):
        return self.total[self.me, rows, :].astype(F32)

    def settle(self):
        for offset in range(self.seqs):
            self.swap(offset).wait_send()
        for phase in range(self.phases):
            for stream in range(2):
                for copy, _ in self.moves(phase, stream):
                    copy.wait_send()


def halves(count):
    return [pl.ds(i * (count // 2), count // 2) for i in range(2)]


def fold_then_spread(folds, spreads, work, aside=lambda: None):
    phases = folds[0].phases
    for fold in folds:
        fold.begin()
        fold.first()
    aside()
    for phase in range(1, phases):
        for fold in folds:
            fold.step(phase)
            aside()
    for fold, spread in zip(folds, spreads):
        fold.last()
        fold.add(work)
        spread.begin()
        aside()
    for phase in range(1, phases):
        for spread in spreads:
            spread.step(phase)
            aside()
    for spread in spreads:
        spread.finish()
    for fold in folds:
        fold.settle()


def by_rows(count, work):
    step = min(32, count)

    def one(i, carry):
        work(pl.ds(pl.multiple_of(i * step, step), step))
        return carry

    lax.fori_loop(0, count // step, one, 0)


def deal_scratch(pieces, seqs):
    blocks = [piece.shape[-2:] for piece in pieces]
    return (
        pair_sems(len(pieces), 2 * seqs)
        + [pltpu.SemaphoreType.DMA((2, len(pieces)))]
        + [pltpu.VMEM(block, piece.dtype) for block, piece in zip(blocks, pieces)]
    )


class Deal:
    def __init__(self, pieces, outs, scratch, core_first=False):
        self.pieces, self.outs = pieces, outs
        self.sems, self.local, self.rooms = scratch[:2], scratch[2], scratch[3:]
        self.me, self.core = here()
        self.core_first = core_first
        self.seqs = outs[0].shape[1 if core_first else 0]

    def piece(self, i, seq, core):
        piece, out = self.pieces[i], self.outs[i]
        return piece.at[seq, core] if len(piece.shape) == len(out.shape) else piece

    def place(self, i):
        out = self.outs[i]
        return out.at[self.core, self.me] if self.core_first else out.at[self.me, self.core]

    def copy(self, i, step, same):
        to_seq = flip(self.me, step)
        to_core = self.core if same else 1 - self.core
        return remote(
            self.piece(i, to_seq, to_core),
            self.place(i),
            self.sems,
            (i, 2 * step + (0 if same else 1)),
            {"seq": to_seq, "core": to_core},
        )

    def copies(self):
        return [
            self.copy(i, step, same)
            for i in range(len(self.pieces))
            for step in range(self.seqs)
            for same in (True, False)
            if step or not same
        ]

    def entering(self):
        return [
            pltpu.make_async_copy(
                self.piece(i, self.me, self.core), self.rooms[i], self.local.at[0, i]
            )
            for i in range(len(self.rooms))
        ]

    def leaving(self):
        return [
            pltpu.make_async_copy(
                self.rooms[i] if self.rooms else self.piece(i, self.me, self.core),
                self.place(i),
                self.local.at[1, i],
            )
            for i in range(len(self.outs))
        ]

    def begin(self):
        for copy in self.copies() + self.entering():
            copy.start()
        for copy in self.entering():
            copy.wait()
        for copy in self.leaving():
            copy.start()

    def arrive_from(self, step):
        if step:
            self.copy(0, step, True).wait_recv()
        else:
            for copy in self.leaving():
                copy.wait()
        self.copy(0, step, False).wait_recv()

    def arrive(self):
        for copy in self.copies():
            copy.wait_recv()
        for copy in self.leaving():
            copy.wait()

    def settle(self):
        for copy in self.copies():
            copy.wait_send()

    def finish(self):
        self.arrive()
        self.settle()


class Ring:
    def __init__(self, whole, sems, part):
        self.whole, self.sems, self.part = whole, sems, part
        self.count = whole.shape[0]
        self.chip = lax.axis_index("z")

    def hop(self, i):
        block = self.whole.at[lax.rem(self.chip + self.count - i, self.count)]
        block = block if self.part is None else block.at[self.part]
        following = lax.rem(self.chip + 1, self.count)
        return remote(block, block, self.sems, (i,), {"z": following})

    def preceding(self):
        return {"z": lax.rem(self.chip + self.count - 1, self.count)}

    def begin(self):
        self.hop(0).start()

    def step(self, i):
        self.hop(i - 1).wait_recv()
        if i < self.count - 1:
            self.hop(i).start()

    def settle(self):
        for i in range(self.count - 1):
            self.hop(i).wait_send()


def deal(pieces, number):
    count = len(pieces)
    seqs = pieces[0].shape[0]

    def body(*refs):
        greet(all_partners(seqs))
        work = Deal(refs[:count], refs[count : 2 * count], refs[2 * count :])
        work.begin()
        work.finish()

    return kernel_call(
        body,
        "deal",
        [*pieces],
        number,
        in_specs=[ANYWHERE] * count,
        out_specs=[ANYWHERE] * count,
        out_shape=[jax.ShapeDtypeStruct(piece.shape, BF) for piece in pieces],
        scratch_shapes=deal_scratch(pieces, seqs),
    )


def cut_into(out, parts):
    for source, places in parts:
        for owner, there, begin, width in places:
            part = source[:, begin : begin + width]
            out[owner // 2, owner % 2, :, there : there + width] = part


def column(row):
    count = row.shape[1]
    shape = (count, count)
    wide = jnp.broadcast_to(row.astype(F32), shape)
    same = lax.broadcasted_iota(jnp.int32, shape, 0) == lax.broadcasted_iota(jnp.int32, shape, 1)
    return jnp.sum(jnp.where(same, wide, 0.0), 1, keepdims=True)


def row(values):
    count = values.shape[0]
    shape = (count, count)
    wide = jnp.broadcast_to(values, shape)
    same = lax.broadcasted_iota(jnp.int32, shape, 0) == lax.broadcasted_iota(jnp.int32, shape, 1)
    return jnp.sum(jnp.where(same, wide, 0.0), 0, keepdims=True)


def frequencies():
    half = HEAD_DIM // 2
    inverse = ROPE_BASE ** (-2.0 * np.arange(half) / HEAD_DIM)
    return np.tile(inverse.astype(np.float32), (8, PAIR // half))


def start(arrays, gains, positions, plans, blocks, seqs, chips, number):
    tokens, w_qkv = arrays[0], arrays[2]
    count, width = tokens.shape
    rows = w_qkv.shape[0]
    (qkv_places, out_places, attend_cols), chunks = plans
    shape = (seqs, 2, rows)
    cuts = [shape + (cols,) for _, _, cols in chunks]
    more = len(chunks) - 1

    def body(*refs):
        sources, places, inverse = refs[:6], refs[8], refs[9]
        acts, whole, piece, tables, gains_out, *moved = refs[10:17]
        cut_out = refs[17 : 17 + more]
        scratch = refs[17 + more :]
        rooms, (sem, attend_cut), scratch = scratch[:6], scratch[6:8], scratch[8:]
        ff_cut, scratch = scratch[: 1 + more], scratch[1 + more :]
        turned, own, scratch = scratch[:2], scratch[2], scratch[3:]
        out_sem, left_sem, scratch = scratch[0], scratch[1], scratch[2:]
        ring_sems, scratch = scratch[: 2 * seqs], scratch[2 * seqs :]
        deal_sems, spread_sems, gain_sems = scratch[:12], scratch[12:17], scratch[17:19]
        own_places, all_places, all_tables, own_gains, all_gains, gain_rows = scratch[19:]
        coming = loads(sources, rooms, sem)
        for i in (2, 3, 0, 4, 5, 1):
            coming[i].start()
        own_places[...] = jnp.broadcast_to(places[...], own_places.shape)
        for i in range(2):
            one = jnp.broadcast_to(refs[6 + i][...].astype(F32), (8, rows))
            own_gains[:, i * rows : (i + 1) * rows] = one
        if 2 * rows < PAIR:
            own_gains[:, 2 * rows :] = jnp.zeros((8, PAIR - 2 * rows), F32)
        me_chip = lax.axis_index("z")
        rings = [
            Ring(whole, ring_sems[2 * i : 2 * i + 2], flip(lax.axis_index("seq"), i))
            for i in range(seqs)
        ]
        greet(all_partners(seqs) + [rings[0].preceding()])
        gain_deal = Deal([own_gains], [all_gains.at[me_chip]], deal_sems[9:12])
        gain_deal.begin()
        coming[2].wait()
        coming[3].wait()
        cut_into(attend_cut, [(rooms[2], qkv_places), (rooms[3], out_places)])
        attend_deal = Deal([attend_cut], [whole.at[me_chip]], deal_sems[:3])
        attend_deal.begin()
        place_deal = Deal([own_places], [all_places], deal_sems[3:6], True)
        place_deal.begin()
        gain_deal.arrive()
        gain_ring = Ring(all_gains, gain_sems, None)
        gain_ring.begin()
        attend_deal.arrive_from(0)
        rings[0].begin()
        coming[0].wait()
        for outer, inner, size in blocks:
            turned[0][:, inner : inner + size] = rooms[0][:, outer : outer + size]
        for i in range(1, max(seqs, chips)):
            if i < chips:
                gain_ring.step(i)
            if i < seqs:
                attend_deal.arrive_from(i)
                rings[i].begin()
        for chip in range(chips):
            for seq in range(seqs):
                for core in range(2):
                    begin = ((chip * seqs + seq) * 2 + core) * rows
                    for i in range(2):
                        gain_rows[i, :, begin : begin + rows] = all_gains[
                            chip, seq, core, :, i * rows : (i + 1) * rows
                        ]

        def norm(at):
            values = turned[0][at, :].astype(F32)
            own[at, :] = (values * norm_scale(values) * gain_rows[0, :1, :]).astype(BF)

        by_rows(count, norm)
        spreading = Spread(own, acts, spread_sems)
        spreading.begin()
        coming[4].wait()
        coming[5].wait()
        for out, (pair, single, _) in zip(ff_cut, chunks):
            cut_into(out, [(rooms[4], pair), (rooms[5], single)])
        coming[1].wait()
        for outer, inner, size in blocks:
            turned[1][:, inner : inner + size] = rooms[1][:, outer : outer + size]
        going = loads(list(turned) + list(ff_cut[1:]), list(moved) + list(cut_out), out_sem)
        for copy in going:
            copy.start()
        for ring in rings[: seqs - 1]:
            ring.step(1)
        for phase in range(1, spreading.phases):
            spreading.step(phase)
        rings[-1].step(1)
        ff_deal = Deal([ff_cut[0]], [piece], deal_sems[6:9])
        ff_deal.begin()
        place_deal.arrive()

        def table(i, carry):
            at, seq = lax.div(i, seqs), lax.rem(i, seqs)
            angles = column(all_places[at, seq][:1]) * inverse[:1, :]
            lane = lax.broadcasted_iota(jnp.int32, angles.shape, 1)
            cosine = lane % HEAD_DIM < HEAD_DIM // 2
            all_tables[at, seq] = jnp.where(cosine, jnp.cos(angles), jnp.sin(angles))
            return carry

        for i in range(1, chips):
            for ring in rings:
                if i > 1:
                    ring.step(i)
            if i <= 2:
                lax.fori_loop((i - 1) * seqs, i * seqs, table, 0)
            if i == 2:
                spreading.finish()
        leaving = loads([all_tables, gain_rows], [tables, gains_out], left_sem)
        for copy in leaving:
            copy.start()
        for ring in rings:
            ring.settle()
        attend_deal.settle()
        place_deal.settle()
        ff_deal.finish()
        gain_ring.settle()
        gain_deal.settle()
        for copy in going + leaving:
            copy.wait()

    like_tokens = jax.ShapeDtypeStruct((count, width), BF)
    deal_sem = pair_sems(1, 2 * seqs) + [pltpu.SemaphoreType.DMA((2, 1))]
    return kernel_call(
        body,
        "start",
        [*arrays, *gains, positions, frequencies()],
        number,
        in_specs=[ANYWHERE] * 6 + [LOCAL] * 4,
        out_specs=[ANYWHERE] * (7 + more),
        out_shape=[
            jax.ShapeDtypeStruct((2, seqs, count, width), BF),
            jax.ShapeDtypeStruct((chips,) + shape + (attend_cols,), BF),
            jax.ShapeDtypeStruct(cuts[0], BF),
            jax.ShapeDtypeStruct((2, seqs, count, PAIR), F32),
            jax.ShapeDtypeStruct((2, 8, width), F32),
            like_tokens,
            like_tokens,
        ]
        + [jax.ShapeDtypeStruct(cut, BF) for cut in cuts[1:]],
        scratch_shapes=like(*arrays)
        + [pltpu.SemaphoreType.DMA((6,)), pltpu.VMEM(shape + (attend_cols,), BF)]
        + [pltpu.VMEM(cut, BF) for cut in cuts]
        + [pltpu.VMEM((count, width), BF)] * 3
        + [pltpu.SemaphoreType.DMA((2 + more,)), pltpu.SemaphoreType.DMA((2,))]
        + pair_sems(chips) * seqs
        + deal_sem * 4
        + spread_scratch(seqs)
        + pair_sems(chips)
        + [pltpu.VMEM((8, count), jnp.int32), pltpu.VMEM((2, seqs, 8, count), jnp.int32)]
        + [pltpu.VMEM((2, seqs, count, PAIR), F32), pltpu.VMEM((8, PAIR), F32)]
        + [pltpu.VMEM((chips, seqs, 2, 8, PAIR), F32), pltpu.VMEM((2, 8, width), F32)],
    )


def two_way_scratch(seqs, count, width):
    return (
        [pltpu.VMEM((count, width), BF)]
        + fold_rooms(seqs, count, width)
        + fold_sems(seqs) * 2
        + spread_scratch(seqs) * 2
    )


def two_way(given, out, scratch, make):
    own, rooms, sems = scratch[0], scratch[1:5], scratch[5:]
    parts = halves(own.shape[0])
    folds = [
        Fold(given, rooms, sems[5 * i : 5 * i + 5], rows, make) for i, rows in enumerate(parts)
    ]
    sems = sems[10:]
    spreads = [Spread(own, out, sems[5 * i : 5 * i + 5], rows) for i, rows in enumerate(parts)]
    for fold in folds:
        fold.load()
    return folds, spreads, own


def product(left, right, seqs, count):
    def make(core, at, rows, columns):
        begin = pl.multiple_of((core * seqs + at) * count + rows.start, rows.size)
        return nt(left[pl.ds(begin, rows.size), :], right[columns, :])

    return make


def middle_acts(attended, weights, tokens, gains, seqs, number):
    count, width = tokens.shape
    cols = attended.shape[1]
    begin = weights.shape[1] - cols

    def body(left_in, given, source_in, gain, middle, out, left, right, source, sems, *scratch):
        coming = loads([left_in, (given, begin, cols), source_in], [left, right, source], sems)
        for copy in coming:
            copy.start()
        folds, spreads, own = two_way(None, out, scratch, product(left, right, seqs, count))
        greet(cube_partners(seqs))
        for copy in coming:
            copy.wait()

        def norm(rows):
            values = source[rows, :].astype(F32) + folds[0].result(rows)
            middle[rows, :] = values
            own[rows, :] = (values * norm_scale(values) * gain[1, :1, :]).astype(BF)

        fold_then_spread(folds, spreads, norm)

    return kernel_call(
        body,
        "middle_acts",
        [attended, weights, tokens, gains],
        number,
        in_specs=[ANYWHERE] * 3 + [LOCAL],
        out_specs=[LOCAL, ANYWHERE],
        out_shape=[
            jax.ShapeDtypeStruct((count, width), F32),
            jax.ShapeDtypeStruct((2, seqs, count, width), BF),
        ],
        scratch_shapes=like(attended)
        + [pltpu.VMEM((width, cols), BF)]
        + like(tokens)
        + [pltpu.SemaphoreType.DMA((3,))]
        + two_way_scratch(seqs, count, width),
    )


def middle_grad(terms, grad_both, cotangent, middle, hidden, weights, gains, number):
    _, seqs, count, width = terms.shape
    tokens = hidden[0].shape[0]
    n = len(hidden)
    block = min(BLOCK, tokens)
    tile = min(2 * BLOCK, width)
    blocks = tokens // block
    parts = [h.shape[1] for h in hidden]

    def body(given, *refs):
        sources, down = refs[: 3 + n], refs[3 + n : 3 + 2 * n]
        gain, grad, out, products = refs[3 + 2 * n : 7 + 2 * n]
        scratch = refs[7 + 2 * n :]
        left, upstream, values = scratch[:3]
        units, room, right = scratch[3 : 3 + n], scratch[3 + n : 3 + 2 * n], scratch[3 + 2 * n]
        stage, sems, leaving = scratch[4 + 2 * n : 7 + 2 * n]
        columns = [(down[i], 2 * parts[i], parts[i]) for i in range(n)]
        coming = loads(
            [sources[0], (down[-1], 0, 2 * parts[-1]), *sources[3:], *columns, *sources[1:3]],
            [left, right, *units, *room, upstream, values],
            sems,
        )
        for copy in coming[:2]:
            copy.start()
        make = product(left, right, seqs, count)
        folds, spreads, own = two_way(given, out, scratch[7 + 2 * n :], make)
        for copy in coming[2:]:
            copy.start()
        greet(cube_partners(seqs))
        for copy in coming[:2]:
            copy.wait()

        def leave(i):
            rows = pl.ds(i * block, block)
            return pltpu.make_async_copy(stage.at[i % 2], products.at[rows], leaving.at[i % 2])

        def multiply(i):
            if i == 0:
                for copy in coming[2:]:
                    copy.wait()
            if i >= 2:
                leave(i - 2).wait()

            def one(j, carry):
                columns = pl.ds(pl.multiple_of(j * tile, tile), tile)
                total = sum(
                    nt(units[k][pl.ds(i * block, block), :], room[k][columns, :])
                    for k in range(n)
                )
                stage[i % 2, :, columns] = total.astype(BF)
                return carry

            lax.fori_loop(0, width // tile, one, 0)
            leave(i).start()

        left_over = list(range(blocks))

        def aside():
            for _ in range(2 if len(left_over) == blocks else max(1, blocks // 8)):
                if left_over:
                    multiply(left_over.pop(0))

        def back(rows):
            held = values[rows, :]
            scale = norm_scale(held)
            result = upstream[rows, :].astype(F32) + norm_back(
                folds[0].result(rows) * gain[1, :1, :], held * scale, scale
            )
            grad[rows, :] = result
            own[rows, :] = result.astype(BF)

        fold_then_spread(folds, spreads, back, aside)
        while left_over:
            multiply(left_over.pop(0))
        for i in range(max(0, blocks - 2), blocks):
            leave(i).wait()

    return kernel_call(
        body,
        "middle_grad",
        [terms, grad_both, cotangent, middle, *hidden, *weights, gains],
        number,
        in_specs=[ANYWHERE] * (4 + 2 * n) + [LOCAL],
        out_specs=[LOCAL, ANYWHERE, ANYWHERE],
        out_shape=[
            jax.ShapeDtypeStruct((count, width), F32),
            jax.ShapeDtypeStruct(terms.shape, BF),
            jax.ShapeDtypeStruct((tokens, width), BF),
        ],
        scratch_shapes=like(grad_both, cotangent, middle, *hidden)
        + [pltpu.VMEM((width, part), BF) for part in parts]
        + [pltpu.VMEM((width, 2 * parts[-1]), BF), pltpu.VMEM((2, block, width), BF)]
        + [pltpu.SemaphoreType.DMA((4 + 2 * n,)), pltpu.SemaphoreType.DMA((2,))]
        + two_way_scratch(seqs, count, width),
    )


def input_grad(grad_mixed, weights, tokens, grad_middle, gains, seqs, number):
    count, width = tokens.shape
    cols = grad_mixed.shape[1]

    def body(left_in, given, source_in, held_in, gain, out, *scratch):
        left, right, source, held, sems, *scratch = scratch
        coming = loads(
            [left_in, (given, 0, cols), source_in, held_in], [left, right, source, held], sems
        )
        for copy in coming:
            copy.start()
        make = product(left, right, seqs, count)
        sems = scratch[4:]
        folds = [
            Fold(None, scratch[:4], sems[5 * i : 5 * i + 5], rows, make)
            for i, rows in enumerate(halves(count))
        ]
        greet(cube_partners(seqs))
        for copy in coming:
            copy.wait()
        for fold in folds:
            fold.begin()
            fold.first()
        for phase in range(1, folds[0].phases):
            for fold in folds:
                fold.step(phase)

        def back(rows):
            values = source[rows, :].astype(F32)
            scale = norm_scale(values)
            grad = folds[0].result(rows) * gain[0, :1, :]
            out[rows, :] = held[rows, :] + norm_back(grad, values * scale, scale)

        for fold in folds:
            fold.last()
            fold.add(back)
        for fold in folds:
            fold.settle()

    return kernel_call(
        body,
        "input_grad",
        [grad_mixed, weights, tokens, grad_middle, gains],
        number,
        in_specs=[ANYWHERE] * 4 + [LOCAL],
        out_specs=LOCAL,
        out_shape=jax.ShapeDtypeStruct((count, width), F32),
        scratch_shapes=like(grad_mixed)
        + [pltpu.VMEM((width, cols), BF)]
        + like(tokens, grad_middle)
        + [pltpu.SemaphoreType.DMA((4,))]
        + fold_rooms(seqs, count, width)
        + fold_sems(seqs) * 2,
    )


class Order:
    def __init__(self):
        self.latest = None

    def enter(self, values):
        if self.latest is None:
            return values
        return lax.optimization_barrier((values, self.latest))[0]

    def run(self, work, *values):
        result = work(*self.enter(values))
        self.latest = jax.tree.leaves(result)
        return result

    def take(self, values):
        if self.latest is not None:
            values = lax.optimization_barrier((values, self.latest))[0]
        self.latest = jax.tree.leaves(values)
        return values


def norm_scale(values):
    return lax.rsqrt(jnp.mean(values * values, -1, keepdims=True) + EPS)


def norm_back(grad, normed, scale):
    return scale * (grad - normed * jnp.mean(grad * normed, -1, keepdims=True))


def per_device(
    mesh, tokens, positions, w_qkv, w_out, gain_attn, w_gate_up, w_down, gain_mlp, cotangent
):
    order = Order()
    seqs, chips = mesh.shape["seq"], mesh.shape["z"]
    owners = 2 * seqs
    token_count, width = tokens.shape[1:]
    ff_width = w_down.shape[1]
    rows = w_qkv.shape[0]
    head_cols = width // owners
    ff_cols = ff_width // owners
    parts = chunk_widths(ff_cols)
    last = len(parts) - 1
    blocks = blocks_in(rows, seqs, chips)

    def by_place(piece):
        return piece.reshape(seqs, 2, rows, -1)

    def gathered(piece):
        piece = order.enter(piece).reshape(seqs, 2 * rows, -1)
        return lax.all_gather(piece, "z", axis=0, tiled=False)

    def flat(value):
        return order.take(value).reshape(width, -1)

    def summed(term):
        split = order.enter(term).reshape(chips, seqs, 2 * rows, -1)
        return lax.psum_scatter(split, "z", scatter_dimension=0, tiled=False)

    def rounded(left, right):
        return tn(left, right).astype(BF)

    qkv_places = list(qkv_columns(owners, head_cols))
    out_places = [(o, 3 * head_cols, o * head_cols, head_cols) for o in range(owners)]
    gate_up_places, down_places = ff_columns(owners, ff_cols)
    chunks = [
        (pair, single, 3 * part) for pair, single, part in zip(gate_up_places, down_places, parts)
    ]
    acts, attend_whole, ff_piece, table, gains, tokens_in, upstream_own, *ff_cut = order.run(
        lambda *a: start(
            a[:6],
            a[6:8],
            a[8],
            ((qkv_places, out_places, 4 * head_cols), chunks),
            blocks,
            seqs,
            chips,
            1,
        ),
        tokens[0],
        cotangent[0],
        w_qkv,
        w_out,
        w_gate_up,
        w_down,
        gain_attn[None],
        gain_mlp[None],
        positions,
    )
    acts = acts.reshape(-1, width)
    attend_whole = attend_whole.reshape(width, -1)
    table = table.reshape(-1, PAIR)
    ff_coming = [gathered(ff_piece)]

    qkv_cols = 3 * head_cols
    mixed = order.run(lambda a, w: nn(a, w[:, :qkv_cols]), acts, attend_whole)
    qkv, attended, logs, upstream, *ff_pieces = order.run(
        lambda m, t, u, *given: attend(m, t, SpreadBeside(seqs, u, given), 2, 3),
        mixed,
        table,
        upstream_own,
        *ff_cut,
    )
    ff_coming += [gathered(piece) for piece in ff_pieces]
    upstream = upstream.reshape(-1, width)
    middle, acts_mid = order.run(
        lambda a, w, x, g: middle_acts(a, w, x, g, seqs, 4),
        attended,
        attend_whole,
        tokens_in,
        gains,
    )
    acts_mid = acts_mid.reshape(-1, width)

    def feed_hidden(both):
        part = both.shape[1] // 2
        gate, up = both[:, :part], both[:, part:]
        return (gate * jax.nn.sigmoid(gate) * up).astype(BF)

    def feed_back(grad_hidden, both):
        part = both.shape[1] // 2
        gate, up = both[:, :part], both[:, part:]
        sigma = jax.nn.sigmoid(gate)
        grad_gate = grad_hidden * up * sigma * (1.0 + gate * (1.0 - sigma))
        grad_up = grad_hidden * gate * sigma
        return jnp.concatenate([grad_gate.astype(BF), grad_up.astype(BF)], 1)

    def both_terms(left, right, left_two, right_two):
        return [rounded(left, right), rounded(left_two, right_two)]

    def add_nt(left, right, total=None):
        result = nt(left, right)
        return (result if total is None else result + total.astype(F32)).astype(BF)

    ff_sums, hiddens, wholes = [], [], []
    norm_mid_terms = ()
    for chunk, part in enumerate(parts):
        cols = 2 * part
        whole = flat(ff_coming[chunk])
        both = order.run(lambda a, w: nn(a, w[:, :cols]), acts_mid, whole)
        hidden = order.run(feed_hidden, both)
        hiddens.append(hidden)
        wholes.append(whole)
        grad_hidden = order.run(lambda a, w: nn(a, w[:, cols:]), upstream, whole)
        grad_both = order.run(feed_back, grad_hidden, both)
        terms = order.run(both_terms, acts_mid, grad_both, upstream, hidden)
        if chunk < len(parts) - 1:
            ff_sums.append(summed(order.run(side_by_side, terms)))
        if chunk < len(parts) - 1:
            norm_mid_terms = (
                order.run(
                    lambda a, w, *t: add_nt(a, w[:, :cols], *t), grad_both, whole, *norm_mid_terms
                ),
            )

    grad_middle, grad_branch, outcome_terms = order.run(
        lambda *a: middle_grad(*a, 5),
        norm_mid_terms[0].reshape(2, seqs, token_count, width),
        grad_both,
        upstream_own,
        middle,
        hiddens,
        wholes,
        gains,
    )
    grad_branch = grad_branch.reshape(-1, width)

    terms.append(order.run(rounded, grad_branch, attended))
    ff_sums.append(summed(order.run(side_by_side, terms)))
    grad_attended = order.run(
        lambda a, w: nn(a, w[:, qkv_cols:]).astype(BF), grad_branch, attend_whole
    )
    first_rows = [by_place(order.take(value)) for value in ff_sums[:-1]]
    grad_mixed, outcome, *ff_dealt = order.run(
        lambda a, b, c, d, e, f, *given: attend_back(
            a, b, c, d, OutputBeside(seqs, e, f, given), 2, 6
        ),
        qkv,
        grad_attended,
        logs,
        table,
        outcome_terms.reshape(2, seqs, token_count, width),
        middle,
        *first_rows,
    )
    qkv_sum = summed(order.run(rounded, acts, grad_mixed))

    grad_inputs = order.run(
        lambda *a: input_grad(*a, seqs, 7),
        grad_mixed,
        attend_whole,
        tokens_in,
        grad_middle,
        gains,
    )
    last_rows = by_place(order.take(ff_sums[-1]))
    ff_dealt += order.run(lambda a: deal([a], 8), last_rows)
    out_at = [(o, 3 * parts[-1], o * head_cols, head_cols) for o in range(owners)]
    grad_gate_up, gain_two_sum, grad_down, grad_out = order.run(
        lambda w, g, *a: join_ff(a, w, g, gate_up_places, down_places, out_at),
        w_gate_up,
        gain_mlp[None],
        *[value.reshape(owners, rows, -1) for value in ff_dealt],
    )
    grad_inputs, outcome = order.run(lambda *a: outside(a, blocks), grad_inputs, outcome)
    qkv_rows = order.take(qkv_sum)
    (qkv_dealt,) = order.run(lambda a: deal([a], 9), by_place(qkv_rows))
    grad_qkv, gain_one_sum = order.run(
        lambda w, g, a: join_qkv(a, w, g, qkv_places),
        w_qkv,
        gain_attn[None],
        qkv_dealt.reshape(owners, rows, -1),
    )
    return (
        outcome[None],
        grad_inputs[None],
        grad_qkv,
        grad_out,
        gain_one_sum[0],
        grad_gate_up,
        grad_down,
        gain_two_sum[0],
    )


def solution(mesh):
    seqs, devices = mesh.shape["seq"], mesh.shape["fsdp"]
    parted = Mesh(mesh.devices.reshape(seqs, devices // 2, 2), ("seq", "z", "core"))
    tokens = P(("z", "core"), "seq", None)
    matrix = P(("seq", "z", "core"), None)
    vector = P(("seq", "z", "core"))
    return jax.shard_map(
        functools.partial(per_device, parted),
        mesh=parted,
        in_specs=(
            tokens,
            P(("z", "core"), "seq"),
            matrix,
            matrix,
            vector,
            matrix,
            matrix,
            vector,
            tokens,
        ),
        out_specs=(tokens, tokens, matrix, matrix, vector, matrix, matrix, vector),
        check_vma=False,
    )
```

```python
import functools
import math

import jax
import jax.numpy as jnp
import numpy as np
from jax import lax
from jax.experimental import pallas as pl
from jax.experimental.pallas import tpu as pltpu
from jax.sharding import Mesh, PartitionSpec as P

HEAD_DIM = 64
PAIR = 2 * HEAD_DIM
BLOCK = 256
EPS = 1e-05
ROPE_BASE = 130000.0
BF = jnp.bfloat16
F32 = jnp.float32
VMEM_MOST = 58 << 20
MESH = pl.DeviceIdType.MESH
ANYWHERE = pl.BlockSpec(memory_space=pltpu.HBM)
LOCAL = pl.BlockSpec(memory_space=pltpu.VMEM)


def room_for(spec, arrays):
    total = 8 << 20
    for room in spec.get("scratch_shapes", ()):
        if hasattr(room, "shape") and room.dtype in (BF, F32):
            total += math.prod(room.shape) * jnp.dtype(room.dtype).itemsize
    outs = spec["out_shape"] if isinstance(spec["out_shape"], list) else [spec["out_shape"]]
    specs = spec.get("out_specs", LOCAL), spec.get("in_specs", LOCAL)
    for values, given in zip((outs, arrays), specs):
        given = given if isinstance(given, list) else [given] * len(values)
        for value, where in zip(values, given):
            if where.block_shape is not None:
                total += 2 * math.prod(where.block_shape) * value.dtype.itemsize
            elif where is not ANYWHERE:
                total += math.prod(value.shape) * value.dtype.itemsize
    return min(total, VMEM_MOST)


def kernel_call(body, name, arrays, number=None, near=False, **spec):
    params = {"vmem_limit_bytes": room_for(spec, arrays)}
    if number is not None:
        if not near:
            params.update(vmem_limit_bytes=VMEM_MOST)
        params.update(collective_id=number, has_side_effects=True)
    return pl.pallas_call(
        body, name=name, compiler_params=pltpu.CompilerParams(**params), **spec
    )(*arrays)


def turn(x, cosine, sine):
    half = HEAD_DIM // 2
    lane = lax.broadcasted_iota(jnp.int32, x.shape, 1)
    swapped = jnp.where(
        lane % HEAD_DIM < half, pltpu.roll(x, PAIR - half, 1), pltpu.roll(x, half, 1)
    )
    return x * cosine + swapped * sine


def nt(left, right):
    return lax.dot_general(left, right, (((1,), (1,)), ((), ())), preferred_element_type=F32)


def tn(left, right):
    return lax.dot_general(left, right, (((0,), (0,)), ((), ())), preferred_element_type=F32)


def nn(left, right):
    return lax.dot_general(left, right, (((1,), (0,)), ((), ())), preferred_element_type=F32)


def masked_scores(queries, keys, block):
    scores = nt(queries, keys)
    rows = lax.broadcasted_iota(jnp.int32, (BLOCK, BLOCK), 0)
    cols = lax.broadcasted_iota(jnp.int32, (BLOCK, BLOCK), 1)
    last = jnp.where(cols <= rows, scores[:, block * BLOCK :], -1e30)
    return jnp.concatenate([scores[:, : block * BLOCK], last], 1) if block else last


def unpack(table):
    half = HEAD_DIM // 2
    cosine, sine = table[:, :half], table[:, half:HEAD_DIM]
    return (
        jnp.concatenate([cosine] * 4, 1),
        jnp.concatenate([-sine, sine] * 2, 1),
    )


def attend_body(mixed, table, qkv, out, logs):
    length = mixed.shape[0]
    cosine, sine = unpack(table[...])
    qkv[:, :PAIR] = turn(mixed[:, :PAIR], cosine, sine).astype(BF)
    qkv[:, PAIR : 2 * PAIR] = turn(mixed[:, PAIR : 2 * PAIR], cosine, sine).astype(BF)
    qkv[:, 2 * PAIR :] = mixed[:, 2 * PAIR :].astype(BF)
    scale = jnp.asarray(1.0 / math.sqrt(HEAD_DIM), BF)
    for block in range(length // BLOCK):
        at = pl.ds(block * BLOCK, BLOCK)
        seen = (block + 1) * BLOCK
        outs = []
        totals = []
        for low in (0, HEAD_DIM):
            high = low + HEAD_DIM
            queries = qkv[at, low:high] * scale
            scores = masked_scores(queries, qkv[:seen, PAIR + low : PAIR + high], block)
            highest = jnp.max(scores, -1, keepdims=True)
            weights = jnp.exp(scores - highest)
            summed = jnp.sum(weights, -1, keepdims=True)
            probs = (weights * (1.0 / summed)).astype(BF)
            outs.append(nn(probs, qkv[:seen, 2 * PAIR + low : 2 * PAIR + high]))
            totals.append(jnp.broadcast_to(highest + jnp.log(summed), (BLOCK, HEAD_DIM)))
        out[at, :] = jnp.concatenate(outs, 1).astype(BF)
        logs[at, :] = jnp.concatenate(totals, 1)


def attend_back_body(qkv, grad, logs, table, grad_qkv, grad_keys, grad_values):
    length = qkv.shape[0]
    scale = 1.0 / math.sqrt(HEAD_DIM)
    cosine, sine = unpack(table[...])
    last = length // BLOCK - 1
    for block in range(last, -1, -1):
        at = pl.ds(block * BLOCK, BLOCK)
        seen = (block + 1) * BLOCK
        rows = slice(block * BLOCK, seen)
        grad_queries = []
        for low in (0, HEAD_DIM):
            high = low + HEAD_DIM
            queries = qkv[at, low:high] * jnp.asarray(scale, BF)
            keys = qkv[:seen, PAIR + low : PAIR + high]
            upstream = grad[at, low:high]
            scores = masked_scores(queries, keys, block)
            probs = jnp.exp(scores - logs[at, low : low + 1])
            grad_probs = nt(upstream, qkv[:seen, 2 * PAIR + low : 2 * PAIR + high])
            inner = jnp.sum(probs * grad_probs, -1, keepdims=True)
            grad_scores = (probs * (grad_probs - inner)).astype(BF)
            grad_queries.append(nn(grad_scores, keys))
            for_keys = tn(grad_scores, queries)
            for_values = tn(probs.astype(BF), upstream)
            if block == last:
                grad_keys[:, low:high] = for_keys
                grad_values[:, low:high] = for_values
            else:
                grad_keys[:seen, low:high] += for_keys
                grad_values[:seen, low:high] += for_values
        rounded = (jnp.concatenate(grad_queries, 1) * scale).astype(BF).astype(F32)
        grad_qkv[at, :PAIR] = turn(rounded, cosine[rows], -sine[rows]).astype(BF)
    rounded = grad_keys[...].astype(BF).astype(F32)
    grad_qkv[:, PAIR : 2 * PAIR] = turn(rounded, cosine, -sine).astype(BF)
    grad_qkv[:, 2 * PAIR :] = grad_values[...].astype(BF)


def heads_call(body, name, arrays, kinds, outs, out_kinds, count, beside, number, scratch):
    tokens = arrays[0].shape[0]
    length = tokens // count
    pairs = arrays[0].shape[1] // (3 * PAIR)
    specs = {
        "wide": pl.BlockSpec((length, 3 * PAIR), lambda s, i: (s, i)),
        "one": pl.BlockSpec((length, PAIR), lambda s, i: (s, i)),
        "table": pl.BlockSpec((length, PAIR), lambda s, i: (s, 0)),
    }
    n_in, n_out = len(arrays), len(outs)
    more_in, more_out = len(beside.arrays), len(beside.outs)

    def whole(*refs):
        ins, given = refs[:n_in], refs[n_in : n_in + more_in]
        rest = refs[n_in + more_in :]
        results, made = rest[:n_out], rest[n_out : n_out + more_out]
        rest = rest[n_out + more_out :]
        room, held = rest[: len(beside.scratch)], rest[len(beside.scratch) :]
        step = pl.program_id(0) * pairs + pl.program_id(1)
        last = count * pairs - 1
        acts = beside.acts(given, made, room)
        when = [(2 * i * (last + 1) + len(acts) - 1) // (2 * len(acts) - 2) for i in range(len(acts))]
        for i, act in enumerate(acts):
            if when[i] <= last:
                pl.when(step == when[i])(act)
        body(*ins, *results, *held)

        @pl.when(step == last)
        def _():
            for i, act in enumerate(acts):
                if when[i] > last:
                    act()

    return kernel_call(
        whole,
        name,
        list(arrays) + list(beside.arrays),
        number,
        grid=(count, pairs),
        in_specs=[specs[kind] for kind in kinds] + [ANYWHERE] * more_in,
        out_specs=[specs[kind] for kind in out_kinds] + [ANYWHERE] * more_out,
        out_shape=list(outs) + list(beside.outs),
        scratch_shapes=list(beside.scratch) + scratch(length),
    )


class SpreadBeside:
    def __init__(self, seqs, own, pieces):
        self.seqs = seqs
        self.arrays = [own] + list(pieces)
        self.outs = [jax.ShapeDtypeStruct((2, seqs) + own.shape, BF)]
        self.outs += [jax.ShapeDtypeStruct(piece.shape, BF) for piece in pieces]
        self.scratch = [pltpu.VMEM(own.shape, BF), pltpu.SemaphoreType.DMA]
        self.scratch += spread_scratch(seqs)
        self.first = len(self.scratch)
        self.scratch += deal_scratch(pieces, seqs) if pieces else []

    def acts(self, given, made, room):
        def dealing():
            return Deal(given[1:], made[1:], room[self.first :])

        def spreading():
            return Spread(room[0], made[0], room[2:])

        def begin():
            copy = pltpu.make_async_copy(given[0], room[0], room[1])
            copy.start()
            greet(all_partners(self.seqs))
            copy.wait()
            spreading().begin()
            if given[1:]:
                dealing().begin()

        def finish():
            spreading().finish()
            if given[1:]:
                dealing().finish()

        def step(phase):
            return lambda: spreading().step(phase)

        return [begin] + [step(i) for i in range(1, len(bits_of(self.seqs)))] + [finish]


class OutputBeside:
    def __init__(self, seqs, terms, middle, pieces):
        self.seqs = seqs
        self.arrays = [terms, middle] + list(pieces)
        self.outs = [jax.ShapeDtypeStruct(middle.shape, BF)]
        self.outs += [jax.ShapeDtypeStruct(piece.shape, BF) for piece in pieces]
        self.scratch = [
            pltpu.VMEM(middle.shape, F32),
            pltpu.VMEM(middle.shape, BF),
            pltpu.SemaphoreType.DMA((2,)),
        ]
        self.scratch += fold_rooms(seqs, *middle.shape, False) + fold_sems(seqs)
        self.first = len(self.scratch)
        self.scratch += deal_scratch(pieces, seqs)

    def acts(self, given, made, room):
        held, rounded, sems = room[:3]

        def dealing():
            return Deal(given[2:], made[1:], room[self.first :])

        def folding():
            return Fold(given[0], room[3:7], room[7:12], pl.ds(0, held.shape[0]))

        def entering():
            return pltpu.make_async_copy(given[1], held, sems.at[0])

        def begin():
            entering().start()
            folding().load()
            greet(all_partners(self.seqs))
            folding().begin()
            dealing().begin()

        def finish():
            fold = folding()
            fold.last()
            entering().wait()

            def add(rows):
                rounded[rows, :] = (held[rows, :] + fold.result(rows)).astype(BF)

            fold.add(add)
            leaving = pltpu.make_async_copy(rounded, made[0], sems.at[1])
            leaving.start()
            fold.settle()
            dealing().finish()
            leaving.wait()

        def step(phase):
            return lambda: folding().step(phase)

        phases = len(bits_of(self.seqs))
        return [begin, lambda: folding().first()] + [step(i) for i in range(1, phases)] + [finish]


def attend(mixed, table, beside, count, number):
    tokens, cols = mixed.shape
    outs = [
        jax.ShapeDtypeStruct((tokens, cols), BF),
        jax.ShapeDtypeStruct((tokens, cols // 3), BF),
        jax.ShapeDtypeStruct((tokens, cols // 3), F32),
    ]
    return heads_call(
        attend_body,
        "attend",
        [mixed, table],
        ["wide", "table"],
        outs,
        ["wide", "one", "one"],
        count,
        beside,
        number,
        lambda length: [],
    )


def attend_back(qkv, grad, logs, table, beside, count, number):
    return heads_call(
        attend_back_body,
        "attend_back",
        [qkv, grad, logs, table],
        ["wide", "one", "one", "table"],
        [jax.ShapeDtypeStruct(qkv.shape, BF)],
        ["wide"],
        count,
        beside,
        number,
        lambda length: [pltpu.VMEM((length, PAIR), F32)] * 2,
    )


def qkv_columns(owners, cols):
    for owner in range(owners):
        for pair in range(cols // PAIR):
            for kind in range(3):
                there = (pair * 3 + kind) * PAIR
                yield owner, there, (kind * owners + owner) * cols + pair * PAIR, PAIR


def chunk_widths(cols):
    units = cols // PAIR
    first = max(1, (5 * units) // 8)
    return [n * PAIR for n in (first, units - first) if n]


def ff_columns(owners, cols):
    begin = 0
    gate_up, down = [], []
    for part in chunk_widths(cols):
        gate_up.append(
            [
                (owner, kind * part, (kind * owners + owner) * cols + begin, part)
                for owner in range(owners)
                for kind in range(2)
            ]
        )
        down.append([(owner, 2 * part, owner * cols + begin, part) for owner in range(owners)])
        begin += part
    return gate_up, down


def side_by_side(parts):
    begins = [sum(part.shape[1] for part in parts[:i]) for i in range(len(parts))]

    def body(*refs):
        out, sems = refs[-2:]
        copies = [
            pltpu.make_async_copy(
                refs[i], out.at[:, pl.ds(begins[i], part.shape[1])], sems.at[i]
            )
            for i, part in enumerate(parts)
        ]
        for copy in copies:
            copy.start()
        for copy in copies:
            copy.wait()

    total = sum(part.shape[1] for part in parts)
    return kernel_call(
        body,
        "side_by_side",
        [*parts],
        in_specs=[LOCAL] * len(parts),
        out_specs=ANYWHERE,
        out_shape=jax.ShapeDtypeStruct((parts[0].shape[0], total), BF),
        scratch_shapes=[pltpu.SemaphoreType.DMA((len(parts),))],
    )


def blocks_in(rows, seqs, chips):
    return [
        ((s * chips + z) * 2 * rows, (z * seqs + s) * 2 * rows, 2 * rows)
        for z in range(chips)
        for s in range(seqs)
    ]


def inside(arrays, blocks):
    n = len(arrays)

    def body(*refs):
        rooms, sems = refs[2 * n : 3 * n], refs[3 * n]
        coming = loads(refs[:n], rooms, sems)
        for copy in coming:
            copy.start()
        for copy, source, out in zip(coming, rooms, refs[n : 2 * n]):
            copy.wait()
            for outer, inner, width in blocks:
                out[:, inner : inner + width] = source[:, outer : outer + width]

    return kernel_call(
        body,
        "inside",
        arrays,
        in_specs=[ANYWHERE] * n,
        out_shape=[jax.ShapeDtypeStruct(a.shape, a.dtype) for a in arrays],
        scratch_shapes=like(*arrays) + [pltpu.SemaphoreType.DMA((n,))],
    )


def outside(arrays, blocks):
    return inside(arrays, [(inner, outer, width) for outer, inner, width in blocks])


def join_ff(sums, w_gate_up, gain, gate_up_places, down_places, out_places):
    rows, total_width = w_gate_up.shape
    count = len(sums)

    def body(*refs):
        weights, gain, out, out_gain, out_down, out_out = refs[count:]
        total = jnp.zeros((rows, PAIR), F32)
        for source, listed in zip(refs[:count], gate_up_places):
            for owner, there, here, width in listed:
                for step in range(0, width, PAIR):
                    part = source[owner, :, there + step : there + step + PAIR].astype(F32)
                    at = slice(here + step, here + step + PAIR)
                    total += part * weights[:, at].astype(F32)
                    out[:, at] = part
        for source, listed in zip(refs[:count], down_places):
            for owner, there, here, width in listed:
                part = source[owner, :, there : there + width].astype(F32)
                out_down[:, here : here + width] = part
        for owner, there, here, width in out_places:
            part = refs[count - 1][owner, :, there : there + width].astype(F32)
            out_out[:, here : here + width] = part
        out_gain[...] = row(jnp.sum(total, 1, keepdims=True)) / gain[...].astype(F32)

    return kernel_call(
        body,
        "join_ff",
        [*sums, w_gate_up, gain],
        out_shape=[
            jax.ShapeDtypeStruct((rows, total_width), F32),
            jax.ShapeDtypeStruct((1, rows), F32),
            jax.ShapeDtypeStruct((rows, total_width // 2), F32),
            jax.ShapeDtypeStruct((rows, sum(p[3] for p in out_places)), F32),
        ],
    )


def join_qkv(sums, w_qkv, gain, qkv_places):
    rows, total_width = w_qkv.shape

    def body(source, weights, gain, out, out_gain):
        total = jnp.zeros((rows, PAIR), F32)
        for owner, there, here, width in qkv_places:
            part = source[owner, :, there : there + width].astype(F32)
            total += part * weights[:, here : here + width].astype(F32)
            out[:, here : here + width] = part
        out_gain[...] = row(jnp.sum(total, 1, keepdims=True)) / gain[...].astype(F32)

    return kernel_call(
        body,
        "join_qkv",
        [sums, w_qkv, gain],
        out_shape=[
            jax.ShapeDtypeStruct((rows, total_width), F32),
            jax.ShapeDtypeStruct((1, rows), F32),
        ],
    )


def flip(index, offset):
    weight = 1
    while weight <= offset:
        if offset & weight:
            index = index + weight - 2 * weight * ((index // weight) % 2)
        weight *= 2
    return index


def greet(partners):
    barrier = pltpu.get_barrier_semaphore()
    for partner in partners:
        pl.semaphore_signal(barrier, inc=1, device_id=partner, device_id_type=MESH)
    pl.semaphore_wait(barrier, len(partners))


def here():
    return lax.axis_index("seq"), lax.axis_index("core")


def bits_of(seqs):
    return [1 << bit for bit in range(seqs.bit_length() - 1)]


def cube_partners(seqs):
    me, core = here()
    partners = [{"seq": flip(me, bit), "core": core} for bit in bits_of(seqs)]
    return partners + [{"seq": me, "core": 1 - core}]


def all_partners(seqs):
    me, core = here()
    return [
        {"seq": flip(me, step), "core": core if same else 1 - core}
        for step in range(seqs)
        for same in (True, False)
        if step or not same
    ]


def orders_of(seqs):
    bits = bits_of(seqs)
    return [bits, bits[1:] + bits[:1]]


def remote(source, target, sems, at, device):
    return pltpu.make_async_remote_copy(
        src_ref=source,
        dst_ref=target,
        send_sem=sems[0].at[at],
        recv_sem=sems[1].at[at],
        device_id=device,
        device_id_type=MESH,
    )


def push(*where):
    copy = remote(*where)
    copy.start()
    return copy


def loads(sources, rooms, sems):
    copies = []
    for i, (source, room) in enumerate(zip(sources, rooms)):
        if isinstance(source, tuple):
            source = source[0].at[:, pl.ds(source[1], source[2])]
        copies.append(pltpu.make_async_copy(source, room, sems.at[i]))
    return copies


def like(*arrays):
    return [pltpu.VMEM(array.shape, array.dtype) for array in arrays]


def pair_sems(*shape):
    return [pltpu.SemaphoreType.DMA(shape)] * 2


def spread_scratch(seqs):
    return pair_sems(2, seqs) + pair_sems(2, seqs) + [pltpu.SemaphoreType.DMA]


class Spread:
    def __init__(self, own, out, scratch, rows=None):
        self.own, self.out = own, out
        self.rows = rows or pl.ds(0, own.shape[0])
        self.across, self.aside, self.local = scratch[0:2], scratch[2:4], scratch[4]
        self.me, self.core = here()
        self.half = out.shape[-1] // 2
        self.orders = orders_of(out.shape[1])
        self.phases = len(self.orders[0])

    def columns(self, ref, stream):
        return ref.at[self.rows, pl.ds(stream * self.half, self.half)]

    def place(self, offset, stream):
        return self.columns(self.out.at[self.core, flip(self.me, offset)], stream)

    def block(self, offset, stream):
        return self.place(offset, stream) if offset else self.columns(self.own, stream)

    def kept(self):
        return pltpu.make_async_copy(
            self.own.at[self.rows], self.out.at[self.core, self.me, self.rows], self.local
        )

    def swap(self, offset, stream):
        sibling = {"seq": self.me, "core": 1 - self.core}
        return remote(
            self.block(offset, stream),
            self.place(offset, stream),
            self.aside,
            (stream, offset),
            sibling,
        )

    def held(self, phase, stream):
        offsets = [0]
        for bit in self.orders[stream][:phase]:
            offsets += [offset + bit for offset in offsets]
        return offsets

    def moves(self, phase):
        found = []
        for stream in range(2):
            bit = self.orders[stream][phase]
            partner = {"seq": flip(self.me, bit), "core": self.core}
            for offset in self.held(phase, stream):
                copy = remote(
                    self.block(offset, stream),
                    self.place(offset, stream),
                    self.across,
                    (stream, offset + bit),
                    partner,
                )
                found.append((copy, offset + bit, stream))
        return found

    def begin(self):
        self.kept().start()
        for copy, _, _ in self.moves(0):
            copy.start()
        for stream in range(2):
            self.swap(0, stream).start()

    def arrive(self, phase):
        for copy, offset, stream in self.moves(phase):
            copy.wait_recv()
            self.swap(offset, stream).start()

    def step(self, phase):
        self.arrive(phase - 1)
        for copy, _, _ in self.moves(phase):
            copy.start()

    def finish(self):
        self.arrive(self.phases - 1)
        for phase in range(self.phases):
            for copy, _, _ in self.moves(phase):
                copy.wait_send()
        for stream in range(2):
            for offset in self.held(self.phases, stream):
                self.swap(offset, stream).wait()
        self.kept().wait()


def fold_rooms(seqs, tokens, width, made=True):
    return [
        pltpu.VMEM((seqs, tokens, width), BF),
        pltpu.VMEM((seqs, tokens, width) if made else (16, PAIR), BF),
        pltpu.VMEM((seqs, tokens, width), BF),
        pltpu.VMEM((2, seqs, tokens, width // 2), BF),
    ]


def fold_sems(seqs):
    return [pltpu.SemaphoreType.DMA((2,))] + pair_sems(seqs) + pair_sems(2, seqs)


class Fold:
    def __init__(self, terms, rooms, sems, rows, make=None):
        self.terms, self.make = terms, make
        self.own, self.give, self.total, self.got = rooms
        self.local, self.aside, self.across = sems[0], sems[1:3], sems[3:5]
        self.rows = rows
        self.me, self.core = here()
        self.seqs = self.total.shape[0]
        self.half = self.total.shape[-1] // 2
        self.orders = orders_of(self.seqs)
        self.phases = len(self.orders[0])

    def taken(self, mine):
        core, room = (self.core, self.own) if mine else (1 - self.core, self.give)
        return pltpu.make_async_copy(
            self.terms.at[core, :, self.rows],
            room.at[:, self.rows],
            self.local.at[1 if mine else 0],
        )

    def fill(self, room, core, at):
        width = room.shape[-1]
        tile = min(2 * BLOCK, width)

        def one(j, carry):
            columns = pl.ds(pl.multiple_of(j * tile, tile), tile)
            value = self.make(core, at, self.rows, columns)
            if self.terms is not None:
                value = value + room[at, self.rows, columns].astype(F32)
            room[at, self.rows, columns] = value.astype(BF)
            return carry

        lax.fori_loop(0, width // tile, one, 0)

    def swap(self, offset):
        at = flip(self.me, offset)
        source = self.give.at[at] if self.make else self.terms.at[1 - self.core, at]
        return remote(
            source.at[self.rows],
            self.total.at[at, self.rows],
            self.aside,
            (offset,),
            {"seq": self.me, "core": 1 - self.core},
        )

    def columns(self, stream):
        return pl.ds(stream * self.half, self.half)

    def moves(self, phase, stream, only=None):
        bit = self.orders[stream][phase]
        done = sum(self.orders[stream][:phase])
        partner = {"seq": flip(self.me, bit), "core": self.core}
        return [
            (
                remote(
                    self.total.at[flip(self.me, offset), self.rows, self.columns(stream)],
                    self.got.at[stream, offset, self.rows],
                    self.across,
                    (stream, offset),
                    partner,
                ),
                offset,
            )
            for offset in range(self.seqs - 1, -1, -1)
            if offset & bit and not offset & done and only in (None, offset)
        ]

    def add(self, work):
        count = self.rows.size
        step = min(32, count)

        def one(i, carry):
            work(pl.ds(pl.multiple_of(self.rows.start + i * step, step), step))
            return carry

        lax.fori_loop(0, count // step, one, 0)

    def load(self):
        if self.terms is not None:
            if self.make:
                self.taken(False).start()
            self.taken(True).start()

    def begin(self):
        if self.make and self.terms is not None:
            self.taken(False).wait()
        for offset in range(self.seqs - 1, -1, -1):
            if self.make:
                self.fill(self.give, 1 - self.core, flip(self.me, offset))
            self.swap(offset).start()

    def first(self):
        if self.terms is not None:
            self.taken(True).wait()
        for offset in range(self.seqs - 1, -1, -1):
            at = flip(self.me, offset)
            if self.make:
                self.fill(self.own, self.core, at)
            self.swap(offset).wait_recv()

            def add_sibling(rows, at=at):
                both = self.total[at, rows, :].astype(F32) + self.own[at, rows, :].astype(F32)
                self.total[at, rows, :] = both.astype(BF)

            self.add(add_sibling)
            for stream in range(2):
                for copy, _ in self.moves(0, stream, offset):
                    copy.start()

    def receive(self, phase, stream):
        bit = self.orders[stream][phase]
        for copy, offset in self.moves(phase, stream):
            copy.wait_recv()
            at = flip(self.me, offset - bit)

            def add_got(rows, at=at, offset=offset):
                columns = self.columns(stream)
                both = self.total[at, rows, columns].astype(F32) + self.got[
                    stream, offset, rows, :
                ].astype(F32)
                self.total[at, rows, columns] = both.astype(BF)

            self.add(add_got)

    def step(self, phase):
        for stream in range(2):
            self.receive(phase - 1, stream)
            for copy, _ in self.moves(phase, stream):
                copy.start()

    def last(self):
        for stream in range(2):
            self.receive(self.phases - 1, stream)

    def result(self, rows):
        return self.total[self.me, rows, :].astype(F32)

    def settle(self):
        for offset in range(self.seqs):
            self.swap(offset).wait_send()
        for phase in range(self.phases):
            for stream in range(2):
                for copy, _ in self.moves(phase, stream):
                    copy.wait_send()


def halves(count):
    return [pl.ds(i * (count // 2), count // 2) for i in range(2)]


def fold_then_spread(folds, spreads, work, aside=lambda: None):
    phases = folds[0].phases
    for fold in folds:
        fold.begin()
        fold.first()
    aside()
    for phase in range(1, phases):
        for fold in folds:
            fold.step(phase)
            aside()
    for fold, spread in zip(folds, spreads):
        fold.last()
        fold.add(work)
        spread.begin()
        aside()
    for phase in range(1, phases):
        for spread in spreads:
            spread.step(phase)
            aside()
    for spread in spreads:
        spread.finish()
    for fold in folds:
        fold.settle()


def by_rows(count, work):
    step = min(32, count)

    def one(i, carry):
        work(pl.ds(pl.multiple_of(i * step, step), step))
        return carry

    lax.fori_loop(0, count // step, one, 0)


def deal_scratch(pieces, seqs):
    blocks = [piece.shape[-2:] for piece in pieces]
    return (
        pair_sems(len(pieces), 2 * seqs)
        + [pltpu.SemaphoreType.DMA((2, len(pieces)))]
        + [pltpu.VMEM(block, piece.dtype) for block, piece in zip(blocks, pieces)]
    )


class Deal:
    def __init__(self, pieces, outs, scratch, core_first=False):
        self.pieces, self.outs = pieces, outs
        self.sems, self.local, self.rooms = scratch[:2], scratch[2], scratch[3:]
        self.me, self.core = here()
        self.core_first = core_first
        self.seqs = outs[0].shape[1 if core_first else 0]

    def piece(self, i, seq, core):
        piece, out = self.pieces[i], self.outs[i]
        return piece.at[seq, core] if len(piece.shape) == len(out.shape) else piece

    def place(self, i):
        out = self.outs[i]
        return out.at[self.core, self.me] if self.core_first else out.at[self.me, self.core]

    def copy(self, i, step, same):
        to_seq = flip(self.me, step)
        to_core = self.core if same else 1 - self.core
        return remote(
            self.piece(i, to_seq, to_core),
            self.place(i),
            self.sems,
            (i, 2 * step + (0 if same else 1)),
            {"seq": to_seq, "core": to_core},
        )

    def copies(self):
        return [
            self.copy(i, step, same)
            for i in range(len(self.pieces))
            for step in range(self.seqs)
            for same in (True, False)
            if step or not same
        ]

    def entering(self):
        return [
            pltpu.make_async_copy(
                self.piece(i, self.me, self.core), self.rooms[i], self.local.at[0, i]
            )
            for i in range(len(self.rooms))
        ]

    def leaving(self):
        return [
            pltpu.make_async_copy(
                self.rooms[i] if self.rooms else self.piece(i, self.me, self.core),
                self.place(i),
                self.local.at[1, i],
            )
            for i in range(len(self.outs))
        ]

    def begin(self):
        for copy in self.copies() + self.entering():
            copy.start()
        for copy in self.entering():
            copy.wait()
        for copy in self.leaving():
            copy.start()

    def arrive_from(self, step):
        if step:
            self.copy(0, step, True).wait_recv()
        else:
            for copy in self.leaving():
                copy.wait()
        self.copy(0, step, False).wait_recv()

    def arrive(self):
        for copy in self.copies():
            copy.wait_recv()
        for copy in self.leaving():
            copy.wait()

    def settle(self):
        for copy in self.copies():
            copy.wait_send()

    def finish(self):
        self.arrive()
        self.settle()


class Ring:
    def __init__(self, whole, sems, part):
        self.whole, self.sems, self.part = whole, sems, part
        self.count = whole.shape[0]
        self.chip = lax.axis_index("z")

    def hop(self, i):
        block = self.whole.at[lax.rem(self.chip + self.count - i, self.count)]
        block = block if self.part is None else block.at[self.part]
        following = lax.rem(self.chip + 1, self.count)
        return remote(block, block, self.sems, (i,), {"z": following})

    def preceding(self):
        return {"z": lax.rem(self.chip + self.count - 1, self.count)}

    def begin(self):
        self.hop(0).start()

    def step(self, i):
        self.hop(i - 1).wait_recv()
        if i < self.count - 1:
            self.hop(i).start()

    def settle(self):
        for i in range(self.count - 1):
            self.hop(i).wait_send()


def deal(pieces, number, near=False):
    count = len(pieces)
    seqs = pieces[0].shape[0]

    def body(*refs):
        greet(all_partners(seqs))
        work = Deal(refs[:count], refs[count : 2 * count], refs[2 * count :])
        work.begin()
        work.finish()

    return kernel_call(
        body,
        "deal",
        [*pieces],
        number,
        in_specs=[ANYWHERE] * count,
        out_specs=[ANYWHERE] * count,
        out_shape=[jax.ShapeDtypeStruct(piece.shape, BF) for piece in pieces],
        scratch_shapes=deal_scratch(pieces, seqs),
    )


def cut_into(out, parts):
    for source, places in parts:
        for owner, there, begin, width in places:
            part = source[:, begin : begin + width]
            out[owner // 2, owner % 2, :, there : there + width] = part


def column(row):
    count = row.shape[1]
    shape = (count, count)
    wide = jnp.broadcast_to(row.astype(F32), shape)
    same = lax.broadcasted_iota(jnp.int32, shape, 0) == lax.broadcasted_iota(jnp.int32, shape, 1)
    return jnp.sum(jnp.where(same, wide, 0.0), 1, keepdims=True)


def row(values):
    count = values.shape[0]
    shape = (count, count)
    wide = jnp.broadcast_to(values, shape)
    same = lax.broadcasted_iota(jnp.int32, shape, 0) == lax.broadcasted_iota(jnp.int32, shape, 1)
    return jnp.sum(jnp.where(same, wide, 0.0), 0, keepdims=True)


def frequencies():
    half = HEAD_DIM // 2
    inverse = ROPE_BASE ** (-2.0 * np.arange(half) / HEAD_DIM)
    return np.tile(inverse.astype(np.float32), (8, PAIR // half))


def start(arrays, gains, positions, plans, blocks, seqs, chips, number):
    tokens, w_qkv = arrays[0], arrays[2]
    count, width = tokens.shape
    rows = w_qkv.shape[0]
    (qkv_places, out_places, attend_cols), chunks = plans
    shape = (seqs, 2, rows)
    cuts = [shape + (cols,) for _, _, cols in chunks]
    more = len(chunks) - 1

    def body(*refs):
        sources, places, inverse = refs[:6], refs[8], refs[9]
        acts, whole, piece, tables, gains_out, *moved = refs[10:17]
        cut_out = refs[17 : 17 + more]
        scratch = refs[17 + more :]
        rooms, (sem, attend_cut), scratch = scratch[:6], scratch[6:8], scratch[8:]
        ff_cut, scratch = scratch[: 1 + more], scratch[1 + more :]
        turned, own, scratch = scratch[:2], scratch[2], scratch[3:]
        out_sem, left_sem, scratch = scratch[0], scratch[1], scratch[2:]
        ring_sems, scratch = scratch[: 2 * seqs], scratch[2 * seqs :]
        deal_sems, spread_sems, gain_sems = scratch[:12], scratch[12:17], scratch[17:19]
        own_places, all_places, all_tables, own_gains, all_gains, gain_rows = scratch[19:]
        coming = loads(sources, rooms, sem)
        for i in (2, 3, 0, 4, 5, 1):
            coming[i].start()
        own_places[...] = jnp.broadcast_to(places[...], own_places.shape)
        for i in range(2):
            one = jnp.broadcast_to(refs[6 + i][...].astype(F32), (8, rows))
            own_gains[:, i * rows : (i + 1) * rows] = one
        if 2 * rows < PAIR:
            own_gains[:, 2 * rows :] = jnp.zeros((8, PAIR - 2 * rows), F32)
        me_chip = lax.axis_index("z")
        rings = [
            Ring(whole, ring_sems[2 * i : 2 * i + 2], flip(lax.axis_index("seq"), i))
            for i in range(seqs)
        ]
        greet(all_partners(seqs) + [rings[0].preceding()])
        gain_deal = Deal([own_gains], [all_gains.at[me_chip]], deal_sems[9:12])
        gain_deal.begin()
        coming[2].wait()
        coming[3].wait()
        cut_into(attend_cut, [(rooms[2], qkv_places), (rooms[3], out_places)])
        attend_deal = Deal([attend_cut], [whole.at[me_chip]], deal_sems[:3])
        attend_deal.begin()
        place_deal = Deal([own_places], [all_places], deal_sems[3:6], True)
        place_deal.begin()
        gain_deal.arrive()
        gain_ring = Ring(all_gains, gain_sems, None)
        gain_ring.begin()
        attend_deal.arrive_from(0)
        rings[0].begin()
        coming[0].wait()
        for outer, inner, size in blocks:
            turned[0][:, inner : inner + size] = rooms[0][:, outer : outer + size]
        for i in range(1, max(seqs, chips)):
            if i < chips:
                gain_ring.step(i)
            if i < seqs:
                attend_deal.arrive_from(i)
                rings[i].begin()
        for chip in range(chips):
            for seq in range(seqs):
                for core in range(2):
                    begin = ((chip * seqs + seq) * 2 + core) * rows
                    for i in range(2):
                        gain_rows[i, :, begin : begin + rows] = all_gains[
                            chip, seq, core, :, i * rows : (i + 1) * rows
                        ]

        def norm(at):
            values = turned[0][at, :].astype(F32)
            own[at, :] = (values * norm_scale(values) * gain_rows[0, :1, :]).astype(BF)

        by_rows(count, norm)
        spreading = Spread(own, acts, spread_sems)
        spreading.begin()
        coming[4].wait()
        coming[5].wait()
        for out, (pair, single, _) in zip(ff_cut, chunks):
            cut_into(out, [(rooms[4], pair), (rooms[5], single)])
        coming[1].wait()
        for outer, inner, size in blocks:
            turned[1][:, inner : inner + size] = rooms[1][:, outer : outer + size]
        going = loads(list(turned) + list(ff_cut[1:]), list(moved) + list(cut_out), out_sem)
        for copy in going:
            copy.start()
        for ring in rings[: seqs - 1]:
            ring.step(1)
        for phase in range(1, spreading.phases):
            spreading.step(phase)
        rings[-1].step(1)
        ff_deal = Deal([ff_cut[0]], [piece], deal_sems[6:9])
        ff_deal.begin()
        place_deal.arrive()

        def table(i, carry):
            at, seq = lax.div(i, seqs), lax.rem(i, seqs)
            angles = column(all_places[at, seq][:1]) * inverse[:1, :]
            lane = lax.broadcasted_iota(jnp.int32, angles.shape, 1)
            cosine = lane % HEAD_DIM < HEAD_DIM // 2
            all_tables[at, seq] = jnp.where(cosine, jnp.cos(angles), jnp.sin(angles))
            return carry

        for i in range(1, chips):
            for ring in rings:
                if i > 1:
                    ring.step(i)
            if i <= 2:
                lax.fori_loop((i - 1) * seqs, i * seqs, table, 0)
            if i == 2:
                spreading.finish()
        leaving = loads([all_tables, gain_rows], [tables, gains_out], left_sem)
        for copy in leaving:
            copy.start()
        for ring in rings:
            ring.settle()
        attend_deal.settle()
        place_deal.settle()
        ff_deal.finish()
        gain_ring.settle()
        gain_deal.settle()
        for copy in going + leaving:
            copy.wait()

    like_tokens = jax.ShapeDtypeStruct((count, width), BF)
    deal_sem = pair_sems(1, 2 * seqs) + [pltpu.SemaphoreType.DMA((2, 1))]
    return kernel_call(
        body,
        "start",
        [*arrays, *gains, positions, frequencies()],
        number,
        in_specs=[ANYWHERE] * 6 + [LOCAL] * 4,
        out_specs=[ANYWHERE] * (7 + more),
        out_shape=[
            jax.ShapeDtypeStruct((2, seqs, count, width), BF),
            jax.ShapeDtypeStruct((chips,) + shape + (attend_cols,), BF),
            jax.ShapeDtypeStruct(cuts[0], BF),
            jax.ShapeDtypeStruct((2, seqs, count, PAIR), F32),
            jax.ShapeDtypeStruct((2, 8, width), F32),
            like_tokens,
            like_tokens,
        ]
        + [jax.ShapeDtypeStruct(cut, BF) for cut in cuts[1:]],
        scratch_shapes=like(*arrays)
        + [pltpu.SemaphoreType.DMA((6,)), pltpu.VMEM(shape + (attend_cols,), BF)]
        + [pltpu.VMEM(cut, BF) for cut in cuts]
        + [pltpu.VMEM((count, width), BF)] * 3
        + [pltpu.SemaphoreType.DMA((2 + more,)), pltpu.SemaphoreType.DMA((2,))]
        + pair_sems(chips) * seqs
        + deal_sem * 4
        + spread_scratch(seqs)
        + pair_sems(chips)
        + [pltpu.VMEM((8, count), jnp.int32), pltpu.VMEM((2, seqs, 8, count), jnp.int32)]
        + [pltpu.VMEM((2, seqs, count, PAIR), F32), pltpu.VMEM((8, PAIR), F32)]
        + [pltpu.VMEM((chips, seqs, 2, 8, PAIR), F32), pltpu.VMEM((2, 8, width), F32)],
    )


def two_way_scratch(seqs, count, width):
    return (
        [pltpu.VMEM((count, width), BF)]
        + fold_rooms(seqs, count, width)
        + fold_sems(seqs) * 2
        + spread_scratch(seqs) * 2
    )


def two_way(given, out, scratch, make):
    own, rooms, sems = scratch[0], scratch[1:5], scratch[5:]
    parts = halves(own.shape[0])
    folds = [
        Fold(given, rooms, sems[5 * i : 5 * i + 5], rows, make) for i, rows in enumerate(parts)
    ]
    sems = sems[10:]
    spreads = [Spread(own, out, sems[5 * i : 5 * i + 5], rows) for i, rows in enumerate(parts)]
    for fold in folds:
        fold.load()
    return folds, spreads, own


def product(left, right, seqs, count):
    def make(core, at, rows, columns):
        begin = pl.multiple_of((core * seqs + at) * count + rows.start, rows.size)
        return nt(left[pl.ds(begin, rows.size), :], right[columns, :])

    return make


def middle_acts(attended, weights, tokens, gains, seqs, number):
    count, width = tokens.shape
    cols = attended.shape[1]
    begin = weights.shape[1] - cols

    def body(left_in, given, source_in, gain, middle, out, left, right, source, sems, *scratch):
        coming = loads([left_in, (given, begin, cols), source_in], [left, right, source], sems)
        for copy in coming:
            copy.start()
        folds, spreads, own = two_way(None, out, scratch, product(left, right, seqs, count))
        greet(cube_partners(seqs))
        for copy in coming:
            copy.wait()

        def norm(rows):
            values = source[rows, :].astype(F32) + folds[0].result(rows)
            middle[rows, :] = values
            own[rows, :] = (values * norm_scale(values) * gain[1, :1, :]).astype(BF)

        fold_then_spread(folds, spreads, norm)

    return kernel_call(
        body,
        "middle_acts",
        [attended, weights, tokens, gains],
        number,
        in_specs=[ANYWHERE] * 3 + [LOCAL],
        out_specs=[LOCAL, ANYWHERE],
        out_shape=[
            jax.ShapeDtypeStruct((count, width), F32),
            jax.ShapeDtypeStruct((2, seqs, count, width), BF),
        ],
        scratch_shapes=like(attended)
        + [pltpu.VMEM((width, cols), BF)]
        + like(tokens)
        + [pltpu.SemaphoreType.DMA((3,))]
        + two_way_scratch(seqs, count, width),
    )


def middle_grad(terms, grad_both, cotangent, middle, hidden, weights, gains, number):
    _, seqs, count, width = terms.shape
    tokens = hidden[0].shape[0]
    n = len(hidden)
    block = min(BLOCK, tokens)
    tile = min(2 * BLOCK, width)
    blocks = tokens // block
    parts = [h.shape[1] for h in hidden]

    def body(given, *refs):
        sources, down = refs[: 3 + n], refs[3 + n : 3 + 2 * n]
        gain, grad, out, products = refs[3 + 2 * n : 7 + 2 * n]
        scratch = refs[7 + 2 * n :]
        left, upstream, values = scratch[:3]
        units, room, right = scratch[3 : 3 + n], scratch[3 + n : 3 + 2 * n], scratch[3 + 2 * n]
        stage, sems, leaving = scratch[4 + 2 * n : 7 + 2 * n]
        columns = [(down[i], 2 * parts[i], parts[i]) for i in range(n)]
        coming = loads(
            [sources[0], (down[-1], 0, 2 * parts[-1]), *sources[3:], *columns, *sources[1:3]],
            [left, right, *units, *room, upstream, values],
            sems,
        )
        for copy in coming[:2]:
            copy.start()
        make = product(left, right, seqs, count)
        folds, spreads, own = two_way(given, out, scratch[7 + 2 * n :], make)
        for copy in coming[2:]:
            copy.start()
        greet(cube_partners(seqs))
        for copy in coming[:2]:
            copy.wait()

        def leave(i):
            rows = pl.ds(i * block, block)
            return pltpu.make_async_copy(stage.at[i % 2], products.at[rows], leaving.at[i % 2])

        def multiply(i):
            if i == 0:
                for copy in coming[2:]:
                    copy.wait()
            if i >= 2:
                leave(i - 2).wait()

            def one(j, carry):
                columns = pl.ds(pl.multiple_of(j * tile, tile), tile)
                total = sum(
                    nt(units[k][pl.ds(i * block, block), :], room[k][columns, :])
                    for k in range(n)
                )
                stage[i % 2, :, columns] = total.astype(BF)
                return carry

            lax.fori_loop(0, width // tile, one, 0)
            leave(i).start()

        left_over = list(range(blocks))

        def aside():
            for _ in range(2 if len(left_over) == blocks else max(1, blocks // 8)):
                if left_over:
                    multiply(left_over.pop(0))

        def back(rows):
            held = values[rows, :]
            scale = norm_scale(held)
            result = upstream[rows, :].astype(F32) + norm_back(
                folds[0].result(rows) * gain[1, :1, :], held * scale, scale
            )
            grad[rows, :] = result
            own[rows, :] = result.astype(BF)

        fold_then_spread(folds, spreads, back, aside)
        while left_over:
            multiply(left_over.pop(0))
        for i in range(max(0, blocks - 2), blocks):
            leave(i).wait()

    return kernel_call(
        body,
        "middle_grad",
        [terms, grad_both, cotangent, middle, *hidden, *weights, gains],
        number,
        in_specs=[ANYWHERE] * (4 + 2 * n) + [LOCAL],
        out_specs=[LOCAL, ANYWHERE, ANYWHERE],
        out_shape=[
            jax.ShapeDtypeStruct((count, width), F32),
            jax.ShapeDtypeStruct(terms.shape, BF),
            jax.ShapeDtypeStruct((tokens, width), BF),
        ],
        scratch_shapes=like(grad_both, cotangent, middle, *hidden)
        + [pltpu.VMEM((width, part), BF) for part in parts]
        + [pltpu.VMEM((width, 2 * parts[-1]), BF), pltpu.VMEM((2, block, width), BF)]
        + [pltpu.SemaphoreType.DMA((4 + 2 * n,)), pltpu.SemaphoreType.DMA((2,))]
        + two_way_scratch(seqs, count, width),
    )


def input_grad(grad_mixed, weights, tokens, grad_middle, gains, seqs, number):
    count, width = tokens.shape
    cols = grad_mixed.shape[1]

    def body(left_in, given, source_in, held_in, gain, out, *scratch):
        left, right, source, held, sems, *scratch = scratch
        coming = loads(
            [left_in, (given, 0, cols), source_in, held_in], [left, right, source, held], sems
        )
        for copy in coming:
            copy.start()
        make = product(left, right, seqs, count)
        sems = scratch[4:]
        folds = [
            Fold(None, scratch[:4], sems[5 * i : 5 * i + 5], rows, make)
            for i, rows in enumerate(halves(count))
        ]
        greet(cube_partners(seqs))
        for copy in coming:
            copy.wait()
        for fold in folds:
            fold.begin()
            fold.first()
        for phase in range(1, folds[0].phases):
            for fold in folds:
                fold.step(phase)

        def back(rows):
            values = source[rows, :].astype(F32)
            scale = norm_scale(values)
            grad = folds[0].result(rows) * gain[0, :1, :]
            out[rows, :] = held[rows, :] + norm_back(grad, values * scale, scale)

        for fold in folds:
            fold.last()
            fold.add(back)
        for fold in folds:
            fold.settle()

    return kernel_call(
        body,
        "input_grad",
        [grad_mixed, weights, tokens, grad_middle, gains],
        number,
        in_specs=[ANYWHERE] * 4 + [LOCAL],
        out_specs=LOCAL,
        out_shape=jax.ShapeDtypeStruct((count, width), F32),
        scratch_shapes=like(grad_mixed)
        + [pltpu.VMEM((width, cols), BF)]
        + like(tokens, grad_middle)
        + [pltpu.SemaphoreType.DMA((4,))]
        + fold_rooms(seqs, count, width)
        + fold_sems(seqs) * 2,
    )


class Order:
    def __init__(self):
        self.latest = None

    def enter(self, values):
        if self.latest is None:
            return values
        return lax.optimization_barrier((values, self.latest))[0]

    def run(self, work, *values):
        result = work(*self.enter(values))
        self.latest = jax.tree.leaves(result)
        return result

    def take(self, values):
        if self.latest is not None:
            values = lax.optimization_barrier((values, self.latest))[0]
        self.latest = jax.tree.leaves(values)
        return values


def norm_scale(values):
    return lax.rsqrt(jnp.mean(values * values, -1, keepdims=True) + EPS)


def norm_back(grad, normed, scale):
    return scale * (grad - normed * jnp.mean(grad * normed, -1, keepdims=True))


def per_device(
    mesh, tokens, positions, w_qkv, w_out, gain_attn, w_gate_up, w_down, gain_mlp, cotangent
):
    order = Order()
    seqs, chips = mesh.shape["seq"], mesh.shape["z"]
    owners = 2 * seqs
    token_count, width = tokens.shape[1:]
    ff_width = w_down.shape[1]
    rows = w_qkv.shape[0]
    head_cols = width // owners
    ff_cols = ff_width // owners
    parts = chunk_widths(ff_cols)
    last = len(parts) - 1
    blocks = blocks_in(rows, seqs, chips)

    def by_place(piece):
        return piece.reshape(seqs, 2, rows, -1)

    def gathered(piece):
        piece = order.enter(piece).reshape(seqs, 2 * rows, -1)
        return lax.all_gather(piece, "z", axis=0, tiled=False)

    def flat(value):
        return order.take(value).reshape(width, -1)

    def summed(term):
        split = order.enter(term).reshape(chips, seqs, 2 * rows, -1)
        return lax.psum_scatter(split, "z", scatter_dimension=0, tiled=False)

    def rounded(left, right):
        return tn(left, right).astype(BF)

    qkv_places = list(qkv_columns(owners, head_cols))
    out_places = [(o, 3 * head_cols, o * head_cols, head_cols) for o in range(owners)]
    gate_up_places, down_places = ff_columns(owners, ff_cols)
    chunks = [
        (pair, single, 3 * part) for pair, single, part in zip(gate_up_places, down_places, parts)
    ]
    acts, attend_whole, ff_piece, table, gains, tokens_in, upstream_own, *ff_cut = order.run(
        lambda *a: start(
            a[:6],
            a[6:8],
            a[8],
            ((qkv_places, out_places, 4 * head_cols), chunks),
            blocks,
            seqs,
            chips,
            1,
        ),
        tokens[0],
        cotangent[0],
        w_qkv,
        w_out,
        w_gate_up,
        w_down,
        gain_attn[None],
        gain_mlp[None],
        positions,
    )
    acts = acts.reshape(-1, width)
    attend_whole = attend_whole.reshape(width, -1)
    table = table.reshape(-1, PAIR)
    ff_coming = [gathered(ff_piece)]

    qkv_cols = 3 * head_cols
    mixed = order.run(lambda a, w: nn(a, w[:, :qkv_cols]), acts, attend_whole)
    qkv, attended, logs, upstream, *ff_pieces = order.run(
        lambda m, t, u, *given: attend(m, t, SpreadBeside(seqs, u, given), 2, 3),
        mixed,
        table,
        upstream_own,
        *ff_cut,
    )
    ff_coming += [gathered(piece) for piece in ff_pieces]
    upstream = upstream.reshape(-1, width)
    middle, acts_mid = order.run(
        lambda a, w, x, g: middle_acts(a, w, x, g, seqs, 4),
        attended,
        attend_whole,
        tokens_in,
        gains,
    )
    acts_mid = acts_mid.reshape(-1, width)

    def feed_hidden(both):
        part = both.shape[1] // 2
        gate, up = both[:, :part], both[:, part:]
        return (gate * jax.nn.sigmoid(gate) * up).astype(BF)

    def feed_back(grad_hidden, both):
        part = both.shape[1] // 2
        gate, up = both[:, :part], both[:, part:]
        sigma = jax.nn.sigmoid(gate)
        grad_gate = grad_hidden * up * sigma * (1.0 + gate * (1.0 - sigma))
        grad_up = grad_hidden * gate * sigma
        return jnp.concatenate([grad_gate.astype(BF), grad_up.astype(BF)], 1)

    def both_terms(left, right, left_two, right_two):
        return [rounded(left, right), rounded(left_two, right_two)]

    def add_nt(left, right, total=None):
        result = nt(left, right)
        return (result if total is None else result + total.astype(F32)).astype(BF)

    ff_sums, hiddens, wholes = [], [], []
    norm_mid_terms = ()
    for chunk, part in enumerate(parts):
        cols = 2 * part
        whole = flat(ff_coming[chunk])
        both = order.run(lambda a, w: nn(a, w[:, :cols]), acts_mid, whole)
        hidden = order.run(feed_hidden, both)
        hiddens.append(hidden)
        wholes.append(whole)
        grad_hidden = order.run(lambda a, w: nn(a, w[:, cols:]), upstream, whole)
        grad_both = order.run(feed_back, grad_hidden, both)
        terms = order.run(both_terms, acts_mid, grad_both, upstream, hidden)
        if chunk < len(parts) - 1:
            ff_sums.append(summed(order.run(side_by_side, terms)))
        if chunk < len(parts) - 1:
            norm_mid_terms = (
                order.run(
                    lambda a, w, *t: add_nt(a, w[:, :cols], *t), grad_both, whole, *norm_mid_terms
                ),
            )

    grad_middle, grad_branch, outcome_terms = order.run(
        lambda *a: middle_grad(*a, 5),
        norm_mid_terms[0].reshape(2, seqs, token_count, width),
        grad_both,
        upstream_own,
        middle,
        hiddens,
        wholes,
        gains,
    )
    grad_branch = grad_branch.reshape(-1, width)

    terms.append(order.run(rounded, grad_branch, attended))
    ff_sums.append(summed(order.run(side_by_side, terms)))
    grad_attended = order.run(
        lambda a, w: nn(a, w[:, qkv_cols:]).astype(BF), grad_branch, attend_whole
    )
    first_rows = [by_place(order.take(value)) for value in ff_sums[:-1]]
    grad_mixed, outcome, *ff_dealt = order.run(
        lambda a, b, c, d, e, f, *given: attend_back(
            a, b, c, d, OutputBeside(seqs, e, f, given), 2, 6
        ),
        qkv,
        grad_attended,
        logs,
        table,
        outcome_terms.reshape(2, seqs, token_count, width),
        middle,
        *first_rows,
    )
    qkv_sum = summed(order.run(rounded, acts, grad_mixed))

    grad_inputs = order.run(
        lambda *a: input_grad(*a, seqs, 7),
        grad_mixed,
        attend_whole,
        tokens_in,
        grad_middle,
        gains,
    )
    last_rows = by_place(order.take(ff_sums[-1]))
    ff_dealt += order.run(lambda a: deal([a], 8), last_rows)
    out_at = [(o, 3 * parts[-1], o * head_cols, head_cols) for o in range(owners)]
    grad_gate_up, gain_two_sum, grad_down, grad_out = order.run(
        lambda w, g, *a: join_ff(a, w, g, gate_up_places, down_places, out_at),
        w_gate_up,
        gain_mlp[None],
        *[value.reshape(owners, rows, -1) for value in ff_dealt],
    )
    grad_inputs, outcome = order.run(lambda *a: outside(a, blocks), grad_inputs, outcome)
    qkv_rows = order.take(qkv_sum)
    (qkv_dealt,) = order.run(lambda a: deal([a], 9, True), by_place(qkv_rows))
    grad_qkv, gain_one_sum = order.run(
        lambda w, g, a: join_qkv(a, w, g, qkv_places),
        w_qkv,
        gain_attn[None],
        qkv_dealt.reshape(owners, rows, -1),
    )
    return (
        outcome[None],
        grad_inputs[None],
        grad_qkv,
        grad_out,
        gain_one_sum[0],
        grad_gate_up,
        grad_down,
        gain_two_sum[0],
    )


def solution(mesh):
    seqs, devices = mesh.shape["seq"], mesh.shape["fsdp"]
    parted = Mesh(mesh.devices.reshape(seqs, devices // 2, 2), ("seq", "z", "core"))
    tokens = P(("z", "core"), "seq", None)
    matrix = P(("seq", "z", "core"), None)
    vector = P(("seq", "z", "core"))
    return jax.shard_map(
        functools.partial(per_device, parted),
        mesh=parted,
        in_specs=(
            tokens,
            P(("z", "core"), "seq"),
            matrix,
            matrix,
            vector,
            matrix,
            matrix,
            vector,
            tokens,
        ),
        out_specs=(tokens, tokens, matrix, matrix, vector, matrix, matrix, vector),
        check_vma=False,
    )
```
